32 devices in a mesh: grp: 2 (over core), blk: 8 (over z, x), real: 2 (over y).
Axes of the slice: x: 2, y: 2, z: 4, core: 2. Of those that a mesh axis runs over, the one named last changes fastest.
Arguments:
- sky_data: float32 [32, 16, 8192], P('real', 'blk', 'grp'), may hold values from -6 to 6
- signal_prev: float32 [32, 16, 8192], P('real', 'blk', 'grp'), may hold values from -6 to 6
- noise_var: float32 [16, 8192], P('blk', 'grp'), may hold values from 1 to 16
- mask_flags: int32 [16, 8192], P('blk', 'grp'), may hold values 0 or 1
- cycle_table: int32 [16], P('blk'), may hold values from 0 to 15, each once
- m_table: int32 [32], replicated, may hold values from 0 to 4095, as said below
- spectrum: float32 [4096], P(('grp', 'real')), may hold values from 0.05 to 5
- legendre: bfloat16 [32, 4096, 16], P('blk', ('grp', 'real')), may hold values from -1.5 to 1.5
Outputs:
- wiener_alm: float32 [32, 2, 32, 4096], P(None, None, 'blk', ('grp', 'real'))
- signal_next: float32 [32, 16, 8192], P('real', 'blk', 'grp')
The draws below stay inside these ranges and needn't reach their ends.
Inputs may be any that keep to these rules, and one draw needn't show every extreme that they name: `m_table`: distinct orders; 0 and 4095 are always among them. `cycle_table`: each cycle number once.
All inputs are finite; a program needn't handle non-finite values. No bound on the sum of `mask_flags` on one device may be relied on, other than what follows from the above.
Results may differ from the reference program's by a relative error of at most 0.0063.
Values may be sent and summed in bfloat16 or wider, within the bound.
No kernel may reach another device: no remote copies, remote signals or barrier semaphores. Data moves between devices by JAX's collectives and lax.ppermute only.
A program may use at most 64 MiB of HBM per device.

```python
import math
import jax
import jax.numpy as jnp
from jax import lax

NPHI = 8192
LBAND = 4096
NREAL = 32
CYCLES = 16
MWIN = 32


def draw_m_table(key, part):
    first_key = jax.random.fold_in(key, 11)
    second_key = jax.random.fold_in(key, 12)
    middle_ids = jax.random.permutation(first_key, LBAND - 2)[:MWIN - 2].astype(jnp.int32) + 1
    values = jnp.concatenate([jnp.array([0, LBAND - 1], dtype=jnp.int32), middle_ids])
    shuffle = jax.random.permutation(second_key, MWIN)
    return values[shuffle].astype(jnp.int32)


def place_ends(values, stream_key, smallest, largest):
    index_at = [jax.random.randint(jax.random.fold_in(stream_key, axis), (), 0, length) for axis, length in enumerate(values.shape)]
    widest = values.shape.index(max(values.shape))
    next_to = index_at[:widest] + [(index_at[widest] + 1) % values.shape[widest]] + index_at[widest + 1:]
    return values.at[tuple(index_at)].set(smallest).at[tuple(next_to)].set(largest)


def block_scale(own_key, extent, cuts, smallest, high):
    def one(dim, blocks):
        draws = jax.random.uniform(jax.random.fold_in(jax.random.fold_in(own_key, 6), dim), (blocks,), jnp.float32, smallest / len(cuts), high / len(cuts))
        return jnp.repeat(jnp.exp(draws), extent[dim] // blocks).reshape((-1,) + (1,) * (len(extent) - dim - 1))

    gain = one(*cuts[0])
    for cut in cuts[1:]:
        gain = gain * one(*cut)
    return gain


def gaussian(stream_key, extent, width, reach, shards=(), kind=jnp.bfloat16):
    result = jax.random.normal(stream_key, extent, jnp.float32) * width
    if len(shards) > 0:
        result = block_scale(stream_key, extent, shards, -0.22, 0.18) * result
    return jnp.clip(result, min=-reach, max=reach).astype(kind)


def setup_inputs(seed: int = 0) -> dict:
    arg_keys = jax.random.split(jax.random.key(seed), 9)
    sky_data = gaussian(arg_keys[0], (NREAL, CYCLES, NPHI), 1.0, 6.0, ((0, 2), (1, 8), (2, 2)), jnp.float32)
    signal_prev = gaussian(arg_keys[1], (NREAL, CYCLES, NPHI), 1.0, 6.0, ((0, 2), (1, 8), (2, 2)), jnp.float32)
    noise_var = jnp.clip(jnp.exp(math.log(16.0) - 2.7725887 * jax.random.uniform(arg_keys[2], (CYCLES, NPHI), jnp.float32) ** block_scale(arg_keys[2], (CYCLES, NPHI), ((0, 8), (1, 2)), -0.2, 0.2)), 1.0, 16.0)
    mask_flags = place_ends((jax.random.randint(arg_keys[3], (CYCLES, NPHI), 0, 5) < 4).astype(jnp.int32), jax.random.fold_in(arg_keys[3], 1), 0, 1)
    cycle_table = jax.random.permutation(arg_keys[4], CYCLES).astype(jnp.int32)
    m_table = draw_m_table(jax.random.fold_in(arg_keys[8], 71), 0)
    spectrum = jnp.clip(jnp.exp(math.log(5.0) - 4.6051702 * jax.random.uniform(arg_keys[6], (LBAND,), jnp.float32) ** block_scale(arg_keys[6], (LBAND,), ((0, 4),), -0.2, 0.2)), 0.05, 5.0)
    legendre = gaussian(arg_keys[7], (MWIN, LBAND, CYCLES), CYCLES ** -0.5, 1.5, ((0, 8), (1, 4)))
    return dict(sky_data=sky_data, signal_prev=signal_prev, noise_var=noise_var, mask_flags=mask_flags, cycle_table=cycle_table, m_table=m_table, spectrum=spectrum, legendre=legendre)


def phase_tables(col_ids, mode_ids, cycle_len):
    product_ids = (col_ids[:, None] * mode_ids[None, :]) % cycle_len
    angles = product_ids.astype(jnp.float32) * (2.0 * math.pi / cycle_len)
    return jnp.cos(angles).astype(jnp.bfloat16), jnp.sin(angles).astype(jnp.bfloat16)


def cycle_offsets(cycle_ids, mode_ids, cycle_len):
    parity = (cycle_ids % 2).astype(jnp.float32)
    shifts = (math.pi / cycle_len) * parity[:, None] * mode_ids[None, :].astype(jnp.float32)
    return jnp.cos(shifts), jnp.sin(shifts)


def reference(sky_data, signal_prev, noise_var, mask_flags, cycle_table, m_table, spectrum, legendre):
    weight = mask_flags.astype(jnp.float32) / (noise_var - 0.5)
    messenger = (weight * sky_data + 2.0 * signal_prev) / (weight + 2.0)
    cos_tab, sin_tab = phase_tables(jnp.arange(NPHI, dtype=jnp.int32), m_table, NPHI)
    cos_shift, sin_shift = cycle_offsets(cycle_table, m_table, NPHI)
    flat_rows = messenger.astype(jnp.bfloat16).reshape(NREAL * CYCLES, NPHI)
    base_cos = jnp.dot(flat_rows, cos_tab, preferred_element_type=jnp.float32).reshape(NREAL, CYCLES, MWIN)
    base_sin = -jnp.dot(flat_rows, sin_tab, preferred_element_type=jnp.float32).reshape(NREAL, CYCLES, MWIN)
    norm_scale = NPHI ** -0.5
    fourier_re = ((base_cos * cos_shift + base_sin * sin_shift) * norm_scale).astype(jnp.bfloat16)
    fourier_im = ((base_sin * cos_shift - base_cos * sin_shift) * norm_scale).astype(jnp.bfloat16)
    fourier = jnp.stack([fourier_re, fourier_im], 1)
    fourier_cols = fourier.transpose(3, 2, 0, 1).reshape(MWIN, CYCLES, NREAL * 2)
    factor = spectrum / (spectrum + 0.5)
    syn_scale = (CYCLES / LBAND) ** 0.5

    def per_order(operands):
        leg_order, fourier_col = operands
        coefficients = jnp.dot(leg_order, fourier_col, preferred_element_type=jnp.float32)
        filtered = coefficients * factor[:, None]
        synthesized = jnp.dot(leg_order.T, filtered.astype(jnp.bfloat16), preferred_element_type=jnp.float32) * syn_scale
        return filtered, synthesized

    filtered, synthesized = lax.map(per_order, (legendre, fourier_cols))
    wiener_alm = filtered.reshape(MWIN, LBAND, NREAL, 2).transpose(2, 3, 0, 1)
    rounded = lax.optimization_barrier(synthesized.astype(jnp.bfloat16))
    cycle_modes = rounded.astype(jnp.float32).reshape(MWIN, CYCLES, NREAL, 2)
    modes_re = cycle_modes[..., 0].transpose(2, 1, 0)
    modes_im = cycle_modes[..., 1].transpose(2, 1, 0)
    rotated_re = (modes_re * cos_shift - modes_im * sin_shift).astype(jnp.bfloat16)
    rotated_im = (modes_im * cos_shift + modes_re * sin_shift).astype(jnp.bfloat16)
    contract = (((1,), (1,)), ((), ()))
    pixel_sum = lax.dot_general(rotated_re.reshape(-1, MWIN), cos_tab, contract, preferred_element_type=jnp.float32)
    pixel_sum = pixel_sum - lax.dot_general(rotated_im.reshape(-1, MWIN), sin_tab, contract, preferred_element_type=jnp.float32)
    signal_next = (pixel_sum * MWIN ** -0.5).reshape(NREAL, CYCLES, NPHI)
    return wiener_alm, signal_next
```

```python
import functools
import math

import jax
import jax.numpy as jnp
from jax import lax
from jax.experimental import pallas as pl
from jax.experimental.pallas import tpu as pltpu
from jax.sharding import PartitionSpec as P

LANES = 128
NT = (((1,), (1,)), ((), ()))
AXES = ("grp", "blk", "real")


def unit_cosine(units, half_turn):
    wrapped = units & (2 * half_turn - 1)
    folded = jnp.minimum(wrapped, 2 * half_turn - wrapped)
    y = (half_turn // 2 - folded).astype(jnp.float32) * (math.pi / half_turn)
    y2 = y * y
    acc = jnp.full_like(y2, -1.0 / math.factorial(11))
    for order, sign in ((9, 1.0), (7, -1.0), (5, 1.0), (3, -1.0), (1, 1.0)):
        acc = acc * y2 + sign / math.factorial(order)
    return acc * y


def lane_ids(shape):
    return lax.broadcasted_iota(jnp.int32, shape, len(shape) - 1)


def row_ids(shape):
    return lax.broadcasted_iota(jnp.int32, shape, len(shape) - 2)


def phase_factors(cycle_ref, mode_ref, cycle_len, half_len, group):
    orders = mode_ref[...]
    modes = orders.shape[1]
    orders = jnp.concatenate([orders] * (LANES // modes), axis=1)
    quarter = lane_ids((1, LANES)) // modes
    quarter_turn = cycle_len // 2
    inner_units = 2 * orders * row_ids((LANES, LANES)) + ((quarter + 1) >> 1) * quarter_turn
    inner = unit_cosine(inner_units, cycle_len)
    rows = 2 * (half_len // LANES)
    row = row_ids((rows, LANES))
    parity = jnp.where((row & 1) == 0, cycle_ref[0] & 1, cycle_ref[1] & 1)
    pixel = group * half_len + LANES * (row >> 1)
    outer_units = orders * (2 * pixel + parity) + (quarter >> 1) * (3 * quarter_turn)
    outer = unit_cosine(outer_units, cycle_len)
    high = inner.astype(jnp.bfloat16)
    low = (inner - high.astype(jnp.float32)).astype(jnp.bfloat16)
    return high, low, outer


def forward_kernel(
    cycle_len, half_len, syn_scale,
    cycle_ref, mode_ref, sky_ref, prev_ref, noise_ref, mask_ref, spectrum_ref, legendre_ref, out_ref,
):
    group = lax.axis_index("grp")
    high, low, outer = phase_factors(cycle_ref, mode_ref, cycle_len, half_len, group)
    pixel_rows = outer.shape[0]
    reals = sky_ref.shape[0] // pixel_rows
    weight = mask_ref[...].astype(jnp.float32) / (noise_ref[...] - 0.5)
    inverse = 1.0 / (weight + 2.0)
    sky_gain = weight * inverse
    prev_gain = 2.0 * inverse
    shape = (reals, pixel_rows, LANES)
    messenger = sky_ref[...].reshape(shape) * sky_gain + prev_ref[...].reshape(shape) * prev_gain
    rows = messenger.reshape(reals * pixel_rows, LANES).astype(jnp.bfloat16)
    partial = jnp.dot(
        jnp.concatenate([rows, rows], axis=1),
        jnp.concatenate([high, low], axis=0),
        preferred_element_type=jnp.float32,
    )
    turned = partial.reshape(shape) * outer
    summed = turned.reshape(reals, pixel_rows // 8, 8, LANES).sum(axis=1)
    summed = summed.reshape(reals * 8, LANES)
    summed = summed + pltpu.roll(summed, LANES // 2, 1)
    own = (row_ids(summed.shape) & 1) == (lane_ids(summed.shape) >= LANES // 2)
    summed = jnp.where(own, summed, 0.0).reshape(reals, 8, LANES).sum(axis=1)
    fourier = (summed * cycle_len**-0.5).astype(jnp.bfloat16)

    table = legendre_ref[...]
    spectrum = spectrum_ref[...]
    factor = spectrum / (spectrum + 0.5)
    filtered = (table.astype(jnp.float32) * factor).astype(jnp.bfloat16)
    gram = lax.dot_general(
        table, jnp.concatenate([filtered, filtered], axis=0), NT, preferred_element_type=jnp.float32
    )
    table_rows = table.shape[0]
    cycles = out_ref.shape[0] - reals
    same = row_ids(gram.shape) // cycles == lane_ids(gram.shape) % table_rows // cycles
    gram = jnp.where(same, gram, 0.0).reshape(table_rows // cycles, cycles, LANES).sum(axis=0)
    gram = gram * syn_scale
    gram_high = gram.astype(jnp.bfloat16).astype(jnp.float32)
    gram = jnp.where(lane_ids(gram.shape) < table_rows, gram_high, gram - gram_high)
    out_ref[...] = jnp.concatenate([fourier, gram.astype(jnp.bfloat16)], axis=0)


def backward_kernel(
    cycle_len, half_len, groups, blocks, real_groups, reals,
    cycle_ref, mode_ref, gathered_ref, spectrum_ref, legendre_ref, wiener_ref, signal_ref,
):
    group = lax.axis_index("grp")
    block = lax.axis_index("blk")
    real_group = lax.axis_index("real")
    high, low, outer = phase_factors(cycle_ref, mode_ref, cycle_len, half_len, group)
    modes = mode_ref.shape[1]
    table_rows = legendre_ref.shape[0]
    per_block = modes // blocks
    cycles = table_rows // per_block
    pixel_rows = outer.shape[0]
    half = LANES // 2
    square = (LANES, LANES)
    row, lane = row_ids(square), lane_ids(square)

    gram_all = gathered_ref[:, reals:, :].reshape(-1, LANES)
    pick = (row % cycles == 2 * block + lane // half) & (
        row % table_rows // cycles == lane % modes % per_block
    )
    gram_rows = jnp.dot(
        gram_all, pick.astype(jnp.float32).astype(jnp.bfloat16), preferred_element_type=jnp.float32
    ).reshape(groups, blocks, real_groups, cycles, LANES)
    holder = lane_ids((cycles, LANES)) % modes // per_block
    gram = jnp.zeros((cycles, LANES), jnp.float32)
    for b in range(blocks):
        one = gram_rows[:, b].reshape(-1, cycles, LANES).sum(axis=0)
        gram = gram + jnp.where(holder == b, one, 0.0)

    first = lane_ids((reals, LANES)) < half
    cycle_modes = jnp.zeros((reals, LANES), jnp.float32)
    for b in range(blocks):
        pair = jnp.zeros((reals, LANES), jnp.float32)
        for g in range(groups):
            source = (g * blocks + b) * real_groups + real_group
            pair = pair + gathered_ref[source, :reals, :].astype(jnp.float32)
        turned = pltpu.roll(pair, half, 1)
        cycle_modes = cycle_modes + jnp.where(first, pair, turned) * gram[2 * b : 2 * b + 1]
        cycle_modes = cycle_modes + jnp.where(first, turned, pair) * gram[2 * b + 1 : 2 * b + 2]
    cycle_modes = cycle_modes * modes**-0.5
    turned = pltpu.roll(cycle_modes, half, 1)
    even = jnp.where(first, cycle_modes, turned)
    odd = jnp.where(first, turned, cycle_modes)
    parity = (row_ids((1, 8, LANES)) & 1) == 0
    spread = jnp.where(parity, even[:, None, :], odd[:, None, :])
    rotated = spread[:, None] * outer.reshape(1, pixel_rows // 8, 8, LANES)
    rotated = rotated.reshape(reals * pixel_rows, LANES).astype(jnp.bfloat16)
    signal_ref[...] = lax.dot_general(
        jnp.concatenate([rotated, rotated], axis=1),
        jnp.concatenate([high, low], axis=1),
        NT,
        preferred_element_type=jnp.float32,
    )

    fourier_all = gathered_ref[:, :reals, :].reshape(-1, LANES)
    pick = (
        (row // half == lane % 2)
        & (row // modes % 2 == lane // half)
        & (row % modes == block * per_block + lane % half // cycles)
    )
    total_reals = real_groups * reals
    coeff_rows = jnp.dot(
        fourier_all, pick.astype(jnp.float32).astype(jnp.bfloat16), preferred_element_type=jnp.float32
    ).reshape(groups, blocks, total_reals, LANES)
    coeff_lane = lane_ids((total_reals, LANES))
    columns = jnp.zeros((total_reals, LANES), jnp.float32)
    for b in range(blocks):
        one = coeff_rows[:, b].sum(axis=0)
        columns = columns + jnp.where(coeff_lane % cycles // 2 == b, one, 0.0)
    pieces = [
        jnp.where((coeff_lane // half == c) & (coeff_lane % half // cycles == s), columns, 0.0)
        for s in range(per_block)
        for c in range(2)
    ]
    table = legendre_ref[...]
    spectrum = spectrum_ref[...]
    filtered = jnp.dot(
        jnp.concatenate(pieces, axis=0).astype(jnp.bfloat16),
        jnp.concatenate([table, table], axis=0),
        preferred_element_type=jnp.float32,
    ) * (spectrum / (spectrum + 0.5))
    tiles = table.shape[1] // LANES
    for s in range(per_block):
        for c in range(2):
            start = (s * 2 + c) * total_reals
            for tile in range(tiles):
                wiener_ref[
                    pl.ds((c * tiles + tile) * per_block + s, total_reals, stride=2 * tiles * per_block), :
                ] = filtered[start : start + total_reals, tile * LANES : (tile + 1) * LANES]


def split_tiles(array):
    lead, rows, columns = array.shape[:-2], array.shape[-2], array.shape[-1]
    split = array.reshape(*lead, rows, columns // LANES, LANES)
    return jnp.swapaxes(split, -2, -3).reshape(-1, LANES)


def gram_program(
    sky_data, signal_prev, noise_var, mask_flags, cycle_table, m_table, spectrum, legendre
):
    reals, cycle_dev, half_len = sky_data.shape
    groups, blocks, real_groups = (lax.axis_size(name) for name in AXES)
    cycle_len = half_len * groups
    per_block, multipoles, cycles = legendre.shape
    total_l = multipoles * groups * real_groups
    tiles = multipoles // LANES
    smem = pl.BlockSpec(memory_space=pltpu.SMEM)
    vmem = pl.BlockSpec(memory_space=pltpu.VMEM)
    orders = m_table[None, :]
    spectrum_row = spectrum[None, :]
    table = legendre.transpose(0, 2, 1).reshape(per_block * cycles, multipoles)
    local = pl.pallas_call(
        functools.partial(forward_kernel, cycle_len, half_len, (cycles / total_l) ** 0.5),
        out_shape=jax.ShapeDtypeStruct((reals + cycles, LANES), jnp.bfloat16),
        in_specs=[smem] + [vmem] * 7,
        out_specs=vmem,
    )(
        cycle_table, orders, split_tiles(sky_data), split_tiles(signal_prev),
        split_tiles(noise_var), split_tiles(mask_flags), spectrum_row, table,
    )
    gathered = lax.all_gather(local, AXES)
    total_reals = reals * real_groups
    wiener, signal = pl.pallas_call(
        functools.partial(backward_kernel, cycle_len, half_len, groups, blocks, real_groups, reals),
        out_shape=(
            jax.ShapeDtypeStruct((total_reals * 2 * tiles * per_block, LANES), jnp.float32),
            jax.ShapeDtypeStruct((reals * cycle_dev * half_len // LANES, LANES), jnp.float32),
        ),
        in_specs=[smem] + [vmem] * 4,
        out_specs=(vmem, vmem),
    )(cycle_table, orders, gathered, spectrum_row, table)
    wiener = wiener.reshape(total_reals, 2, tiles, per_block, LANES).transpose(0, 1, 3, 2, 4)
    signal = signal.reshape(reals, half_len // LANES, cycle_dev, LANES).transpose(0, 2, 1, 3)
    return (
        wiener.reshape(total_reals, 2, per_block, multipoles),
        signal.reshape(sky_data.shape),
    )


def gram_form_fits(mesh, sky_data, m_table, legendre):
    groups, blocks, real_groups = (mesh.shape[name] for name in AXES)
    reals, cycles, cycle_len = sky_data.shape
    modes = m_table.shape[0]
    per_block = modes // blocks
    multipoles = legendre.shape[1] // (groups * real_groups)
    half_len = cycle_len // groups
    reals_dev = reals // real_groups
    return (
        cycles < 2 * reals
        and 4 * modes == LANES
        and cycles == 2 * blocks
        and 2 * per_block * cycles == LANES
        and cycle_len & (cycle_len - 1) == 0
        and half_len % (4 * LANES) == 0
        and multipoles % LANES == 0
        and reals_dev % 16 == 0
        and cycles % 16 == 0
    )


def phase_tables(col_ids, mode_ids, cycle_len):
    product_ids = col_ids[:, None] * mode_ids[None, :] % cycle_len
    angles = product_ids.astype(jnp.float32) * (2.0 * math.pi / cycle_len)
    return (jnp.cos(angles).astype(jnp.bfloat16), jnp.sin(angles).astype(jnp.bfloat16))


def cycle_offsets(cycle_ids, mode_ids, cycle_len):
    parity = (cycle_ids % 2).astype(jnp.float32)
    shifts = math.pi / cycle_len * parity[:, None] * mode_ids[None, :].astype(jnp.float32)
    return (jnp.cos(shifts), jnp.sin(shifts))


def forward_modes(re_part, im_part):
    summed = lax.psum((re_part, im_part), "grp")
    fourier_pair = (summed[0].astype(jnp.bfloat16), summed[1].astype(jnp.bfloat16))
    fourier_pair = (
        lax.all_gather(fourier_pair[0], "real", axis=0, tiled=True),
        lax.all_gather(fourier_pair[1], "real", axis=0, tiled=True),
    )
    fourier_pair = (
        lax.all_to_all(fourier_pair[0], "blk", split_axis=2, concat_axis=1, tiled=True),
        lax.all_to_all(fourier_pair[1], "blk", split_axis=2, concat_axis=1, tiled=True),
    )
    return fourier_pair


def backward_cycles(partial_value):
    summed = lax.psum_scatter(partial_value, "real", scatter_dimension=0, tiled=True)
    reduced = lax.psum(summed, "grp")
    cycle_pair = lax.all_to_all(
        reduced.astype(jnp.bfloat16), "blk", split_axis=2, concat_axis=3, tiled=True
    )
    return cycle_pair


def per_device(
    sky_data, signal_prev, noise_var, mask_flags, cycle_table, m_table, spectrum, legendre
):
    real_dev, cycle_dev, half_len = sky_data.shape
    cycle_len = half_len * lax.axis_size("grp")
    mode_count = m_table.shape[0]
    col_ids = lax.axis_index("grp") * half_len + jnp.arange(half_len, dtype=jnp.int32)
    cos_tab, sin_tab = phase_tables(col_ids, m_table, cycle_len)
    cos_shift, sin_shift = cycle_offsets(cycle_table, m_table, cycle_len)
    weight = mask_flags.astype(jnp.float32) / (noise_var - 0.5)
    messenger = (weight * sky_data + 2.0 * signal_prev) / (weight + 2.0)
    flat_rows = messenger.astype(jnp.bfloat16).reshape(real_dev * cycle_dev, half_len)
    base_cos = jnp.dot(flat_rows, cos_tab, preferred_element_type=jnp.float32).reshape(
        real_dev, cycle_dev, mode_count
    )
    base_sin = -jnp.dot(flat_rows, sin_tab, preferred_element_type=jnp.float32).reshape(
        real_dev, cycle_dev, mode_count
    )
    norm_scale = cycle_len ** (-0.5)
    re_part = (base_cos * cos_shift + base_sin * sin_shift) * norm_scale
    im_part = (base_sin * cos_shift - base_cos * sin_shift) * norm_scale
    fourier_re, fourier_im = forward_modes(re_part, im_part)
    fourier = jnp.stack([fourier_re, fourier_im], 1)
    coefficients = jnp.einsum(
        "mlr,kcrm->kcml", legendre, fourier, preferred_element_type=jnp.float32
    )
    factor = spectrum / (spectrum + 0.5)
    wiener_alm = coefficients * factor
    total_l = legendre.shape[1] * lax.axis_size("grp") * lax.axis_size("real")
    syn_scale = (legendre.shape[2] / total_l) ** 0.5
    partial_value = (
        jnp.einsum(
            "mlr,kcml->kcrm",
            legendre,
            wiener_alm.astype(jnp.bfloat16),
            preferred_element_type=jnp.float32,
        )
        * syn_scale
    )
    cycle_pair = backward_cycles(partial_value)
    cycle_modes = cycle_pair.astype(jnp.float32)
    modes_re = cycle_modes[:, 0]
    modes_im = cycle_modes[:, 1]
    rotated_re = (modes_re * cos_shift - modes_im * sin_shift).astype(jnp.bfloat16)
    rotated_im = (modes_im * cos_shift + modes_re * sin_shift).astype(jnp.bfloat16)
    contract = (((1,), (1,)), ((), ()))
    pixel_sum = lax.dot_general(
        rotated_re.reshape(-1, mode_count), cos_tab, contract, preferred_element_type=jnp.float32
    )
    pixel_sum = pixel_sum - lax.dot_general(
        rotated_im.reshape(-1, mode_count), sin_tab, contract, preferred_element_type=jnp.float32
    )
    signal_next = (pixel_sum * mode_count ** (-0.5)).reshape(real_dev, cycle_dev, half_len)
    return (wiener_alm, signal_next)


def solution(mesh):
    in_specs = (
        P("real", "blk", "grp"),
        P("real", "blk", "grp"),
        P("blk", "grp"),
        P("blk", "grp"),
        P("blk"),
        P(),
        P(("grp", "real")),
        P("blk", ("grp", "real"), None),
    )
    out_specs = (P(None, None, "blk", ("grp", "real")), P("real", "blk", "grp"))

    def step(sky_data, signal_prev, noise_var, mask_flags, cycle_table, m_table, spectrum, legendre):
        fits = gram_form_fits(mesh, sky_data, m_table, legendre)
        return jax.shard_map(
            gram_program if fits else per_device,
            mesh=mesh,
            in_specs=in_specs,
            out_specs=out_specs,
            check_vma=False,
        )(sky_data, signal_prev, noise_var, mask_flags, cycle_table, m_table, spectrum, legendre)

    return step
```

```python
import functools
import math

import jax
import jax.numpy as jnp
from jax import lax
from jax.experimental import pallas as pl
from jax.experimental.pallas import tpu as pltpu
from jax.sharding import PartitionSpec as P

LANES = 128
NT = (((1,), (1,)), ((), ()))
AXES = ("grp", "blk", "real")


def unit_cosine(units, half_turn):
    wrapped = units & (2 * half_turn - 1)
    folded = jnp.minimum(wrapped, 2 * half_turn - wrapped)
    y = (half_turn // 2 - folded).astype(jnp.float32) * (math.pi / half_turn)
    y2 = y * y
    acc = jnp.full_like(y2, -1.0 / math.factorial(11))
    for order, sign in ((9, 1.0), (7, -1.0), (5, 1.0), (3, -1.0), (1, 1.0)):
        acc = acc * y2 + sign / math.factorial(order)
    return acc * y


def lane_ids(shape):
    return lax.broadcasted_iota(jnp.int32, shape, len(shape) - 1)


def row_ids(shape):
    return lax.broadcasted_iota(jnp.int32, shape, len(shape) - 2)


def phase_factors(cycle_ref, mode_ref, cycle_len, half_len, group):
    orders = mode_ref[...]
    modes = orders.shape[1]
    orders = jnp.concatenate([orders] * (LANES // modes), axis=1)
    quarter = lane_ids((1, LANES)) // modes
    quarter_turn = cycle_len // 2
    inner_units = 2 * orders * row_ids((LANES, LANES)) + ((quarter + 1) >> 1) * quarter_turn
    inner = unit_cosine(inner_units, cycle_len)
    rows = 2 * (half_len // LANES)
    row = row_ids((rows, LANES))
    parity = jnp.where((row & 1) == 0, cycle_ref[0] & 1, cycle_ref[1] & 1)
    pixel = group * half_len + LANES * (row >> 1)
    outer_units = orders * (2 * pixel + parity) + (quarter >> 1) * (3 * quarter_turn)
    outer = unit_cosine(outer_units, cycle_len)
    high = inner.astype(jnp.bfloat16)
    low = (inner - high.astype(jnp.float32)).astype(jnp.bfloat16)
    return high, low, outer


def forward_kernel(
    cycle_len, half_len, syn_scale,
    cycle_ref, mode_ref, sky_ref, prev_ref, noise_ref, mask_ref, spectrum_ref, legendre_ref, out_ref,
):
    group = lax.axis_index("grp")
    high, low, outer = phase_factors(cycle_ref, mode_ref, cycle_len, half_len, group)
    pixel_rows = outer.shape[0]
    reals = sky_ref.shape[0] // pixel_rows
    weight = mask_ref[...].astype(jnp.float32) / (noise_ref[...] - 0.5)
    inverse = 1.0 / (weight + 2.0)
    sky_gain = weight * inverse
    prev_gain = 2.0 * inverse
    shape = (reals, pixel_rows, LANES)
    messenger = sky_ref[...].reshape(shape) * sky_gain + prev_ref[...].reshape(shape) * prev_gain
    rows = messenger.reshape(reals * pixel_rows, LANES).astype(jnp.bfloat16)
    partial = jnp.dot(
        jnp.concatenate([rows, rows], axis=1),
        jnp.concatenate([high, low], axis=0),
        preferred_element_type=jnp.float32,
    )
    turned = partial.reshape(shape) * outer
    summed = turned.reshape(reals, pixel_rows // 8, 8, LANES).sum(axis=1)
    summed = summed.reshape(reals * 8, LANES)
    summed = summed + pltpu.roll(summed, LANES // 2, 1)
    own = (row_ids(summed.shape) & 1) == (lane_ids(summed.shape) >= LANES // 2)
    summed = jnp.where(own, summed, 0.0).reshape(reals, 8, LANES).sum(axis=1)
    fourier = (summed * cycle_len**-0.5).astype(jnp.bfloat16)

    table = legendre_ref[...]
    spectrum = spectrum_ref[...]
    factor = spectrum / (spectrum + 0.5)
    filtered = (table.astype(jnp.float32) * factor).astype(jnp.bfloat16)
    gram = lax.dot_general(
        table, jnp.concatenate([filtered, filtered], axis=0), NT, preferred_element_type=jnp.float32
    )
    table_rows = table.shape[0]
    cycles = out_ref.shape[0] - reals
    same = row_ids(gram.shape) // cycles == lane_ids(gram.shape) % table_rows // cycles
    gram = jnp.where(same, gram, 0.0).reshape(table_rows // cycles, cycles, LANES).sum(axis=0)
    gram = gram * syn_scale
    gram_high = gram.astype(jnp.bfloat16).astype(jnp.float32)
    gram = jnp.where(lane_ids(gram.shape) < table_rows, gram_high, gram - gram_high)
    out_ref[...] = jnp.concatenate([fourier, gram.astype(jnp.bfloat16)], axis=0)


def merge_kernel(reals, own_ref, across_ref, other_ref, far_ref, out_ref):
    parts = [ref[...].astype(jnp.float32) for ref in (own_ref, across_ref, other_ref, far_ref)]
    own = parts[0] + parts[1]
    other = parts[2] + parts[3]
    gram = own[reals:] + other[reals:]
    gram = gram + pltpu.roll(gram, LANES // 2, 1)
    gram_high = gram.astype(jnp.bfloat16).astype(jnp.float32)
    gram = jnp.where(lane_ids(gram.shape) < LANES // 2, gram_high, gram - gram_high)
    out_ref[...] = jnp.concatenate([own[:reals], other[:reals], gram], axis=0).astype(jnp.bfloat16)


def backward_kernel(cycle_len, half_len, blocks, reals, cycle_ref, mode_ref, spectrum_ref, legendre_ref, *refs):
    sources, (wiener_ref, signal_ref, gram_ref) = refs[:blocks], refs[blocks:]
    group = lax.axis_index("grp")
    block = lax.axis_index("blk")
    real_group = lax.axis_index("real")
    high, low, outer = phase_factors(cycle_ref, mode_ref, cycle_len, half_len, group)
    modes = mode_ref.shape[1]
    table_rows = legendre_ref.shape[0]
    per_block = modes // blocks
    cycles = table_rows // per_block
    pixel_rows = outer.shape[0]
    half = LANES // 2
    square = (LANES, LANES)
    row, lane = row_ids(square), lane_ids(square)

    gram_all = jnp.concatenate([ref[2 * reals :, :] for ref in sources], axis=0)
    pick = (row % cycles == 2 * block + lane // half) & (
        row % table_rows // cycles == lane % modes % per_block
    )
    gram_rows = jnp.dot(
        gram_all, pick.astype(jnp.float32).astype(jnp.bfloat16), preferred_element_type=jnp.float32
    ).reshape(blocks, cycles, LANES)
    holder = lane_ids((cycles, LANES)) % modes // per_block
    gram = jnp.zeros((cycles, LANES), jnp.float32)
    for d in range(blocks):
        gram = gram + jnp.where(holder == (block ^ d), gram_rows[d], 0.0)
    gram_ref[...] = gram

    first = lane_ids((reals, LANES)) < half
    cycle_modes = jnp.zeros((reals, LANES), jnp.float32)
    for d in range(blocks):
        pair = sources[d][:reals, :].astype(jnp.float32)
        turned = pltpu.roll(pair, half, 1)
        source = block ^ d
        cycle_modes = cycle_modes + jnp.where(first, pair, turned) * gram_ref[pl.ds(2 * source, 1), :]
        cycle_modes = cycle_modes + jnp.where(first, turned, pair) * gram_ref[pl.ds(2 * source + 1, 1), :]
    cycle_modes = cycle_modes * modes**-0.5
    turned = pltpu.roll(cycle_modes, half, 1)
    even = jnp.where(first, cycle_modes, turned)
    odd = jnp.where(first, turned, cycle_modes)
    parity = (row_ids((1, 8, LANES)) & 1) == 0
    spread = jnp.where(parity, even[:, None, :], odd[:, None, :])
    rotated = spread[:, None] * outer.reshape(1, pixel_rows // 8, 8, LANES)
    rotated = rotated.reshape(reals * pixel_rows, LANES).astype(jnp.bfloat16)
    signal_ref[...] = lax.dot_general(
        jnp.concatenate([rotated, rotated], axis=1),
        jnp.concatenate([high, low], axis=1),
        NT,
        preferred_element_type=jnp.float32,
    )

    fourier_all = jnp.concatenate([ref[: 2 * reals, :] for ref in sources], axis=0)
    pick = (
        (row // half == lane % 2)
        & (row // modes % 2 == lane // half)
        & (row % modes == block * per_block + lane % half // cycles)
    )
    coeff_rows = jnp.dot(
        fourier_all, pick.astype(jnp.float32).astype(jnp.bfloat16), preferred_element_type=jnp.float32
    ).reshape(blocks, 2 * reals, LANES)
    coeff_lane = lane_ids((2 * reals, LANES))
    columns = jnp.zeros((2 * reals, LANES), jnp.float32)
    for d in range(blocks):
        columns = columns + jnp.where(coeff_lane % cycles // 2 == (block ^ d), coeff_rows[d], 0.0)
    swapped = jnp.concatenate([columns[reals:], columns[:reals]], axis=0)
    columns = jnp.where(real_group == 0, columns, swapped)
    pieces = [
        jnp.where((coeff_lane // half == c) & (coeff_lane % half // cycles == s), columns, 0.0)
        for s in range(per_block)
        for c in range(2)
    ]
    table = legendre_ref[...]
    spectrum = spectrum_ref[...]
    filtered = jnp.dot(
        jnp.concatenate(pieces, axis=0).astype(jnp.bfloat16),
        jnp.concatenate([table, table], axis=0),
        preferred_element_type=jnp.float32,
    ) * (spectrum / (spectrum + 0.5))
    tiles = table.shape[1] // LANES
    for s in range(per_block):
        for c in range(2):
            start = (s * 2 + c) * 2 * reals
            for tile in range(tiles):
                wiener_ref[
                    pl.ds((c * tiles + tile) * per_block + s, 2 * reals, stride=2 * tiles * per_block), :
                ] = filtered[start : start + 2 * reals, tile * LANES : (tile + 1) * LANES]


def split_tiles(array):
    lead, rows, columns = array.shape[:-2], array.shape[-2], array.shape[-1]
    split = array.reshape(*lead, rows, columns // LANES, LANES)
    return jnp.swapaxes(split, -2, -3).reshape(-1, LANES)


def gram_program(
    sky_data, signal_prev, noise_var, mask_flags, cycle_table, m_table, spectrum, legendre
):
    reals, cycle_dev, half_len = sky_data.shape
    groups, blocks, real_groups = (lax.axis_size(name) for name in AXES)
    cycle_len = half_len * groups
    per_block, multipoles, cycles = legendre.shape
    total_l = multipoles * groups * real_groups
    tiles = multipoles // LANES
    smem = pl.BlockSpec(memory_space=pltpu.SMEM)
    vmem = pl.BlockSpec(memory_space=pltpu.VMEM)
    orders = m_table[None, :]
    spectrum_row = spectrum[None, :]
    table = legendre.transpose(0, 2, 1).reshape(per_block * cycles, multipoles)
    local = pl.pallas_call(
        functools.partial(forward_kernel, cycle_len, half_len, (cycles / total_l) ** 0.5),
        out_shape=jax.ShapeDtypeStruct((reals + cycles, LANES), jnp.bfloat16),
        in_specs=[smem] + [vmem] * 7,
        out_specs=vmem,
    )(
        cycle_table, orders, split_tiles(sky_data), split_tiles(signal_prev),
        split_tiles(noise_var), split_tiles(mask_flags), spectrum_row, table,
    )
    corner = groups * real_groups
    steps = (real_groups, 1, real_groups + 1)
    received = [
        lax.ppermute(local, ("grp", "real"), [(i, i ^ step) for i in range(corner)]) for step in steps
    ]
    merged = pl.pallas_call(
        functools.partial(merge_kernel, reals),
        out_shape=jax.ShapeDtypeStruct((2 * reals + cycles, LANES), jnp.bfloat16),
        in_specs=[vmem] * 4,
        out_specs=vmem,
    )(local, *received)
    sources = [merged] + [
        lax.ppermute(merged, "blk", [(i, i ^ step) for i in range(blocks)]) for step in range(1, blocks)
    ]
    total_reals = reals * real_groups
    wiener, signal = pl.pallas_call(
        functools.partial(backward_kernel, cycle_len, half_len, blocks, reals),
        out_shape=(
            jax.ShapeDtypeStruct((total_reals * 2 * tiles * per_block, LANES), jnp.float32),
            jax.ShapeDtypeStruct((reals * cycle_dev * half_len // LANES, LANES), jnp.float32),
        ),
        in_specs=[smem] + [vmem] * (3 + blocks),
        out_specs=(vmem, vmem),
        scratch_shapes=[pltpu.VMEM((cycles, LANES), jnp.float32)],
    )(cycle_table, orders, spectrum_row, table, *sources)
    wiener = wiener.reshape(total_reals, 2, tiles, per_block, LANES).transpose(0, 1, 3, 2, 4)
    signal = signal.reshape(reals, half_len // LANES, cycle_dev, LANES).transpose(0, 2, 1, 3)
    return (
        wiener.reshape(total_reals, 2, per_block, multipoles),
        signal.reshape(sky_data.shape),
    )


def gram_form_fits(mesh, sky_data, m_table, legendre):
    groups, blocks, real_groups = (mesh.shape[name] for name in AXES)
    reals, cycles, cycle_len = sky_data.shape
    modes = m_table.shape[0]
    per_block = modes // blocks
    multipoles = legendre.shape[1] // (groups * real_groups)
    half_len = cycle_len // groups
    reals_dev = reals // real_groups
    return (
        cycles < 2 * reals
        and groups == 2
        and real_groups == 2
        and blocks & (blocks - 1) == 0
        and 4 * modes == LANES
        and cycles == 2 * blocks
        and 2 * per_block * cycles == LANES
        and cycle_len & (cycle_len - 1) == 0
        and half_len % (4 * LANES) == 0
        and multipoles % LANES == 0
        and reals_dev % 16 == 0
        and cycles % 16 == 0
    )


def phase_tables(col_ids, mode_ids, cycle_len):
    product_ids = col_ids[:, None] * mode_ids[None, :] % cycle_len
    angles = product_ids.astype(jnp.float32) * (2.0 * math.pi / cycle_len)
    return (jnp.cos(angles).astype(jnp.bfloat16), jnp.sin(angles).astype(jnp.bfloat16))


def cycle_offsets(cycle_ids, mode_ids, cycle_len):
    parity = (cycle_ids % 2).astype(jnp.float32)
    shifts = math.pi / cycle_len * parity[:, None] * mode_ids[None, :].astype(jnp.float32)
    return (jnp.cos(shifts), jnp.sin(shifts))


def forward_modes(re_part, im_part):
    summed = lax.psum((re_part, im_part), "grp")
    fourier_pair = (summed[0].astype(jnp.bfloat16), summed[1].astype(jnp.bfloat16))
    fourier_pair = (
        lax.all_gather(fourier_pair[0], "real", axis=0, tiled=True),
        lax.all_gather(fourier_pair[1], "real", axis=0, tiled=True),
    )
    fourier_pair = (
        lax.all_to_all(fourier_pair[0], "blk", split_axis=2, concat_axis=1, tiled=True),
        lax.all_to_all(fourier_pair[1], "blk", split_axis=2, concat_axis=1, tiled=True),
    )
    return fourier_pair


def backward_cycles(partial_value):
    summed = lax.psum_scatter(partial_value, "real", scatter_dimension=0, tiled=True)
    reduced = lax.psum(summed, "grp")
    cycle_pair = lax.all_to_all(
        reduced.astype(jnp.bfloat16), "blk", split_axis=2, concat_axis=3, tiled=True
    )
    return cycle_pair


def per_device(
    sky_data, signal_prev, noise_var, mask_flags, cycle_table, m_table, spectrum, legendre
):
    real_dev, cycle_dev, half_len = sky_data.shape
    cycle_len = half_len * lax.axis_size("grp")
    mode_count = m_table.shape[0]
    col_ids = lax.axis_index("grp") * half_len + jnp.arange(half_len, dtype=jnp.int32)
    cos_tab, sin_tab = phase_tables(col_ids, m_table, cycle_len)
    cos_shift, sin_shift = cycle_offsets(cycle_table, m_table, cycle_len)
    weight = mask_flags.astype(jnp.float32) / (noise_var - 0.5)
    messenger = (weight * sky_data + 2.0 * signal_prev) / (weight + 2.0)
    flat_rows = messenger.astype(jnp.bfloat16).reshape(real_dev * cycle_dev, half_len)
    base_cos = jnp.dot(flat_rows, cos_tab, preferred_element_type=jnp.float32).reshape(
        real_dev, cycle_dev, mode_count
    )
    base_sin = -jnp.dot(flat_rows, sin_tab, preferred_element_type=jnp.float32).reshape(
        real_dev, cycle_dev, mode_count
    )
    norm_scale = cycle_len ** (-0.5)
    re_part = (base_cos * cos_shift + base_sin * sin_shift) * norm_scale
    im_part = (base_sin * cos_shift - base_cos * sin_shift) * norm_scale
    fourier_re, fourier_im = forward_modes(re_part, im_part)
    fourier = jnp.stack([fourier_re, fourier_im], 1)
    coefficients = jnp.einsum(
        "mlr,kcrm->kcml", legendre, fourier, preferred_element_type=jnp.float32
    )
    factor = spectrum / (spectrum + 0.5)
    wiener_alm = coefficients * factor
    total_l = legendre.shape[1] * lax.axis_size("grp") * lax.axis_size("real")
    syn_scale = (legendre.shape[2] / total_l) ** 0.5
    partial_value = (
        jnp.einsum(
            "mlr,kcml->kcrm",
            legendre,
            wiener_alm.astype(jnp.bfloat16),
            preferred_element_type=jnp.float32,
        )
        * syn_scale
    )
    cycle_pair = backward_cycles(partial_value)
    cycle_modes = cycle_pair.astype(jnp.float32)
    modes_re = cycle_modes[:, 0]
    modes_im = cycle_modes[:, 1]
    rotated_re = (modes_re * cos_shift - modes_im * sin_shift).astype(jnp.bfloat16)
    rotated_im = (modes_im * cos_shift + modes_re * sin_shift).astype(jnp.bfloat16)
    contract = (((1,), (1,)), ((), ()))
    pixel_sum = lax.dot_general(
        rotated_re.reshape(-1, mode_count), cos_tab, contract, preferred_element_type=jnp.float32
    )
    pixel_sum = pixel_sum - lax.dot_general(
        rotated_im.reshape(-1, mode_count), sin_tab, contract, preferred_element_type=jnp.float32
    )
    signal_next = (pixel_sum * mode_count ** (-0.5)).reshape(real_dev, cycle_dev, half_len)
    return (wiener_alm, signal_next)


def solution(mesh):
    in_specs = (
        P("real", "blk", "grp"),
        P("real", "blk", "grp"),
        P("blk", "grp"),
        P("blk", "grp"),
        P("blk"),
        P(),
        P(("grp", "real")),
        P("blk", ("grp", "real"), None),
    )
    out_specs = (P(None, None, "blk", ("grp", "real")), P("real", "blk", "grp"))

    def step(sky_data, signal_prev, noise_var, mask_flags, cycle_table, m_table, spectrum, legendre):
        fits = gram_form_fits(mesh, sky_data, m_table, legendre)
        return jax.shard_map(
            gram_program if fits else per_device,
            mesh=mesh,
            in_specs=in_specs,
            out_specs=out_specs,
            check_vma=False,
        )(sky_data, signal_prev, noise_var, mask_flags, cycle_table, m_table, spectrum, legendre)

    return step
```

```python
import functools
import math

import jax
import jax.numpy as jnp
from jax import lax
from jax.experimental import pallas as pl
from jax.experimental.pallas import tpu as pltpu
from jax.sharding import PartitionSpec as P

LANES = 128
NT = (((1,), (1,)), ((), ()))
AXES = ("grp", "blk", "real")


def unit_cosine(units, half_turn):
    wrapped = units & (2 * half_turn - 1)
    folded = jnp.minimum(wrapped, 2 * half_turn - wrapped)
    y = (half_turn // 2 - folded).astype(jnp.float32) * (math.pi / half_turn)
    y2 = y * y
    acc = jnp.full_like(y2, -1.0 / math.factorial(11))
    for order, sign in ((9, 1.0), (7, -1.0), (5, 1.0), (3, -1.0), (1, 1.0)):
        acc = acc * y2 + sign / math.factorial(order)
    return acc * y


def lane_ids(shape):
    return lax.broadcasted_iota(jnp.int32, shape, len(shape) - 1)


def row_ids(shape):
    return lax.broadcasted_iota(jnp.int32, shape, len(shape) - 2)


def phase_factors(cycle_ref, mode_ref, cycle_len, half_len, group):
    orders = mode_ref[...]
    modes = orders.shape[1]
    orders = jnp.concatenate([orders] * (LANES // modes), axis=1)
    quarter = lane_ids((1, LANES)) // modes
    quarter_turn = cycle_len // 2
    inner_units = 2 * orders * row_ids((LANES, LANES)) + ((quarter + 1) >> 1) * quarter_turn
    inner = unit_cosine(inner_units, cycle_len)
    rows = 2 * (half_len // LANES)
    row = row_ids((rows, LANES))
    parity = jnp.where((row & 1) == 0, cycle_ref[0] & 1, cycle_ref[1] & 1)
    pixel = group * half_len + LANES * (row >> 1)
    outer_units = orders * (2 * pixel + parity) + (quarter >> 1) * (3 * quarter_turn)
    outer = unit_cosine(outer_units, cycle_len)
    high = inner.astype(jnp.bfloat16)
    low = (inner - high.astype(jnp.float32)).astype(jnp.bfloat16)
    return high, low, outer


def forward_kernel(
    cycle_len, half_len, syn_scale,
    cycle_ref, mode_ref, sky_ref, prev_ref, noise_ref, mask_ref, spectrum_ref, legendre_ref, out_ref,
):
    group = lax.axis_index("grp")
    high, low, outer = phase_factors(cycle_ref, mode_ref, cycle_len, half_len, group)
    pixel_rows = outer.shape[0]
    reals = sky_ref.shape[0] // pixel_rows
    weight = mask_ref[...].astype(jnp.float32) / (noise_ref[...] - 0.5)
    inverse = 1.0 / (weight + 2.0)
    sky_gain = weight * inverse
    prev_gain = 2.0 * inverse
    shape = (reals, pixel_rows, LANES)
    messenger = sky_ref[...].reshape(shape) * sky_gain + prev_ref[...].reshape(shape) * prev_gain
    rows = messenger.reshape(reals * pixel_rows, LANES).astype(jnp.bfloat16)
    partial = jnp.dot(
        jnp.concatenate([rows, rows], axis=1),
        jnp.concatenate([high, low], axis=0),
        preferred_element_type=jnp.float32,
    )
    turned = partial.reshape(shape) * outer
    summed = turned.reshape(reals, pixel_rows // 8, 8, LANES).sum(axis=1)
    summed = summed.reshape(reals * 8, LANES)
    summed = summed + pltpu.roll(summed, LANES // 2, 1)
    own = (row_ids(summed.shape) & 1) == (lane_ids(summed.shape) >= LANES // 2)
    summed = jnp.where(own, summed, 0.0).reshape(reals, 8, LANES).sum(axis=1)
    fourier = (summed * cycle_len**-0.5).astype(jnp.bfloat16)

    table = legendre_ref[...]
    spectrum = spectrum_ref[...]
    factor = spectrum / (spectrum + 0.5)
    filtered = (table.astype(jnp.float32) * factor).astype(jnp.bfloat16)
    gram = lax.dot_general(
        table, jnp.concatenate([filtered, filtered], axis=0), NT, preferred_element_type=jnp.float32
    )
    table_rows = table.shape[0]
    cycles = out_ref.shape[1] - reals
    same = row_ids(gram.shape) // cycles == lane_ids(gram.shape) % table_rows // cycles
    gram = jnp.where(same, gram, 0.0).reshape(table_rows // cycles, cycles, LANES).sum(axis=0)
    gram = gram * syn_scale
    gram_high = gram.astype(jnp.bfloat16).astype(jnp.float32)
    gram = jnp.where(lane_ids(gram.shape) < table_rows, gram_high, gram - gram_high)
    block = jnp.concatenate([fourier, gram.astype(jnp.bfloat16)], axis=0)
    for target in range(out_ref.shape[0]):
        out_ref[target] = block


def backward_kernel(
    cycle_len, half_len, groups, blocks, real_groups, reals,
    cycle_ref, mode_ref, gathered_ref, spectrum_ref, legendre_ref, wiener_ref, signal_ref,
):
    group = lax.axis_index("grp")
    block = lax.axis_index("blk")
    real_group = lax.axis_index("real")
    high, low, outer = phase_factors(cycle_ref, mode_ref, cycle_len, half_len, group)
    modes = mode_ref.shape[1]
    table_rows = legendre_ref.shape[0]
    per_block = modes // blocks
    cycles = table_rows // per_block
    pixel_rows = outer.shape[0]
    half = LANES // 2
    square = (LANES, LANES)
    row, lane = row_ids(square), lane_ids(square)

    gram_all = gathered_ref[:, reals:, :].reshape(-1, LANES)
    pick = (row % cycles == 2 * block + lane // half) & (
        row % table_rows // cycles == lane % modes % per_block
    )
    gram_rows = jnp.dot(
        gram_all, pick.astype(jnp.float32).astype(jnp.bfloat16), preferred_element_type=jnp.float32
    ).reshape(groups, blocks, real_groups, cycles, LANES)
    holder = lane_ids((cycles, LANES)) % modes // per_block
    gram = jnp.zeros((cycles, LANES), jnp.float32)
    for b in range(blocks):
        one = gram_rows[:, b].reshape(-1, cycles, LANES).sum(axis=0)
        gram = gram + jnp.where(holder == b, one, 0.0)

    first = lane_ids((reals, LANES)) < half
    cycle_modes = jnp.zeros((reals, LANES), jnp.float32)
    for b in range(blocks):
        pair = jnp.zeros((reals, LANES), jnp.float32)
        for g in range(groups):
            source = (g * blocks + b) * real_groups + real_group
            pair = pair + gathered_ref[source, :reals, :].astype(jnp.float32)
        turned = pltpu.roll(pair, half, 1)
        cycle_modes = cycle_modes + jnp.where(first, pair, turned) * gram[2 * b : 2 * b + 1]
        cycle_modes = cycle_modes + jnp.where(first, turned, pair) * gram[2 * b + 1 : 2 * b + 2]
    cycle_modes = cycle_modes * modes**-0.5
    turned = pltpu.roll(cycle_modes, half, 1)
    even = jnp.where(first, cycle_modes, turned)
    odd = jnp.where(first, turned, cycle_modes)
    parity = (row_ids((1, 8, LANES)) & 1) == 0
    spread = jnp.where(parity, even[:, None, :], odd[:, None, :])
    rotated = spread[:, None] * outer.reshape(1, pixel_rows // 8, 8, LANES)
    rotated = rotated.reshape(reals * pixel_rows, LANES).astype(jnp.bfloat16)
    signal_ref[...] = lax.dot_general(
        jnp.concatenate([rotated, rotated], axis=1),
        jnp.concatenate([high, low], axis=1),
        NT,
        preferred_element_type=jnp.float32,
    )

    fourier_all = gathered_ref[:, :reals, :].reshape(-1, LANES)
    pick = (
        (row // half == lane % 2)
        & (row // modes % 2 == lane // half)
        & (row % modes == block * per_block + lane % half // cycles)
    )
    total_reals = real_groups * reals
    coeff_rows = jnp.dot(
        fourier_all, pick.astype(jnp.float32).astype(jnp.bfloat16), preferred_element_type=jnp.float32
    ).reshape(groups, blocks, total_reals, LANES)
    coeff_lane = lane_ids((total_reals, LANES))
    columns = jnp.zeros((total_reals, LANES), jnp.float32)
    for b in range(blocks):
        one = coeff_rows[:, b].sum(axis=0)
        columns = columns + jnp.where(coeff_lane % cycles // 2 == b, one, 0.0)
    pieces = [
        jnp.where((coeff_lane // half == c) & (coeff_lane % half // cycles == s), columns, 0.0)
        for s in range(per_block)
        for c in range(2)
    ]
    table = legendre_ref[...]
    spectrum = spectrum_ref[...]
    filtered = jnp.dot(
        jnp.concatenate(pieces, axis=0).astype(jnp.bfloat16),
        jnp.concatenate([table, table], axis=0),
        preferred_element_type=jnp.float32,
    ) * (spectrum / (spectrum + 0.5))
    tiles = table.shape[1] // LANES
    for s in range(per_block):
        for c in range(2):
            start = (s * 2 + c) * total_reals
            for tile in range(tiles):
                wiener_ref[
                    pl.ds((c * tiles + tile) * per_block + s, total_reals, stride=2 * tiles * per_block), :
                ] = filtered[start : start + total_reals, tile * LANES : (tile + 1) * LANES]


def split_tiles(array):
    lead, rows, columns = array.shape[:-2], array.shape[-2], array.shape[-1]
    split = array.reshape(*lead, rows, columns // LANES, LANES)
    return jnp.swapaxes(split, -2, -3).reshape(-1, LANES)


def gram_program(
    sky_data, signal_prev, noise_var, mask_flags, cycle_table, m_table, spectrum, legendre
):
    reals, cycle_dev, half_len = sky_data.shape
    groups, blocks, real_groups = (lax.axis_size(name) for name in AXES)
    cycle_len = half_len * groups
    per_block, multipoles, cycles = legendre.shape
    total_l = multipoles * groups * real_groups
    tiles = multipoles // LANES
    smem = pl.BlockSpec(memory_space=pltpu.SMEM)
    vmem = pl.BlockSpec(memory_space=pltpu.VMEM)
    orders = m_table[None, :]
    spectrum_row = spectrum[None, :]
    table = legendre.transpose(0, 2, 1).reshape(per_block * cycles, multipoles)
    local = pl.pallas_call(
        functools.partial(forward_kernel, cycle_len, half_len, (cycles / total_l) ** 0.5),
        out_shape=jax.ShapeDtypeStruct(
            (groups * blocks * real_groups, reals + cycles, LANES), jnp.bfloat16
        ),
        in_specs=[smem] + [vmem] * 7,
        out_specs=vmem,
    )(
        cycle_table, orders, split_tiles(sky_data), split_tiles(signal_prev),
        split_tiles(noise_var), split_tiles(mask_flags), spectrum_row, table,
    )
    gathered = lax.all_to_all(local, AXES, 0, 0, tiled=True)
    total_reals = reals * real_groups
    wiener, signal = pl.pallas_call(
        functools.partial(backward_kernel, cycle_len, half_len, groups, blocks, real_groups, reals),
        out_shape=(
            jax.ShapeDtypeStruct((total_reals * 2 * tiles * per_block, LANES), jnp.float32),
            jax.ShapeDtypeStruct((reals * cycle_dev * half_len // LANES, LANES), jnp.float32),
        ),
        in_specs=[smem] + [vmem] * 4,
        out_specs=(vmem, vmem),
    )(cycle_table, orders, gathered, spectrum_row, table)
    wiener = wiener.reshape(total_reals, 2, tiles, per_block, LANES).transpose(0, 1, 3, 2, 4)
    signal = signal.reshape(reals, half_len // LANES, cycle_dev, LANES).transpose(0, 2, 1, 3)
    return (
        wiener.reshape(total_reals, 2, per_block, multipoles),
        signal.reshape(sky_data.shape),
    )


def gram_form_fits(mesh, sky_data, m_table, legendre):
    groups, blocks, real_groups = (mesh.shape[name] for name in AXES)
    reals, cycles, cycle_len = sky_data.shape
    modes = m_table.shape[0]
    per_block = modes // blocks
    multipoles = legendre.shape[1] // (groups * real_groups)
    half_len = cycle_len // groups
    reals_dev = reals // real_groups
    return (
        cycles < 2 * reals
        and 4 * modes == LANES
        and cycles == 2 * blocks
        and 2 * per_block * cycles == LANES
        and cycle_len & (cycle_len - 1) == 0
        and half_len % (4 * LANES) == 0
        and multipoles % LANES == 0
        and reals_dev % 16 == 0
        and cycles % 16 == 0
    )


def phase_tables(col_ids, mode_ids, cycle_len):
    product_ids = col_ids[:, None] * mode_ids[None, :] % cycle_len
    angles = product_ids.astype(jnp.float32) * (2.0 * math.pi / cycle_len)
    return (jnp.cos(angles).astype(jnp.bfloat16), jnp.sin(angles).astype(jnp.bfloat16))


def cycle_offsets(cycle_ids, mode_ids, cycle_len):
    parity = (cycle_ids % 2).astype(jnp.float32)
    shifts = math.pi / cycle_len * parity[:, None] * mode_ids[None, :].astype(jnp.float32)
    return (jnp.cos(shifts), jnp.sin(shifts))


def forward_modes(re_part, im_part):
    summed = lax.psum((re_part, im_part), "grp")
    fourier_pair = (summed[0].astype(jnp.bfloat16), summed[1].astype(jnp.bfloat16))
    fourier_pair = (
        lax.all_gather(fourier_pair[0], "real", axis=0, tiled=True),
        lax.all_gather(fourier_pair[1], "real", axis=0, tiled=True),
    )
    fourier_pair = (
        lax.all_to_all(fourier_pair[0], "blk", split_axis=2, concat_axis=1, tiled=True),
        lax.all_to_all(fourier_pair[1], "blk", split_axis=2, concat_axis=1, tiled=True),
    )
    return fourier_pair


def backward_cycles(partial_value):
    summed = lax.psum_scatter(partial_value, "real", scatter_dimension=0, tiled=True)
    reduced = lax.psum(summed, "grp")
    cycle_pair = lax.all_to_all(
        reduced.astype(jnp.bfloat16), "blk", split_axis=2, concat_axis=3, tiled=True
    )
    return cycle_pair


def per_device(
    sky_data, signal_prev, noise_var, mask_flags, cycle_table, m_table, spectrum, legendre
):
    real_dev, cycle_dev, half_len = sky_data.shape
    cycle_len = half_len * lax.axis_size("grp")
    mode_count = m_table.shape[0]
    col_ids = lax.axis_index("grp") * half_len + jnp.arange(half_len, dtype=jnp.int32)
    cos_tab, sin_tab = phase_tables(col_ids, m_table, cycle_len)
    cos_shift, sin_shift = cycle_offsets(cycle_table, m_table, cycle_len)
    weight = mask_flags.astype(jnp.float32) / (noise_var - 0.5)
    messenger = (weight * sky_data + 2.0 * signal_prev) / (weight + 2.0)
    flat_rows = messenger.astype(jnp.bfloat16).reshape(real_dev * cycle_dev, half_len)
    base_cos = jnp.dot(flat_rows, cos_tab, preferred_element_type=jnp.float32).reshape(
        real_dev, cycle_dev, mode_count
    )
    base_sin = -jnp.dot(flat_rows, sin_tab, preferred_element_type=jnp.float32).reshape(
        real_dev, cycle_dev, mode_count
    )
    norm_scale = cycle_len ** (-0.5)
    re_part = (base_cos * cos_shift + base_sin * sin_shift) * norm_scale
    im_part = (base_sin * cos_shift - base_cos * sin_shift) * norm_scale
    fourier_re, fourier_im = forward_modes(re_part, im_part)
    fourier = jnp.stack([fourier_re, fourier_im], 1)
    coefficients = jnp.einsum(
        "mlr,kcrm->kcml", legendre, fourier, preferred_element_type=jnp.float32
    )
    factor = spectrum / (spectrum + 0.5)
    wiener_alm = coefficients * factor
    total_l = legendre.shape[1] * lax.axis_size("grp") * lax.axis_size("real")
    syn_scale = (legendre.shape[2] / total_l) ** 0.5
    partial_value = (
        jnp.einsum(
            "mlr,kcml->kcrm",
            legendre,
            wiener_alm.astype(jnp.bfloat16),
            preferred_element_type=jnp.float32,
        )
        * syn_scale
    )
    cycle_pair = backward_cycles(partial_value)
    cycle_modes = cycle_pair.astype(jnp.float32)
    modes_re = cycle_modes[:, 0]
    modes_im = cycle_modes[:, 1]
    rotated_re = (modes_re * cos_shift - modes_im * sin_shift).astype(jnp.bfloat16)
    rotated_im = (modes_im * cos_shift + modes_re * sin_shift).astype(jnp.bfloat16)
    contract = (((1,), (1,)), ((), ()))
    pixel_sum = lax.dot_general(
        rotated_re.reshape(-1, mode_count), cos_tab, contract, preferred_element_type=jnp.float32
    )
    pixel_sum = pixel_sum - lax.dot_general(
        rotated_im.reshape(-1, mode_count), sin_tab, contract, preferred_element_type=jnp.float32
    )
    signal_next = (pixel_sum * mode_count ** (-0.5)).reshape(real_dev, cycle_dev, half_len)
    return (wiener_alm, signal_next)


def solution(mesh):
    in_specs = (
        P("real", "blk", "grp"),
        P("real", "blk", "grp"),
        P("blk", "grp"),
        P("blk", "grp"),
        P("blk"),
        P(),
        P(("grp", "real")),
        P("blk", ("grp", "real"), None),
    )
    out_specs = (P(None, None, "blk", ("grp", "real")), P("real", "blk", "grp"))

    def step(sky_data, signal_prev, noise_var, mask_flags, cycle_table, m_table, spectrum, legendre):
        fits = gram_form_fits(mesh, sky_data, m_table, legendre)
        return jax.shard_map(
            gram_program if fits else per_device,
            mesh=mesh,
            in_specs=in_specs,
            out_specs=out_specs,
            check_vma=False,
        )(sky_data, signal_prev, noise_var, mask_flags, cycle_table, m_table, spectrum, legendre)

    return step
```

```python
import functools
import math

import jax
import jax.numpy as jnp
from jax import lax
from jax.experimental import pallas as pl
from jax.experimental.pallas import tpu as pltpu
from jax.sharding import PartitionSpec as P

LANES = 128
NT = (((1,), (1,)), ((), ()))
AXES = ("grp", "blk", "real")
PARTS = 4


def unit_cosine(units, half_turn):
    wrapped = units & (2 * half_turn - 1)
    folded = jnp.minimum(wrapped, 2 * half_turn - wrapped)
    y = (half_turn // 2 - folded).astype(jnp.float32) * (math.pi / half_turn)
    y2 = y * y
    acc = jnp.full_like(y2, -1.0 / math.factorial(11))
    for order, sign in ((9, 1.0), (7, -1.0), (5, 1.0), (3, -1.0), (1, 1.0)):
        acc = acc * y2 + sign / math.factorial(order)
    return acc * y


def lane_ids(shape):
    return lax.broadcasted_iota(jnp.int32, shape, len(shape) - 1)


def row_ids(shape):
    return lax.broadcasted_iota(jnp.int32, shape, len(shape) - 2)


def phase_factors(cycle_ref, orders, cycle_len, half_len, group):
    modes = orders.shape[1]
    orders = jnp.concatenate([orders] * (LANES // modes), axis=1)
    quarter = lane_ids((1, LANES)) // modes
    quarter_turn = cycle_len // 2
    inner_units = 2 * orders * row_ids((LANES, LANES)) + ((quarter + 1) >> 1) * quarter_turn
    inner = unit_cosine(inner_units, cycle_len)
    rows = 2 * (half_len // LANES)
    row = row_ids((rows, LANES))
    parity = jnp.where((row & 1) == 0, cycle_ref[0] & 1, cycle_ref[1] & 1)
    pixel = group * half_len + LANES * (row >> 1)
    outer_units = orders * (2 * pixel + parity) + (quarter >> 1) * (3 * quarter_turn)
    outer = unit_cosine(outer_units, cycle_len)
    high = inner.astype(jnp.bfloat16)
    low = (inner - high.astype(jnp.float32)).astype(jnp.bfloat16)
    return high, low, outer


def start_copies(sources, targets, sems, first=0):
    copies = [
        pltpu.make_async_copy(source, target, sems.at[first + i])
        for i, (source, target) in enumerate(zip(sources, targets))
    ]
    for copy in copies:
        copy.start()
    return copies


def row_parts(ref, parts):
    size = ref.shape[0] // parts
    return [ref.at[pl.ds(i * size, size)] for i in range(parts)]


def forward_kernel(
    cycle_len, half_len, syn_scale, parts,
    cycle_hbm, mode_hbm, noise_hbm, mask_hbm, spectrum_hbm, legendre_hbm, sky_hbm, prev_hbm, out_ref,
    cycle_ref, mode_ref, noise_ref, mask_ref, spectrum_ref, legendre_ref, sky_ref, prev_ref, sems,
):
    small = start_copies(
        (cycle_hbm, mode_hbm, noise_hbm, mask_hbm, spectrum_hbm, legendre_hbm),
        (cycle_ref, mode_ref, noise_ref, mask_ref, spectrum_ref, legendre_ref),
        sems,
    )
    sources = [part for pair in zip(row_parts(sky_hbm, parts), row_parts(prev_hbm, parts)) for part in pair]
    targets = [part for pair in zip(row_parts(sky_ref, parts), row_parts(prev_ref, parts)) for part in pair]
    large = start_copies(sources, targets, sems, len(small))
    group = lax.axis_index("grp")
    small[0].wait()
    small[1].wait()
    high, low, outer = phase_factors(cycle_ref, mode_ref[...], cycle_len, half_len, group)
    inner = jnp.concatenate([high, low], axis=0)
    small[2].wait()
    small[3].wait()
    weight = mask_ref[...].astype(jnp.float32) / (noise_ref[...] - 0.5)
    inverse = 1.0 / (weight + 2.0)
    sky_gain = weight * inverse
    prev_gain = 2.0 * inverse

    small[4].wait()
    small[5].wait()
    table = legendre_ref[...]
    spectrum = spectrum_ref[...]
    factor = spectrum / (spectrum + 0.5)
    filtered = (table.astype(jnp.float32) * factor).astype(jnp.bfloat16)
    gram = lax.dot_general(
        table, jnp.concatenate([filtered, filtered], axis=0), NT, preferred_element_type=jnp.float32
    )
    table_rows = table.shape[0]
    pixel_rows = outer.shape[0]
    reals = sky_ref.shape[0] // pixel_rows
    cycles = 2 * (out_ref.shape[1] - reals)
    same = row_ids(gram.shape) // cycles == lane_ids(gram.shape) % table_rows // cycles
    gram = jnp.where(same, gram, 0.0).reshape(table_rows // cycles, cycles, LANES).sum(axis=0)
    gram = gram * syn_scale
    low_rows, high_rows = gram[: cycles // 2], gram[cycles // 2 :]
    gram = jnp.where(lane_ids(low_rows.shape) < LANES // 2, low_rows, high_rows).astype(jnp.bfloat16)

    part_reals = reals // parts
    shape = (part_reals, pixel_rows, LANES)
    fourier = []
    for i in range(parts):
        large[2 * i].wait()
        large[2 * i + 1].wait()
        span = pl.ds(i * part_reals * pixel_rows, part_reals * pixel_rows)
        sky = sky_ref[span, :].reshape(shape)
        prev = prev_ref[span, :].reshape(shape)
        rows = (sky * sky_gain + prev * prev_gain).reshape(-1, LANES).astype(jnp.bfloat16)
        partial = jnp.dot(
            jnp.concatenate([rows, rows], axis=1), inner, preferred_element_type=jnp.float32
        )
        turned = partial.reshape(shape) * outer
        summed = turned.reshape(part_reals, pixel_rows // 8, 8, LANES).sum(axis=1)
        summed = summed.reshape(part_reals * 8, LANES)
        summed = summed + pltpu.roll(summed, LANES // 2, 1)
        own = (row_ids(summed.shape) & 1) == (lane_ids(summed.shape) >= LANES // 2)
        fourier.append(jnp.where(own, summed, 0.0).reshape(part_reals, 8, LANES).sum(axis=1))
    fourier = (jnp.concatenate(fourier, axis=0) * cycle_len**-0.5).astype(jnp.bfloat16)
    block = jnp.concatenate([fourier, gram], axis=0)
    for target in range(out_ref.shape[0]):
        out_ref[target] = block


def backward_kernel(
    cycle_len, half_len, groups, blocks, real_groups, reals, parts,
    cycle_hbm, mode_hbm, gathered_hbm, legendre_hbm, spectrum_hbm, wiener_hbm, signal_hbm,
    cycle_ref, mode_ref, gathered_ref, legendre_ref, spectrum_ref, wiener_ref, signal_ref, sems, out_sems,
):
    loads = start_copies(
        (cycle_hbm, mode_hbm, gathered_hbm, legendre_hbm, spectrum_hbm),
        (cycle_ref, mode_ref, gathered_ref, legendre_ref, spectrum_ref),
        sems,
    )
    group = lax.axis_index("grp")
    block = lax.axis_index("blk")
    real_group = lax.axis_index("real")
    loads[0].wait()
    loads[1].wait()
    high, low, outer = phase_factors(cycle_ref, mode_ref[...], cycle_len, half_len, group)
    modes = mode_ref.shape[1]
    table_rows = legendre_ref.shape[0]
    per_block = modes // blocks
    cycles = table_rows // per_block
    pixel_rows = outer.shape[0]
    half = LANES // 2
    square = (LANES, LANES)
    row, lane = row_ids(square), lane_ids(square)
    coeff_pick = (
        (row // half == lane % 2)
        & (row // modes % 2 == lane // half)
        & (row % modes == block * per_block + lane % half // cycles)
    )
    coeff_pick = coeff_pick.astype(jnp.float32).astype(jnp.bfloat16)
    gram_pick = (row % cycles == 2 * block + lane // half) & (
        row % table_rows // cycles == lane % modes % per_block
    )
    gram_pick = jnp.concatenate([gram_pick & (row < half), gram_pick & (row >= half)], axis=1)
    gram_pick = gram_pick.astype(jnp.float32).astype(jnp.bfloat16)
    loads[2].wait()

    fourier_all = gathered_ref[:, :reals, :].reshape(-1, LANES)
    total_reals = real_groups * reals
    coeff_rows = jnp.dot(fourier_all, coeff_pick, preferred_element_type=jnp.float32).reshape(
        groups, blocks, total_reals, LANES
    )
    coeff_lane = lane_ids((total_reals, LANES))
    columns = jnp.zeros((total_reals, LANES), jnp.float32)
    for b in range(blocks):
        one = coeff_rows[:, b].sum(axis=0)
        columns = columns + jnp.where(coeff_lane % cycles // 2 == b, one, 0.0)
    loads[3].wait()
    loads[4].wait()
    table = legendre_ref[...]
    table = jnp.concatenate([table, table], axis=0)
    spectrum = spectrum_ref[...]
    factor = spectrum / (spectrum + 0.5)
    tiles = table.shape[1] // LANES
    stride = 2 * tiles * per_block
    stores = []
    lane = lane_ids((reals, LANES))
    for y in range(real_groups):
        pieces = [
            jnp.where(
                (lane // half == c) & (lane % half // cycles == s), columns[y * reals : (y + 1) * reals], 0.0
            )
            for s in range(per_block)
            for c in range(2)
        ]
        filtered = factor * jnp.dot(
            jnp.concatenate(pieces, axis=0).astype(jnp.bfloat16), table, preferred_element_type=jnp.float32
        )
        for s in range(per_block):
            for c in range(2):
                start = (s * 2 + c) * reals
                for tile in range(tiles):
                    first_row = y * reals * stride + (c * tiles + tile) * per_block + s
                    wiener_ref[pl.ds(first_row, reals, stride=stride), :] = filtered[
                        start : start + reals, tile * LANES : (tile + 1) * LANES
                    ]
        span = pl.ds(y * reals * stride, reals * stride)
        stores += start_copies([wiener_ref.at[span]], [wiener_hbm.at[span]], out_sems, len(stores))

    gram_all = gathered_ref[:, reals:, :].reshape(-1, LANES)
    gram_rows = jnp.dot(gram_all, gram_pick, preferred_element_type=jnp.float32)
    gram_rows = gram_rows.reshape(groups, blocks, real_groups, cycles // 2, 2 * LANES)
    holder = lane_ids((cycles // 2, 2 * LANES)) % modes // per_block
    gram = jnp.zeros(holder.shape, jnp.float32)
    for b in range(blocks):
        one = gram_rows[:, b].reshape(-1, cycles // 2, 2 * LANES).sum(axis=0)
        gram = gram + jnp.where(holder == b, one, 0.0)
    gram = jnp.concatenate([gram[:, :LANES], gram[:, LANES:]], axis=0)

    first = lane < half
    cycle_modes = jnp.zeros((reals, LANES), jnp.float32)
    for b in range(blocks):
        pair = jnp.zeros((reals, LANES), jnp.float32)
        for g in range(groups):
            source = (g * blocks + b) * real_groups + real_group
            pair = pair + gathered_ref[source, :reals, :].astype(jnp.float32)
        turned = pltpu.roll(pair, half, 1)
        cycle_modes = cycle_modes + jnp.where(first, pair, turned) * gram[2 * b : 2 * b + 1]
        cycle_modes = cycle_modes + jnp.where(first, turned, pair) * gram[2 * b + 1 : 2 * b + 2]
    cycle_modes = cycle_modes * modes**-0.5
    turned = pltpu.roll(cycle_modes, half, 1)
    even = jnp.where(first, cycle_modes, turned)
    odd = jnp.where(first, turned, cycle_modes)
    parity = (row_ids((1, 8, LANES)) & 1) == 0
    spread = jnp.where(parity, even[:, None, :], odd[:, None, :])
    inner = jnp.concatenate([high, low], axis=1)
    outer = outer.reshape(1, pixel_rows // 8, 8, LANES)
    part_reals = reals // parts
    for i in range(parts):
        rotated = spread[i * part_reals : (i + 1) * part_reals, None] * outer
        rotated = rotated.reshape(part_reals * pixel_rows, LANES).astype(jnp.bfloat16)
        span = pl.ds(i * part_reals * pixel_rows, part_reals * pixel_rows)
        signal_ref[span, :] = lax.dot_general(
            jnp.concatenate([rotated, rotated], axis=1), inner, NT, preferred_element_type=jnp.float32
        )
        stores += start_copies([signal_ref.at[span]], [signal_hbm.at[span]], out_sems, len(stores))
    for store in stores:
        store.wait()


def split_tiles(array):
    lead, rows, columns = array.shape[:-2], array.shape[-2], array.shape[-1]
    split = array.reshape(*lead, rows, columns // LANES, LANES)
    return jnp.swapaxes(split, -2, -3).reshape(-1, LANES)


def gram_program(
    sky_data, signal_prev, noise_var, mask_flags, cycle_table, m_table, spectrum, legendre
):
    reals, cycle_dev, half_len = sky_data.shape
    groups, blocks, real_groups = (lax.axis_size(name) for name in AXES)
    cycle_len = half_len * groups
    per_block, multipoles, cycles = legendre.shape
    total_l = multipoles * groups * real_groups
    tiles = multipoles // LANES
    hbm = pl.BlockSpec(memory_space=pl.ANY)
    vmem = pl.BlockSpec(memory_space=pltpu.VMEM)
    orders = m_table[None, :]
    spectrum_row = spectrum[None, :]
    table = legendre.transpose(0, 2, 1).reshape(per_block * cycles, multipoles)
    inputs = (
        cycle_table, orders, split_tiles(noise_var), split_tiles(mask_flags), spectrum_row, table,
        split_tiles(sky_data), split_tiles(signal_prev),
    )
    spaces = [pltpu.SMEM] + [pltpu.VMEM] * 7
    sources = groups * blocks * real_groups
    local = pl.pallas_call(
        functools.partial(forward_kernel, cycle_len, half_len, (cycles / total_l) ** 0.5, PARTS),
        out_shape=jax.ShapeDtypeStruct((sources, reals + cycles // 2, LANES), jnp.bfloat16),
        in_specs=[hbm] * 8,
        out_specs=vmem,
        scratch_shapes=[space(x.shape, x.dtype) for space, x in zip(spaces, inputs)]
        + [pltpu.SemaphoreType.DMA((6 + 2 * PARTS,))],
    )(*inputs)
    gathered = lax.all_to_all(local, AXES, 0, 0, tiled=True)
    total_reals = reals * real_groups
    inputs = (cycle_table, orders, gathered, table, spectrum_row)
    outputs = (
        jax.ShapeDtypeStruct((total_reals * 2 * tiles * per_block, LANES), jnp.float32),
        jax.ShapeDtypeStruct((reals * cycle_dev * half_len // LANES, LANES), jnp.float32),
    )
    wiener, signal = pl.pallas_call(
        functools.partial(backward_kernel, cycle_len, half_len, groups, blocks, real_groups, reals, PARTS),
        out_shape=outputs,
        in_specs=[hbm] * 5,
        out_specs=(hbm, hbm),
        scratch_shapes=[space(x.shape, x.dtype) for space, x in zip(spaces, inputs)]
        + [pltpu.VMEM(x.shape, x.dtype) for x in outputs]
        + [pltpu.SemaphoreType.DMA((5,)), pltpu.SemaphoreType.DMA((real_groups + PARTS,))],
    )(*inputs)
    wiener = wiener.reshape(total_reals, 2, tiles, per_block, LANES).transpose(0, 1, 3, 2, 4)
    signal = signal.reshape(reals, half_len // LANES, cycle_dev, LANES).transpose(0, 2, 1, 3)
    return (
        wiener.reshape(total_reals, 2, per_block, multipoles),
        signal.reshape(sky_data.shape),
    )


def gram_form_fits(mesh, sky_data, m_table, legendre):
    groups, blocks, real_groups = (mesh.shape[name] for name in AXES)
    reals, cycles, cycle_len = sky_data.shape
    modes = m_table.shape[0]
    per_block = modes // blocks
    multipoles = legendre.shape[1] // (groups * real_groups)
    half_len = cycle_len // groups
    reals_dev = reals // real_groups
    return (
        cycles < 2 * reals
        and 4 * modes == LANES
        and cycles == 2 * blocks
        and 2 * per_block * cycles == LANES
        and cycle_len & (cycle_len - 1) == 0
        and half_len % (4 * LANES) == 0
        and multipoles % LANES == 0
        and reals_dev % 16 == 0
        and reals_dev % PARTS == 0
        and cycles % 16 == 0
    )


def phase_tables(col_ids, mode_ids, cycle_len):
    product_ids = col_ids[:, None] * mode_ids[None, :] % cycle_len
    angles = product_ids.astype(jnp.float32) * (2.0 * math.pi / cycle_len)
    return (jnp.cos(angles).astype(jnp.bfloat16), jnp.sin(angles).astype(jnp.bfloat16))


def cycle_offsets(cycle_ids, mode_ids, cycle_len):
    parity = (cycle_ids % 2).astype(jnp.float32)
    shifts = math.pi / cycle_len * parity[:, None] * mode_ids[None, :].astype(jnp.float32)
    return (jnp.cos(shifts), jnp.sin(shifts))


def forward_modes(re_part, im_part):
    summed = lax.psum((re_part, im_part), "grp")
    fourier_pair = (summed[0].astype(jnp.bfloat16), summed[1].astype(jnp.bfloat16))
    fourier_pair = (
        lax.all_gather(fourier_pair[0], "real", axis=0, tiled=True),
        lax.all_gather(fourier_pair[1], "real", axis=0, tiled=True),
    )
    fourier_pair = (
        lax.all_to_all(fourier_pair[0], "blk", split_axis=2, concat_axis=1, tiled=True),
        lax.all_to_all(fourier_pair[1], "blk", split_axis=2, concat_axis=1, tiled=True),
    )
    return fourier_pair


def backward_cycles(partial_value):
    summed = lax.psum_scatter(partial_value, "real", scatter_dimension=0, tiled=True)
    reduced = lax.psum(summed, "grp")
    cycle_pair = lax.all_to_all(
        reduced.astype(jnp.bfloat16), "blk", split_axis=2, concat_axis=3, tiled=True
    )
    return cycle_pair


def per_device(
    sky_data, signal_prev, noise_var, mask_flags, cycle_table, m_table, spectrum, legendre
):
    real_dev, cycle_dev, half_len = sky_data.shape
    cycle_len = half_len * lax.axis_size("grp")
    mode_count = m_table.shape[0]
    col_ids = lax.axis_index("grp") * half_len + jnp.arange(half_len, dtype=jnp.int32)
    cos_tab, sin_tab = phase_tables(col_ids, m_table, cycle_len)
    cos_shift, sin_shift = cycle_offsets(cycle_table, m_table, cycle_len)
    weight = mask_flags.astype(jnp.float32) / (noise_var - 0.5)
    messenger = (weight * sky_data + 2.0 * signal_prev) / (weight + 2.0)
    flat_rows = messenger.astype(jnp.bfloat16).reshape(real_dev * cycle_dev, half_len)
    base_cos = jnp.dot(flat_rows, cos_tab, preferred_element_type=jnp.float32).reshape(
        real_dev, cycle_dev, mode_count
    )
    base_sin = -jnp.dot(flat_rows, sin_tab, preferred_element_type=jnp.float32).reshape(
        real_dev, cycle_dev, mode_count
    )
    norm_scale = cycle_len ** (-0.5)
    re_part = (base_cos * cos_shift + base_sin * sin_shift) * norm_scale
    im_part = (base_sin * cos_shift - base_cos * sin_shift) * norm_scale
    fourier_re, fourier_im = forward_modes(re_part, im_part)
    fourier = jnp.stack([fourier_re, fourier_im], 1)
    coefficients = jnp.einsum(
        "mlr,kcrm->kcml", legendre, fourier, preferred_element_type=jnp.float32
    )
    factor = spectrum / (spectrum + 0.5)
    wiener_alm = coefficients * factor
    total_l = legendre.shape[1] * lax.axis_size("grp") * lax.axis_size("real")
    syn_scale = (legendre.shape[2] / total_l) ** 0.5
    partial_value = (
        jnp.einsum(
            "mlr,kcml->kcrm",
            legendre,
            wiener_alm.astype(jnp.bfloat16),
            preferred_element_type=jnp.float32,
        )
        * syn_scale
    )
    cycle_pair = backward_cycles(partial_value)
    cycle_modes = cycle_pair.astype(jnp.float32)
    modes_re = cycle_modes[:, 0]
    modes_im = cycle_modes[:, 1]
    rotated_re = (modes_re * cos_shift - modes_im * sin_shift).astype(jnp.bfloat16)
    rotated_im = (modes_im * cos_shift + modes_re * sin_shift).astype(jnp.bfloat16)
    contract = (((1,), (1,)), ((), ()))
    pixel_sum = lax.dot_general(
        rotated_re.reshape(-1, mode_count), cos_tab, contract, preferred_element_type=jnp.float32
    )
    pixel_sum = pixel_sum - lax.dot_general(
        rotated_im.reshape(-1, mode_count), sin_tab, contract, preferred_element_type=jnp.float32
    )
    signal_next = (pixel_sum * mode_count ** (-0.5)).reshape(real_dev, cycle_dev, half_len)
    return (wiener_alm, signal_next)


def solution(mesh):
    in_specs = (
        P("real", "blk", "grp"),
        P("real", "blk", "grp"),
        P("blk", "grp"),
        P("blk", "grp"),
        P("blk"),
        P(),
        P(("grp", "real")),
        P("blk", ("grp", "real"), None),
    )
    out_specs = (P(None, None, "blk", ("grp", "real")), P("real", "blk", "grp"))

    def step(sky_data, signal_prev, noise_var, mask_flags, cycle_table, m_table, spectrum, legendre):
        fits = gram_form_fits(mesh, sky_data, m_table, legendre)
        return jax.shard_map(
            gram_program if fits else per_device,
            mesh=mesh,
            in_specs=in_specs,
            out_specs=out_specs,
            check_vma=False,
        )(sky_data, signal_prev, noise_var, mask_flags, cycle_table, m_table, spectrum, legendre)

    return step
```

```python
import functools
import math

import jax
import jax.numpy as jnp
from jax import lax
from jax.experimental import pallas as pl
from jax.experimental.pallas import tpu as pltpu
from jax.sharding import PartitionSpec as P

LANES = 128
NT = (((1,), (1,)), ((), ()))
AXES = ("grp", "blk", "real")
PARTS = 2


def unit_cosine(units, half_turn):
    wrapped = units & (2 * half_turn - 1)
    folded = jnp.minimum(wrapped, 2 * half_turn - wrapped)
    y = (half_turn // 2 - folded).astype(jnp.float32) * (math.pi / half_turn)
    y2 = y * y
    acc = jnp.full_like(y2, -1.0 / math.factorial(11))
    for order, sign in ((9, 1.0), (7, -1.0), (5, 1.0), (3, -1.0), (1, 1.0)):
        acc = acc * y2 + sign / math.factorial(order)
    return acc * y


def log2(size):
    return size.bit_length() - 1


def lane_ids(shape):
    return lax.broadcasted_iota(jnp.int32, shape, len(shape) - 1)


def row_ids(shape):
    return lax.broadcasted_iota(jnp.int32, shape, len(shape) - 2)


def phase_factors(cycle_ref, orders, cycle_len, half_len, group):
    modes = orders.shape[1]
    orders = jnp.concatenate([orders] * (LANES // modes), axis=1)
    quarter = lane_ids((1, LANES)) >> log2(modes)
    quarter_turn = cycle_len // 2
    inner_units = 2 * orders * row_ids((LANES, LANES)) + ((quarter + 1) >> 1) * quarter_turn
    inner = unit_cosine(inner_units, cycle_len)
    rows = 2 * (half_len // LANES)
    row = row_ids((rows, LANES))
    parity = jnp.where((row & 1) == 0, cycle_ref[0] & 1, cycle_ref[1] & 1)
    pixel = group * half_len + LANES * (row >> 1)
    outer_units = orders * (2 * pixel + parity) + (quarter >> 1) * (3 * quarter_turn)
    outer = unit_cosine(outer_units, cycle_len)
    high = inner.astype(jnp.bfloat16)
    low = (inner - high.astype(jnp.float32)).astype(jnp.bfloat16)
    return high, low, outer


def start_copies(sources, targets, sems, first=0):
    copies = [
        pltpu.make_async_copy(source, target, sems.at[first + i])
        for i, (source, target) in enumerate(zip(sources, targets))
    ]
    for copy in copies:
        copy.start()
    return copies


def row_parts(ref, parts):
    size = ref.shape[0] // parts
    return [ref.at[pl.ds(i * size, size)] for i in range(parts)]


def forward_kernel(
    cycle_len, half_len, syn_scale, parts,
    cycle_hbm, mode_hbm, noise_hbm, mask_hbm, spectrum_hbm, legendre_hbm, sky_hbm, prev_hbm, out_ref,
    cycle_ref, mode_ref, noise_ref, mask_ref, spectrum_ref, legendre_ref, sky_ref, prev_ref, sems,
):
    small = start_copies(
        (cycle_hbm, mode_hbm, noise_hbm, mask_hbm, spectrum_hbm, legendre_hbm),
        (cycle_ref, mode_ref, noise_ref, mask_ref, spectrum_ref, legendre_ref),
        sems,
    )
    sources = [part for pair in zip(row_parts(sky_hbm, parts), row_parts(prev_hbm, parts)) for part in pair]
    targets = [part for pair in zip(row_parts(sky_ref, parts), row_parts(prev_ref, parts)) for part in pair]
    large = start_copies(sources, targets, sems, len(small))
    group = lax.axis_index("grp")
    small[0].wait()
    small[1].wait()
    high, low, outer = phase_factors(cycle_ref, mode_ref[...], cycle_len, half_len, group)
    inner = jnp.concatenate([high, low], axis=0)
    small[2].wait()
    small[3].wait()
    weight = mask_ref[...].astype(jnp.float32) / (noise_ref[...] - 0.5)
    inverse = 1.0 / (weight + 2.0)
    sky_gain = weight * inverse
    prev_gain = 2.0 * inverse

    small[4].wait()
    small[5].wait()
    table = legendre_ref[...]
    spectrum = spectrum_ref[...]
    factor = spectrum / (spectrum + 0.5)
    filtered = (table.astype(jnp.float32) * factor).astype(jnp.bfloat16)
    gram = lax.dot_general(
        table, jnp.concatenate([filtered, filtered], axis=0), NT, preferred_element_type=jnp.float32
    )
    table_rows = table.shape[0]
    pixel_rows = outer.shape[0]
    reals = sky_ref.shape[0] // pixel_rows
    cycles = 2 * (out_ref.shape[1] - reals)
    order = (lane_ids((1, LANES)) & (table_rows - 1)) >> log2(cycles)
    same = (row_ids(gram.shape) >> log2(cycles)) == order
    gram = jnp.where(same, gram, 0.0).reshape(table_rows // cycles, cycles, LANES).sum(axis=0)
    gram = gram * syn_scale
    low_rows, high_rows = gram[: cycles // 2], gram[cycles // 2 :]
    gram = jnp.where(lane_ids(low_rows.shape) < LANES // 2, low_rows, high_rows).astype(jnp.bfloat16)

    part_reals = reals // parts
    shape = (part_reals, pixel_rows, LANES)
    fourier = []
    for i in range(parts):
        large[2 * i].wait()
        large[2 * i + 1].wait()
        span = pl.ds(i * part_reals * pixel_rows, part_reals * pixel_rows)
        sky = sky_ref[span, :].reshape(shape)
        prev = prev_ref[span, :].reshape(shape)
        rows = (sky * sky_gain + prev * prev_gain).reshape(-1, LANES).astype(jnp.bfloat16)
        partial = jnp.dot(
            jnp.concatenate([rows, rows], axis=1), inner, preferred_element_type=jnp.float32
        )
        turned = partial.reshape(shape) * outer
        summed = turned.reshape(part_reals, pixel_rows // 8, 8, LANES).sum(axis=1)
        summed = summed.reshape(part_reals * 8, LANES)
        summed = summed + pltpu.roll(summed, LANES // 2, 1)
        own = (row_ids(summed.shape) & 1) == (lane_ids(summed.shape) >= LANES // 2)
        fourier.append(jnp.where(own, summed, 0.0).reshape(part_reals, 8, LANES).sum(axis=1))
    fourier = (jnp.concatenate(fourier, axis=0) * cycle_len**-0.5).astype(jnp.bfloat16)
    block = jnp.concatenate([fourier, gram], axis=0)
    for target in range(out_ref.shape[0]):
        out_ref[target] = block


def backward_kernel(
    cycle_len, half_len, groups, blocks, real_groups, reals, parts,
    cycle_hbm, mode_hbm, gathered_hbm, legendre_hbm, spectrum_hbm, wiener_hbm, signal_hbm,
    cycle_ref, mode_ref, gathered_ref, legendre_ref, spectrum_ref, wiener_ref, signal_ref, sems, out_sems,
):
    loads = start_copies(
        (cycle_hbm, mode_hbm, gathered_hbm, legendre_hbm, spectrum_hbm),
        (cycle_ref, mode_ref, gathered_ref, legendre_ref, spectrum_ref),
        sems,
    )
    group = lax.axis_index("grp")
    block = lax.axis_index("blk")
    real_group = lax.axis_index("real")
    loads[0].wait()
    loads[1].wait()
    high, low, outer = phase_factors(cycle_ref, mode_ref[...], cycle_len, half_len, group)
    modes = mode_ref.shape[1]
    table_rows = legendre_ref.shape[0]
    per_block = modes // blocks
    cycles = table_rows // per_block
    pixel_rows = outer.shape[0]
    half = LANES // 2
    lane = lane_ids((1, LANES))
    row = row_ids((LANES, LANES))
    lane_order = (lane & (half - 1)) >> log2(cycles)
    lane_row = (lane & 1) * half + (lane >> log2(half)) * modes + block * per_block + lane_order
    coeff_pick = (row == lane_row).astype(jnp.float32).astype(jnp.bfloat16)
    lane_row = (lane & (per_block - 1)) * cycles + 2 * block + (lane >> log2(half))
    gram_pick = jnp.concatenate([row == lane_row, row == lane_row + half], axis=1)
    gram_pick = gram_pick.astype(jnp.float32).astype(jnp.bfloat16)
    holder = (lane & (modes - 1)) >> log2(per_block)
    lane_block = (lane & (cycles - 1)) >> 1
    loads[2].wait()

    fourier_all = gathered_ref[:, :reals, :].reshape(-1, LANES)
    total_reals = real_groups * reals
    coeff_rows = jnp.dot(fourier_all, coeff_pick, preferred_element_type=jnp.float32).reshape(
        groups, blocks, total_reals, LANES
    )
    columns = jnp.zeros((total_reals, LANES), jnp.float32)
    for b in range(blocks):
        one = coeff_rows[:, b].sum(axis=0)
        columns = columns + jnp.where(lane_block == b, one, 0.0)
    loads[3].wait()
    loads[4].wait()
    table = legendre_ref[...]
    table = jnp.concatenate([table, table], axis=0)
    spectrum = spectrum_ref[...]
    factor = spectrum / (spectrum + 0.5)
    tiles = table.shape[1] // LANES
    stride = 2 * tiles * per_block
    stores = []
    for y in range(real_groups):
        pieces = [
            jnp.where((lane >> log2(cycles)) == c * per_block + s, columns[y * reals : (y + 1) * reals], 0.0)
            for s in range(per_block)
            for c in range(2)
        ]
        filtered = factor * jnp.dot(
            jnp.concatenate(pieces, axis=0).astype(jnp.bfloat16), table, preferred_element_type=jnp.float32
        )
        for s in range(per_block):
            for c in range(2):
                start = (s * 2 + c) * reals
                for tile in range(tiles):
                    first_row = y * reals * stride + (c * tiles + tile) * per_block + s
                    wiener_ref[pl.ds(first_row, reals, stride=stride), :] = filtered[
                        start : start + reals, tile * LANES : (tile + 1) * LANES
                    ]
        span = pl.ds(y * reals * stride, reals * stride)
        stores += start_copies([wiener_ref.at[span]], [wiener_hbm.at[span]], out_sems, len(stores))

    gram_all = gathered_ref[:, reals:, :].reshape(-1, LANES)
    gram_rows = jnp.dot(gram_all, gram_pick, preferred_element_type=jnp.float32)
    gram_rows = gram_rows.reshape(groups, blocks, real_groups, cycles // 2, 2 * LANES)
    holder = jnp.concatenate([holder, holder], axis=1)
    gram = jnp.zeros((cycles // 2, 2 * LANES), jnp.float32)
    for b in range(blocks):
        one = gram_rows[:, b].reshape(-1, cycles // 2, 2 * LANES).sum(axis=0)
        gram = gram + jnp.where(holder == b, one, 0.0)
    gram = jnp.concatenate([gram[:, :LANES], gram[:, LANES:]], axis=0)

    first = lane < half
    cycle_modes = jnp.zeros((reals, LANES), jnp.float32)
    for b in range(blocks):
        pair = jnp.zeros((reals, LANES), jnp.float32)
        for g in range(groups):
            source = (g * blocks + b) * real_groups + real_group
            pair = pair + gathered_ref[source, :reals, :].astype(jnp.float32)
        turned = pltpu.roll(pair, half, 1)
        cycle_modes = cycle_modes + jnp.where(first, pair, turned) * gram[2 * b : 2 * b + 1]
        cycle_modes = cycle_modes + jnp.where(first, turned, pair) * gram[2 * b + 1 : 2 * b + 2]
    cycle_modes = cycle_modes * modes**-0.5
    turned = pltpu.roll(cycle_modes, half, 1)
    even = jnp.where(first, cycle_modes, turned)
    odd = jnp.where(first, turned, cycle_modes)
    parity = (row_ids((1, 8, LANES)) & 1) == 0
    spread = jnp.where(parity, even[:, None, :], odd[:, None, :])
    inner = jnp.concatenate([high, low], axis=1)
    outer = outer.reshape(1, pixel_rows // 8, 8, LANES)
    part_reals = reals // parts
    for i in range(parts):
        rotated = spread[i * part_reals : (i + 1) * part_reals, None] * outer
        rotated = rotated.reshape(part_reals * pixel_rows, LANES).astype(jnp.bfloat16)
        span = pl.ds(i * part_reals * pixel_rows, part_reals * pixel_rows)
        signal_ref[span, :] = lax.dot_general(
            jnp.concatenate([rotated, rotated], axis=1), inner, NT, preferred_element_type=jnp.float32
        )
        stores += start_copies([signal_ref.at[span]], [signal_hbm.at[span]], out_sems, len(stores))
    for store in stores:
        store.wait()


def split_tiles(array):
    lead, rows, columns = array.shape[:-2], array.shape[-2], array.shape[-1]
    split = array.reshape(*lead, rows, columns // LANES, LANES)
    return jnp.swapaxes(split, -2, -3).reshape(-1, LANES)


def gram_program(
    sky_data, signal_prev, noise_var, mask_flags, cycle_table, m_table, spectrum, legendre
):
    reals, cycle_dev, half_len = sky_data.shape
    groups, blocks, real_groups = (lax.axis_size(name) for name in AXES)
    cycle_len = half_len * groups
    per_block, multipoles, cycles = legendre.shape
    total_l = multipoles * groups * real_groups
    tiles = multipoles // LANES
    hbm = pl.BlockSpec(memory_space=pl.ANY)
    vmem = pl.BlockSpec(memory_space=pltpu.VMEM)
    orders = m_table[None, :]
    spectrum_row = spectrum[None, :]
    table = legendre.transpose(0, 2, 1).reshape(per_block * cycles, multipoles)
    inputs = (
        cycle_table, orders, split_tiles(noise_var), split_tiles(mask_flags), spectrum_row, table,
        split_tiles(sky_data), split_tiles(signal_prev),
    )
    spaces = [pltpu.SMEM] + [pltpu.VMEM] * 7
    sources = groups * blocks * real_groups
    local = pl.pallas_call(
        functools.partial(forward_kernel, cycle_len, half_len, (cycles / total_l) ** 0.5, PARTS),
        out_shape=jax.ShapeDtypeStruct((sources, reals + cycles // 2, LANES), jnp.bfloat16),
        in_specs=[hbm] * 8,
        out_specs=vmem,
        scratch_shapes=[space(x.shape, x.dtype) for space, x in zip(spaces, inputs)]
        + [pltpu.SemaphoreType.DMA((6 + 2 * PARTS,))],
    )(*inputs)
    gathered = lax.all_to_all(local, AXES, 0, 0, tiled=True)
    total_reals = reals * real_groups
    inputs = (cycle_table, orders, gathered, table, spectrum_row)
    outputs = (
        jax.ShapeDtypeStruct((total_reals * 2 * tiles * per_block, LANES), jnp.float32),
        jax.ShapeDtypeStruct((reals * cycle_dev * half_len // LANES, LANES), jnp.float32),
    )
    wiener, signal = pl.pallas_call(
        functools.partial(backward_kernel, cycle_len, half_len, groups, blocks, real_groups, reals, PARTS),
        out_shape=outputs,
        in_specs=[hbm] * 5,
        out_specs=(hbm, hbm),
        scratch_shapes=[space(x.shape, x.dtype) for space, x in zip(spaces, inputs)]
        + [pltpu.VMEM(x.shape, x.dtype) for x in outputs]
        + [pltpu.SemaphoreType.DMA((5,)), pltpu.SemaphoreType.DMA((real_groups + PARTS,))],
    )(*inputs)
    wiener = wiener.reshape(total_reals, 2, tiles, per_block, LANES).transpose(0, 1, 3, 2, 4)
    signal = signal.reshape(reals, half_len // LANES, cycle_dev, LANES).transpose(0, 2, 1, 3)
    return (
        wiener.reshape(total_reals, 2, per_block, multipoles),
        signal.reshape(sky_data.shape),
    )


def gram_form_fits(mesh, sky_data, m_table, legendre):
    groups, blocks, real_groups = (mesh.shape[name] for name in AXES)
    reals, cycles, cycle_len = sky_data.shape
    modes = m_table.shape[0]
    per_block = modes // blocks
    multipoles = legendre.shape[1] // (groups * real_groups)
    half_len = cycle_len // groups
    reals_dev = reals // real_groups
    return (
        cycles < 2 * reals
        and 4 * modes == LANES
        and cycles == 2 * blocks
        and all(size & (size - 1) == 0 for size in (blocks, modes, cycles))
        and 2 * per_block * cycles == LANES
        and cycle_len & (cycle_len - 1) == 0
        and half_len % (4 * LANES) == 0
        and multipoles % LANES == 0
        and reals_dev % 16 == 0
        and reals_dev % PARTS == 0
        and cycles % 16 == 0
    )


def phase_tables(col_ids, mode_ids, cycle_len):
    product_ids = col_ids[:, None] * mode_ids[None, :] % cycle_len
    angles = product_ids.astype(jnp.float32) * (2.0 * math.pi / cycle_len)
    return (jnp.cos(angles).astype(jnp.bfloat16), jnp.sin(angles).astype(jnp.bfloat16))


def cycle_offsets(cycle_ids, mode_ids, cycle_len):
    parity = (cycle_ids % 2).astype(jnp.float32)
    shifts = math.pi / cycle_len * parity[:, None] * mode_ids[None, :].astype(jnp.float32)
    return (jnp.cos(shifts), jnp.sin(shifts))


def forward_modes(re_part, im_part):
    summed = lax.psum((re_part, im_part), "grp")
    fourier_pair = (summed[0].astype(jnp.bfloat16), summed[1].astype(jnp.bfloat16))
    fourier_pair = (
        lax.all_gather(fourier_pair[0], "real", axis=0, tiled=True),
        lax.all_gather(fourier_pair[1], "real", axis=0, tiled=True),
    )
    fourier_pair = (
        lax.all_to_all(fourier_pair[0], "blk", split_axis=2, concat_axis=1, tiled=True),
        lax.all_to_all(fourier_pair[1], "blk", split_axis=2, concat_axis=1, tiled=True),
    )
    return fourier_pair


def backward_cycles(partial_value):
    summed = lax.psum_scatter(partial_value, "real", scatter_dimension=0, tiled=True)
    reduced = lax.psum(summed, "grp")
    cycle_pair = lax.all_to_all(
        reduced.astype(jnp.bfloat16), "blk", split_axis=2, concat_axis=3, tiled=True
    )
    return cycle_pair


def per_device(
    sky_data, signal_prev, noise_var, mask_flags, cycle_table, m_table, spectrum, legendre
):
    real_dev, cycle_dev, half_len = sky_data.shape
    cycle_len = half_len * lax.axis_size("grp")
    mode_count = m_table.shape[0]
    col_ids = lax.axis_index("grp") * half_len + jnp.arange(half_len, dtype=jnp.int32)
    cos_tab, sin_tab = phase_tables(col_ids, m_table, cycle_len)
    cos_shift, sin_shift = cycle_offsets(cycle_table, m_table, cycle_len)
    weight = mask_flags.astype(jnp.float32) / (noise_var - 0.5)
    messenger = (weight * sky_data + 2.0 * signal_prev) / (weight + 2.0)
    flat_rows = messenger.astype(jnp.bfloat16).reshape(real_dev * cycle_dev, half_len)
    base_cos = jnp.dot(flat_rows, cos_tab, preferred_element_type=jnp.float32).reshape(
        real_dev, cycle_dev, mode_count
    )
    base_sin = -jnp.dot(flat_rows, sin_tab, preferred_element_type=jnp.float32).reshape(
        real_dev, cycle_dev, mode_count
    )
    norm_scale = cycle_len ** (-0.5)
    re_part = (base_cos * cos_shift + base_sin * sin_shift) * norm_scale
    im_part = (base_sin * cos_shift - base_cos * sin_shift) * norm_scale
    fourier_re, fourier_im = forward_modes(re_part, im_part)
    fourier = jnp.stack([fourier_re, fourier_im], 1)
    coefficients = jnp.einsum(
        "mlr,kcrm->kcml", legendre, fourier, preferred_element_type=jnp.float32
    )
    factor = spectrum / (spectrum + 0.5)
    wiener_alm = coefficients * factor
    total_l = legendre.shape[1] * lax.axis_size("grp") * lax.axis_size("real")
    syn_scale = (legendre.shape[2] / total_l) ** 0.5
    partial_value = (
        jnp.einsum(
            "mlr,kcml->kcrm",
            legendre,
            wiener_alm.astype(jnp.bfloat16),
            preferred_element_type=jnp.float32,
        )
        * syn_scale
    )
    cycle_pair = backward_cycles(partial_value)
    cycle_modes = cycle_pair.astype(jnp.float32)
    modes_re = cycle_modes[:, 0]
    modes_im = cycle_modes[:, 1]
    rotated_re = (modes_re * cos_shift - modes_im * sin_shift).astype(jnp.bfloat16)
    rotated_im = (modes_im * cos_shift + modes_re * sin_shift).astype(jnp.bfloat16)
    contract = (((1,), (1,)), ((), ()))
    pixel_sum = lax.dot_general(
        rotated_re.reshape(-1, mode_count), cos_tab, contract, preferred_element_type=jnp.float32
    )
    pixel_sum = pixel_sum - lax.dot_general(
        rotated_im.reshape(-1, mode_count), sin_tab, contract, preferred_element_type=jnp.float32
    )
    signal_next = (pixel_sum * mode_count ** (-0.5)).reshape(real_dev, cycle_dev, half_len)
    return (wiener_alm, signal_next)


def solution(mesh):
    in_specs = (
        P("real", "blk", "grp"),
        P("real", "blk", "grp"),
        P("blk", "grp"),
        P("blk", "grp"),
        P("blk"),
        P(),
        P(("grp", "real")),
        P("blk", ("grp", "real"), None),
    )
    out_specs = (P(None, None, "blk", ("grp", "real")), P("real", "blk", "grp"))

    def step(sky_data, signal_prev, noise_var, mask_flags, cycle_table, m_table, spectrum, legendre):
        fits = gram_form_fits(mesh, sky_data, m_table, legendre)
        return jax.shard_map(
            gram_program if fits else per_device,
            mesh=mesh,
            in_specs=in_specs,
            out_specs=out_specs,
            check_vma=False,
        )(sky_data, signal_prev, noise_var, mask_flags, cycle_table, m_table, spectrum, legendre)

    return step
```

```python
import functools
import math

import jax
import jax.numpy as jnp
from jax import lax
from jax.experimental import pallas as pl
from jax.experimental.pallas import tpu as pltpu
from jax.sharding import PartitionSpec as P

LANES = 128
NT = (((1,), (1,)), ((), ()))
AXES = ("grp", "blk", "real")
PARTS = 2
BACKWARD_VMEM = 16 << 20


def unit_cosine(units, half_turn):
    wrapped = units & (2 * half_turn - 1)
    folded = jnp.minimum(wrapped, 2 * half_turn - wrapped)
    y = (half_turn // 2 - folded).astype(jnp.float32) * (math.pi / half_turn)
    y2 = y * y
    acc = jnp.full_like(y2, -1.0 / math.factorial(11))
    for order, sign in ((9, 1.0), (7, -1.0), (5, 1.0), (3, -1.0), (1, 1.0)):
        acc = acc * y2 + sign / math.factorial(order)
    return acc * y


def log2(size):
    return size.bit_length() - 1


def lane_ids(shape):
    return lax.broadcasted_iota(jnp.int32, shape, len(shape) - 1)


def row_ids(shape):
    return lax.broadcasted_iota(jnp.int32, shape, len(shape) - 2)


def phase_factors(cycle_ref, orders, cycle_len, half_len, group):
    modes = orders.shape[1]
    orders = jnp.concatenate([orders] * (LANES // modes), axis=1)
    quarter = lane_ids((1, LANES)) >> log2(modes)
    quarter_turn = cycle_len // 2
    inner_units = 2 * orders * row_ids((LANES, LANES)) + ((quarter + 1) >> 1) * quarter_turn
    inner = unit_cosine(inner_units, cycle_len)
    rows = 2 * (half_len // LANES)
    row = row_ids((rows, LANES))
    parity = jnp.where((row & 1) == 0, cycle_ref[0] & 1, cycle_ref[1] & 1)
    pixel = group * half_len + LANES * (row >> 1)
    outer_units = orders * (2 * pixel + parity) + (quarter >> 1) * (3 * quarter_turn)
    outer = unit_cosine(outer_units, cycle_len)
    high = inner.astype(jnp.bfloat16)
    low = (inner - high.astype(jnp.float32)).astype(jnp.bfloat16)
    return high, low, outer


def start_copies(sources, targets, sems, first=0):
    copies = [
        pltpu.make_async_copy(source, target, sems.at[first + i])
        for i, (source, target) in enumerate(zip(sources, targets))
    ]
    for copy in copies:
        copy.start()
    return copies


def row_parts(ref, parts):
    size = ref.shape[0] // parts
    return [ref.at[pl.ds(i * size, size)] for i in range(parts)]


def forward_kernel(
    cycle_len, half_len, syn_scale, parts,
    cycle_hbm, mode_hbm, noise_hbm, mask_hbm, spectrum_hbm, legendre_hbm, sky_hbm, prev_hbm, out_ref,
    cycle_ref, mode_ref, noise_ref, mask_ref, spectrum_ref, legendre_ref, sky_ref, prev_ref, sems,
):
    small = start_copies(
        (cycle_hbm, mode_hbm, noise_hbm, mask_hbm, spectrum_hbm, legendre_hbm),
        (cycle_ref, mode_ref, noise_ref, mask_ref, spectrum_ref, legendre_ref),
        sems,
    )
    sources = [part for pair in zip(row_parts(sky_hbm, parts), row_parts(prev_hbm, parts)) for part in pair]
    targets = [part for pair in zip(row_parts(sky_ref, parts), row_parts(prev_ref, parts)) for part in pair]
    large = start_copies(sources, targets, sems, len(small))
    group = lax.axis_index("grp")
    small[0].wait()
    small[1].wait()
    high, low, outer = phase_factors(cycle_ref, mode_ref[...], cycle_len, half_len, group)
    inner = jnp.concatenate([high, low], axis=0)
    small[2].wait()
    small[3].wait()
    weight = mask_ref[...].astype(jnp.float32) / (noise_ref[...] - 0.5)
    inverse = 1.0 / (weight + 2.0)
    sky_gain = weight * inverse
    prev_gain = 2.0 * inverse

    small[4].wait()
    small[5].wait()
    table = legendre_ref[...]
    spectrum = spectrum_ref[...]
    factor = spectrum / (spectrum + 0.5)
    filtered = (table.astype(jnp.float32) * factor).astype(jnp.bfloat16)
    gram = lax.dot_general(table, filtered, NT, preferred_element_type=jnp.float32)
    table_rows = table.shape[0]
    pixel_rows = outer.shape[0]
    reals = sky_ref.shape[0] // pixel_rows
    cycles = 2 * (out_ref.shape[1] - reals)
    same = (row_ids(gram.shape) >> log2(cycles)) == (lane_ids((1, table_rows)) >> log2(cycles))
    gram = jnp.where(same, gram, 0.0).reshape(table_rows // cycles, cycles, table_rows).sum(axis=0)
    gram = gram * syn_scale
    gram = jnp.concatenate([gram[: cycles // 2], gram[cycles // 2 :]], axis=1).astype(jnp.bfloat16)

    part_reals = reals // parts
    shape = (part_reals, pixel_rows, LANES)
    fourier = []
    for i in range(parts):
        large[2 * i].wait()
        large[2 * i + 1].wait()
        span = pl.ds(i * part_reals * pixel_rows, part_reals * pixel_rows)
        sky = sky_ref[span, :].reshape(shape)
        prev = prev_ref[span, :].reshape(shape)
        rows = (sky * sky_gain + prev * prev_gain).reshape(-1, LANES).astype(jnp.bfloat16)
        partial = jnp.dot(
            jnp.concatenate([rows, rows], axis=1), inner, preferred_element_type=jnp.float32
        )
        turned = partial.reshape(shape) * outer
        summed = turned.reshape(part_reals, pixel_rows // 8, 8, LANES).sum(axis=1)
        summed = summed.reshape(part_reals * 8, LANES)
        summed = summed + pltpu.roll(summed, LANES // 2, 1)
        own = (row_ids(summed.shape) & 1) == (lane_ids(summed.shape) >= LANES // 2)
        fourier.append(jnp.where(own, summed, 0.0).reshape(part_reals, 8, LANES).sum(axis=1))
    fourier = (jnp.concatenate(fourier, axis=0) * cycle_len**-0.5).astype(jnp.bfloat16)
    block = jnp.concatenate([fourier, gram], axis=0)
    for target in range(out_ref.shape[0]):
        out_ref[target] = block


def backward_kernel(
    cycle_len, half_len, groups, blocks, real_groups, reals, parts,
    gathered_ref, cycle_hbm, mode_hbm, legendre_hbm, spectrum_hbm, wiener_hbm, signal_hbm,
    cycle_ref, mode_ref, legendre_ref, spectrum_ref, wiener_ref, signal_ref, sems, out_sems,
):
    loads = start_copies(
        (cycle_hbm, mode_hbm, legendre_hbm, spectrum_hbm),
        (cycle_ref, mode_ref, legendre_ref, spectrum_ref),
        sems,
    )
    group = lax.axis_index("grp")
    block = lax.axis_index("blk")
    real_group = lax.axis_index("real")
    loads[0].wait()
    loads[1].wait()
    high, low, outer = phase_factors(cycle_ref, mode_ref[...], cycle_len, half_len, group)
    modes = mode_ref.shape[1]
    table_rows = legendre_ref.shape[0]
    per_block = modes // blocks
    cycles = table_rows // per_block
    pixel_rows = outer.shape[0]
    half = LANES // 2
    lane = lane_ids((1, LANES))
    row = row_ids((LANES, LANES))
    lane_order = (lane & (half - 1)) >> log2(cycles)
    lane_row = (lane & 1) * half + (lane >> log2(half)) * modes + block * per_block + lane_order
    coeff_pick = (row == lane_row).astype(jnp.float32).astype(jnp.bfloat16)
    lane_row = (lane & (per_block - 1)) * cycles + 2 * block + (lane >> log2(half))
    gram_pick = jnp.concatenate([row == lane_row, row == lane_row + half], axis=1)
    gram_pick = gram_pick.astype(jnp.float32).astype(jnp.bfloat16)
    holder = (lane & (modes - 1)) >> log2(per_block)
    lane_block = (lane & (cycles - 1)) >> 1

    fourier_all = gathered_ref[:, :reals, :].reshape(-1, LANES)
    total_reals = real_groups * reals
    coeff_rows = jnp.dot(fourier_all, coeff_pick, preferred_element_type=jnp.float32).reshape(
        groups, blocks, total_reals, LANES
    )
    columns = jnp.zeros((total_reals, LANES), jnp.float32)
    for b in range(blocks):
        one = coeff_rows[:, b].sum(axis=0)
        columns = columns + jnp.where(lane_block == b, one, 0.0)
    loads[2].wait()
    loads[3].wait()
    table = legendre_ref[...]
    table = jnp.concatenate([table, table], axis=0)
    spectrum = spectrum_ref[...]
    factor = spectrum / (spectrum + 0.5)
    tiles = table.shape[1] // LANES
    stride = 2 * tiles * per_block
    stores = []
    for y in range(real_groups):
        pieces = [
            jnp.where((lane >> log2(cycles)) == c * per_block + s, columns[y * reals : (y + 1) * reals], 0.0)
            for s in range(per_block)
            for c in range(2)
        ]
        filtered = factor * jnp.dot(
            jnp.concatenate(pieces, axis=0).astype(jnp.bfloat16), table, preferred_element_type=jnp.float32
        )
        for s in range(per_block):
            for c in range(2):
                start = (s * 2 + c) * reals
                for tile in range(tiles):
                    first_row = y * reals * stride + (c * tiles + tile) * per_block + s
                    wiener_ref[pl.ds(first_row, reals, stride=stride), :] = filtered[
                        start : start + reals, tile * LANES : (tile + 1) * LANES
                    ]
        span = pl.ds(y * reals * stride, reals * stride)
        stores += start_copies([wiener_ref.at[span]], [wiener_hbm.at[span]], out_sems, len(stores))

    gram_all = gathered_ref[:, reals:, :].reshape(-1, LANES)
    gram_rows = jnp.dot(gram_all, gram_pick, preferred_element_type=jnp.float32)
    gram_rows = gram_rows.reshape(groups, blocks, real_groups, cycles // 2, 2 * LANES)
    holder = jnp.concatenate([holder, holder], axis=1)
    gram = jnp.zeros((cycles // 2, 2 * LANES), jnp.float32)
    for b in range(blocks):
        one = gram_rows[:, b].reshape(-1, cycles // 2, 2 * LANES).sum(axis=0)
        gram = gram + jnp.where(holder == b, one, 0.0)
    gram = jnp.concatenate([gram[:, :LANES], gram[:, LANES:]], axis=0)

    first = lane < half
    cycle_modes = jnp.zeros((reals, LANES), jnp.float32)
    for b in range(blocks):
        pair = jnp.zeros((reals, LANES), jnp.float32)
        for g in range(groups):
            source = (g * blocks + b) * real_groups + real_group
            pair = pair + gathered_ref[source, :reals, :].astype(jnp.float32)
        turned = pltpu.roll(pair, half, 1)
        cycle_modes = cycle_modes + jnp.where(first, pair, turned) * gram[2 * b : 2 * b + 1]
        cycle_modes = cycle_modes + jnp.where(first, turned, pair) * gram[2 * b + 1 : 2 * b + 2]
    cycle_modes = cycle_modes * modes**-0.5
    turned = pltpu.roll(cycle_modes, half, 1)
    even = jnp.where(first, cycle_modes, turned)
    odd = jnp.where(first, turned, cycle_modes)
    parity = (row_ids((1, 8, LANES)) & 1) == 0
    spread = jnp.where(parity, even[:, None, :], odd[:, None, :])
    inner = jnp.concatenate([high, low], axis=1)
    outer = outer.reshape(1, pixel_rows // 8, 8, LANES)
    part_reals = reals // parts
    for i in range(parts):
        rotated = spread[i * part_reals : (i + 1) * part_reals, None] * outer
        rotated = rotated.reshape(part_reals * pixel_rows, LANES).astype(jnp.bfloat16)
        span = pl.ds(i * part_reals * pixel_rows, part_reals * pixel_rows)
        signal_ref[span, :] = lax.dot_general(
            jnp.concatenate([rotated, rotated], axis=1), inner, NT, preferred_element_type=jnp.float32
        )
        stores += start_copies([signal_ref.at[span]], [signal_hbm.at[span]], out_sems, len(stores))
    for store in stores:
        store.wait()


def split_tiles(array):
    lead, rows, columns = array.shape[:-2], array.shape[-2], array.shape[-1]
    split = array.reshape(*lead, rows, columns // LANES, LANES)
    return jnp.swapaxes(split, -2, -3).reshape(-1, LANES)


def gram_program(
    sky_data, signal_prev, noise_var, mask_flags, cycle_table, m_table, spectrum, legendre
):
    reals, cycle_dev, half_len = sky_data.shape
    groups, blocks, real_groups = (lax.axis_size(name) for name in AXES)
    cycle_len = half_len * groups
    per_block, multipoles, cycles = legendre.shape
    total_l = multipoles * groups * real_groups
    tiles = multipoles // LANES
    hbm = pl.BlockSpec(memory_space=pltpu.HBM)
    vmem = pl.BlockSpec(memory_space=pltpu.VMEM)
    orders = m_table[None, :]
    spectrum_row = spectrum[None, :]
    table = legendre.transpose(0, 2, 1).reshape(per_block * cycles, multipoles)
    inputs = (
        cycle_table, orders, split_tiles(noise_var), split_tiles(mask_flags), spectrum_row, table,
        split_tiles(sky_data), split_tiles(signal_prev),
    )
    spaces = [pltpu.SMEM] + [pltpu.VMEM] * 7
    sources = groups * blocks * real_groups
    local = pl.pallas_call(
        functools.partial(forward_kernel, cycle_len, half_len, (cycles / total_l) ** 0.5, 1),
        out_shape=jax.ShapeDtypeStruct((sources, reals + cycles // 2, LANES), jnp.bfloat16),
        in_specs=[hbm] * 8,
        out_specs=vmem,
        scratch_shapes=[space(x.shape, x.dtype) for space, x in zip(spaces, inputs)]
        + [pltpu.SemaphoreType.DMA((8,))],
    )(*inputs)
    gathered = lax.all_to_all(local, AXES, 0, 0, tiled=True)
    total_reals = reals * real_groups
    inputs = (cycle_table, orders, table, spectrum_row)
    outputs = (
        jax.ShapeDtypeStruct((total_reals * 2 * tiles * per_block, LANES), jnp.float32),
        jax.ShapeDtypeStruct((reals * cycle_dev * half_len // LANES, LANES), jnp.float32),
    )
    wiener, signal = pl.pallas_call(
        functools.partial(backward_kernel, cycle_len, half_len, groups, blocks, real_groups, reals, PARTS),
        out_shape=outputs,
        in_specs=[vmem] + [hbm] * 4,
        out_specs=(hbm, hbm),
        scratch_shapes=[space(x.shape, x.dtype) for space, x in zip(spaces, inputs)]
        + [pltpu.VMEM(x.shape, x.dtype) for x in outputs]
        + [pltpu.SemaphoreType.DMA((4,)), pltpu.SemaphoreType.DMA((real_groups + PARTS,))],
        compiler_params=pltpu.CompilerParams(vmem_limit_bytes=BACKWARD_VMEM),
    )(gathered, *inputs)
    wiener = wiener.reshape(total_reals, 2, tiles, per_block, LANES).transpose(0, 1, 3, 2, 4)
    signal = signal.reshape(reals, half_len // LANES, cycle_dev, LANES).transpose(0, 2, 1, 3)
    return (
        wiener.reshape(total_reals, 2, per_block, multipoles),
        signal.reshape(sky_data.shape),
    )


def gram_form_fits(mesh, sky_data, m_table, legendre):
    groups, blocks, real_groups = (mesh.shape[name] for name in AXES)
    reals, cycles, cycle_len = sky_data.shape
    modes = m_table.shape[0]
    per_block = modes // blocks
    multipoles = legendre.shape[1] // (groups * real_groups)
    half_len = cycle_len // groups
    reals_dev = reals // real_groups
    return (
        cycles < 2 * reals
        and 4 * modes == LANES
        and cycles == 2 * blocks
        and all(size & (size - 1) == 0 for size in (blocks, modes, cycles))
        and 2 * per_block * cycles == LANES
        and cycle_len & (cycle_len - 1) == 0
        and half_len % (4 * LANES) == 0
        and multipoles % LANES == 0
        and reals_dev % 16 == 0
        and reals_dev % PARTS == 0
        and cycles % 16 == 0
    )


def phase_tables(col_ids, mode_ids, cycle_len):
    product_ids = col_ids[:, None] * mode_ids[None, :] % cycle_len
    angles = product_ids.astype(jnp.float32) * (2.0 * math.pi / cycle_len)
    return (jnp.cos(angles).astype(jnp.bfloat16), jnp.sin(angles).astype(jnp.bfloat16))


def cycle_offsets(cycle_ids, mode_ids, cycle_len):
    parity = (cycle_ids % 2).astype(jnp.float32)
    shifts = math.pi / cycle_len * parity[:, None] * mode_ids[None, :].astype(jnp.float32)
    return (jnp.cos(shifts), jnp.sin(shifts))


def forward_modes(re_part, im_part):
    summed = lax.psum((re_part, im_part), "grp")
    fourier_pair = (summed[0].astype(jnp.bfloat16), summed[1].astype(jnp.bfloat16))
    fourier_pair = (
        lax.all_gather(fourier_pair[0], "real", axis=0, tiled=True),
        lax.all_gather(fourier_pair[1], "real", axis=0, tiled=True),
    )
    fourier_pair = (
        lax.all_to_all(fourier_pair[0], "blk", split_axis=2, concat_axis=1, tiled=True),
        lax.all_to_all(fourier_pair[1], "blk", split_axis=2, concat_axis=1, tiled=True),
    )
    return fourier_pair


def backward_cycles(partial_value):
    summed = lax.psum_scatter(partial_value, "real", scatter_dimension=0, tiled=True)
    reduced = lax.psum(summed, "grp")
    cycle_pair = lax.all_to_all(
        reduced.astype(jnp.bfloat16), "blk", split_axis=2, concat_axis=3, tiled=True
    )
    return cycle_pair


def per_device(
    sky_data, signal_prev, noise_var, mask_flags, cycle_table, m_table, spectrum, legendre
):
    real_dev, cycle_dev, half_len = sky_data.shape
    cycle_len = half_len * lax.axis_size("grp")
    mode_count = m_table.shape[0]
    col_ids = lax.axis_index("grp") * half_len + jnp.arange(half_len, dtype=jnp.int32)
    cos_tab, sin_tab = phase_tables(col_ids, m_table, cycle_len)
    cos_shift, sin_shift = cycle_offsets(cycle_table, m_table, cycle_len)
    weight = mask_flags.astype(jnp.float32) / (noise_var - 0.5)
    messenger = (weight * sky_data + 2.0 * signal_prev) / (weight + 2.0)
    flat_rows = messenger.astype(jnp.bfloat16).reshape(real_dev * cycle_dev, half_len)
    base_cos = jnp.dot(flat_rows, cos_tab, preferred_element_type=jnp.float32).reshape(
        real_dev, cycle_dev, mode_count
    )
    base_sin = -jnp.dot(flat_rows, sin_tab, preferred_element_type=jnp.float32).reshape(
        real_dev, cycle_dev, mode_count
    )
    norm_scale = cycle_len ** (-0.5)
    re_part = (base_cos * cos_shift + base_sin * sin_shift) * norm_scale
    im_part = (base_sin * cos_shift - base_cos * sin_shift) * norm_scale
    fourier_re, fourier_im = forward_modes(re_part, im_part)
    fourier = jnp.stack([fourier_re, fourier_im], 1)
    coefficients = jnp.einsum(
        "mlr,kcrm->kcml", legendre, fourier, preferred_element_type=jnp.float32
    )
    factor = spectrum / (spectrum + 0.5)
    wiener_alm = coefficients * factor
    total_l = legendre.shape[1] * lax.axis_size("grp") * lax.axis_size("real")
    syn_scale = (legendre.shape[2] / total_l) ** 0.5
    partial_value = (
        jnp.einsum(
            "mlr,kcml->kcrm",
            legendre,
            wiener_alm.astype(jnp.bfloat16),
            preferred_element_type=jnp.float32,
        )
        * syn_scale
    )
    cycle_pair = backward_cycles(partial_value)
    cycle_modes = cycle_pair.astype(jnp.float32)
    modes_re = cycle_modes[:, 0]
    modes_im = cycle_modes[:, 1]
    rotated_re = (modes_re * cos_shift - modes_im * sin_shift).astype(jnp.bfloat16)
    rotated_im = (modes_im * cos_shift + modes_re * sin_shift).astype(jnp.bfloat16)
    contract = (((1,), (1,)), ((), ()))
    pixel_sum = lax.dot_general(
        rotated_re.reshape(-1, mode_count), cos_tab, contract, preferred_element_type=jnp.float32
    )
    pixel_sum = pixel_sum - lax.dot_general(
        rotated_im.reshape(-1, mode_count), sin_tab, contract, preferred_element_type=jnp.float32
    )
    signal_next = (pixel_sum * mode_count ** (-0.5)).reshape(real_dev, cycle_dev, half_len)
    return (wiener_alm, signal_next)


def solution(mesh):
    in_specs = (
        P("real", "blk", "grp"),
        P("real", "blk", "grp"),
        P("blk", "grp"),
        P("blk", "grp"),
        P("blk"),
        P(),
        P(("grp", "real")),
        P("blk", ("grp", "real"), None),
    )
    out_specs = (P(None, None, "blk", ("grp", "real")), P("real", "blk", "grp"))

    def step(sky_data, signal_prev, noise_var, mask_flags, cycle_table, m_table, spectrum, legendre):
        fits = gram_form_fits(mesh, sky_data, m_table, legendre)
        return jax.shard_map(
            gram_program if fits else per_device,
            mesh=mesh,
            in_specs=in_specs,
            out_specs=out_specs,
            check_vma=False,
        )(sky_data, signal_prev, noise_var, mask_flags, cycle_table, m_table, spectrum, legendre)

    return step
```

```python
import functools
import math

import jax
import jax.numpy as jnp
from jax import lax
from jax.experimental import pallas as pl
from jax.experimental.pallas import tpu as pltpu
from jax.sharding import PartitionSpec as P

LANES = 128
NT = (((1,), (1,)), ((), ()))
AXES = ("grp", "blk", "real")
PARTS = 2
BACKWARD_VMEM = 16 << 20


def unit_cosine(units, half_turn):
    wrapped = units & (2 * half_turn - 1)
    folded = jnp.minimum(wrapped, 2 * half_turn - wrapped)
    y = (half_turn // 2 - folded).astype(jnp.float32) * (math.pi / half_turn)
    y2 = y * y
    acc = jnp.full_like(y2, -1.0 / math.factorial(11))
    for order, sign in ((9, 1.0), (7, -1.0), (5, 1.0), (3, -1.0), (1, 1.0)):
        acc = acc * y2 + sign / math.factorial(order)
    return acc * y


def log2(size):
    return size.bit_length() - 1


def lane_ids(shape):
    return lax.broadcasted_iota(jnp.int32, shape, len(shape) - 1)


def row_ids(shape):
    return lax.broadcasted_iota(jnp.int32, shape, len(shape) - 2)


def phase_factors(cycle_ref, orders, cycle_len, half_len, group):
    modes = orders.shape[1]
    orders = jnp.concatenate([orders] * (LANES // modes), axis=1)
    quarter = lane_ids((1, LANES)) >> log2(modes)
    quarter_turn = cycle_len // 2
    inner_units = 2 * orders * row_ids((LANES, LANES)) + ((quarter + 1) >> 1) * quarter_turn
    inner = unit_cosine(inner_units, cycle_len)
    rows = 2 * (half_len // LANES)
    row = row_ids((rows, LANES))
    parity = jnp.where((row & 1) == 0, cycle_ref[0] & 1, cycle_ref[1] & 1)
    pixel = group * half_len + LANES * (row >> 1)
    outer_units = orders * (2 * pixel + parity) + (quarter >> 1) * (3 * quarter_turn)
    outer = unit_cosine(outer_units, cycle_len)
    high = inner.astype(jnp.bfloat16)
    low = (inner - high.astype(jnp.float32)).astype(jnp.bfloat16)
    return high, low, outer


def start_copies(sources, targets, sems, first=0):
    copies = [
        pltpu.make_async_copy(source, target, sems.at[first + i])
        for i, (source, target) in enumerate(zip(sources, targets))
    ]
    for copy in copies:
        copy.start()
    return copies


def row_parts(ref, parts):
    size = ref.shape[0] // parts
    return [ref.at[pl.ds(i * size, size)] for i in range(parts)]


def forward_kernel(
    cycle_len, half_len, syn_scale, parts,
    cycle_hbm, mode_hbm, noise_hbm, mask_hbm, spectrum_hbm, legendre_hbm, sky_hbm, prev_hbm, out_ref,
    cycle_ref, mode_ref, noise_ref, mask_ref, spectrum_ref, legendre_ref, sky_ref, prev_ref, sems,
):
    small = start_copies(
        (cycle_hbm, mode_hbm, noise_hbm, mask_hbm, spectrum_hbm, legendre_hbm),
        (cycle_ref, mode_ref, noise_ref, mask_ref, spectrum_ref, legendre_ref),
        sems,
    )
    sources = [part for pair in zip(row_parts(sky_hbm, parts), row_parts(prev_hbm, parts)) for part in pair]
    targets = [part for pair in zip(row_parts(sky_ref, parts), row_parts(prev_ref, parts)) for part in pair]
    large = start_copies(sources, targets, sems, len(small))
    group = lax.axis_index("grp")
    small[0].wait()
    small[1].wait()
    high, low, outer = phase_factors(cycle_ref, mode_ref[...], cycle_len, half_len, group)
    inner = jnp.concatenate([high, low], axis=0)
    small[2].wait()
    small[3].wait()
    weight = mask_ref[...].astype(jnp.float32) / (noise_ref[...] - 0.5)
    inverse = 1.0 / (weight + 2.0)
    sky_gain = weight * inverse
    prev_gain = 2.0 * inverse

    small[4].wait()
    small[5].wait()
    table = legendre_ref[...]
    spectrum = spectrum_ref[...]
    factor = spectrum / (spectrum + 0.5)
    filtered = (table.astype(jnp.float32) * factor).astype(jnp.bfloat16)
    gram = lax.dot_general(table, filtered, NT, preferred_element_type=jnp.float32)
    table_rows = table.shape[0]
    pixel_rows = outer.shape[0]
    reals = sky_ref.shape[0] // pixel_rows
    cycles = 2 * lax.axis_size("blk")
    same = (row_ids(gram.shape) >> log2(cycles)) == (lane_ids((1, table_rows)) >> log2(cycles))
    gram = jnp.where(same, gram, 0.0).reshape(table_rows // cycles, cycles, table_rows).sum(axis=0)
    gram = gram * syn_scale
    gram = jnp.concatenate([gram[: cycles // 2], gram[cycles // 2 :]], axis=1).astype(jnp.bfloat16)

    part_reals = reals // parts
    shape = (part_reals, pixel_rows, LANES)
    fourier = []
    for i in range(parts):
        large[2 * i].wait()
        large[2 * i + 1].wait()
        span = pl.ds(i * part_reals * pixel_rows, part_reals * pixel_rows)
        sky = sky_ref[span, :].reshape(shape)
        prev = prev_ref[span, :].reshape(shape)
        rows = (sky * sky_gain + prev * prev_gain).reshape(-1, LANES).astype(jnp.bfloat16)
        partial = jnp.dot(
            jnp.concatenate([rows, rows], axis=1), inner, preferred_element_type=jnp.float32
        )
        turned = partial.reshape(shape) * outer
        summed = turned.reshape(part_reals, pixel_rows // 8, 8, LANES).sum(axis=1)
        summed = summed.reshape(part_reals * 8, LANES)
        summed = summed + pltpu.roll(summed, LANES // 2, 1)
        own = (row_ids(summed.shape) & 1) == (lane_ids(summed.shape) >= LANES // 2)
        fourier.append(jnp.where(own, summed, 0.0).reshape(part_reals, 8, LANES).sum(axis=1))
    fourier = (jnp.concatenate(fourier, axis=0) * cycle_len**-0.5).astype(jnp.bfloat16)
    out_ref[...] = jnp.zeros_like(out_ref)
    blocks = lax.axis_size("blk")
    block = lax.axis_index("blk")
    first_row = pl.multiple_of((lax.axis_index("real") * blocks + block) * reals, reals)
    out_ref[pl.ds(first_row, reals), :] = fourier
    first_row = lax.axis_size("real") * blocks * reals
    out_ref[pl.ds(pl.multiple_of(first_row + block * (cycles // 2), cycles // 2), cycles // 2), :] = gram


def backward_kernel(
    cycle_len, half_len, blocks, real_groups, reals, parts,
    gathered_ref, cycle_hbm, mode_hbm, legendre_hbm, spectrum_hbm, wiener_hbm, signal_hbm,
    cycle_ref, mode_ref, legendre_ref, spectrum_ref, wiener_ref, signal_ref, sems, out_sems,
):
    loads = start_copies(
        (cycle_hbm, mode_hbm, legendre_hbm, spectrum_hbm),
        (cycle_ref, mode_ref, legendre_ref, spectrum_ref),
        sems,
    )
    group = lax.axis_index("grp")
    block = lax.axis_index("blk")
    real_group = lax.axis_index("real")
    loads[0].wait()
    loads[1].wait()
    high, low, outer = phase_factors(cycle_ref, mode_ref[...], cycle_len, half_len, group)
    modes = mode_ref.shape[1]
    table_rows = legendre_ref.shape[0]
    per_block = modes // blocks
    cycles = table_rows // per_block
    pixel_rows = outer.shape[0]
    half = LANES // 2
    lane = lane_ids((1, LANES))
    row = row_ids((LANES, LANES))
    lane_order = (lane & (half - 1)) >> log2(cycles)
    lane_row = (lane & 1) * half + (lane >> log2(half)) * modes + block * per_block + lane_order
    coeff_pick = (row == lane_row).astype(jnp.float32).astype(jnp.bfloat16)
    lane_row = (lane & (per_block - 1)) * cycles + 2 * block + (lane >> log2(half))
    gram_pick = jnp.concatenate([row == lane_row, row == lane_row + half], axis=1)
    gram_pick = gram_pick.astype(jnp.float32).astype(jnp.bfloat16)
    holder = (lane & (modes - 1)) >> log2(per_block)
    lane_block = (lane & (cycles - 1)) >> 1

    total_reals = real_groups * reals
    fourier_rows = blocks * total_reals
    coeff_rows = jnp.dot(
        gathered_ref[:fourier_rows, :], coeff_pick, preferred_element_type=jnp.float32
    ).reshape(real_groups, blocks, reals, LANES)
    columns = jnp.zeros((total_reals, LANES), jnp.float32)
    for b in range(blocks):
        one = coeff_rows[:, b].reshape(total_reals, LANES)
        columns = columns + jnp.where(lane_block == b, one, 0.0)
    loads[2].wait()
    loads[3].wait()
    table = legendre_ref[...]
    table = jnp.concatenate([table, table], axis=0)
    spectrum = spectrum_ref[...]
    factor = spectrum / (spectrum + 0.5)
    tiles = table.shape[1] // LANES
    stride = 2 * tiles * per_block
    stores = []
    for y in range(real_groups):
        pieces = [
            jnp.where((lane >> log2(cycles)) == c * per_block + s, columns[y * reals : (y + 1) * reals], 0.0)
            for s in range(per_block)
            for c in range(2)
        ]
        filtered = factor * jnp.dot(
            jnp.concatenate(pieces, axis=0).astype(jnp.bfloat16), table, preferred_element_type=jnp.float32
        )
        for s in range(per_block):
            for c in range(2):
                start = (s * 2 + c) * reals
                for tile in range(tiles):
                    first_row = y * reals * stride + (c * tiles + tile) * per_block + s
                    wiener_ref[pl.ds(first_row, reals, stride=stride), :] = filtered[
                        start : start + reals, tile * LANES : (tile + 1) * LANES
                    ]
        span = pl.ds(y * reals * stride, reals * stride)
        stores += start_copies([wiener_ref.at[span]], [wiener_hbm.at[span]], out_sems, len(stores))

    gram_all = gathered_ref[fourier_rows:, :]
    gram_rows = jnp.dot(gram_all, gram_pick, preferred_element_type=jnp.float32)
    gram_rows = gram_rows.reshape(blocks, cycles // 2, 2 * LANES)
    holder = jnp.concatenate([holder, holder], axis=1)
    gram = jnp.zeros((cycles // 2, 2 * LANES), jnp.float32)
    for b in range(blocks):
        gram = gram + jnp.where(holder == b, gram_rows[b], 0.0)
    gram = jnp.concatenate([gram[:, :LANES], gram[:, LANES:]], axis=0)

    first = lane < half
    cycle_modes = jnp.zeros((reals, LANES), jnp.float32)
    for b in range(blocks):
        first_row = pl.multiple_of((real_group * blocks + b) * reals, reals)
        pair = gathered_ref[pl.ds(first_row, reals), :].astype(jnp.float32)
        turned = pltpu.roll(pair, half, 1)
        cycle_modes = cycle_modes + jnp.where(first, pair, turned) * gram[2 * b : 2 * b + 1]
        cycle_modes = cycle_modes + jnp.where(first, turned, pair) * gram[2 * b + 1 : 2 * b + 2]
    cycle_modes = cycle_modes * modes**-0.5
    turned = pltpu.roll(cycle_modes, half, 1)
    even = jnp.where(first, cycle_modes, turned)
    odd = jnp.where(first, turned, cycle_modes)
    parity = (row_ids((1, 8, LANES)) & 1) == 0
    spread = jnp.where(parity, even[:, None, :], odd[:, None, :])
    inner = jnp.concatenate([high, low], axis=1)
    outer = outer.reshape(1, pixel_rows // 8, 8, LANES)
    part_reals = reals // parts
    for i in range(parts):
        rotated = spread[i * part_reals : (i + 1) * part_reals, None] * outer
        rotated = rotated.reshape(part_reals * pixel_rows, LANES).astype(jnp.bfloat16)
        span = pl.ds(i * part_reals * pixel_rows, part_reals * pixel_rows)
        signal_ref[span, :] = lax.dot_general(
            jnp.concatenate([rotated, rotated], axis=1), inner, NT, preferred_element_type=jnp.float32
        )
        stores += start_copies([signal_ref.at[span]], [signal_hbm.at[span]], out_sems, len(stores))
    for store in stores:
        store.wait()


def split_tiles(array):
    lead, rows, columns = array.shape[:-2], array.shape[-2], array.shape[-1]
    split = array.reshape(*lead, rows, columns // LANES, LANES)
    return jnp.swapaxes(split, -2, -3).reshape(-1, LANES)


def gram_program(
    sky_data, signal_prev, noise_var, mask_flags, cycle_table, m_table, spectrum, legendre
):
    reals, cycle_dev, half_len = sky_data.shape
    groups, blocks, real_groups = (lax.axis_size(name) for name in AXES)
    cycle_len = half_len * groups
    per_block, multipoles, cycles = legendre.shape
    total_l = multipoles * groups * real_groups
    tiles = multipoles // LANES
    hbm = pl.BlockSpec(memory_space=pltpu.HBM)
    vmem = pl.BlockSpec(memory_space=pltpu.VMEM)
    orders = m_table[None, :]
    spectrum_row = spectrum[None, :]
    table = legendre.transpose(0, 2, 1).reshape(per_block * cycles, multipoles)
    inputs = (
        cycle_table, orders, split_tiles(noise_var), split_tiles(mask_flags), spectrum_row, table,
        split_tiles(sky_data), split_tiles(signal_prev),
    )
    spaces = [pltpu.SMEM] + [pltpu.VMEM] * 7
    rows = blocks * (real_groups * reals + cycles // 2)
    local = pl.pallas_call(
        functools.partial(forward_kernel, cycle_len, half_len, (cycles / total_l) ** 0.5, 1),
        out_shape=jax.ShapeDtypeStruct((rows, LANES), jnp.bfloat16),
        in_specs=[hbm] * 8,
        out_specs=vmem,
        scratch_shapes=[space(x.shape, x.dtype) for space, x in zip(spaces, inputs)]
        + [pltpu.SemaphoreType.DMA((8,))],
    )(*inputs)
    gathered = lax.psum(local, AXES)
    total_reals = reals * real_groups
    inputs = (cycle_table, orders, table, spectrum_row)
    outputs = (
        jax.ShapeDtypeStruct((total_reals * 2 * tiles * per_block, LANES), jnp.float32),
        jax.ShapeDtypeStruct((reals * cycle_dev * half_len // LANES, LANES), jnp.float32),
    )
    wiener, signal = pl.pallas_call(
        functools.partial(backward_kernel, cycle_len, half_len, blocks, real_groups, reals, PARTS),
        out_shape=outputs,
        in_specs=[vmem] + [hbm] * 4,
        out_specs=(hbm, hbm),
        scratch_shapes=[space(x.shape, x.dtype) for space, x in zip(spaces, inputs)]
        + [pltpu.VMEM(x.shape, x.dtype) for x in outputs]
        + [pltpu.SemaphoreType.DMA((4,)), pltpu.SemaphoreType.DMA((real_groups + PARTS,))],
        compiler_params=pltpu.CompilerParams(vmem_limit_bytes=BACKWARD_VMEM),
    )(gathered, *inputs)
    wiener = wiener.reshape(total_reals, 2, tiles, per_block, LANES).transpose(0, 1, 3, 2, 4)
    signal = signal.reshape(reals, half_len // LANES, cycle_dev, LANES).transpose(0, 2, 1, 3)
    return (
        wiener.reshape(total_reals, 2, per_block, multipoles),
        signal.reshape(sky_data.shape),
    )


def gram_form_fits(mesh, sky_data, m_table, legendre):
    groups, blocks, real_groups = (mesh.shape[name] for name in AXES)
    reals, cycles, cycle_len = sky_data.shape
    modes = m_table.shape[0]
    per_block = modes // blocks
    multipoles = legendre.shape[1] // (groups * real_groups)
    half_len = cycle_len // groups
    reals_dev = reals // real_groups
    return (
        cycles < 2 * reals
        and 4 * modes == LANES
        and cycles == 2 * blocks
        and all(size & (size - 1) == 0 for size in (blocks, modes, cycles))
        and 2 * per_block * cycles == LANES
        and cycle_len & (cycle_len - 1) == 0
        and half_len % (4 * LANES) == 0
        and multipoles % LANES == 0
        and reals_dev % 16 == 0
        and reals_dev % PARTS == 0
        and cycles % 16 == 0
    )


def phase_tables(col_ids, mode_ids, cycle_len):
    product_ids = col_ids[:, None] * mode_ids[None, :] % cycle_len
    angles = product_ids.astype(jnp.float32) * (2.0 * math.pi / cycle_len)
    return (jnp.cos(angles).astype(jnp.bfloat16), jnp.sin(angles).astype(jnp.bfloat16))


def cycle_offsets(cycle_ids, mode_ids, cycle_len):
    parity = (cycle_ids % 2).astype(jnp.float32)
    shifts = math.pi / cycle_len * parity[:, None] * mode_ids[None, :].astype(jnp.float32)
    return (jnp.cos(shifts), jnp.sin(shifts))


def forward_modes(re_part, im_part):
    summed = lax.psum((re_part, im_part), "grp")
    fourier_pair = (summed[0].astype(jnp.bfloat16), summed[1].astype(jnp.bfloat16))
    fourier_pair = (
        lax.all_gather(fourier_pair[0], "real", axis=0, tiled=True),
        lax.all_gather(fourier_pair[1], "real", axis=0, tiled=True),
    )
    fourier_pair = (
        lax.all_to_all(fourier_pair[0], "blk", split_axis=2, concat_axis=1, tiled=True),
        lax.all_to_all(fourier_pair[1], "blk", split_axis=2, concat_axis=1, tiled=True),
    )
    return fourier_pair


def backward_cycles(partial_value):
    summed = lax.psum_scatter(partial_value, "real", scatter_dimension=0, tiled=True)
    reduced = lax.psum(summed, "grp")
    cycle_pair = lax.all_to_all(
        reduced.astype(jnp.bfloat16), "blk", split_axis=2, concat_axis=3, tiled=True
    )
    return cycle_pair


def per_device(
    sky_data, signal_prev, noise_var, mask_flags, cycle_table, m_table, spectrum, legendre
):
    real_dev, cycle_dev, half_len = sky_data.shape
    cycle_len = half_len * lax.axis_size("grp")
    mode_count = m_table.shape[0]
    col_ids = lax.axis_index("grp") * half_len + jnp.arange(half_len, dtype=jnp.int32)
    cos_tab, sin_tab = phase_tables(col_ids, m_table, cycle_len)
    cos_shift, sin_shift = cycle_offsets(cycle_table, m_table, cycle_len)
    weight = mask_flags.astype(jnp.float32) / (noise_var - 0.5)
    messenger = (weight * sky_data + 2.0 * signal_prev) / (weight + 2.0)
    flat_rows = messenger.astype(jnp.bfloat16).reshape(real_dev * cycle_dev, half_len)
    base_cos = jnp.dot(flat_rows, cos_tab, preferred_element_type=jnp.float32).reshape(
        real_dev, cycle_dev, mode_count
    )
    base_sin = -jnp.dot(flat_rows, sin_tab, preferred_element_type=jnp.float32).reshape(
        real_dev, cycle_dev, mode_count
    )
    norm_scale = cycle_len ** (-0.5)
    re_part = (base_cos * cos_shift + base_sin * sin_shift) * norm_scale
    im_part = (base_sin * cos_shift - base_cos * sin_shift) * norm_scale
    fourier_re, fourier_im = forward_modes(re_part, im_part)
    fourier = jnp.stack([fourier_re, fourier_im], 1)
    coefficients = jnp.einsum(
        "mlr,kcrm->kcml", legendre, fourier, preferred_element_type=jnp.float32
    )
    factor = spectrum / (spectrum + 0.5)
    wiener_alm = coefficients * factor
    total_l = legendre.shape[1] * lax.axis_size("grp") * lax.axis_size("real")
    syn_scale = (legendre.shape[2] / total_l) ** 0.5
    partial_value = (
        jnp.einsum(
            "mlr,kcml->kcrm",
            legendre,
            wiener_alm.astype(jnp.bfloat16),
            preferred_element_type=jnp.float32,
        )
        * syn_scale
    )
    cycle_pair = backward_cycles(partial_value)
    cycle_modes = cycle_pair.astype(jnp.float32)
    modes_re = cycle_modes[:, 0]
    modes_im = cycle_modes[:, 1]
    rotated_re = (modes_re * cos_shift - modes_im * sin_shift).astype(jnp.bfloat16)
    rotated_im = (modes_im * cos_shift + modes_re * sin_shift).astype(jnp.bfloat16)
    contract = (((1,), (1,)), ((), ()))
    pixel_sum = lax.dot_general(
        rotated_re.reshape(-1, mode_count), cos_tab, contract, preferred_element_type=jnp.float32
    )
    pixel_sum = pixel_sum - lax.dot_general(
        rotated_im.reshape(-1, mode_count), sin_tab, contract, preferred_element_type=jnp.float32
    )
    signal_next = (pixel_sum * mode_count ** (-0.5)).reshape(real_dev, cycle_dev, half_len)
    return (wiener_alm, signal_next)


def solution(mesh):
    in_specs = (
        P("real", "blk", "grp"),
        P("real", "blk", "grp"),
        P("blk", "grp"),
        P("blk", "grp"),
        P("blk"),
        P(),
        P(("grp", "real")),
        P("blk", ("grp", "real"), None),
    )
    out_specs = (P(None, None, "blk", ("grp", "real")), P("real", "blk", "grp"))

    def step(sky_data, signal_prev, noise_var, mask_flags, cycle_table, m_table, spectrum, legendre):
        fits = gram_form_fits(mesh, sky_data, m_table, legendre)
        return jax.shard_map(
            gram_program if fits else per_device,
            mesh=mesh,
            in_specs=in_specs,
            out_specs=out_specs,
            check_vma=False,
        )(sky_data, signal_prev, noise_var, mask_flags, cycle_table, m_table, spectrum, legendre)

    return step
```

```python
import functools
import math

import jax
import jax.numpy as jnp
from jax import lax
from jax.experimental import pallas as pl
from jax.experimental.pallas import tpu as pltpu
from jax.sharding import PartitionSpec as P

LANES = 128
NT = (((1,), (1,)), ((), ()))
AXES = ("grp", "blk", "real")
PARTS = 2
FORWARD_VMEM = 63_290_000
BACKWARD_VMEM = 16 << 20


def unit_cosine(units, half_turn):
    wrapped = units & (2 * half_turn - 1)
    folded = jnp.minimum(wrapped, 2 * half_turn - wrapped)
    y = (half_turn // 2 - folded).astype(jnp.float32) * (math.pi / half_turn)
    y2 = y * y
    acc = jnp.full_like(y2, -1.0 / math.factorial(11))
    for order, sign in ((9, 1.0), (7, -1.0), (5, 1.0), (3, -1.0), (1, 1.0)):
        acc = acc * y2 + sign / math.factorial(order)
    return acc * y


def log2(size):
    return size.bit_length() - 1


def lane_ids(shape):
    return lax.broadcasted_iota(jnp.int32, shape, len(shape) - 1)


def row_ids(shape):
    return lax.broadcasted_iota(jnp.int32, shape, len(shape) - 2)


def phase_factors(cycles, orders, cycle_len, half_len, group):
    modes = orders.shape[1]
    orders = jnp.concatenate([orders] * (LANES // modes), axis=1)
    quarter = lane_ids((1, LANES)) >> log2(modes)
    quarter_turn = cycle_len // 2
    inner_units = 2 * orders * row_ids((LANES, LANES)) + ((quarter + 1) >> 1) * quarter_turn
    inner = unit_cosine(inner_units, cycle_len)
    rows = 2 * (half_len // LANES)
    row = row_ids((rows, LANES))
    parity = jnp.where((row & 1) == 0, cycles[:, :1], cycles[:, 1:]) & 1
    pixel = group * half_len + LANES * (row >> 1)
    outer_units = orders * (2 * pixel + parity) + (quarter >> 1) * (3 * quarter_turn)
    outer = unit_cosine(outer_units, cycle_len)
    high = inner.astype(jnp.bfloat16)
    low = (inner - high.astype(jnp.float32)).astype(jnp.bfloat16)
    return high, low, outer


def start_copies(sources, targets, sems, first=0):
    copies = [
        pltpu.make_async_copy(source, target, sems.at[first + i])
        for i, (source, target) in enumerate(zip(sources, targets))
    ]
    for copy in copies:
        copy.start()
    return copies


def row_parts(ref, parts):
    size = ref.shape[0] // parts
    return [ref.at[pl.ds(i * size, size)] for i in range(parts)]


def forward_kernel(
    cycle_len, half_len, syn_scale, parts,
    cycle_hbm, mode_hbm, noise_hbm, mask_hbm, spectrum_hbm, legendre_hbm, sky_hbm, prev_hbm, out_ref,
    cycle_ref, mode_ref, noise_ref, mask_ref, spectrum_ref, legendre_ref, sky_ref, prev_ref, sems,
):
    small = start_copies(
        (cycle_hbm, mode_hbm, noise_hbm, mask_hbm, spectrum_hbm, legendre_hbm),
        (cycle_ref, mode_ref, noise_ref, mask_ref, spectrum_ref, legendre_ref),
        sems,
    )
    sources = [part for pair in zip(row_parts(sky_hbm, parts), row_parts(prev_hbm, parts)) for part in pair]
    targets = [part for pair in zip(row_parts(sky_ref, parts), row_parts(prev_ref, parts)) for part in pair]
    large = start_copies(sources, targets, sems, len(small))
    group = lax.axis_index("grp")
    small[0].wait()
    small[1].wait()
    high, low, outer = phase_factors(cycle_ref[...], mode_ref[...], cycle_len, half_len, group)
    inner = jnp.concatenate([high, low], axis=0)
    small[2].wait()
    small[3].wait()
    weight = mask_ref[...].astype(jnp.float32) / (noise_ref[...] - 0.5)
    inverse = 1.0 / (weight + 2.0)
    sky_gain = weight * inverse
    prev_gain = 2.0 * inverse

    small[4].wait()
    small[5].wait()
    table = legendre_ref[...]
    spectrum = spectrum_ref[...]
    factor = spectrum / (spectrum + 0.5)
    filtered = (table.astype(jnp.float32) * factor).astype(jnp.bfloat16)
    gram = lax.dot_general(table, filtered, NT, preferred_element_type=jnp.float32)
    table_rows = table.shape[0]
    pixel_rows = outer.shape[0]
    reals = sky_ref.shape[0] // pixel_rows
    cycles = 2 * (out_ref.shape[1] - reals)
    same = (row_ids(gram.shape) >> log2(cycles)) == (lane_ids((1, table_rows)) >> log2(cycles))
    gram = jnp.where(same, gram, 0.0).reshape(table_rows // cycles, cycles, table_rows).sum(axis=0)
    gram = gram * syn_scale
    gram = jnp.concatenate([gram[: cycles // 2], gram[cycles // 2 :]], axis=1).astype(jnp.bfloat16)

    part_reals = reals // parts
    shape = (part_reals, pixel_rows, LANES)
    fourier = []
    for i in range(parts):
        large[2 * i].wait()
        large[2 * i + 1].wait()
        span = pl.ds(i * part_reals * pixel_rows, part_reals * pixel_rows)
        sky = sky_ref[span, :].reshape(shape)
        prev = prev_ref[span, :].reshape(shape)
        rows = (sky * sky_gain + prev * prev_gain).reshape(-1, LANES).astype(jnp.bfloat16)
        partial = jnp.dot(
            jnp.concatenate([rows, rows], axis=1), inner, preferred_element_type=jnp.float32
        )
        turned = partial.reshape(shape) * outer
        summed = turned.reshape(part_reals, pixel_rows // 8, 8, LANES).sum(axis=1)
        summed = summed.reshape(part_reals * 8, LANES)
        summed = summed + pltpu.roll(summed, LANES // 2, 1)
        own = (row_ids(summed.shape) & 1) == (lane_ids(summed.shape) >= LANES // 2)
        fourier.append(jnp.where(own, summed, 0.0).reshape(part_reals, 8, LANES).sum(axis=1))
    fourier = (jnp.concatenate(fourier, axis=0) * cycle_len**-0.5).astype(jnp.bfloat16)
    block = jnp.concatenate([fourier, gram], axis=0)
    for target in range(out_ref.shape[0]):
        out_ref[target] = block


def backward_kernel(
    cycle_len, half_len, groups, blocks, real_groups, reals, parts,
    gathered_ref, cycle_ref, mode_ref, legendre_ref, spectrum_ref, wiener_hbm, signal_hbm,
    wiener_ref, signal_ref, out_sems,
):
    group = lax.axis_index("grp")
    block = lax.axis_index("blk")
    real_group = lax.axis_index("real")
    high, low, outer = phase_factors(cycle_ref[...], mode_ref[...], cycle_len, half_len, group)
    modes = mode_ref.shape[1]
    table_rows = legendre_ref.shape[0]
    per_block = modes // blocks
    cycles = table_rows // per_block
    pixel_rows = outer.shape[0]
    half = LANES // 2
    lane = lane_ids((1, LANES))
    row = row_ids((LANES, LANES))
    lane_order = (lane & (half - 1)) >> log2(cycles)
    lane_row = (lane & 1) * half + (lane >> log2(half)) * modes + block * per_block + lane_order
    coeff_pick = (row == lane_row).astype(jnp.float32).astype(jnp.bfloat16)
    lane_row = (lane & (per_block - 1)) * cycles + 2 * block + (lane >> log2(half))
    gram_pick = jnp.concatenate([row == lane_row, row == lane_row + half], axis=1)
    gram_pick = gram_pick.astype(jnp.float32).astype(jnp.bfloat16)
    holder = (lane & (modes - 1)) >> log2(per_block)
    lane_block = (lane & (cycles - 1)) >> 1

    fourier_all = gathered_ref[:, :reals, :].reshape(-1, LANES)
    total_reals = real_groups * reals
    coeff_rows = jnp.dot(fourier_all, coeff_pick, preferred_element_type=jnp.float32).reshape(
        groups, blocks, total_reals, LANES
    )
    columns = jnp.zeros((total_reals, LANES), jnp.float32)
    for b in range(blocks):
        one = coeff_rows[:, b].sum(axis=0)
        columns = columns + jnp.where(lane_block == b, one, 0.0)
    table = legendre_ref[...]
    table = jnp.concatenate([table, table], axis=0)
    spectrum = spectrum_ref[...]
    factor = spectrum / (spectrum + 0.5)
    stores = []
    own = (lane >> log2(cycles)) == row_ids((2 * per_block, LANES))
    upper = row_ids((1, 2 * per_block, LANES)) < per_block
    for y in range(real_groups):
        span = slice(y * reals, (y + 1) * reals)
        pieces = jnp.where(own, columns[span, None, :], 0.0)
        filtered = factor * jnp.dot(
            pieces.reshape(-1, LANES).astype(jnp.bfloat16), table, preferred_element_type=jnp.float32
        )
        for pair in range(wiener_ref.shape[2]):
            one, two = (
                filtered[:, tile * LANES : (tile + 1) * LANES].reshape(reals, 2 * per_block, LANES)
                for tile in (2 * pair, 2 * pair + 1)
            )
            wiener_ref[span, 0, pair] = jnp.where(upper, one, pltpu.roll(two, per_block, 1))
            wiener_ref[span, 1, pair] = jnp.where(upper, pltpu.roll(one, per_block, 1), two)
        span = pl.ds(y * reals, reals)
        stores += start_copies([wiener_ref.at[span]], [wiener_hbm.at[span]], out_sems, len(stores))

    gram_all = gathered_ref[:, reals:, :].reshape(-1, LANES)
    gram_rows = jnp.dot(gram_all, gram_pick, preferred_element_type=jnp.float32)
    gram_rows = gram_rows.reshape(groups, blocks, real_groups, cycles // 2, 2 * LANES)
    holder = jnp.concatenate([holder, holder], axis=1)
    gram = jnp.zeros((cycles // 2, 2 * LANES), jnp.float32)
    for b in range(blocks):
        one = gram_rows[:, b].reshape(-1, cycles // 2, 2 * LANES).sum(axis=0)
        gram = gram + jnp.where(holder == b, one, 0.0)
    gram = jnp.concatenate([gram[:, :LANES], gram[:, LANES:]], axis=0)

    first = lane < half
    cycle_modes = jnp.zeros((reals, LANES), jnp.float32)
    for b in range(blocks):
        pair = jnp.zeros((reals, LANES), jnp.float32)
        for g in range(groups):
            source = (g * blocks + b) * real_groups + real_group
            pair = pair + gathered_ref[source, :reals, :].astype(jnp.float32)
        turned = pltpu.roll(pair, half, 1)
        cycle_modes = cycle_modes + jnp.where(first, pair, turned) * gram[2 * b : 2 * b + 1]
        cycle_modes = cycle_modes + jnp.where(first, turned, pair) * gram[2 * b + 1 : 2 * b + 2]
    cycle_modes = cycle_modes * modes**-0.5
    turned = pltpu.roll(cycle_modes, half, 1)
    even = jnp.where(first, cycle_modes, turned)
    odd = jnp.where(first, turned, cycle_modes)
    parity = (row_ids((1, 8, LANES)) & 1) == 0
    spread = jnp.where(parity, even[:, None, :], odd[:, None, :])
    inner = jnp.concatenate([high, low], axis=1)
    outer = outer.reshape(1, pixel_rows // 8, 8, LANES)
    part_reals = reals // parts
    for i in range(parts):
        rotated = spread[i * part_reals : (i + 1) * part_reals, None] * outer
        rotated = rotated.reshape(part_reals * pixel_rows, LANES).astype(jnp.bfloat16)
        span = pl.ds(i * part_reals * pixel_rows, part_reals * pixel_rows)
        signal_ref[span, :] = lax.dot_general(
            jnp.concatenate([rotated, rotated], axis=1), inner, NT, preferred_element_type=jnp.float32
        )
        stores += start_copies([signal_ref.at[span]], [signal_hbm.at[span]], out_sems, len(stores))
    for store in stores:
        store.wait()


def split_tiles(array):
    lead, rows, columns = array.shape[:-2], array.shape[-2], array.shape[-1]
    split = array.reshape(*lead, rows, columns // LANES, LANES)
    return jnp.swapaxes(split, -2, -3).reshape(-1, LANES)


def gram_program(
    sky_data, signal_prev, noise_var, mask_flags, cycle_table, m_table, spectrum, legendre
):
    reals, cycle_dev, half_len = sky_data.shape
    groups, blocks, real_groups = (lax.axis_size(name) for name in AXES)
    cycle_len = half_len * groups
    per_block, multipoles, cycles = legendre.shape
    total_l = multipoles * groups * real_groups
    tiles = multipoles // LANES
    hbm = pl.BlockSpec(memory_space=pltpu.HBM)
    vmem = pl.BlockSpec(memory_space=pltpu.VMEM)
    orders = m_table[None, :]
    cycles_row = cycle_table[None, :]
    spectrum_row = spectrum[None, :]
    table = legendre.transpose(0, 2, 1).reshape(per_block * cycles, multipoles)
    inputs = (
        cycles_row, orders, split_tiles(noise_var), split_tiles(mask_flags), spectrum_row, table,
        split_tiles(sky_data), split_tiles(signal_prev),
    )
    sources = groups * blocks * real_groups
    local = pl.pallas_call(
        functools.partial(forward_kernel, cycle_len, half_len, (cycles / total_l) ** 0.5, 1),
        out_shape=jax.ShapeDtypeStruct((sources, reals + cycles // 2, LANES), jnp.bfloat16),
        in_specs=[hbm] * 8,
        out_specs=vmem,
        scratch_shapes=[pltpu.VMEM(x.shape, x.dtype) for x in inputs]
        + [pltpu.SemaphoreType.DMA((8,))],
        compiler_params=pltpu.CompilerParams(vmem_limit_bytes=FORWARD_VMEM),
    )(*inputs)
    gathered = lax.all_to_all(local, AXES, 0, 0, tiled=True)
    total_reals = reals * real_groups
    outputs = (
        jax.ShapeDtypeStruct((total_reals, 2, tiles // 2, 2 * per_block, LANES), jnp.float32),
        jax.ShapeDtypeStruct((reals * cycle_dev * half_len // LANES, LANES), jnp.float32),
    )
    wiener, signal = pl.pallas_call(
        functools.partial(backward_kernel, cycle_len, half_len, groups, blocks, real_groups, reals, PARTS),
        out_shape=outputs,
        in_specs=[vmem] * 5,
        out_specs=(hbm, hbm),
        scratch_shapes=[pltpu.VMEM(x.shape, x.dtype) for x in outputs]
        + [pltpu.SemaphoreType.DMA((real_groups + PARTS,))],
        compiler_params=pltpu.CompilerParams(vmem_limit_bytes=BACKWARD_VMEM),
    )(gathered, cycles_row, orders, table, spectrum_row)
    wiener = wiener.reshape(total_reals, 2, tiles, per_block, LANES).transpose(0, 1, 3, 2, 4)
    signal = signal.reshape(reals, half_len // LANES, cycle_dev, LANES).transpose(0, 2, 1, 3)
    return (
        wiener.reshape(total_reals, 2, per_block, multipoles),
        signal.reshape(sky_data.shape),
    )


def gram_form_fits(mesh, sky_data, m_table, legendre):
    groups, blocks, real_groups = (mesh.shape[name] for name in AXES)
    reals, cycles, cycle_len = sky_data.shape
    modes = m_table.shape[0]
    per_block = modes // blocks
    multipoles = legendre.shape[1] // (groups * real_groups)
    half_len = cycle_len // groups
    reals_dev = reals // real_groups
    return (
        cycles < 2 * reals
        and 4 * modes == LANES
        and cycles == 2 * blocks
        and all(size & (size - 1) == 0 for size in (blocks, modes, cycles))
        and 2 * per_block * cycles == LANES
        and cycle_len & (cycle_len - 1) == 0
        and half_len % (4 * LANES) == 0
        and multipoles % (2 * LANES) == 0
        and per_block == 4
        and reals_dev % 16 == 0
        and reals_dev % PARTS == 0
        and cycles % 16 == 0
    )


def phase_tables(col_ids, mode_ids, cycle_len):
    product_ids = col_ids[:, None] * mode_ids[None, :] % cycle_len
    angles = product_ids.astype(jnp.float32) * (2.0 * math.pi / cycle_len)
    return (jnp.cos(angles).astype(jnp.bfloat16), jnp.sin(angles).astype(jnp.bfloat16))


def cycle_offsets(cycle_ids, mode_ids, cycle_len):
    parity = (cycle_ids % 2).astype(jnp.float32)
    shifts = math.pi / cycle_len * parity[:, None] * mode_ids[None, :].astype(jnp.float32)
    return (jnp.cos(shifts), jnp.sin(shifts))


def forward_modes(re_part, im_part):
    summed = lax.psum((re_part, im_part), "grp")
    fourier_pair = (summed[0].astype(jnp.bfloat16), summed[1].astype(jnp.bfloat16))
    fourier_pair = (
        lax.all_gather(fourier_pair[0], "real", axis=0, tiled=True),
        lax.all_gather(fourier_pair[1], "real", axis=0, tiled=True),
    )
    fourier_pair = (
        lax.all_to_all(fourier_pair[0], "blk", split_axis=2, concat_axis=1, tiled=True),
        lax.all_to_all(fourier_pair[1], "blk", split_axis=2, concat_axis=1, tiled=True),
    )
    return fourier_pair


def backward_cycles(partial_value):
    summed = lax.psum_scatter(partial_value, "real", scatter_dimension=0, tiled=True)
    reduced = lax.psum(summed, "grp")
    cycle_pair = lax.all_to_all(
        reduced.astype(jnp.bfloat16), "blk", split_axis=2, concat_axis=3, tiled=True
    )
    return cycle_pair


def per_device(
    sky_data, signal_prev, noise_var, mask_flags, cycle_table, m_table, spectrum, legendre
):
    real_dev, cycle_dev, half_len = sky_data.shape
    cycle_len = half_len * lax.axis_size("grp")
    mode_count = m_table.shape[0]
    col_ids = lax.axis_index("grp") * half_len + jnp.arange(half_len, dtype=jnp.int32)
    cos_tab, sin_tab = phase_tables(col_ids, m_table, cycle_len)
    cos_shift, sin_shift = cycle_offsets(cycle_table, m_table, cycle_len)
    weight = mask_flags.astype(jnp.float32) / (noise_var - 0.5)
    messenger = (weight * sky_data + 2.0 * signal_prev) / (weight + 2.0)
    flat_rows = messenger.astype(jnp.bfloat16).reshape(real_dev * cycle_dev, half_len)
    base_cos = jnp.dot(flat_rows, cos_tab, preferred_element_type=jnp.float32).reshape(
        real_dev, cycle_dev, mode_count
    )
    base_sin = -jnp.dot(flat_rows, sin_tab, preferred_element_type=jnp.float32).reshape(
        real_dev, cycle_dev, mode_count
    )
    norm_scale = cycle_len ** (-0.5)
    re_part = (base_cos * cos_shift + base_sin * sin_shift) * norm_scale
    im_part = (base_sin * cos_shift - base_cos * sin_shift) * norm_scale
    fourier_re, fourier_im = forward_modes(re_part, im_part)
    fourier = jnp.stack([fourier_re, fourier_im], 1)
    coefficients = jnp.einsum(
        "mlr,kcrm->kcml", legendre, fourier, preferred_element_type=jnp.float32
    )
    factor = spectrum / (spectrum + 0.5)
    wiener_alm = coefficients * factor
    total_l = legendre.shape[1] * lax.axis_size("grp") * lax.axis_size("real")
    syn_scale = (legendre.shape[2] / total_l) ** 0.5
    partial_value = (
        jnp.einsum(
            "mlr,kcml->kcrm",
            legendre,
            wiener_alm.astype(jnp.bfloat16),
            preferred_element_type=jnp.float32,
        )
        * syn_scale
    )
    cycle_pair = backward_cycles(partial_value)
    cycle_modes = cycle_pair.astype(jnp.float32)
    modes_re = cycle_modes[:, 0]
    modes_im = cycle_modes[:, 1]
    rotated_re = (modes_re * cos_shift - modes_im * sin_shift).astype(jnp.bfloat16)
    rotated_im = (modes_im * cos_shift + modes_re * sin_shift).astype(jnp.bfloat16)
    contract = (((1,), (1,)), ((), ()))
    pixel_sum = lax.dot_general(
        rotated_re.reshape(-1, mode_count), cos_tab, contract, preferred_element_type=jnp.float32
    )
    pixel_sum = pixel_sum - lax.dot_general(
        rotated_im.reshape(-1, mode_count), sin_tab, contract, preferred_element_type=jnp.float32
    )
    signal_next = (pixel_sum * mode_count ** (-0.5)).reshape(real_dev, cycle_dev, half_len)
    return (wiener_alm, signal_next)


def solution(mesh):
    in_specs = (
        P("real", "blk", "grp"),
        P("real", "blk", "grp"),
        P("blk", "grp"),
        P("blk", "grp"),
        P("blk"),
        P(),
        P(("grp", "real")),
        P("blk", ("grp", "real"), None),
    )
    out_specs = (P(None, None, "blk", ("grp", "real")), P("real", "blk", "grp"))

    def step(sky_data, signal_prev, noise_var, mask_flags, cycle_table, m_table, spectrum, legendre):
        fits = gram_form_fits(mesh, sky_data, m_table, legendre)
        return jax.shard_map(
            gram_program if fits else per_device,
            mesh=mesh,
            in_specs=in_specs,
            out_specs=out_specs,
            check_vma=False,
        )(sky_data, signal_prev, noise_var, mask_flags, cycle_table, m_table, spectrum, legendre)

    return step
```

```python
import functools
import math

import jax
import jax.numpy as jnp
from jax import lax
from jax.experimental import pallas as pl
from jax.experimental.pallas import tpu as pltpu
from jax.sharding import PartitionSpec as P

LANES = 128
NT = (((1,), (1,)), ((), ()))
AXES = ("grp", "blk", "real")
PARTS = 2
FORWARD_VMEM = 63_290_000
BACKWARD_VMEM = 16 << 20


def unit_cosine(units, half_turn):
    wrapped = units & (2 * half_turn - 1)
    folded = jnp.minimum(wrapped, 2 * half_turn - wrapped)
    y = (half_turn // 2 - folded).astype(jnp.float32) * (math.pi / half_turn)
    y2 = y * y
    acc = jnp.full_like(y2, -1.0 / math.factorial(11))
    for order, sign in ((9, 1.0), (7, -1.0), (5, 1.0), (3, -1.0), (1, 1.0)):
        acc = acc * y2 + sign / math.factorial(order)
    return acc * y


def log2(size):
    return size.bit_length() - 1


def lane_ids(shape):
    return lax.broadcasted_iota(jnp.int32, shape, len(shape) - 1)


def row_ids(shape):
    return lax.broadcasted_iota(jnp.int32, shape, len(shape) - 2)


def phase_factors(cycles, orders, cycle_len, half_len, group):
    modes = orders.shape[1]
    orders = jnp.concatenate([orders] * (LANES // modes), axis=1)
    quarter = lane_ids((1, LANES)) >> log2(modes)
    quarter_turn = cycle_len // 2
    inner_units = 2 * orders * row_ids((LANES, LANES)) + ((quarter + 1) >> 1) * quarter_turn
    inner = unit_cosine(inner_units, cycle_len)
    rows = 2 * (half_len // LANES)
    row = row_ids((rows, LANES))
    parity = jnp.where((row & 1) == 0, cycles[:, :1], cycles[:, 1:]) & 1
    pixel = group * half_len + LANES * (row >> 1)
    outer_units = orders * (2 * pixel + parity) + (quarter >> 1) * (3 * quarter_turn)
    outer = unit_cosine(outer_units, cycle_len)
    high = inner.astype(jnp.bfloat16)
    low = (inner - high.astype(jnp.float32)).astype(jnp.bfloat16)
    return high, low, outer


def start_copies(sources, targets, sems, first=0):
    copies = [
        pltpu.make_async_copy(source, target, sems.at[first + i])
        for i, (source, target) in enumerate(zip(sources, targets))
    ]
    for copy in copies:
        copy.start()
    return copies


def row_parts(ref, parts):
    size = ref.shape[0] // parts
    return [ref.at[pl.ds(i * size, size)] for i in range(parts)]


def forward_kernel(
    cycle_len, half_len, syn_scale, parts,
    cycle_hbm, mode_hbm, noise_hbm, mask_hbm, spectrum_hbm, legendre_hbm, sky_hbm, prev_hbm, out_ref,
    cycle_ref, mode_ref, noise_ref, mask_ref, spectrum_ref, legendre_ref, sky_ref, prev_ref, gram_ref, sems,
):
    small = start_copies(
        (cycle_hbm, mode_hbm, noise_hbm, mask_hbm, spectrum_hbm, legendre_hbm),
        (cycle_ref, mode_ref, noise_ref, mask_ref, spectrum_ref, legendre_ref),
        sems,
    )
    sources = [part for pair in zip(row_parts(sky_hbm, parts), row_parts(prev_hbm, parts)) for part in pair]
    targets = [part for pair in zip(row_parts(sky_ref, parts), row_parts(prev_ref, parts)) for part in pair]
    large = start_copies(sources, targets, sems, len(small))
    group = lax.axis_index("grp")
    small[0].wait()
    small[1].wait()
    high, low, outer = phase_factors(cycle_ref[...], mode_ref[...], cycle_len, half_len, group)
    inner = jnp.concatenate([high, low], axis=0)
    small[2].wait()
    small[3].wait()
    weight = mask_ref[...].astype(jnp.float32) / (noise_ref[...] - 0.5)
    inverse = 1.0 / (weight + 2.0)
    sky_gain = weight * inverse
    prev_gain = 2.0 * inverse

    small[4].wait()
    small[5].wait()
    table = legendre_ref[...]
    spectrum = spectrum_ref[...]
    factor = spectrum / (spectrum + 0.5)
    filtered = (table.astype(jnp.float32) * factor).astype(jnp.bfloat16)
    gram = lax.dot_general(table, filtered, NT, preferred_element_type=jnp.float32)
    table_rows = table.shape[0]
    pixel_rows = outer.shape[0]
    reals = sky_ref.shape[0] // pixel_rows
    blocks, real_groups = lax.axis_size("blk"), lax.axis_size("real")
    cycles = 2 * blocks
    same = (row_ids(gram.shape) >> log2(cycles)) == (lane_ids((1, table_rows)) >> log2(cycles))
    gram = jnp.where(same, gram, 0.0).reshape(table_rows // cycles, cycles, table_rows).sum(axis=0)
    gram = gram * syn_scale
    gram_ref[...] = jnp.concatenate([gram, gram], axis=1)
    even, odd = gram_ref[pl.ds(0, blocks, stride=2), :], gram_ref[pl.ds(1, blocks, stride=2), :]
    gram = jnp.where(lane_ids(even.shape) < LANES // 2, even, odd)
    gram_high = gram.astype(jnp.bfloat16).astype(jnp.float32)
    gram_low = gram - gram_high

    part_reals = reals // parts
    shape = (part_reals, pixel_rows, LANES)
    fourier = []
    for i in range(parts):
        large[2 * i].wait()
        large[2 * i + 1].wait()
        span = pl.ds(i * part_reals * pixel_rows, part_reals * pixel_rows)
        sky = sky_ref[span, :].reshape(shape)
        prev = prev_ref[span, :].reshape(shape)
        rows = (sky * sky_gain + prev * prev_gain).reshape(-1, LANES).astype(jnp.bfloat16)
        partial = jnp.dot(
            jnp.concatenate([rows, rows], axis=1), inner, preferred_element_type=jnp.float32
        )
        turned = partial.reshape(shape) * outer
        summed = turned.reshape(part_reals, pixel_rows // 8, 8, LANES).sum(axis=1)
        summed = summed.reshape(part_reals * 8, LANES)
        summed = summed + pltpu.roll(summed, LANES // 2, 1)
        own = (row_ids(summed.shape) & 1) == (lane_ids(summed.shape) >= LANES // 2)
        fourier.append(jnp.where(own, summed, 0.0).reshape(part_reals, 8, LANES).sum(axis=1))
    fourier = jnp.concatenate(fourier, axis=0) * cycle_len**-0.5
    rows = []
    for b in range(blocks):
        rows += [fourier, gram_high[b : b + 1], gram_low[b : b + 1]] * real_groups
    rows = jnp.concatenate(rows, axis=0).astype(jnp.bfloat16)
    for g in range(lax.axis_size("grp")):
        out_ref[pl.ds(g * rows.shape[0], rows.shape[0]), :] = rows


def backward_kernel(
    cycle_len, half_len, blocks, real_groups, reals, parts,
    gathered_ref, cycle_ref, mode_ref, legendre_ref, spectrum_ref, wiener_hbm, signal_hbm,
    wiener_ref, signal_ref, fourier_ref, out_sems,
):
    group = lax.axis_index("grp")
    block = lax.axis_index("blk")
    real_group = lax.axis_index("real")
    high, low, outer = phase_factors(cycle_ref[...], mode_ref[...], cycle_len, half_len, group)
    modes = mode_ref.shape[1]
    table_rows = legendre_ref.shape[0]
    per_block = modes // blocks
    cycles = table_rows // per_block
    pixel_rows = outer.shape[0]
    half = LANES // 2
    lane = lane_ids((1, LANES))
    row = row_ids((LANES, LANES))
    lane_order = (lane & (half - 1)) >> log2(cycles)
    lane_row = (lane & 1) * half + (lane >> log2(half)) * modes + block * per_block + lane_order
    coeff_pick = (row == lane_row).astype(jnp.float32).astype(jnp.bfloat16)
    lane_row = (lane >> log2(half)) * per_block + (lane & (per_block - 1))
    gram_pick = ((row >> log2(cycles)) == lane_row).astype(jnp.float32).astype(jnp.bfloat16)
    holder = (lane & (modes - 1)) >> log2(per_block)
    lane_block = (lane & (cycles - 1)) >> 1

    total_reals = real_groups * reals
    fourier_rows = blocks * total_reals
    spacing = reals + 2
    column = lane_ids((1, gathered_ref.shape[0]))
    source = (column * (2**16 // spacing + 1)) >> 16
    inside = column - source * spacing
    source = source & (blocks * real_groups - 1)
    source_block = source >> log2(real_groups)
    target = ((source & (real_groups - 1)) * blocks + source_block) * reals + inside
    target = jnp.where(inside < reals, target, fourier_rows + source_block)
    place = (row_ids((fourier_rows + blocks, column.shape[1])) == target).astype(jnp.float32)
    placed = jnp.dot(place.astype(jnp.bfloat16), gathered_ref[...], preferred_element_type=jnp.float32)
    fourier_ref[...] = placed[:fourier_rows]

    coeff_rows = jnp.dot(
        placed[:fourier_rows].astype(jnp.bfloat16), coeff_pick, preferred_element_type=jnp.float32
    ).reshape(real_groups, blocks, reals, LANES)
    columns = jnp.zeros((total_reals, LANES), jnp.float32)
    for b in range(blocks):
        one = coeff_rows[:, b].reshape(total_reals, LANES)
        columns = columns + jnp.where(lane_block == b, one, 0.0)
    table = legendre_ref[...]
    table = jnp.concatenate([table, table], axis=0)
    spectrum = spectrum_ref[...]
    factor = spectrum / (spectrum + 0.5)
    stores = []
    own = (lane >> log2(cycles)) == row_ids((2 * per_block, LANES))
    upper = row_ids((1, 2 * per_block, LANES)) < per_block
    for y in range(real_groups):
        span = slice(y * reals, (y + 1) * reals)
        pieces = jnp.where(own, columns[span, None, :], 0.0)
        filtered = factor * jnp.dot(
            pieces.reshape(-1, LANES).astype(jnp.bfloat16), table, preferred_element_type=jnp.float32
        )
        for pair in range(wiener_ref.shape[2]):
            one, two = (
                filtered[:, tile * LANES : (tile + 1) * LANES].reshape(reals, 2 * per_block, LANES)
                for tile in (2 * pair, 2 * pair + 1)
            )
            wiener_ref[span, 0, pair] = jnp.where(upper, one, pltpu.roll(two, per_block, 1))
            wiener_ref[span, 1, pair] = jnp.where(upper, pltpu.roll(one, per_block, 1), two)
        span = pl.ds(y * reals, reals)
        stores += start_copies([wiener_ref.at[span]], [wiener_hbm.at[span]], out_sems, len(stores))

    gram_all = jnp.where(
        (lane & (cycles - 1)) == row_ids((cycles, LANES)), placed[fourier_rows:, None, :], 0.0
    ).reshape(blocks * cycles, LANES)
    gram_high = gram_all.astype(jnp.bfloat16)
    gram_low = (gram_all - gram_high.astype(jnp.float32)).astype(jnp.bfloat16)
    gram_rows = jnp.dot(
        jnp.concatenate([gram_high, gram_low], axis=1),
        jnp.concatenate([gram_pick, gram_pick], axis=0),
        preferred_element_type=jnp.float32,
    ).reshape(blocks, cycles, LANES)
    gram = jnp.zeros((cycles, LANES), jnp.float32)
    for b in range(blocks):
        gram = gram + jnp.where(holder == b, gram_rows[b], 0.0)

    first = lane < half
    cycle_modes = jnp.zeros((reals, LANES), jnp.float32)
    for b in range(blocks):
        first_row = pl.multiple_of((real_group * blocks + b) * reals, reals)
        pair = fourier_ref[pl.ds(first_row, reals), :]
        turned = pltpu.roll(pair, half, 1)
        cycle_modes = cycle_modes + jnp.where(first, pair, turned) * gram[2 * b : 2 * b + 1]
        cycle_modes = cycle_modes + jnp.where(first, turned, pair) * gram[2 * b + 1 : 2 * b + 2]
    cycle_modes = cycle_modes * modes**-0.5
    turned = pltpu.roll(cycle_modes, half, 1)
    even = jnp.where(first, cycle_modes, turned)
    odd = jnp.where(first, turned, cycle_modes)
    parity = (row_ids((1, 8, LANES)) & 1) == 0
    spread = jnp.where(parity, even[:, None, :], odd[:, None, :])
    inner = jnp.concatenate([high, low], axis=1)
    outer = outer.reshape(1, pixel_rows // 8, 8, LANES)
    part_reals = reals // parts
    for i in range(parts):
        rotated = spread[i * part_reals : (i + 1) * part_reals, None] * outer
        rotated = rotated.reshape(part_reals * pixel_rows, LANES).astype(jnp.bfloat16)
        span = pl.ds(i * part_reals * pixel_rows, part_reals * pixel_rows)
        signal_ref[span, :] = lax.dot_general(
            jnp.concatenate([rotated, rotated], axis=1), inner, NT, preferred_element_type=jnp.float32
        )
        stores += start_copies([signal_ref.at[span]], [signal_hbm.at[span]], out_sems, len(stores))
    for store in stores:
        store.wait()


def split_tiles(array):
    lead, rows, columns = array.shape[:-2], array.shape[-2], array.shape[-1]
    split = array.reshape(*lead, rows, columns // LANES, LANES)
    return jnp.swapaxes(split, -2, -3).reshape(-1, LANES)


def gram_program(
    sky_data, signal_prev, noise_var, mask_flags, cycle_table, m_table, spectrum, legendre
):
    reals, cycle_dev, half_len = sky_data.shape
    groups, blocks, real_groups = (lax.axis_size(name) for name in AXES)
    cycle_len = half_len * groups
    per_block, multipoles, cycles = legendre.shape
    total_l = multipoles * groups * real_groups
    tiles = multipoles // LANES
    hbm = pl.BlockSpec(memory_space=pltpu.HBM)
    vmem = pl.BlockSpec(memory_space=pltpu.VMEM)
    orders = m_table[None, :]
    cycles_row = cycle_table[None, :]
    spectrum_row = spectrum[None, :]
    table = legendre.transpose(0, 2, 1).reshape(per_block * cycles, multipoles)
    inputs = (
        cycles_row, orders, split_tiles(noise_var), split_tiles(mask_flags), spectrum_row, table,
        split_tiles(sky_data), split_tiles(signal_prev),
    )
    sources = groups * blocks * real_groups
    local = pl.pallas_call(
        functools.partial(forward_kernel, cycle_len, half_len, (cycles / total_l) ** 0.5, 1),
        out_shape=jax.ShapeDtypeStruct((sources * (reals + 2), LANES), jnp.bfloat16),
        in_specs=[hbm] * 8,
        out_specs=vmem,
        scratch_shapes=[pltpu.VMEM(x.shape, x.dtype) for x in inputs]
        + [pltpu.VMEM((cycles, LANES), jnp.float32), pltpu.SemaphoreType.DMA((8,))],
        compiler_params=pltpu.CompilerParams(vmem_limit_bytes=FORWARD_VMEM),
    )(*inputs)
    pairs = local.reshape(sources, reals // 2 + 1, 2, LANES)
    gathered = lax.all_to_all(pairs, AXES, 0, 0, tiled=True).reshape(local.shape)
    total_reals = reals * real_groups
    outputs = (
        jax.ShapeDtypeStruct((total_reals, 2, tiles // 2, 2 * per_block, LANES), jnp.float32),
        jax.ShapeDtypeStruct((reals * cycle_dev * half_len // LANES, LANES), jnp.float32),
    )
    wiener, signal = pl.pallas_call(
        functools.partial(backward_kernel, cycle_len, half_len, blocks, real_groups, reals, PARTS),
        out_shape=outputs,
        in_specs=[vmem] * 5,
        out_specs=(hbm, hbm),
        scratch_shapes=[pltpu.VMEM(x.shape, x.dtype) for x in outputs]
        + [pltpu.VMEM((blocks * total_reals, LANES), jnp.float32)]
        + [pltpu.SemaphoreType.DMA((real_groups + PARTS,))],
        compiler_params=pltpu.CompilerParams(vmem_limit_bytes=BACKWARD_VMEM),
    )(gathered, cycles_row, orders, table, spectrum_row)
    wiener = wiener.reshape(total_reals, 2, tiles, per_block, LANES).transpose(0, 1, 3, 2, 4)
    signal = signal.reshape(reals, half_len // LANES, cycle_dev, LANES).transpose(0, 2, 1, 3)
    return (
        wiener.reshape(total_reals, 2, per_block, multipoles),
        signal.reshape(sky_data.shape),
    )


def gram_form_fits(mesh, sky_data, m_table, legendre):
    groups, blocks, real_groups = (mesh.shape[name] for name in AXES)
    reals, cycles, cycle_len = sky_data.shape
    modes = m_table.shape[0]
    per_block = modes // blocks
    multipoles = legendre.shape[1] // (groups * real_groups)
    half_len = cycle_len // groups
    reals_dev = reals // real_groups
    return (
        cycles < 2 * reals
        and 4 * modes == LANES
        and cycles == 2 * blocks
        and all(size & (size - 1) == 0 for size in (blocks, modes, cycles, real_groups))
        and 2 * reals * cycles < 2**12
        and 2 * per_block * cycles == LANES
        and cycle_len & (cycle_len - 1) == 0
        and half_len % (4 * LANES) == 0
        and multipoles % (2 * LANES) == 0
        and per_block == 4
        and reals_dev % 16 == 0
        and reals_dev % PARTS == 0
        and cycles % 16 == 0
    )


def phase_tables(col_ids, mode_ids, cycle_len):
    product_ids = col_ids[:, None] * mode_ids[None, :] % cycle_len
    angles = product_ids.astype(jnp.float32) * (2.0 * math.pi / cycle_len)
    return (jnp.cos(angles).astype(jnp.bfloat16), jnp.sin(angles).astype(jnp.bfloat16))


def cycle_offsets(cycle_ids, mode_ids, cycle_len):
    parity = (cycle_ids % 2).astype(jnp.float32)
    shifts = math.pi / cycle_len * parity[:, None] * mode_ids[None, :].astype(jnp.float32)
    return (jnp.cos(shifts), jnp.sin(shifts))


def forward_modes(re_part, im_part):
    summed = lax.psum((re_part, im_part), "grp")
    fourier_pair = (summed[0].astype(jnp.bfloat16), summed[1].astype(jnp.bfloat16))
    fourier_pair = (
        lax.all_gather(fourier_pair[0], "real", axis=0, tiled=True),
        lax.all_gather(fourier_pair[1], "real", axis=0, tiled=True),
    )
    fourier_pair = (
        lax.all_to_all(fourier_pair[0], "blk", split_axis=2, concat_axis=1, tiled=True),
        lax.all_to_all(fourier_pair[1], "blk", split_axis=2, concat_axis=1, tiled=True),
    )
    return fourier_pair


def backward_cycles(partial_value):
    summed = lax.psum_scatter(partial_value, "real", scatter_dimension=0, tiled=True)
    reduced = lax.psum(summed, "grp")
    cycle_pair = lax.all_to_all(
        reduced.astype(jnp.bfloat16), "blk", split_axis=2, concat_axis=3, tiled=True
    )
    return cycle_pair


def per_device(
    sky_data, signal_prev, noise_var, mask_flags, cycle_table, m_table, spectrum, legendre
):
    real_dev, cycle_dev, half_len = sky_data.shape
    cycle_len = half_len * lax.axis_size("grp")
    mode_count = m_table.shape[0]
    col_ids = lax.axis_index("grp") * half_len + jnp.arange(half_len, dtype=jnp.int32)
    cos_tab, sin_tab = phase_tables(col_ids, m_table, cycle_len)
    cos_shift, sin_shift = cycle_offsets(cycle_table, m_table, cycle_len)
    weight = mask_flags.astype(jnp.float32) / (noise_var - 0.5)
    messenger = (weight * sky_data + 2.0 * signal_prev) / (weight + 2.0)
    flat_rows = messenger.astype(jnp.bfloat16).reshape(real_dev * cycle_dev, half_len)
    base_cos = jnp.dot(flat_rows, cos_tab, preferred_element_type=jnp.float32).reshape(
        real_dev, cycle_dev, mode_count
    )
    base_sin = -jnp.dot(flat_rows, sin_tab, preferred_element_type=jnp.float32).reshape(
        real_dev, cycle_dev, mode_count
    )
    norm_scale = cycle_len ** (-0.5)
    re_part = (base_cos * cos_shift + base_sin * sin_shift) * norm_scale
    im_part = (base_sin * cos_shift - base_cos * sin_shift) * norm_scale
    fourier_re, fourier_im = forward_modes(re_part, im_part)
    fourier = jnp.stack([fourier_re, fourier_im], 1)
    coefficients = jnp.einsum(
        "mlr,kcrm->kcml", legendre, fourier, preferred_element_type=jnp.float32
    )
    factor = spectrum / (spectrum + 0.5)
    wiener_alm = coefficients * factor
    total_l = legendre.shape[1] * lax.axis_size("grp") * lax.axis_size("real")
    syn_scale = (legendre.shape[2] / total_l) ** 0.5
    partial_value = (
        jnp.einsum(
            "mlr,kcml->kcrm",
            legendre,
            wiener_alm.astype(jnp.bfloat16),
            preferred_element_type=jnp.float32,
        )
        * syn_scale
    )
    cycle_pair = backward_cycles(partial_value)
    cycle_modes = cycle_pair.astype(jnp.float32)
    modes_re = cycle_modes[:, 0]
    modes_im = cycle_modes[:, 1]
    rotated_re = (modes_re * cos_shift - modes_im * sin_shift).astype(jnp.bfloat16)
    rotated_im = (modes_im * cos_shift + modes_re * sin_shift).astype(jnp.bfloat16)
    contract = (((1,), (1,)), ((), ()))
    pixel_sum = lax.dot_general(
        rotated_re.reshape(-1, mode_count), cos_tab, contract, preferred_element_type=jnp.float32
    )
    pixel_sum = pixel_sum - lax.dot_general(
        rotated_im.reshape(-1, mode_count), sin_tab, contract, preferred_element_type=jnp.float32
    )
    signal_next = (pixel_sum * mode_count ** (-0.5)).reshape(real_dev, cycle_dev, half_len)
    return (wiener_alm, signal_next)


def solution(mesh):
    in_specs = (
        P("real", "blk", "grp"),
        P("real", "blk", "grp"),
        P("blk", "grp"),
        P("blk", "grp"),
        P("blk"),
        P(),
        P(("grp", "real")),
        P("blk", ("grp", "real"), None),
    )
    out_specs = (P(None, None, "blk", ("grp", "real")), P("real", "blk", "grp"))

    def step(sky_data, signal_prev, noise_var, mask_flags, cycle_table, m_table, spectrum, legendre):
        fits = gram_form_fits(mesh, sky_data, m_table, legendre)
        return jax.shard_map(
            gram_program if fits else per_device,
            mesh=mesh,
            in_specs=in_specs,
            out_specs=out_specs,
            check_vma=False,
        )(sky_data, signal_prev, noise_var, mask_flags, cycle_table, m_table, spectrum, legendre)

    return step
```

```python
import functools
import math

import jax
import jax.numpy as jnp
from jax import lax
from jax.experimental import pallas as pl
from jax.experimental.pallas import tpu as pltpu
from jax.sharding import PartitionSpec as P

LANES = 128
NT = (((1,), (1,)), ((), ()))
AXES = ("grp", "blk", "real")
PARTS = 2
VMEM_LIMIT = 63_487_900


def unit_cosine(units, half_turn):
    wrapped = units & (2 * half_turn - 1)
    folded = jnp.minimum(wrapped, 2 * half_turn - wrapped)
    y = (half_turn // 2 - folded).astype(jnp.float32) * (math.pi / half_turn)
    y2 = y * y
    acc = jnp.full_like(y2, -1.0 / math.factorial(11))
    for order, sign in ((9, 1.0), (7, -1.0), (5, 1.0), (3, -1.0), (1, 1.0)):
        acc = acc * y2 + sign / math.factorial(order)
    return acc * y


def log2(size):
    return size.bit_length() - 1


def lane_ids(shape):
    return lax.broadcasted_iota(jnp.int32, shape, len(shape) - 1)


def row_ids(shape):
    return lax.broadcasted_iota(jnp.int32, shape, len(shape) - 2)


def phase_factors(cycles, orders, cycle_len, half_len, group):
    modes = orders.shape[1]
    orders = jnp.concatenate([orders] * (LANES // modes), axis=1)
    quarter = lane_ids((1, LANES)) >> log2(modes)
    quarter_turn = cycle_len // 2
    inner_units = 2 * orders * row_ids((LANES, LANES)) + ((quarter + 1) >> 1) * quarter_turn
    inner = unit_cosine(inner_units, cycle_len)
    rows = 2 * (half_len // LANES)
    row = row_ids((rows, LANES))
    parity = jnp.where((row & 1) == 0, cycles[:, :1], cycles[:, 1:]) & 1
    pixel = group * half_len + LANES * (row >> 1)
    outer_units = orders * (2 * pixel + parity) + (quarter >> 1) * (3 * quarter_turn)
    outer = unit_cosine(outer_units, cycle_len)
    high = inner.astype(jnp.bfloat16)
    low = (inner - high.astype(jnp.float32)).astype(jnp.bfloat16)
    return high, low, outer


def start_copies(sources, targets, sems, first=0):
    copies = [
        pltpu.make_async_copy(source, target, sems.at[first + i])
        for i, (source, target) in enumerate(zip(sources, targets))
    ]
    for copy in copies:
        copy.start()
    return copies


def row_parts(ref, parts):
    size = ref.shape[0] // parts
    return [ref.at[pl.ds(i * size, size)] for i in range(parts)]


def forward_kernel(
    cycle_len, half_len, syn_scale, parts,
    cycle_hbm, mode_hbm, noise_hbm, mask_hbm, spectrum_hbm, legendre_hbm, sky_hbm, prev_hbm, out_ref,
    cycle_ref, mode_ref, noise_ref, mask_ref, spectrum_ref, legendre_ref, sky_ref, prev_ref, gram_ref, sems,
):
    small = start_copies(
        (cycle_hbm, mode_hbm, noise_hbm, mask_hbm, spectrum_hbm, legendre_hbm),
        (cycle_ref, mode_ref, noise_ref, mask_ref, spectrum_ref, legendre_ref),
        sems,
    )
    sources = [part for pair in zip(row_parts(sky_hbm, parts), row_parts(prev_hbm, parts)) for part in pair]
    targets = [part for pair in zip(row_parts(sky_ref, parts), row_parts(prev_ref, parts)) for part in pair]
    large = start_copies(sources, targets, sems, len(small))
    group = lax.axis_index("grp")
    small[0].wait()
    small[1].wait()
    high, low, outer = phase_factors(cycle_ref[...], mode_ref[...], cycle_len, half_len, group)
    inner = jnp.concatenate([high, low], axis=0)
    small[2].wait()
    small[3].wait()
    weight = mask_ref[...].astype(jnp.float32) / (noise_ref[...] - 0.5)
    inverse = 1.0 / (weight + 2.0)
    sky_gain = weight * inverse
    prev_gain = 2.0 * inverse

    small[4].wait()
    small[5].wait()
    table = legendre_ref[...]
    spectrum = spectrum_ref[...]
    factor = spectrum / (spectrum + 0.5)
    filtered = (table.astype(jnp.float32) * factor).astype(jnp.bfloat16)
    gram = lax.dot_general(table, filtered, NT, preferred_element_type=jnp.float32)
    table_rows = table.shape[0]
    pixel_rows = outer.shape[0]
    reals = sky_ref.shape[0] // pixel_rows
    blocks, real_groups = lax.axis_size("blk"), lax.axis_size("real")
    cycles = 2 * blocks
    same = (row_ids(gram.shape) >> log2(cycles)) == (lane_ids((1, table_rows)) >> log2(cycles))
    gram = jnp.where(same, gram, 0.0).reshape(table_rows // cycles, cycles, table_rows).sum(axis=0)
    gram = gram * syn_scale
    gram_ref[...] = jnp.concatenate([gram, gram], axis=1)
    even, odd = gram_ref[pl.ds(0, blocks, stride=2), :], gram_ref[pl.ds(1, blocks, stride=2), :]
    gram = jnp.where(lane_ids(even.shape) < LANES // 2, even, odd)
    gram_high = gram.astype(jnp.bfloat16).astype(jnp.float32)
    gram_low = gram - gram_high

    part_reals = reals // parts
    shape = (part_reals, pixel_rows, LANES)
    fourier = []
    for i in range(parts):
        large[2 * i].wait()
        large[2 * i + 1].wait()
        span = pl.ds(i * part_reals * pixel_rows, part_reals * pixel_rows)
        sky = sky_ref[span, :].reshape(shape)
        prev = prev_ref[span, :].reshape(shape)
        rows = (sky * sky_gain + prev * prev_gain).reshape(-1, LANES).astype(jnp.bfloat16)
        partial = jnp.dot(
            jnp.concatenate([rows, rows], axis=1), inner, preferred_element_type=jnp.float32
        )
        turned = partial.reshape(shape) * outer
        summed = turned.reshape(part_reals, pixel_rows // 8, 8, LANES).sum(axis=1)
        summed = summed.reshape(part_reals * 8, LANES)
        summed = summed + pltpu.roll(summed, LANES // 2, 1)
        own = (row_ids(summed.shape) & 1) == (lane_ids(summed.shape) >= LANES // 2)
        fourier.append(jnp.where(own, summed, 0.0).reshape(part_reals, 8, LANES).sum(axis=1))
    fourier = jnp.concatenate(fourier, axis=0) * cycle_len**-0.5
    rows = []
    for b in range(blocks):
        rows += [fourier, gram_high[b : b + 1], gram_low[b : b + 1]] * real_groups
    rows = jnp.concatenate(rows, axis=0).astype(jnp.bfloat16)
    for g in range(lax.axis_size("grp")):
        out_ref[pl.ds(g * rows.shape[0], rows.shape[0]), :] = rows


def backward_kernel(
    cycle_len, half_len, blocks, real_groups, reals, parts,
    gathered_ref, legendre_hbm, spectrum_hbm, cycle_hbm, mode_hbm, wiener_hbm, signal_hbm,
    legendre_ref, spectrum_ref, cycle_ref, mode_ref, wiener_ref, signal_ref, fourier_ref, sems, out_sems,
):
    loads = start_copies(
        (legendre_hbm, spectrum_hbm, cycle_hbm, mode_hbm),
        (legendre_ref, spectrum_ref, cycle_ref, mode_ref),
        sems,
    )
    group = lax.axis_index("grp")
    block = lax.axis_index("blk")
    real_group = lax.axis_index("real")
    modes = mode_ref.shape[1]
    table_rows = legendre_ref.shape[0]
    per_block = modes // blocks
    cycles = table_rows // per_block
    half = LANES // 2
    lane = lane_ids((1, LANES))
    row = row_ids((LANES, LANES))
    lane_order = (lane & (half - 1)) >> log2(cycles)
    lane_row = (lane & 1) * half + (lane >> log2(half)) * modes + block * per_block + lane_order
    coeff_pick = (row == lane_row).astype(jnp.float32).astype(jnp.bfloat16)
    lane_row = (lane >> log2(half)) * per_block + (lane & (per_block - 1))
    gram_pick = ((row >> log2(cycles)) == lane_row).astype(jnp.float32).astype(jnp.bfloat16)
    holder = (lane & (modes - 1)) >> log2(per_block)
    lane_block = (lane & (cycles - 1)) >> 1

    total_reals = real_groups * reals
    fourier_rows = blocks * total_reals
    spacing = reals + 2
    column = lane_ids((1, gathered_ref.shape[0]))
    source = (column * (2**16 // spacing + 1)) >> 16
    inside = column - source * spacing
    source = source & (blocks * real_groups - 1)
    source_block = source >> log2(real_groups)
    target = ((source & (real_groups - 1)) * blocks + source_block) * reals + inside
    target = jnp.where(inside < reals, target, fourier_rows + source_block)
    place = (row_ids((fourier_rows + blocks, column.shape[1])) == target).astype(jnp.float32)
    placed = jnp.dot(place.astype(jnp.bfloat16), gathered_ref[...], preferred_element_type=jnp.float32)
    fourier_ref[...] = placed[:fourier_rows]

    coeff_rows = jnp.dot(
        placed[:fourier_rows].astype(jnp.bfloat16), coeff_pick, preferred_element_type=jnp.float32
    ).reshape(real_groups, blocks, reals, LANES)
    columns = jnp.zeros((total_reals, LANES), jnp.float32)
    for b in range(blocks):
        one = coeff_rows[:, b].reshape(total_reals, LANES)
        columns = columns + jnp.where(lane_block == b, one, 0.0)
    loads[0].wait()
    loads[1].wait()
    table = legendre_ref[...]
    table = jnp.concatenate([table, table], axis=0)
    spectrum = spectrum_ref[...]
    factor = spectrum / (spectrum + 0.5)
    stores = []
    own = (lane >> log2(cycles)) == row_ids((2 * per_block, LANES))
    upper = row_ids((1, 2 * per_block, LANES)) < per_block
    for y in range(real_groups):
        span = slice(y * reals, (y + 1) * reals)
        pieces = jnp.where(own, columns[span, None, :], 0.0)
        filtered = factor * jnp.dot(
            pieces.reshape(-1, LANES).astype(jnp.bfloat16), table, preferred_element_type=jnp.float32
        )
        for pair in range(wiener_ref.shape[2]):
            one, two = (
                filtered[:, tile * LANES : (tile + 1) * LANES].reshape(reals, 2 * per_block, LANES)
                for tile in (2 * pair, 2 * pair + 1)
            )
            wiener_ref[span, 0, pair] = jnp.where(upper, one, pltpu.roll(two, per_block, 1))
            wiener_ref[span, 1, pair] = jnp.where(upper, pltpu.roll(one, per_block, 1), two)
        span = pl.ds(y * reals, reals)
        stores += start_copies([wiener_ref.at[span]], [wiener_hbm.at[span]], out_sems, len(stores))

    gram_all = jnp.where(
        (lane & (cycles - 1)) == row_ids((cycles, LANES)), placed[fourier_rows:, None, :], 0.0
    ).reshape(blocks * cycles, LANES)
    gram_high = gram_all.astype(jnp.bfloat16)
    gram_low = (gram_all - gram_high.astype(jnp.float32)).astype(jnp.bfloat16)
    gram_rows = jnp.dot(
        jnp.concatenate([gram_high, gram_low], axis=1),
        jnp.concatenate([gram_pick, gram_pick], axis=0),
        preferred_element_type=jnp.float32,
    ).reshape(blocks, cycles, LANES)
    gram = jnp.zeros((cycles, LANES), jnp.float32)
    for b in range(blocks):
        gram = gram + jnp.where(holder == b, gram_rows[b], 0.0)

    first = lane < half
    cycle_modes = jnp.zeros((reals, LANES), jnp.float32)
    for b in range(blocks):
        first_row = pl.multiple_of((real_group * blocks + b) * reals, reals)
        pair = fourier_ref[pl.ds(first_row, reals), :]
        turned = pltpu.roll(pair, half, 1)
        cycle_modes = cycle_modes + jnp.where(first, pair, turned) * gram[2 * b : 2 * b + 1]
        cycle_modes = cycle_modes + jnp.where(first, turned, pair) * gram[2 * b + 1 : 2 * b + 2]
    cycle_modes = cycle_modes * modes**-0.5
    turned = pltpu.roll(cycle_modes, half, 1)
    even = jnp.where(first, cycle_modes, turned)
    odd = jnp.where(first, turned, cycle_modes)
    parity = (row_ids((1, 8, LANES)) & 1) == 0
    spread = jnp.where(parity, even[:, None, :], odd[:, None, :])
    loads[2].wait()
    loads[3].wait()
    high, low, outer = phase_factors(cycle_ref[...], mode_ref[...], cycle_len, half_len, group)
    pixel_rows = outer.shape[0]
    inner = jnp.concatenate([high, low], axis=1)
    outer = outer.reshape(1, pixel_rows // 8, 8, LANES)
    part_reals = reals // parts
    for i in range(parts):
        rotated = spread[i * part_reals : (i + 1) * part_reals, None] * outer
        rotated = rotated.reshape(part_reals * pixel_rows, LANES).astype(jnp.bfloat16)
        span = pl.ds(i * part_reals * pixel_rows, part_reals * pixel_rows)
        signal_ref[span, :] = lax.dot_general(
            jnp.concatenate([rotated, rotated], axis=1), inner, NT, preferred_element_type=jnp.float32
        )
        stores += start_copies([signal_ref.at[span]], [signal_hbm.at[span]], out_sems, len(stores))
    for store in stores:
        store.wait()


def split_tiles(array):
    lead, rows, columns = array.shape[:-2], array.shape[-2], array.shape[-1]
    split = array.reshape(*lead, rows, columns // LANES, LANES)
    return jnp.swapaxes(split, -2, -3).reshape(-1, LANES)


def gram_program(
    sky_data, signal_prev, noise_var, mask_flags, cycle_table, m_table, spectrum, legendre
):
    reals, cycle_dev, half_len = sky_data.shape
    groups, blocks, real_groups = (lax.axis_size(name) for name in AXES)
    cycle_len = half_len * groups
    per_block, multipoles, cycles = legendre.shape
    total_l = multipoles * groups * real_groups
    tiles = multipoles // LANES
    hbm = pl.BlockSpec(memory_space=pltpu.HBM)
    vmem = pl.BlockSpec(memory_space=pltpu.VMEM)
    orders = m_table[None, :]
    cycles_row = cycle_table[None, :]
    spectrum_row = spectrum[None, :]
    table = legendre.transpose(0, 2, 1).reshape(per_block * cycles, multipoles)
    inputs = (
        cycles_row, orders, split_tiles(noise_var), split_tiles(mask_flags), spectrum_row, table,
        split_tiles(sky_data), split_tiles(signal_prev),
    )
    sources = groups * blocks * real_groups
    local = pl.pallas_call(
        functools.partial(forward_kernel, cycle_len, half_len, (cycles / total_l) ** 0.5, 1),
        out_shape=jax.ShapeDtypeStruct((sources * (reals + 2), LANES), jnp.bfloat16),
        in_specs=[hbm] * 8,
        out_specs=vmem,
        scratch_shapes=[pltpu.VMEM(x.shape, x.dtype) for x in inputs]
        + [pltpu.VMEM((cycles, LANES), jnp.float32), pltpu.SemaphoreType.DMA((8,))],
        compiler_params=pltpu.CompilerParams(vmem_limit_bytes=VMEM_LIMIT),
    )(*inputs)
    pairs = local.reshape(sources, reals // 2 + 1, 2, LANES)
    gathered = lax.all_to_all(pairs, AXES, 0, 0, tiled=True).reshape(local.shape)
    total_reals = reals * real_groups
    inputs = (table, spectrum_row, cycles_row, orders)
    outputs = (
        jax.ShapeDtypeStruct((total_reals, 2, tiles // 2, 2 * per_block, LANES), jnp.float32),
        jax.ShapeDtypeStruct((reals * cycle_dev * half_len // LANES, LANES), jnp.float32),
    )
    wiener, signal = pl.pallas_call(
        functools.partial(backward_kernel, cycle_len, half_len, blocks, real_groups, reals, PARTS),
        out_shape=outputs,
        in_specs=[vmem] + [hbm] * 4,
        out_specs=(hbm, hbm),
        scratch_shapes=[pltpu.VMEM(x.shape, x.dtype) for x in inputs + outputs]
        + [pltpu.VMEM((blocks * total_reals, LANES), jnp.float32)]
        + [pltpu.SemaphoreType.DMA((4,)), pltpu.SemaphoreType.DMA((real_groups + PARTS,))],
        compiler_params=pltpu.CompilerParams(vmem_limit_bytes=VMEM_LIMIT),
    )(gathered, *inputs)
    wiener = wiener.reshape(total_reals, 2, tiles, per_block, LANES).transpose(0, 1, 3, 2, 4)
    signal = signal.reshape(reals, half_len // LANES, cycle_dev, LANES).transpose(0, 2, 1, 3)
    return (
        wiener.reshape(total_reals, 2, per_block, multipoles),
        signal.reshape(sky_data.shape),
    )


def gram_form_fits(mesh, sky_data, m_table, legendre):
    groups, blocks, real_groups = (mesh.shape[name] for name in AXES)
    reals, cycles, cycle_len = sky_data.shape
    modes = m_table.shape[0]
    per_block = modes // blocks
    multipoles = legendre.shape[1] // (groups * real_groups)
    half_len = cycle_len // groups
    reals_dev = reals // real_groups
    return (
        cycles < 2 * reals
        and 4 * modes == LANES
        and cycles == 2 * blocks
        and all(size & (size - 1) == 0 for size in (blocks, modes, cycles, real_groups))
        and 2 * reals * cycles < 2**12
        and 2 * per_block * cycles == LANES
        and cycle_len & (cycle_len - 1) == 0
        and half_len % (4 * LANES) == 0
        and multipoles % (2 * LANES) == 0
        and per_block == 4
        and reals_dev % 16 == 0
        and reals_dev % PARTS == 0
        and cycles % 16 == 0
    )


def phase_tables(col_ids, mode_ids, cycle_len):
    product_ids = col_ids[:, None] * mode_ids[None, :] % cycle_len
    angles = product_ids.astype(jnp.float32) * (2.0 * math.pi / cycle_len)
    return (jnp.cos(angles).astype(jnp.bfloat16), jnp.sin(angles).astype(jnp.bfloat16))


def cycle_offsets(cycle_ids, mode_ids, cycle_len):
    parity = (cycle_ids % 2).astype(jnp.float32)
    shifts = math.pi / cycle_len * parity[:, None] * mode_ids[None, :].astype(jnp.float32)
    return (jnp.cos(shifts), jnp.sin(shifts))


def forward_modes(re_part, im_part):
    summed = lax.psum((re_part, im_part), "grp")
    fourier_pair = (summed[0].astype(jnp.bfloat16), summed[1].astype(jnp.bfloat16))
    fourier_pair = (
        lax.all_gather(fourier_pair[0], "real", axis=0, tiled=True),
        lax.all_gather(fourier_pair[1], "real", axis=0, tiled=True),
    )
    fourier_pair = (
        lax.all_to_all(fourier_pair[0], "blk", split_axis=2, concat_axis=1, tiled=True),
        lax.all_to_all(fourier_pair[1], "blk", split_axis=2, concat_axis=1, tiled=True),
    )
    return fourier_pair


def backward_cycles(partial_value):
    summed = lax.psum_scatter(partial_value, "real", scatter_dimension=0, tiled=True)
    reduced = lax.psum(summed, "grp")
    cycle_pair = lax.all_to_all(
        reduced.astype(jnp.bfloat16), "blk", split_axis=2, concat_axis=3, tiled=True
    )
    return cycle_pair


def per_device(
    sky_data, signal_prev, noise_var, mask_flags, cycle_table, m_table, spectrum, legendre
):
    real_dev, cycle_dev, half_len = sky_data.shape
    cycle_len = half_len * lax.axis_size("grp")
    mode_count = m_table.shape[0]
    col_ids = lax.axis_index("grp") * half_len + jnp.arange(half_len, dtype=jnp.int32)
    cos_tab, sin_tab = phase_tables(col_ids, m_table, cycle_len)
    cos_shift, sin_shift = cycle_offsets(cycle_table, m_table, cycle_len)
    weight = mask_flags.astype(jnp.float32) / (noise_var - 0.5)
    messenger = (weight * sky_data + 2.0 * signal_prev) / (weight + 2.0)
    flat_rows = messenger.astype(jnp.bfloat16).reshape(real_dev * cycle_dev, half_len)
    base_cos = jnp.dot(flat_rows, cos_tab, preferred_element_type=jnp.float32).reshape(
        real_dev, cycle_dev, mode_count
    )
    base_sin = -jnp.dot(flat_rows, sin_tab, preferred_element_type=jnp.float32).reshape(
        real_dev, cycle_dev, mode_count
    )
    norm_scale = cycle_len ** (-0.5)
    re_part = (base_cos * cos_shift + base_sin * sin_shift) * norm_scale
    im_part = (base_sin * cos_shift - base_cos * sin_shift) * norm_scale
    fourier_re, fourier_im = forward_modes(re_part, im_part)
    fourier = jnp.stack([fourier_re, fourier_im], 1)
    coefficients = jnp.einsum(
        "mlr,kcrm->kcml", legendre, fourier, preferred_element_type=jnp.float32
    )
    factor = spectrum / (spectrum + 0.5)
    wiener_alm = coefficients * factor
    total_l = legendre.shape[1] * lax.axis_size("grp") * lax.axis_size("real")
    syn_scale = (legendre.shape[2] / total_l) ** 0.5
    partial_value = (
        jnp.einsum(
            "mlr,kcml->kcrm",
            legendre,
            wiener_alm.astype(jnp.bfloat16),
            preferred_element_type=jnp.float32,
        )
        * syn_scale
    )
    cycle_pair = backward_cycles(partial_value)
    cycle_modes = cycle_pair.astype(jnp.float32)
    modes_re = cycle_modes[:, 0]
    modes_im = cycle_modes[:, 1]
    rotated_re = (modes_re * cos_shift - modes_im * sin_shift).astype(jnp.bfloat16)
    rotated_im = (modes_im * cos_shift + modes_re * sin_shift).astype(jnp.bfloat16)
    contract = (((1,), (1,)), ((), ()))
    pixel_sum = lax.dot_general(
        rotated_re.reshape(-1, mode_count), cos_tab, contract, preferred_element_type=jnp.float32
    )
    pixel_sum = pixel_sum - lax.dot_general(
        rotated_im.reshape(-1, mode_count), sin_tab, contract, preferred_element_type=jnp.float32
    )
    signal_next = (pixel_sum * mode_count ** (-0.5)).reshape(real_dev, cycle_dev, half_len)
    return (wiener_alm, signal_next)


def solution(mesh):
    in_specs = (
        P("real", "blk", "grp"),
        P("real", "blk", "grp"),
        P("blk", "grp"),
        P("blk", "grp"),
        P("blk"),
        P(),
        P(("grp", "real")),
        P("blk", ("grp", "real"), None),
    )
    out_specs = (P(None, None, "blk", ("grp", "real")), P("real", "blk", "grp"))

    def step(sky_data, signal_prev, noise_var, mask_flags, cycle_table, m_table, spectrum, legendre):
        fits = gram_form_fits(mesh, sky_data, m_table, legendre)
        return jax.shard_map(
            gram_program if fits else per_device,
            mesh=mesh,
            in_specs=in_specs,
            out_specs=out_specs,
            check_vma=False,
        )(sky_data, signal_prev, noise_var, mask_flags, cycle_table, m_table, spectrum, legendre)

    return step
```

```python
import functools
import math

import jax
import jax.numpy as jnp
from jax import lax
from jax.experimental import pallas as pl
from jax.experimental.pallas import tpu as pltpu
from jax.sharding import PartitionSpec as P

LANES = 128
NT = (((1,), (1,)), ((), ()))
AXES = ("grp", "blk", "real")
PARTS = 2
FORWARD_VMEM = 63_290_000
BACKWARD_VMEM = 16 << 20


def unit_cosine(units, half_turn):
    wrapped = units & (2 * half_turn - 1)
    folded = jnp.minimum(wrapped, 2 * half_turn - wrapped)
    y = (half_turn // 2 - folded).astype(jnp.float32) * (math.pi / half_turn)
    y2 = y * y
    acc = jnp.full_like(y2, -1.0 / math.factorial(11))
    for order, sign in ((9, 1.0), (7, -1.0), (5, 1.0), (3, -1.0), (1, 1.0)):
        acc = acc * y2 + sign / math.factorial(order)
    return acc * y


def log2(size):
    return size.bit_length() - 1


def lane_ids(shape):
    return lax.broadcasted_iota(jnp.int32, shape, len(shape) - 1)


def row_ids(shape):
    return lax.broadcasted_iota(jnp.int32, shape, len(shape) - 2)


def phase_factors(cycles, orders, cycle_len, half_len, group):
    modes = orders.shape[1]
    orders = jnp.concatenate([orders] * (LANES // modes), axis=1)
    quarter = lane_ids((1, LANES)) >> log2(modes)
    quarter_turn = cycle_len // 2
    inner_units = 2 * orders * row_ids((LANES, LANES)) + ((quarter + 1) >> 1) * quarter_turn
    inner = unit_cosine(inner_units, cycle_len)
    rows = 2 * (half_len // LANES)
    row = row_ids((rows, LANES))
    parity = jnp.where((row & 1) == 0, cycles[:, :1], cycles[:, 1:]) & 1
    pixel = group * half_len + LANES * (row >> 1)
    outer_units = orders * (2 * pixel + parity) + (quarter >> 1) * (3 * quarter_turn)
    outer = unit_cosine(outer_units, cycle_len)
    high = inner.astype(jnp.bfloat16)
    low = (inner - high.astype(jnp.float32)).astype(jnp.bfloat16)
    return high, low, outer


def start_copies(sources, targets, sems, first=0):
    copies = [
        pltpu.make_async_copy(source, target, sems.at[first + i])
        for i, (source, target) in enumerate(zip(sources, targets))
    ]
    for copy in copies:
        copy.start()
    return copies


def row_parts(ref, parts):
    size = ref.shape[0] // parts
    return [ref.at[pl.ds(i * size, size)] for i in range(parts)]


def forward_kernel(
    cycle_len, half_len, syn_scale, parts,
    cycle_hbm, mode_hbm, noise_hbm, mask_hbm, spectrum_hbm, legendre_hbm, sky_hbm, prev_hbm, out_ref,
    cycle_ref, mode_ref, noise_ref, mask_ref, spectrum_ref, legendre_ref, sky_ref, prev_ref, gram_ref, sems,
):
    small = start_copies(
        (cycle_hbm, mode_hbm, noise_hbm, mask_hbm, spectrum_hbm, legendre_hbm),
        (cycle_ref, mode_ref, noise_ref, mask_ref, spectrum_ref, legendre_ref),
        sems,
    )
    sources = [part for pair in zip(row_parts(sky_hbm, parts), row_parts(prev_hbm, parts)) for part in pair]
    targets = [part for pair in zip(row_parts(sky_ref, parts), row_parts(prev_ref, parts)) for part in pair]
    large = start_copies(sources, targets, sems, len(small))
    group = lax.axis_index("grp")
    small[0].wait()
    small[1].wait()
    high, low, outer = phase_factors(cycle_ref[...], mode_ref[...], cycle_len, half_len, group)
    inner = jnp.concatenate([high, low], axis=0)
    small[2].wait()
    small[3].wait()
    weight = mask_ref[...].astype(jnp.float32) / (noise_ref[...] - 0.5)
    inverse = 1.0 / (weight + 2.0)
    sky_gain = weight * inverse
    prev_gain = 2.0 * inverse

    small[4].wait()
    small[5].wait()
    table = legendre_ref[...]
    spectrum = spectrum_ref[...]
    factor = spectrum / (spectrum + 0.5)
    filtered = (table.astype(jnp.float32) * factor).astype(jnp.bfloat16)
    gram = lax.dot_general(table, filtered, NT, preferred_element_type=jnp.float32)
    table_rows = table.shape[0]
    pixel_rows = outer.shape[0]
    reals = sky_ref.shape[0] // pixel_rows
    blocks, real_groups = lax.axis_size("blk"), lax.axis_size("real")
    cycles = 2 * blocks
    same = (row_ids(gram.shape) >> log2(cycles)) == (lane_ids((1, table_rows)) >> log2(cycles))
    gram = jnp.where(same, gram, 0.0).reshape(table_rows // cycles, cycles, table_rows).sum(axis=0)
    gram = gram * syn_scale
    gram_ref[...] = jnp.concatenate([gram, gram], axis=1)
    even, odd = gram_ref[pl.ds(0, blocks, stride=2), :], gram_ref[pl.ds(1, blocks, stride=2), :]
    gram = jnp.where(lane_ids(even.shape) < LANES // 2, even, odd)
    gram_high = gram.astype(jnp.bfloat16).astype(jnp.float32)
    gram_low = gram - gram_high

    part_reals = reals // parts
    shape = (part_reals, pixel_rows, LANES)
    fourier = []
    for i in range(parts):
        large[2 * i].wait()
        large[2 * i + 1].wait()
        span = pl.ds(i * part_reals * pixel_rows, part_reals * pixel_rows)
        sky = sky_ref[span, :].reshape(shape)
        prev = prev_ref[span, :].reshape(shape)
        rows = (sky * sky_gain + prev * prev_gain).reshape(-1, LANES).astype(jnp.bfloat16)
        partial = jnp.dot(
            jnp.concatenate([rows, rows], axis=1), inner, preferred_element_type=jnp.float32
        )
        turned = partial.reshape(shape) * outer
        summed = turned.reshape(part_reals, pixel_rows // 8, 8, LANES).sum(axis=1)
        summed = summed.reshape(part_reals * 8, LANES)
        summed = summed + pltpu.roll(summed, LANES // 2, 1)
        own = (row_ids(summed.shape) & 1) == (lane_ids(summed.shape) >= LANES // 2)
        fourier.append(jnp.where(own, summed, 0.0).reshape(part_reals, 8, LANES).sum(axis=1))
    fourier = jnp.concatenate(fourier, axis=0) * cycle_len**-0.5
    rows = []
    for b in range(blocks):
        rows += [fourier, gram_high[b : b + 1], gram_low[b : b + 1]] * real_groups
    rows = jnp.concatenate(rows, axis=0).astype(jnp.bfloat16)
    for g in range(lax.axis_size("grp")):
        out_ref[pl.ds(g * rows.shape[0], rows.shape[0]), :] = rows


def prepare_kernel(
    cycle_len, half_len, per_block, reals,
    cycle_ref, mode_ref, inner_ref, outer_ref, place_ref, pick_ref,
):
    group = lax.axis_index("grp")
    block = lax.axis_index("blk")
    blocks, real_groups = lax.axis_size("blk"), lax.axis_size("real")
    high, low, outer_ref[...] = phase_factors(cycle_ref[...], mode_ref[...], cycle_len, half_len, group)
    inner_ref[...] = jnp.concatenate([high, low], axis=1)
    modes, cycles, half = per_block * blocks, 2 * blocks, LANES // 2

    lane = lane_ids((1, LANES))
    row = row_ids((LANES, LANES))
    lane_order = (lane & (half - 1)) >> log2(cycles)
    lane_row = (lane & 1) * half + (lane >> log2(half)) * modes + block * per_block + lane_order
    pick_ref[0] = (row == lane_row).astype(jnp.float32).astype(jnp.bfloat16)
    lane_row = (lane >> log2(half)) * per_block + (lane & (per_block - 1))
    pick_ref[1] = ((row >> log2(cycles)) == lane_row).astype(jnp.float32).astype(jnp.bfloat16)

    spacing = reals + 2
    column = lane_ids((1, place_ref.shape[1]))
    source = (column * (2**16 // spacing + 1)) >> 16
    inside = column - source * spacing
    source = source & (blocks * real_groups - 1)
    source_block = source >> log2(real_groups)
    target = ((source & (real_groups - 1)) * blocks + source_block) * reals + inside
    target = jnp.where(inside < reals, target, blocks * real_groups * reals + source_block)
    place = (row_ids(place_ref.shape) == target).astype(jnp.float32)
    place_ref[...] = place.astype(jnp.bfloat16)


def backward_kernel(
    blocks, real_groups, reals, parts,
    gathered_ref, inner_ref, outer_ref, place_ref, pick_ref, legendre_ref, spectrum_ref,
    wiener_hbm, signal_hbm, wiener_ref, signal_ref, fourier_ref, out_sems,
):
    real_group = lax.axis_index("real")
    cycles = 2 * blocks
    per_block = legendre_ref.shape[0] // cycles
    modes = per_block * blocks
    pixel_rows = outer_ref.shape[0]
    half = LANES // 2
    lane = lane_ids((1, LANES))
    holder = (lane & (modes - 1)) >> log2(per_block)
    lane_block = (lane & (cycles - 1)) >> 1
    total_reals = real_groups * reals
    fourier_rows = blocks * total_reals
    placed = jnp.dot(place_ref[...], gathered_ref[...], preferred_element_type=jnp.float32)
    fourier_ref[...] = placed[:fourier_rows]

    coeff_rows = jnp.dot(
        placed[:fourier_rows].astype(jnp.bfloat16), pick_ref[0], preferred_element_type=jnp.float32
    ).reshape(real_groups, blocks, reals, LANES)
    columns = jnp.zeros((total_reals, LANES), jnp.float32)
    for b in range(blocks):
        one = coeff_rows[:, b].reshape(total_reals, LANES)
        columns = columns + jnp.where(lane_block == b, one, 0.0)
    table = legendre_ref[...]
    table = jnp.concatenate([table, table], axis=0)
    spectrum = spectrum_ref[...]
    factor = spectrum / (spectrum + 0.5)
    stores = []
    own = (lane >> log2(cycles)) == row_ids((2 * per_block, LANES))
    upper = row_ids((1, 2 * per_block, LANES)) < per_block
    for y in range(real_groups):
        span = slice(y * reals, (y + 1) * reals)
        pieces = jnp.where(own, columns[span, None, :], 0.0)
        filtered = factor * jnp.dot(
            pieces.reshape(-1, LANES).astype(jnp.bfloat16), table, preferred_element_type=jnp.float32
        )
        for pair in range(wiener_ref.shape[2]):
            one, two = (
                filtered[:, tile * LANES : (tile + 1) * LANES].reshape(reals, 2 * per_block, LANES)
                for tile in (2 * pair, 2 * pair + 1)
            )
            wiener_ref[span, 0, pair] = jnp.where(upper, one, pltpu.roll(two, per_block, 1))
            wiener_ref[span, 1, pair] = jnp.where(upper, pltpu.roll(one, per_block, 1), two)
        span = pl.ds(y * reals, reals)
        stores += start_copies([wiener_ref.at[span]], [wiener_hbm.at[span]], out_sems, len(stores))

    gram_all = jnp.where(
        (lane & (cycles - 1)) == row_ids((cycles, LANES)), placed[fourier_rows:, None, :], 0.0
    ).reshape(blocks * cycles, LANES)
    gram_high = gram_all.astype(jnp.bfloat16)
    gram_low = (gram_all - gram_high.astype(jnp.float32)).astype(jnp.bfloat16)
    gram_rows = jnp.dot(
        jnp.concatenate([gram_high, gram_low], axis=1),
        jnp.concatenate([pick_ref[1], pick_ref[1]], axis=0),
        preferred_element_type=jnp.float32,
    ).reshape(blocks, cycles, LANES)
    gram = jnp.zeros((cycles, LANES), jnp.float32)
    for b in range(blocks):
        gram = gram + jnp.where(holder == b, gram_rows[b], 0.0)

    first = lane < half
    cycle_modes = jnp.zeros((reals, LANES), jnp.float32)
    for b in range(blocks):
        first_row = pl.multiple_of((real_group * blocks + b) * reals, reals)
        pair = fourier_ref[pl.ds(first_row, reals), :]
        turned = pltpu.roll(pair, half, 1)
        cycle_modes = cycle_modes + jnp.where(first, pair, turned) * gram[2 * b : 2 * b + 1]
        cycle_modes = cycle_modes + jnp.where(first, turned, pair) * gram[2 * b + 1 : 2 * b + 2]
    cycle_modes = cycle_modes * modes**-0.5
    turned = pltpu.roll(cycle_modes, half, 1)
    even = jnp.where(first, cycle_modes, turned)
    odd = jnp.where(first, turned, cycle_modes)
    parity = (row_ids((1, 8, LANES)) & 1) == 0
    spread = jnp.where(parity, even[:, None, :], odd[:, None, :])
    inner = inner_ref[...]
    outer = outer_ref[...].reshape(1, pixel_rows // 8, 8, LANES)
    part_reals = reals // parts
    for i in range(parts):
        rotated = spread[i * part_reals : (i + 1) * part_reals, None] * outer
        rotated = rotated.reshape(part_reals * pixel_rows, LANES).astype(jnp.bfloat16)
        span = pl.ds(i * part_reals * pixel_rows, part_reals * pixel_rows)
        signal_ref[span, :] = lax.dot_general(
            jnp.concatenate([rotated, rotated], axis=1), inner, NT, preferred_element_type=jnp.float32
        )
        stores += start_copies([signal_ref.at[span]], [signal_hbm.at[span]], out_sems, len(stores))
    for store in stores:
        store.wait()


def split_tiles(array):
    lead, rows, columns = array.shape[:-2], array.shape[-2], array.shape[-1]
    split = array.reshape(*lead, rows, columns // LANES, LANES)
    return jnp.swapaxes(split, -2, -3).reshape(-1, LANES)


def gram_program(
    sky_data, signal_prev, noise_var, mask_flags, cycle_table, m_table, spectrum, legendre
):
    reals, cycle_dev, half_len = sky_data.shape
    groups, blocks, real_groups = (lax.axis_size(name) for name in AXES)
    cycle_len = half_len * groups
    per_block, multipoles, cycles = legendre.shape
    total_l = multipoles * groups * real_groups
    tiles = multipoles // LANES
    hbm = pl.BlockSpec(memory_space=pltpu.HBM)
    vmem = pl.BlockSpec(memory_space=pltpu.VMEM)
    orders = m_table[None, :]
    cycles_row = cycle_table[None, :]
    spectrum_row = spectrum[None, :]
    table = legendre.transpose(0, 2, 1).reshape(per_block * cycles, multipoles)
    inputs = (
        cycles_row, orders, split_tiles(noise_var), split_tiles(mask_flags), spectrum_row, table,
        split_tiles(sky_data), split_tiles(signal_prev),
    )
    sources = groups * blocks * real_groups
    local = pl.pallas_call(
        functools.partial(forward_kernel, cycle_len, half_len, (cycles / total_l) ** 0.5, 1),
        out_shape=jax.ShapeDtypeStruct((sources * (reals + 2), LANES), jnp.bfloat16),
        in_specs=[hbm] * 8,
        out_specs=vmem,
        scratch_shapes=[pltpu.VMEM(x.shape, x.dtype) for x in inputs]
        + [pltpu.VMEM((cycles, LANES), jnp.float32), pltpu.SemaphoreType.DMA((8,))],
        compiler_params=pltpu.CompilerParams(vmem_limit_bytes=FORWARD_VMEM),
    )(*inputs)
    pairs = local.reshape(sources, reals // 2 + 1, 2, LANES)
    gathered = lax.all_to_all(pairs, AXES, 0, 0, tiled=True).reshape(local.shape)
    total_reals = reals * real_groups
    prepared = pl.pallas_call(
        functools.partial(prepare_kernel, cycle_len, half_len, per_block, reals),
        out_shape=(
            jax.ShapeDtypeStruct((LANES, 2 * LANES), jnp.bfloat16),
            jax.ShapeDtypeStruct((cycle_dev * half_len // LANES, LANES), jnp.float32),
            jax.ShapeDtypeStruct((blocks * (total_reals + 1), local.shape[0]), jnp.bfloat16),
            jax.ShapeDtypeStruct((2, LANES, LANES), jnp.bfloat16),
        ),
        in_specs=[vmem] * 2,
        out_specs=(vmem,) * 4,
        compiler_params=pltpu.CompilerParams(vmem_limit_bytes=BACKWARD_VMEM),
        cost_estimate=pl.CostEstimate(flops=4_000_000, bytes_accessed=600_000, transcendentals=0),
    )(cycles_row, orders)
    outputs = (
        jax.ShapeDtypeStruct((total_reals, 2, tiles // 2, 2 * per_block, LANES), jnp.float32),
        jax.ShapeDtypeStruct((reals * cycle_dev * half_len // LANES, LANES), jnp.float32),
    )
    wiener, signal = pl.pallas_call(
        functools.partial(backward_kernel, blocks, real_groups, reals, PARTS),
        out_shape=outputs,
        in_specs=[vmem] * 7,
        out_specs=(hbm, hbm),
        scratch_shapes=[pltpu.VMEM(x.shape, x.dtype) for x in outputs]
        + [pltpu.VMEM((blocks * total_reals, LANES), jnp.float32)]
        + [pltpu.SemaphoreType.DMA((real_groups + PARTS,))],
        compiler_params=pltpu.CompilerParams(vmem_limit_bytes=BACKWARD_VMEM),
    )(gathered, *prepared, table, spectrum_row)
    wiener = wiener.reshape(total_reals, 2, tiles, per_block, LANES).transpose(0, 1, 3, 2, 4)
    signal = signal.reshape(reals, half_len // LANES, cycle_dev, LANES).transpose(0, 2, 1, 3)
    return (
        wiener.reshape(total_reals, 2, per_block, multipoles),
        signal.reshape(sky_data.shape),
    )


def gram_form_fits(mesh, sky_data, m_table, legendre):
    groups, blocks, real_groups = (mesh.shape[name] for name in AXES)
    reals, cycles, cycle_len = sky_data.shape
    modes = m_table.shape[0]
    per_block = modes // blocks
    multipoles = legendre.shape[1] // (groups * real_groups)
    half_len = cycle_len // groups
    reals_dev = reals // real_groups
    return (
        cycles < 2 * reals
        and 4 * modes == LANES
        and cycles == 2 * blocks
        and all(size & (size - 1) == 0 for size in (blocks, modes, cycles, real_groups))
        and 2 * reals * cycles < 2**12
        and 2 * per_block * cycles == LANES
        and cycle_len & (cycle_len - 1) == 0
        and half_len % (4 * LANES) == 0
        and multipoles % (2 * LANES) == 0
        and per_block == 4
        and reals_dev % 16 == 0
        and reals_dev % PARTS == 0
        and cycles % 16 == 0
    )


def phase_tables(col_ids, mode_ids, cycle_len):
    product_ids = col_ids[:, None] * mode_ids[None, :] % cycle_len
    angles = product_ids.astype(jnp.float32) * (2.0 * math.pi / cycle_len)
    return (jnp.cos(angles).astype(jnp.bfloat16), jnp.sin(angles).astype(jnp.bfloat16))


def cycle_offsets(cycle_ids, mode_ids, cycle_len):
    parity = (cycle_ids % 2).astype(jnp.float32)
    shifts = math.pi / cycle_len * parity[:, None] * mode_ids[None, :].astype(jnp.float32)
    return (jnp.cos(shifts), jnp.sin(shifts))


def forward_modes(re_part, im_part):
    summed = lax.psum((re_part, im_part), "grp")
    fourier_pair = (summed[0].astype(jnp.bfloat16), summed[1].astype(jnp.bfloat16))
    fourier_pair = (
        lax.all_gather(fourier_pair[0], "real", axis=0, tiled=True),
        lax.all_gather(fourier_pair[1], "real", axis=0, tiled=True),
    )
    fourier_pair = (
        lax.all_to_all(fourier_pair[0], "blk", split_axis=2, concat_axis=1, tiled=True),
        lax.all_to_all(fourier_pair[1], "blk", split_axis=2, concat_axis=1, tiled=True),
    )
    return fourier_pair


def backward_cycles(partial_value):
    summed = lax.psum_scatter(partial_value, "real", scatter_dimension=0, tiled=True)
    reduced = lax.psum(summed, "grp")
    cycle_pair = lax.all_to_all(
        reduced.astype(jnp.bfloat16), "blk", split_axis=2, concat_axis=3, tiled=True
    )
    return cycle_pair


def per_device(
    sky_data, signal_prev, noise_var, mask_flags, cycle_table, m_table, spectrum, legendre
):
    real_dev, cycle_dev, half_len = sky_data.shape
    cycle_len = half_len * lax.axis_size("grp")
    mode_count = m_table.shape[0]
    col_ids = lax.axis_index("grp") * half_len + jnp.arange(half_len, dtype=jnp.int32)
    cos_tab, sin_tab = phase_tables(col_ids, m_table, cycle_len)
    cos_shift, sin_shift = cycle_offsets(cycle_table, m_table, cycle_len)
    weight = mask_flags.astype(jnp.float32) / (noise_var - 0.5)
    messenger = (weight * sky_data + 2.0 * signal_prev) / (weight + 2.0)
    flat_rows = messenger.astype(jnp.bfloat16).reshape(real_dev * cycle_dev, half_len)
    base_cos = jnp.dot(flat_rows, cos_tab, preferred_element_type=jnp.float32).reshape(
        real_dev, cycle_dev, mode_count
    )
    base_sin = -jnp.dot(flat_rows, sin_tab, preferred_element_type=jnp.float32).reshape(
        real_dev, cycle_dev, mode_count
    )
    norm_scale = cycle_len ** (-0.5)
    re_part = (base_cos * cos_shift + base_sin * sin_shift) * norm_scale
    im_part = (base_sin * cos_shift - base_cos * sin_shift) * norm_scale
    fourier_re, fourier_im = forward_modes(re_part, im_part)
    fourier = jnp.stack([fourier_re, fourier_im], 1)
    coefficients = jnp.einsum(
        "mlr,kcrm->kcml", legendre, fourier, preferred_element_type=jnp.float32
    )
    factor = spectrum / (spectrum + 0.5)
    wiener_alm = coefficients * factor
    total_l = legendre.shape[1] * lax.axis_size("grp") * lax.axis_size("real")
    syn_scale = (legendre.shape[2] / total_l) ** 0.5
    partial_value = (
        jnp.einsum(
            "mlr,kcml->kcrm",
            legendre,
            wiener_alm.astype(jnp.bfloat16),
            preferred_element_type=jnp.float32,
        )
        * syn_scale
    )
    cycle_pair = backward_cycles(partial_value)
    cycle_modes = cycle_pair.astype(jnp.float32)
    modes_re = cycle_modes[:, 0]
    modes_im = cycle_modes[:, 1]
    rotated_re = (modes_re * cos_shift - modes_im * sin_shift).astype(jnp.bfloat16)
    rotated_im = (modes_im * cos_shift + modes_re * sin_shift).astype(jnp.bfloat16)
    contract = (((1,), (1,)), ((), ()))
    pixel_sum = lax.dot_general(
        rotated_re.reshape(-1, mode_count), cos_tab, contract, preferred_element_type=jnp.float32
    )
    pixel_sum = pixel_sum - lax.dot_general(
        rotated_im.reshape(-1, mode_count), sin_tab, contract, preferred_element_type=jnp.float32
    )
    signal_next = (pixel_sum * mode_count ** (-0.5)).reshape(real_dev, cycle_dev, half_len)
    return (wiener_alm, signal_next)


def solution(mesh):
    in_specs = (
        P("real", "blk", "grp"),
        P("real", "blk", "grp"),
        P("blk", "grp"),
        P("blk", "grp"),
        P("blk"),
        P(),
        P(("grp", "real")),
        P("blk", ("grp", "real"), None),
    )
    out_specs = (P(None, None, "blk", ("grp", "real")), P("real", "blk", "grp"))

    def step(sky_data, signal_prev, noise_var, mask_flags, cycle_table, m_table, spectrum, legendre):
        fits = gram_form_fits(mesh, sky_data, m_table, legendre)
        return jax.shard_map(
            gram_program if fits else per_device,
            mesh=mesh,
            in_specs=in_specs,
            out_specs=out_specs,
            check_vma=False,
        )(sky_data, signal_prev, noise_var, mask_flags, cycle_table, m_table, spectrum, legendre)

    return step
```

```python
import functools
import math

import jax
import jax.numpy as jnp
from jax import lax
from jax.experimental import pallas as pl
from jax.experimental.pallas import tpu as pltpu
from jax.sharding import PartitionSpec as P

LANES = 128
NT = (((1,), (1,)), ((), ()))
AXES = ("grp", "blk", "real")
PARTS = 2
FORWARD_VMEM = 63_150_000
BACKWARD_VMEM = 16 << 20


def unit_cosine(units, half_turn):
    wrapped = units & (2 * half_turn - 1)
    folded = jnp.minimum(wrapped, 2 * half_turn - wrapped)
    y = (half_turn // 2 - folded).astype(jnp.float32) * (math.pi / half_turn)
    y2 = y * y
    acc = jnp.full_like(y2, -1.0 / math.factorial(11))
    for order, sign in ((9, 1.0), (7, -1.0), (5, 1.0), (3, -1.0), (1, 1.0)):
        acc = acc * y2 + sign / math.factorial(order)
    return acc * y


def log2(size):
    return size.bit_length() - 1


def lane_ids(shape):
    return lax.broadcasted_iota(jnp.int32, shape, len(shape) - 1)


def row_ids(shape):
    return lax.broadcasted_iota(jnp.int32, shape, len(shape) - 2)


def phase_factors(cycles, orders, cycle_len, half_len, group):
    modes = orders.shape[1]
    orders = jnp.concatenate([orders] * (LANES // modes), axis=1)
    quarter = lane_ids((1, LANES)) >> log2(modes)
    quarter_turn = cycle_len // 2
    inner_units = 2 * orders * row_ids((LANES, LANES)) + ((quarter + 1) >> 1) * quarter_turn
    inner = unit_cosine(inner_units, cycle_len)
    rows = 2 * (half_len // LANES)
    row = row_ids((rows, LANES))
    parity = jnp.where((row & 1) == 0, cycles[:, :1], cycles[:, 1:]) & 1
    pixel = group * half_len + LANES * (row >> 1)
    outer_units = orders * (2 * pixel + parity) + (quarter >> 1) * (3 * quarter_turn)
    outer = unit_cosine(outer_units, cycle_len)
    high = inner.astype(jnp.bfloat16)
    low = (inner - high.astype(jnp.float32)).astype(jnp.bfloat16)
    return high, low, outer


def start_copies(sources, targets, sems, first=0):
    copies = [
        pltpu.make_async_copy(source, target, sems.at[first + i])
        for i, (source, target) in enumerate(zip(sources, targets))
    ]
    for copy in copies:
        copy.start()
    return copies


def row_parts(ref, parts):
    size = ref.shape[0] // parts
    return [ref.at[pl.ds(i * size, size)] for i in range(parts)]


def forward_kernel(
    cycle_len, half_len, syn_scale, parts,
    cycle_hbm, mode_hbm, noise_hbm, mask_hbm, spectrum_hbm, legendre_hbm, sky_hbm, prev_hbm, out_ref,
    cycle_ref, mode_ref, noise_ref, mask_ref, spectrum_ref, legendre_ref, sky_ref, prev_ref, gram_ref, sems,
):
    small = start_copies(
        (cycle_hbm, mode_hbm, noise_hbm, mask_hbm, spectrum_hbm, legendre_hbm),
        (cycle_ref, mode_ref, noise_ref, mask_ref, spectrum_ref, legendre_ref),
        sems,
    )
    sources = [part for pair in zip(row_parts(sky_hbm, parts), row_parts(prev_hbm, parts)) for part in pair]
    targets = [part for pair in zip(row_parts(sky_ref, parts), row_parts(prev_ref, parts)) for part in pair]
    large = start_copies(sources, targets, sems, len(small))
    group = lax.axis_index("grp")
    small[0].wait()
    small[1].wait()
    high, low, outer = phase_factors(cycle_ref[...], mode_ref[...], cycle_len, half_len, group)
    inner = jnp.concatenate([high, low], axis=0)
    small[2].wait()
    small[3].wait()
    weight = mask_ref[...].astype(jnp.float32) / (noise_ref[...] - 0.5)
    inverse = 1.0 / (weight + 2.0)
    sky_gain = weight * inverse
    prev_gain = 2.0 * inverse

    small[4].wait()
    small[5].wait()
    table = legendre_ref[...]
    spectrum = spectrum_ref[...]
    factor = spectrum / (spectrum + 0.5)
    filtered = (table.astype(jnp.float32) * factor).astype(jnp.bfloat16)
    gram = lax.dot_general(table, filtered, NT, preferred_element_type=jnp.float32)
    table_rows = table.shape[0]
    pixel_rows = outer.shape[0]
    reals = sky_ref.shape[0] // pixel_rows
    blocks, real_groups = lax.axis_size("blk"), lax.axis_size("real")
    cycles = 2 * blocks
    same = (row_ids(gram.shape) >> log2(cycles)) == (lane_ids((1, table_rows)) >> log2(cycles))
    gram = jnp.where(same, gram, 0.0).reshape(table_rows // cycles, cycles, table_rows).sum(axis=0)
    gram = gram * syn_scale
    gram_ref[...] = jnp.concatenate([gram, gram], axis=1)
    even, odd = gram_ref[pl.ds(0, blocks, stride=2), :], gram_ref[pl.ds(1, blocks, stride=2), :]
    gram = jnp.where(lane_ids(even.shape) < LANES // 2, even, odd)
    gram_high = gram.astype(jnp.bfloat16).astype(jnp.float32)
    gram_low = gram - gram_high

    part_reals = reals // parts
    shape = (part_reals, pixel_rows, LANES)
    fourier = []
    for i in range(parts):
        large[2 * i].wait()
        large[2 * i + 1].wait()
        span = pl.ds(i * part_reals * pixel_rows, part_reals * pixel_rows)
        sky = sky_ref[span, :].reshape(shape)
        prev = prev_ref[span, :].reshape(shape)
        rows = (sky * sky_gain + prev * prev_gain).reshape(-1, LANES).astype(jnp.bfloat16)
        partial = jnp.dot(
            jnp.concatenate([rows, rows], axis=1), inner, preferred_element_type=jnp.float32
        )
        turned = partial.reshape(shape) * outer
        summed = turned.reshape(part_reals, pixel_rows // 8, 8, LANES).sum(axis=1)
        summed = summed.reshape(part_reals * 8, LANES)
        summed = summed + pltpu.roll(summed, LANES // 2, 1)
        own = (row_ids(summed.shape) & 1) == (lane_ids(summed.shape) >= LANES // 2)
        fourier.append(jnp.where(own, summed, 0.0).reshape(part_reals, 8, LANES).sum(axis=1))
    fourier = jnp.concatenate(fourier, axis=0) * cycle_len**-0.5
    rows = []
    for b in range(blocks):
        rows += [fourier, gram_high[b : b + 1], gram_low[b : b + 1]] * real_groups
    rows = jnp.concatenate(rows, axis=0).astype(jnp.bfloat16)
    for g in range(lax.axis_size("grp")):
        out_ref[pl.ds(g * rows.shape[0], rows.shape[0]), :] = rows


def prepare_kernel(
    cycle_len, half_len, per_block, reals,
    cycle_ref, mode_ref, legendre_ref, spectrum_ref,
    inner_ref, outer_ref, place_ref, pick_ref, table_ref, factor_ref,
):
    table = legendre_ref[...]
    table_ref[...] = jnp.concatenate([table, table], axis=0)
    spectrum = spectrum_ref[...]
    factor_ref[...] = spectrum / (spectrum + 0.5)
    group = lax.axis_index("grp")
    block = lax.axis_index("blk")
    blocks, real_groups = lax.axis_size("blk"), lax.axis_size("real")
    high, low, outer_ref[...] = phase_factors(cycle_ref[...], mode_ref[...], cycle_len, half_len, group)
    inner_ref[...] = jnp.concatenate([high, low], axis=1)
    modes, cycles, half = per_block * blocks, 2 * blocks, LANES // 2

    lane = lane_ids((1, LANES))
    row = row_ids((LANES, LANES))
    lane_order = (lane & (half - 1)) >> log2(cycles)
    lane_row = (lane & 1) * half + (lane >> log2(half)) * modes + block * per_block + lane_order
    pick_ref[0] = (row == lane_row).astype(jnp.float32).astype(jnp.bfloat16)
    lane_row = (lane >> log2(half)) * per_block + (lane & (per_block - 1))
    pick_ref[1] = ((row >> log2(cycles)) == lane_row).astype(jnp.float32).astype(jnp.bfloat16)

    spacing = reals + 2
    column = lane_ids((1, place_ref.shape[1]))
    source = (column * (2**16 // spacing + 1)) >> 16
    inside = column - source * spacing
    source = source & (blocks * real_groups - 1)
    source_block = source >> log2(real_groups)
    target = ((source & (real_groups - 1)) * blocks + source_block) * reals + inside
    target = jnp.where(inside < reals, target, blocks * real_groups * reals + source_block)
    place = (row_ids(place_ref.shape) == target).astype(jnp.float32)
    place_ref[...] = place.astype(jnp.bfloat16)


def backward_kernel(
    blocks, real_groups, reals, parts,
    gathered_ref, inner_ref, outer_ref, place_ref, pick_ref, table_ref, factor_ref,
    wiener_hbm, signal_hbm, wiener_ref, signal_ref, fourier_ref, out_sems,
):
    real_group = lax.axis_index("real")
    cycles = 2 * blocks
    per_block = table_ref.shape[0] // (2 * cycles)
    modes = per_block * blocks
    pixel_rows = outer_ref.shape[0]
    half = LANES // 2
    lane = lane_ids((1, LANES))
    holder = (lane & (modes - 1)) >> log2(per_block)
    lane_block = (lane & (cycles - 1)) >> 1
    total_reals = real_groups * reals
    fourier_rows = blocks * total_reals
    placed = jnp.dot(place_ref[...], gathered_ref[...], preferred_element_type=jnp.float32)
    fourier_ref[...] = placed[:fourier_rows]

    coeff_rows = jnp.dot(
        placed[:fourier_rows].astype(jnp.bfloat16), pick_ref[0], preferred_element_type=jnp.float32
    ).reshape(real_groups, blocks, reals, LANES)
    columns = jnp.zeros((total_reals, LANES), jnp.float32)
    for b in range(blocks):
        one = coeff_rows[:, b].reshape(total_reals, LANES)
        columns = columns + jnp.where(lane_block == b, one, 0.0)
    table = table_ref[...]
    factor = factor_ref[...]
    stores = []
    own = (lane >> log2(cycles)) == row_ids((2 * per_block, LANES))
    upper = row_ids((1, 2 * per_block, LANES)) < per_block
    for y in range(real_groups):
        span = slice(y * reals, (y + 1) * reals)
        pieces = jnp.where(own, columns[span, None, :], 0.0)
        filtered = factor * jnp.dot(
            pieces.reshape(-1, LANES).astype(jnp.bfloat16), table, preferred_element_type=jnp.float32
        )
        for pair in range(wiener_ref.shape[2]):
            one, two = (
                filtered[:, tile * LANES : (tile + 1) * LANES].reshape(reals, 2 * per_block, LANES)
                for tile in (2 * pair, 2 * pair + 1)
            )
            wiener_ref[span, 0, pair] = jnp.where(upper, one, pltpu.roll(two, per_block, 1))
            wiener_ref[span, 1, pair] = jnp.where(upper, pltpu.roll(one, per_block, 1), two)
        span = pl.ds(y * reals, reals)
        stores += start_copies([wiener_ref.at[span]], [wiener_hbm.at[span]], out_sems, len(stores))

    gram_all = jnp.where(
        (lane & (cycles - 1)) == row_ids((cycles, LANES)), placed[fourier_rows:, None, :], 0.0
    ).reshape(blocks * cycles, LANES)
    gram_high = gram_all.astype(jnp.bfloat16)
    gram_low = (gram_all - gram_high.astype(jnp.float32)).astype(jnp.bfloat16)
    gram_rows = jnp.dot(
        jnp.concatenate([gram_high, gram_low], axis=1),
        jnp.concatenate([pick_ref[1], pick_ref[1]], axis=0),
        preferred_element_type=jnp.float32,
    ).reshape(blocks, cycles, LANES)
    gram = jnp.zeros((cycles, LANES), jnp.float32)
    for b in range(blocks):
        gram = gram + jnp.where(holder == b, gram_rows[b], 0.0)

    first = lane < half
    cycle_modes = jnp.zeros((reals, LANES), jnp.float32)
    for b in range(blocks):
        first_row = pl.multiple_of((real_group * blocks + b) * reals, reals)
        pair = fourier_ref[pl.ds(first_row, reals), :]
        turned = pltpu.roll(pair, half, 1)
        cycle_modes = cycle_modes + jnp.where(first, pair, turned) * gram[2 * b : 2 * b + 1]
        cycle_modes = cycle_modes + jnp.where(first, turned, pair) * gram[2 * b + 1 : 2 * b + 2]
    cycle_modes = cycle_modes * modes**-0.5
    turned = pltpu.roll(cycle_modes, half, 1)
    even = jnp.where(first, cycle_modes, turned)
    odd = jnp.where(first, turned, cycle_modes)
    parity = (row_ids((1, 8, LANES)) & 1) == 0
    spread = jnp.where(parity, even[:, None, :], odd[:, None, :])
    inner = inner_ref[...]
    outer = outer_ref[...].reshape(1, pixel_rows // 8, 8, LANES)
    part_reals = reals // parts
    for i in range(parts):
        rotated = spread[i * part_reals : (i + 1) * part_reals, None] * outer
        rotated = rotated.reshape(part_reals * pixel_rows, LANES).astype(jnp.bfloat16)
        span = pl.ds(i * part_reals * pixel_rows, part_reals * pixel_rows)
        signal_ref[span, :] = lax.dot_general(
            jnp.concatenate([rotated, rotated], axis=1), inner, NT, preferred_element_type=jnp.float32
        )
        stores += start_copies([signal_ref.at[span]], [signal_hbm.at[span]], out_sems, len(stores))
    for store in stores:
        store.wait()


def split_tiles(array):
    lead, rows, columns = array.shape[:-2], array.shape[-2], array.shape[-1]
    split = array.reshape(*lead, rows, columns // LANES, LANES)
    return jnp.swapaxes(split, -2, -3).reshape(-1, LANES)


def gram_program(
    sky_data, signal_prev, noise_var, mask_flags, cycle_table, m_table, spectrum, legendre
):
    reals, cycle_dev, half_len = sky_data.shape
    groups, blocks, real_groups = (lax.axis_size(name) for name in AXES)
    cycle_len = half_len * groups
    per_block, multipoles, cycles = legendre.shape
    total_l = multipoles * groups * real_groups
    tiles = multipoles // LANES
    hbm = pl.BlockSpec(memory_space=pltpu.HBM)
    vmem = pl.BlockSpec(memory_space=pltpu.VMEM)
    orders = m_table[None, :]
    cycles_row = cycle_table[None, :]
    spectrum_row = spectrum[None, :]
    table = legendre.transpose(0, 2, 1).reshape(per_block * cycles, multipoles)
    inputs = (
        cycles_row, orders, split_tiles(noise_var), split_tiles(mask_flags), spectrum_row, table,
        split_tiles(sky_data), split_tiles(signal_prev),
    )
    sources = groups * blocks * real_groups
    local = pl.pallas_call(
        functools.partial(forward_kernel, cycle_len, half_len, (cycles / total_l) ** 0.5, 1),
        out_shape=jax.ShapeDtypeStruct((sources * (reals + 2), LANES), jnp.bfloat16),
        in_specs=[hbm] * 8,
        out_specs=vmem,
        scratch_shapes=[pltpu.VMEM(x.shape, x.dtype) for x in inputs]
        + [pltpu.VMEM((cycles, LANES), jnp.float32), pltpu.SemaphoreType.DMA((8,))],
        compiler_params=pltpu.CompilerParams(vmem_limit_bytes=FORWARD_VMEM),
    )(*inputs)
    pairs = local.reshape(sources, reals // 2 + 1, 2, LANES)
    gathered = lax.all_to_all(pairs, AXES, 0, 0, tiled=True).reshape(local.shape)
    total_reals = reals * real_groups
    prepared = pl.pallas_call(
        functools.partial(prepare_kernel, cycle_len, half_len, per_block, reals),
        out_shape=(
            jax.ShapeDtypeStruct((LANES, 2 * LANES), jnp.bfloat16),
            jax.ShapeDtypeStruct((cycle_dev * half_len // LANES, LANES), jnp.float32),
            jax.ShapeDtypeStruct((blocks * (total_reals + 1), local.shape[0]), jnp.bfloat16),
            jax.ShapeDtypeStruct((2, LANES, LANES), jnp.bfloat16),
            jax.ShapeDtypeStruct((2 * table.shape[0], multipoles), jnp.bfloat16),
            jax.ShapeDtypeStruct((1, multipoles), jnp.float32),
        ),
        in_specs=[vmem] * 4,
        out_specs=(vmem,) * 6,
        compiler_params=pltpu.CompilerParams(vmem_limit_bytes=BACKWARD_VMEM),
        cost_estimate=pl.CostEstimate(flops=4_000_000, bytes_accessed=600_000, transcendentals=0),
    )(cycles_row, orders, table, spectrum_row)
    outputs = (
        jax.ShapeDtypeStruct((total_reals, 2, tiles // 2, 2 * per_block, LANES), jnp.float32),
        jax.ShapeDtypeStruct((reals * cycle_dev * half_len // LANES, LANES), jnp.float32),
    )
    wiener, signal = pl.pallas_call(
        functools.partial(backward_kernel, blocks, real_groups, reals, PARTS),
        out_shape=outputs,
        in_specs=[vmem] * 7,
        out_specs=(hbm, hbm),
        scratch_shapes=[pltpu.VMEM(x.shape, x.dtype) for x in outputs]
        + [pltpu.VMEM((blocks * total_reals, LANES), jnp.float32)]
        + [pltpu.SemaphoreType.DMA((real_groups + PARTS,))],
        compiler_params=pltpu.CompilerParams(vmem_limit_bytes=BACKWARD_VMEM),
    )(gathered, *prepared)
    wiener = wiener.reshape(total_reals, 2, tiles, per_block, LANES).transpose(0, 1, 3, 2, 4)
    signal = signal.reshape(reals, half_len // LANES, cycle_dev, LANES).transpose(0, 2, 1, 3)
    return (
        wiener.reshape(total_reals, 2, per_block, multipoles),
        signal.reshape(sky_data.shape),
    )


def gram_form_fits(mesh, sky_data, m_table, legendre):
    groups, blocks, real_groups = (mesh.shape[name] for name in AXES)
    reals, cycles, cycle_len = sky_data.shape
    modes = m_table.shape[0]
    per_block = modes // blocks
    multipoles = legendre.shape[1] // (groups * real_groups)
    half_len = cycle_len // groups
    reals_dev = reals // real_groups
    return (
        cycles < 2 * reals
        and 4 * modes == LANES
        and cycles == 2 * blocks
        and all(size & (size - 1) == 0 for size in (blocks, modes, cycles, real_groups))
        and 2 * reals * cycles < 2**12
        and 2 * per_block * cycles == LANES
        and cycle_len & (cycle_len - 1) == 0
        and half_len % (4 * LANES) == 0
        and multipoles % (2 * LANES) == 0
        and per_block == 4
        and reals_dev % 16 == 0
        and reals_dev % PARTS == 0
        and cycles % 16 == 0
    )


def phase_tables(col_ids, mode_ids, cycle_len):
    product_ids = col_ids[:, None] * mode_ids[None, :] % cycle_len
    angles = product_ids.astype(jnp.float32) * (2.0 * math.pi / cycle_len)
    return (jnp.cos(angles).astype(jnp.bfloat16), jnp.sin(angles).astype(jnp.bfloat16))


def cycle_offsets(cycle_ids, mode_ids, cycle_len):
    parity = (cycle_ids % 2).astype(jnp.float32)
    shifts = math.pi / cycle_len * parity[:, None] * mode_ids[None, :].astype(jnp.float32)
    return (jnp.cos(shifts), jnp.sin(shifts))


def forward_modes(re_part, im_part):
    summed = lax.psum((re_part, im_part), "grp")
    fourier_pair = (summed[0].astype(jnp.bfloat16), summed[1].astype(jnp.bfloat16))
    fourier_pair = (
        lax.all_gather(fourier_pair[0], "real", axis=0, tiled=True),
        lax.all_gather(fourier_pair[1], "real", axis=0, tiled=True),
    )
    fourier_pair = (
        lax.all_to_all(fourier_pair[0], "blk", split_axis=2, concat_axis=1, tiled=True),
        lax.all_to_all(fourier_pair[1], "blk", split_axis=2, concat_axis=1, tiled=True),
    )
    return fourier_pair


def backward_cycles(partial_value):
    summed = lax.psum_scatter(partial_value, "real", scatter_dimension=0, tiled=True)
    reduced = lax.psum(summed, "grp")
    cycle_pair = lax.all_to_all(
        reduced.astype(jnp.bfloat16), "blk", split_axis=2, concat_axis=3, tiled=True
    )
    return cycle_pair


def per_device(
    sky_data, signal_prev, noise_var, mask_flags, cycle_table, m_table, spectrum, legendre
):
    real_dev, cycle_dev, half_len = sky_data.shape
    cycle_len = half_len * lax.axis_size("grp")
    mode_count = m_table.shape[0]
    col_ids = lax.axis_index("grp") * half_len + jnp.arange(half_len, dtype=jnp.int32)
    cos_tab, sin_tab = phase_tables(col_ids, m_table, cycle_len)
    cos_shift, sin_shift = cycle_offsets(cycle_table, m_table, cycle_len)
    weight = mask_flags.astype(jnp.float32) / (noise_var - 0.5)
    messenger = (weight * sky_data + 2.0 * signal_prev) / (weight + 2.0)
    flat_rows = messenger.astype(jnp.bfloat16).reshape(real_dev * cycle_dev, half_len)
    base_cos = jnp.dot(flat_rows, cos_tab, preferred_element_type=jnp.float32).reshape(
        real_dev, cycle_dev, mode_count
    )
    base_sin = -jnp.dot(flat_rows, sin_tab, preferred_element_type=jnp.float32).reshape(
        real_dev, cycle_dev, mode_count
    )
    norm_scale = cycle_len ** (-0.5)
    re_part = (base_cos * cos_shift + base_sin * sin_shift) * norm_scale
    im_part = (base_sin * cos_shift - base_cos * sin_shift) * norm_scale
    fourier_re, fourier_im = forward_modes(re_part, im_part)
    fourier = jnp.stack([fourier_re, fourier_im], 1)
    coefficients = jnp.einsum(
        "mlr,kcrm->kcml", legendre, fourier, preferred_element_type=jnp.float32
    )
    factor = spectrum / (spectrum + 0.5)
    wiener_alm = coefficients * factor
    total_l = legendre.shape[1] * lax.axis_size("grp") * lax.axis_size("real")
    syn_scale = (legendre.shape[2] / total_l) ** 0.5
    partial_value = (
        jnp.einsum(
            "mlr,kcml->kcrm",
            legendre,
            wiener_alm.astype(jnp.bfloat16),
            preferred_element_type=jnp.float32,
        )
        * syn_scale
    )
    cycle_pair = backward_cycles(partial_value)
    cycle_modes = cycle_pair.astype(jnp.float32)
    modes_re = cycle_modes[:, 0]
    modes_im = cycle_modes[:, 1]
    rotated_re = (modes_re * cos_shift - modes_im * sin_shift).astype(jnp.bfloat16)
    rotated_im = (modes_im * cos_shift + modes_re * sin_shift).astype(jnp.bfloat16)
    contract = (((1,), (1,)), ((), ()))
    pixel_sum = lax.dot_general(
        rotated_re.reshape(-1, mode_count), cos_tab, contract, preferred_element_type=jnp.float32
    )
    pixel_sum = pixel_sum - lax.dot_general(
        rotated_im.reshape(-1, mode_count), sin_tab, contract, preferred_element_type=jnp.float32
    )
    signal_next = (pixel_sum * mode_count ** (-0.5)).reshape(real_dev, cycle_dev, half_len)
    return (wiener_alm, signal_next)


def solution(mesh):
    in_specs = (
        P("real", "blk", "grp"),
        P("real", "blk", "grp"),
        P("blk", "grp"),
        P("blk", "grp"),
        P("blk"),
        P(),
        P(("grp", "real")),
        P("blk", ("grp", "real"), None),
    )
    out_specs = (P(None, None, "blk", ("grp", "real")), P("real", "blk", "grp"))

    def step(sky_data, signal_prev, noise_var, mask_flags, cycle_table, m_table, spectrum, legendre):
        fits = gram_form_fits(mesh, sky_data, m_table, legendre)
        return jax.shard_map(
            gram_program if fits else per_device,
            mesh=mesh,
            in_specs=in_specs,
            out_specs=out_specs,
            check_vma=False,
        )(sky_data, signal_prev, noise_var, mask_flags, cycle_table, m_table, spectrum, legendre)

    return step
```

```python
import functools
import math

import jax
import jax.numpy as jnp
from jax import lax
from jax.experimental import pallas as pl
from jax.experimental.pallas import tpu as pltpu
from jax.sharding import PartitionSpec as P

LANES = 128
NT = (((1,), (1,)), ((), ()))
AXES = ("grp", "blk", "real")
PARTS = 2
FORWARD_VMEM = 63_150_000
BACKWARD_VMEM = 16 << 20


def unit_cosine(units, half_turn):
    wrapped = units & (2 * half_turn - 1)
    folded = jnp.minimum(wrapped, 2 * half_turn - wrapped)
    y = (half_turn // 2 - folded).astype(jnp.float32) * (math.pi / half_turn)
    y2 = y * y
    acc = jnp.full_like(y2, -1.0 / math.factorial(11))
    for order, sign in ((9, 1.0), (7, -1.0), (5, 1.0), (3, -1.0), (1, 1.0)):
        acc = acc * y2 + sign / math.factorial(order)
    return acc * y


def log2(size):
    return size.bit_length() - 1


def lane_ids(shape):
    return lax.broadcasted_iota(jnp.int32, shape, len(shape) - 1)


def row_ids(shape):
    return lax.broadcasted_iota(jnp.int32, shape, len(shape) - 2)


def phase_factors(cycles, orders, cycle_len, half_len, group):
    modes = orders.shape[1]
    orders = jnp.concatenate([orders] * (LANES // modes), axis=1)
    quarter = lane_ids((1, LANES)) >> log2(modes)
    quarter_turn = cycle_len // 2
    inner_units = 2 * orders * row_ids((LANES, LANES)) + ((quarter + 1) >> 1) * quarter_turn
    inner = unit_cosine(inner_units, cycle_len)
    rows = 2 * (half_len // LANES)
    row = row_ids((rows, LANES))
    parity = jnp.where((row & 1) == 0, cycles[:, :1], cycles[:, 1:]) & 1
    pixel = group * half_len + LANES * (row >> 1)
    outer_units = orders * (2 * pixel + parity) + (quarter >> 1) * (3 * quarter_turn)
    outer = unit_cosine(outer_units, cycle_len)
    high = inner.astype(jnp.bfloat16)
    low = (inner - high.astype(jnp.float32)).astype(jnp.bfloat16)
    return high, low, outer


def start_copies(sources, targets, sems, first=0):
    copies = [
        pltpu.make_async_copy(source, target, sems.at[first + i])
        for i, (source, target) in enumerate(zip(sources, targets))
    ]
    for copy in copies:
        copy.start()
    return copies


def forward_kernel(
    cycle_len, half_len, syn_scale,
    cycle_hbm, mode_hbm, noise_hbm, mask_hbm, spectrum_hbm, legendre_hbm, sky_hbm, prev_hbm, out_ref,
    cycle_ref, mode_ref, noise_ref, mask_ref, spectrum_ref, legendre_ref, sky_ref, prev_ref, gram_ref, sems,
):
    small = start_copies(
        (cycle_hbm, mode_hbm, noise_hbm, mask_hbm, spectrum_hbm, legendre_hbm),
        (cycle_ref, mode_ref, noise_ref, mask_ref, spectrum_ref, legendre_ref),
        sems,
    )
    large = start_copies((sky_hbm, prev_hbm), (sky_ref, prev_ref), sems, len(small))
    group = lax.axis_index("grp")
    small[0].wait()
    small[1].wait()
    high, low, outer = phase_factors(cycle_ref[...], mode_ref[...], cycle_len, half_len, group)
    inner = jnp.concatenate([high, low], axis=0)
    small[2].wait()
    small[3].wait()
    weight = mask_ref[...].astype(jnp.float32) / (noise_ref[...] - 0.5)
    inverse = 1.0 / (weight + 2.0)
    sky_gain = weight * inverse
    prev_gain = 2.0 * inverse

    for copy in small[4:] + large:
        copy.wait()
    table = legendre_ref[...]
    spectrum = spectrum_ref[...]
    factor = spectrum / (spectrum + 0.5)
    filtered = (table.astype(jnp.float32) * factor).astype(jnp.bfloat16)
    gram = lax.dot_general(table, filtered, NT, preferred_element_type=jnp.float32)
    table_rows = table.shape[0]
    pixel_rows = outer.shape[0]
    reals = sky_ref.shape[0] // pixel_rows
    blocks, real_groups = lax.axis_size("blk"), lax.axis_size("real")
    cycles = 2 * blocks
    same = (row_ids(gram.shape) >> log2(cycles)) == (lane_ids((1, table_rows)) >> log2(cycles))
    gram = jnp.where(same, gram, 0.0).reshape(table_rows // cycles, cycles, table_rows).sum(axis=0)
    gram = gram * syn_scale
    gram_ref[...] = jnp.concatenate([gram, gram], axis=1)
    even, odd = gram_ref[pl.ds(0, blocks, stride=2), :], gram_ref[pl.ds(1, blocks, stride=2), :]
    gram = jnp.where(lane_ids(even.shape) < LANES // 2, even, odd)
    gram_high = gram.astype(jnp.bfloat16).astype(jnp.float32)
    gram_low = gram - gram_high

    shape = (reals, pixel_rows, LANES)
    messenger = sky_ref[...].reshape(shape) * sky_gain + prev_ref[...].reshape(shape) * prev_gain
    rows = messenger.reshape(-1, LANES).astype(jnp.bfloat16)
    partial = jnp.dot(jnp.concatenate([rows, rows], axis=1), inner, preferred_element_type=jnp.float32)
    turned = partial.reshape(shape) * outer
    summed = turned.reshape(reals, pixel_rows // 8, 8, LANES).sum(axis=1)
    summed = summed.reshape(reals * 8, LANES)
    summed = summed + pltpu.roll(summed, LANES // 2, 1)
    own = (row_ids(summed.shape) & 1) == (lane_ids(summed.shape) >= LANES // 2)
    fourier = jnp.where(own, summed, 0.0).reshape(reals, 8, LANES).sum(axis=1) * cycle_len**-0.5
    rows = []
    for b in range(blocks):
        rows += [fourier, gram_high[b : b + 1], gram_low[b : b + 1]] * real_groups
    rows = jnp.concatenate(rows, axis=0).astype(jnp.bfloat16)
    for g in range(lax.axis_size("grp")):
        out_ref[pl.ds(g * rows.shape[0], rows.shape[0]), :] = rows


def prepare_kernel(
    cycle_len, half_len, per_block, reals,
    cycle_ref, mode_ref, legendre_ref, spectrum_ref,
    inner_ref, outer_ref, place_ref, pick_ref, table_ref, factor_ref,
):
    table = legendre_ref[...]
    table_ref[...] = jnp.concatenate([table, table], axis=0)
    spectrum = spectrum_ref[...]
    factor_ref[...] = spectrum / (spectrum + 0.5)
    group = lax.axis_index("grp")
    block = lax.axis_index("blk")
    blocks, real_groups = lax.axis_size("blk"), lax.axis_size("real")
    high, low, outer_ref[...] = phase_factors(cycle_ref[...], mode_ref[...], cycle_len, half_len, group)
    inner_ref[...] = jnp.concatenate([high, low], axis=1)
    modes, cycles, half = per_block * blocks, 2 * blocks, LANES // 2

    lane = lane_ids((1, LANES))
    row = row_ids((LANES, LANES))
    lane_order = (lane & (half - 1)) >> log2(cycles)
    lane_row = (lane & 1) * half + (lane >> log2(half)) * modes + block * per_block + lane_order
    pick_ref[0] = (row == lane_row).astype(jnp.float32).astype(jnp.bfloat16)
    lane_row = (lane >> log2(half)) * per_block + (lane & (per_block - 1))
    pick_ref[1] = ((row >> log2(cycles)) == lane_row).astype(jnp.float32).astype(jnp.bfloat16)

    spacing = reals + 2
    column = lane_ids((1, place_ref.shape[1]))
    source = (column * (2**16 // spacing + 1)) >> 16
    inside = column - source * spacing
    source = source & (blocks * real_groups - 1)
    source_block = source >> log2(real_groups)
    target = ((source & (real_groups - 1)) * blocks + source_block) * reals + inside
    target = jnp.where(inside < reals, target, blocks * real_groups * reals + source_block)
    place = (row_ids(place_ref.shape) == target).astype(jnp.float32)
    place_ref[...] = place.astype(jnp.bfloat16)


def backward_kernel(
    blocks, real_groups, reals, parts,
    gathered_ref, inner_ref, outer_ref, place_ref, pick_ref, table_ref, factor_ref,
    wiener_hbm, signal_hbm, wiener_ref, signal_ref, fourier_ref, out_sems,
):
    real_group = lax.axis_index("real")
    cycles = 2 * blocks
    per_block = table_ref.shape[0] // (2 * cycles)
    modes = per_block * blocks
    pixel_rows = outer_ref.shape[0]
    half = LANES // 2
    lane = lane_ids((1, LANES))
    holder = (lane & (modes - 1)) >> log2(per_block)
    lane_block = (lane & (cycles - 1)) >> 1
    total_reals = real_groups * reals
    fourier_rows = blocks * total_reals
    placed = jnp.dot(place_ref[...], gathered_ref[...], preferred_element_type=jnp.float32)
    fourier_ref[...] = placed[:fourier_rows]

    coeff_rows = jnp.dot(
        placed[:fourier_rows].astype(jnp.bfloat16), pick_ref[0], preferred_element_type=jnp.float32
    ).reshape(real_groups, blocks, reals, LANES)
    columns = jnp.zeros((total_reals, LANES), jnp.float32)
    for b in range(blocks):
        one = coeff_rows[:, b].reshape(total_reals, LANES)
        columns = columns + jnp.where(lane_block == b, one, 0.0)
    gram_all = jnp.where(
        (lane & (cycles - 1)) == row_ids((cycles, LANES)), placed[fourier_rows:, None, :], 0.0
    ).reshape(blocks * cycles, LANES)
    gram_high = gram_all.astype(jnp.bfloat16)
    gram_low = (gram_all - gram_high.astype(jnp.float32)).astype(jnp.bfloat16)
    gram_rows = jnp.dot(
        jnp.concatenate([gram_high, gram_low], axis=1),
        jnp.concatenate([pick_ref[1], pick_ref[1]], axis=0),
        preferred_element_type=jnp.float32,
    ).reshape(blocks, cycles, LANES)
    gram = jnp.zeros((cycles, LANES), jnp.float32)
    for b in range(blocks):
        gram = gram + jnp.where(holder == b, gram_rows[b], 0.0)

    first = lane < half
    cycle_modes = jnp.zeros((reals, LANES), jnp.float32)
    for b in range(blocks):
        first_row = pl.multiple_of((real_group * blocks + b) * reals, reals)
        pair = fourier_ref[pl.ds(first_row, reals), :]
        turned = pltpu.roll(pair, half, 1)
        cycle_modes = cycle_modes + jnp.where(first, pair, turned) * gram[2 * b : 2 * b + 1]
        cycle_modes = cycle_modes + jnp.where(first, turned, pair) * gram[2 * b + 1 : 2 * b + 2]
    cycle_modes = cycle_modes * modes**-0.5
    turned = pltpu.roll(cycle_modes, half, 1)
    even = jnp.where(first, cycle_modes, turned)
    odd = jnp.where(first, turned, cycle_modes)
    parity = (row_ids((1, 8, LANES)) & 1) == 0
    spread = jnp.where(parity, even[:, None, :], odd[:, None, :])
    table = table_ref[...]
    factor = factor_ref[...]
    stores = []
    own = (lane >> log2(cycles)) == row_ids((2 * per_block, LANES))
    upper = row_ids((1, 2 * per_block, LANES)) < per_block
    for y in range(real_groups):
        span = slice(y * reals, (y + 1) * reals)
        pieces = jnp.where(own, columns[span, None, :], 0.0)
        filtered = factor * jnp.dot(
            pieces.reshape(-1, LANES).astype(jnp.bfloat16), table, preferred_element_type=jnp.float32
        )
        for pair in range(wiener_ref.shape[2]):
            one, two = (
                filtered[:, tile * LANES : (tile + 1) * LANES].reshape(reals, 2 * per_block, LANES)
                for tile in (2 * pair, 2 * pair + 1)
            )
            wiener_ref[span, 0, pair] = jnp.where(upper, one, pltpu.roll(two, per_block, 1))
            wiener_ref[span, 1, pair] = jnp.where(upper, pltpu.roll(one, per_block, 1), two)
        span = pl.ds(y * reals, reals)
        stores += start_copies([wiener_ref.at[span]], [wiener_hbm.at[span]], out_sems, len(stores))

    inner = inner_ref[...]
    outer = outer_ref[...].reshape(1, pixel_rows // 8, 8, LANES)
    part_reals = reals // parts
    for i in range(parts):
        rotated = spread[i * part_reals : (i + 1) * part_reals, None] * outer
        rotated = rotated.reshape(part_reals * pixel_rows, LANES).astype(jnp.bfloat16)
        span = pl.ds(i * part_reals * pixel_rows, part_reals * pixel_rows)
        signal_ref[span, :] = lax.dot_general(
            jnp.concatenate([rotated, rotated], axis=1), inner, NT, preferred_element_type=jnp.float32
        )
        stores += start_copies([signal_ref.at[span]], [signal_hbm.at[span]], out_sems, len(stores))
    for store in stores:
        store.wait()


def split_tiles(array):
    lead, rows, columns = array.shape[:-2], array.shape[-2], array.shape[-1]
    split = array.reshape(*lead, rows, columns // LANES, LANES)
    return jnp.swapaxes(split, -2, -3).reshape(-1, LANES)


def gram_program(
    sky_data, signal_prev, noise_var, mask_flags, cycle_table, m_table, spectrum, legendre
):
    reals, cycle_dev, half_len = sky_data.shape
    groups, blocks, real_groups = (lax.axis_size(name) for name in AXES)
    cycle_len = half_len * groups
    per_block, multipoles, cycles = legendre.shape
    total_l = multipoles * groups * real_groups
    tiles = multipoles // LANES
    hbm = pl.BlockSpec(memory_space=pltpu.HBM)
    vmem = pl.BlockSpec(memory_space=pltpu.VMEM)
    orders = m_table[None, :]
    cycles_row = cycle_table[None, :]
    spectrum_row = spectrum[None, :]
    table = legendre.transpose(0, 2, 1).reshape(per_block * cycles, multipoles)
    inputs = (
        cycles_row, orders, split_tiles(noise_var), split_tiles(mask_flags), spectrum_row, table,
        split_tiles(sky_data), split_tiles(signal_prev),
    )
    sources = groups * blocks * real_groups
    local = pl.pallas_call(
        functools.partial(forward_kernel, cycle_len, half_len, (cycles / total_l) ** 0.5),
        out_shape=jax.ShapeDtypeStruct((sources * (reals + 2), LANES), jnp.bfloat16),
        in_specs=[hbm] * 8,
        out_specs=vmem,
        scratch_shapes=[pltpu.VMEM(x.shape, x.dtype) for x in inputs]
        + [pltpu.VMEM((cycles, LANES), jnp.float32), pltpu.SemaphoreType.DMA((8,))],
        compiler_params=pltpu.CompilerParams(vmem_limit_bytes=FORWARD_VMEM),
    )(*inputs)
    pairs = local.reshape(sources, reals // 2 + 1, 2, LANES)
    gathered = lax.all_to_all(pairs, AXES, 0, 0, tiled=True).reshape(local.shape)
    total_reals = reals * real_groups
    prepared = pl.pallas_call(
        functools.partial(prepare_kernel, cycle_len, half_len, per_block, reals),
        out_shape=(
            jax.ShapeDtypeStruct((LANES, 2 * LANES), jnp.bfloat16),
            jax.ShapeDtypeStruct((cycle_dev * half_len // LANES, LANES), jnp.float32),
            jax.ShapeDtypeStruct((blocks * (total_reals + 1), local.shape[0]), jnp.bfloat16),
            jax.ShapeDtypeStruct((2, LANES, LANES), jnp.bfloat16),
            jax.ShapeDtypeStruct((2 * table.shape[0], multipoles), jnp.bfloat16),
            jax.ShapeDtypeStruct((1, multipoles), jnp.float32),
        ),
        in_specs=[vmem] * 4,
        out_specs=(vmem,) * 6,
        compiler_params=pltpu.CompilerParams(vmem_limit_bytes=BACKWARD_VMEM),
        cost_estimate=pl.CostEstimate(flops=4_000_000, bytes_accessed=600_000, transcendentals=0),
    )(cycles_row, orders, table, spectrum_row)
    outputs = (
        jax.ShapeDtypeStruct((total_reals, 2, tiles // 2, 2 * per_block, LANES), jnp.float32),
        jax.ShapeDtypeStruct((reals * cycle_dev * half_len // LANES, LANES), jnp.float32),
    )
    wiener, signal = pl.pallas_call(
        functools.partial(backward_kernel, blocks, real_groups, reals, PARTS),
        out_shape=outputs,
        in_specs=[vmem] * 7,
        out_specs=(hbm, hbm),
        scratch_shapes=[pltpu.VMEM(x.shape, x.dtype) for x in outputs]
        + [pltpu.VMEM((blocks * total_reals, LANES), jnp.float32)]
        + [pltpu.SemaphoreType.DMA((real_groups + PARTS,))],
        compiler_params=pltpu.CompilerParams(vmem_limit_bytes=BACKWARD_VMEM),
    )(gathered, *prepared)
    wiener = wiener.reshape(total_reals, 2, tiles, per_block, LANES).transpose(0, 1, 3, 2, 4)
    signal = signal.reshape(reals, half_len // LANES, cycle_dev, LANES).transpose(0, 2, 1, 3)
    return (
        wiener.reshape(total_reals, 2, per_block, multipoles),
        signal.reshape(sky_data.shape),
    )


def gram_form_fits(mesh, sky_data, m_table, legendre):
    groups, blocks, real_groups = (mesh.shape[name] for name in AXES)
    reals, cycles, cycle_len = sky_data.shape
    modes = m_table.shape[0]
    per_block = modes // blocks
    multipoles = legendre.shape[1] // (groups * real_groups)
    half_len = cycle_len // groups
    reals_dev = reals // real_groups
    return (
        cycles < 2 * reals
        and 4 * modes == LANES
        and cycles == 2 * blocks
        and all(size & (size - 1) == 0 for size in (blocks, modes, cycles, real_groups))
        and 2 * reals * cycles < 2**12
        and 2 * per_block * cycles == LANES
        and cycle_len & (cycle_len - 1) == 0
        and half_len % (4 * LANES) == 0
        and multipoles % (2 * LANES) == 0
        and per_block == 4
        and reals_dev % 16 == 0
        and reals_dev % PARTS == 0
        and cycles % 16 == 0
    )


def phase_tables(col_ids, mode_ids, cycle_len):
    product_ids = col_ids[:, None] * mode_ids[None, :] % cycle_len
    angles = product_ids.astype(jnp.float32) * (2.0 * math.pi / cycle_len)
    return (jnp.cos(angles).astype(jnp.bfloat16), jnp.sin(angles).astype(jnp.bfloat16))


def cycle_offsets(cycle_ids, mode_ids, cycle_len):
    parity = (cycle_ids % 2).astype(jnp.float32)
    shifts = math.pi / cycle_len * parity[:, None] * mode_ids[None, :].astype(jnp.float32)
    return (jnp.cos(shifts), jnp.sin(shifts))


def forward_modes(re_part, im_part):
    summed = lax.psum((re_part, im_part), "grp")
    fourier_pair = (summed[0].astype(jnp.bfloat16), summed[1].astype(jnp.bfloat16))
    fourier_pair = (
        lax.all_gather(fourier_pair[0], "real", axis=0, tiled=True),
        lax.all_gather(fourier_pair[1], "real", axis=0, tiled=True),
    )
    fourier_pair = (
        lax.all_to_all(fourier_pair[0], "blk", split_axis=2, concat_axis=1, tiled=True),
        lax.all_to_all(fourier_pair[1], "blk", split_axis=2, concat_axis=1, tiled=True),
    )
    return fourier_pair


def backward_cycles(partial_value):
    summed = lax.psum_scatter(partial_value, "real", scatter_dimension=0, tiled=True)
    reduced = lax.psum(summed, "grp")
    cycle_pair = lax.all_to_all(
        reduced.astype(jnp.bfloat16), "blk", split_axis=2, concat_axis=3, tiled=True
    )
    return cycle_pair


def per_device(
    sky_data, signal_prev, noise_var, mask_flags, cycle_table, m_table, spectrum, legendre
):
    real_dev, cycle_dev, half_len = sky_data.shape
    cycle_len = half_len * lax.axis_size("grp")
    mode_count = m_table.shape[0]
    col_ids = lax.axis_index("grp") * half_len + jnp.arange(half_len, dtype=jnp.int32)
    cos_tab, sin_tab = phase_tables(col_ids, m_table, cycle_len)
    cos_shift, sin_shift = cycle_offsets(cycle_table, m_table, cycle_len)
    weight = mask_flags.astype(jnp.float32) / (noise_var - 0.5)
    messenger = (weight * sky_data + 2.0 * signal_prev) / (weight + 2.0)
    flat_rows = messenger.astype(jnp.bfloat16).reshape(real_dev * cycle_dev, half_len)
    base_cos = jnp.dot(flat_rows, cos_tab, preferred_element_type=jnp.float32).reshape(
        real_dev, cycle_dev, mode_count
    )
    base_sin = -jnp.dot(flat_rows, sin_tab, preferred_element_type=jnp.float32).reshape(
        real_dev, cycle_dev, mode_count
    )
    norm_scale = cycle_len ** (-0.5)
    re_part = (base_cos * cos_shift + base_sin * sin_shift) * norm_scale
    im_part = (base_sin * cos_shift - base_cos * sin_shift) * norm_scale
    fourier_re, fourier_im = forward_modes(re_part, im_part)
    fourier = jnp.stack([fourier_re, fourier_im], 1)
    coefficients = jnp.einsum(
        "mlr,kcrm->kcml", legendre, fourier, preferred_element_type=jnp.float32
    )
    factor = spectrum / (spectrum + 0.5)
    wiener_alm = coefficients * factor
    total_l = legendre.shape[1] * lax.axis_size("grp") * lax.axis_size("real")
    syn_scale = (legendre.shape[2] / total_l) ** 0.5
    partial_value = (
        jnp.einsum(
            "mlr,kcml->kcrm",
            legendre,
            wiener_alm.astype(jnp.bfloat16),
            preferred_element_type=jnp.float32,
        )
        * syn_scale
    )
    cycle_pair = backward_cycles(partial_value)
    cycle_modes = cycle_pair.astype(jnp.float32)
    modes_re = cycle_modes[:, 0]
    modes_im = cycle_modes[:, 1]
    rotated_re = (modes_re * cos_shift - modes_im * sin_shift).astype(jnp.bfloat16)
    rotated_im = (modes_im * cos_shift + modes_re * sin_shift).astype(jnp.bfloat16)
    contract = (((1,), (1,)), ((), ()))
    pixel_sum = lax.dot_general(
        rotated_re.reshape(-1, mode_count), cos_tab, contract, preferred_element_type=jnp.float32
    )
    pixel_sum = pixel_sum - lax.dot_general(
        rotated_im.reshape(-1, mode_count), sin_tab, contract, preferred_element_type=jnp.float32
    )
    signal_next = (pixel_sum * mode_count ** (-0.5)).reshape(real_dev, cycle_dev, half_len)
    return (wiener_alm, signal_next)


def solution(mesh):
    in_specs = (
        P("real", "blk", "grp"),
        P("real", "blk", "grp"),
        P("blk", "grp"),
        P("blk", "grp"),
        P("blk"),
        P(),
        P(("grp", "real")),
        P("blk", ("grp", "real"), None),
    )
    out_specs = (P(None, None, "blk", ("grp", "real")), P("real", "blk", "grp"))

    def step(sky_data, signal_prev, noise_var, mask_flags, cycle_table, m_table, spectrum, legendre):
        fits = gram_form_fits(mesh, sky_data, m_table, legendre)
        return jax.shard_map(
            gram_program if fits else per_device,
            mesh=mesh,
            in_specs=in_specs,
            out_specs=out_specs,
            check_vma=False,
        )(sky_data, signal_prev, noise_var, mask_flags, cycle_table, m_table, spectrum, legendre)

    return step
```

```python
import functools
import math

import jax
import jax.numpy as jnp
from jax import lax
from jax.experimental import pallas as pl
from jax.experimental.pallas import tpu as pltpu
from jax.sharding import PartitionSpec as P

LANES = 128
NT = (((1,), (1,)), ((), ()))
AXES = ("grp", "blk", "real")
PARTS = 2
FORWARD_VMEM = 32 << 20
BACKWARD_VMEM = 16 << 20


def unit_cosine(units, half_turn):
    wrapped = units & (2 * half_turn - 1)
    folded = jnp.minimum(wrapped, 2 * half_turn - wrapped)
    y = (half_turn // 2 - folded).astype(jnp.float32) * (math.pi / half_turn)
    y2 = y * y
    acc = jnp.full_like(y2, -1.0 / math.factorial(11))
    for order, sign in ((9, 1.0), (7, -1.0), (5, 1.0), (3, -1.0), (1, 1.0)):
        acc = acc * y2 + sign / math.factorial(order)
    return acc * y


def log2(size):
    return size.bit_length() - 1


def lane_ids(shape):
    return lax.broadcasted_iota(jnp.int32, shape, len(shape) - 1)


def row_ids(shape):
    return lax.broadcasted_iota(jnp.int32, shape, len(shape) - 2)


def phase_factors(cycles, orders, cycle_len, half_len, group):
    modes = orders.shape[1]
    orders = jnp.concatenate([orders] * (LANES // modes), axis=1)
    quarter = lane_ids((1, LANES)) >> log2(modes)
    quarter_turn = cycle_len // 2
    inner_units = 2 * orders * row_ids((LANES, LANES)) + ((quarter + 1) >> 1) * quarter_turn
    inner = unit_cosine(inner_units, cycle_len)
    rows = 2 * (half_len // LANES)
    row = row_ids((rows, LANES))
    parity = jnp.where((row & 1) == 0, cycles[:, :1], cycles[:, 1:]) & 1
    pixel = group * half_len + LANES * (row >> 1)
    outer_units = orders * (2 * pixel + parity) + (quarter >> 1) * (3 * quarter_turn)
    outer = unit_cosine(outer_units, cycle_len)
    high = inner.astype(jnp.bfloat16)
    low = (inner - high.astype(jnp.float32)).astype(jnp.bfloat16)
    return high, low, outer


def start_copies(sources, targets, sems, first=0):
    copies = [
        pltpu.make_async_copy(source, target, sems.at[first + i])
        for i, (source, target) in enumerate(zip(sources, targets))
    ]
    for copy in copies:
        copy.start()
    return copies


def selections(place_ref, pick_ref, per_block, reals):
    block = lax.axis_index("blk")
    blocks, real_groups = lax.axis_size("blk"), lax.axis_size("real")
    modes, cycles, half = per_block * blocks, 2 * blocks, LANES // 2

    lane = lane_ids((1, LANES))
    row = row_ids((LANES, LANES))
    lane_order = (lane & (half - 1)) >> log2(cycles)
    lane_row = (lane & 1) * half + (lane >> log2(half)) * modes + block * per_block + lane_order
    pick_ref[0] = (row == lane_row).astype(jnp.float32).astype(jnp.bfloat16)
    lane_row = (lane >> log2(half)) * per_block + (lane & (per_block - 1))
    pick_ref[1] = ((row >> log2(cycles)) == lane_row).astype(jnp.float32).astype(jnp.bfloat16)

    spacing = reals + 2
    column = lane_ids((1, place_ref.shape[1]))
    source = (column * (2**16 // spacing + 1)) >> 16
    inside = column - source * spacing
    source = source & (blocks * real_groups - 1)
    source_block = source >> log2(real_groups)
    target = ((source & (real_groups - 1)) * blocks + source_block) * reals + inside
    target = jnp.where(inside < reals, target, blocks * real_groups * reals + source_block)
    place = (row_ids(place_ref.shape) == target).astype(jnp.float32)
    place_ref[...] = place.astype(jnp.bfloat16)


def forward_kernel(
    cycle_len, half_len, syn_scale, reals,
    cycle_hbm, mode_hbm, noise_hbm, mask_hbm, spectrum_hbm, legendre_hbm, sky_hbm, prev_hbm,
    out_ref, inner_ref, outer_ref, place_ref, pick_ref, doubled_ref, factor_ref,
    cycle_ref, mode_ref, noise_ref, mask_ref, spectrum_ref, legendre_ref, sky_ref, prev_ref, gram_ref, sems,
):
    small = start_copies(
        (cycle_hbm, mode_hbm, noise_hbm, mask_hbm, spectrum_hbm, legendre_hbm),
        (cycle_ref, mode_ref, noise_ref, mask_ref, spectrum_ref, legendre_ref),
        sems,
    )
    large = start_copies((sky_hbm, prev_hbm), (sky_ref, prev_ref), sems, len(small))
    group = lax.axis_index("grp")
    per_block = legendre_ref.shape[0] // (2 * lax.axis_size("blk"))
    selections(place_ref, pick_ref, per_block, reals)
    small[0].wait()
    small[1].wait()
    high, low, outer = phase_factors(cycle_ref[...], mode_ref[...], cycle_len, half_len, group)
    inner = jnp.concatenate([high, low], axis=0)
    inner_ref[...] = jnp.concatenate([high, low], axis=1)
    outer_ref[...] = outer
    small[2].wait()
    small[3].wait()
    weight = mask_ref[...].astype(jnp.float32) / (noise_ref[...] - 0.5)
    inverse = 1.0 / (weight + 2.0)
    sky_gain = weight * inverse
    prev_gain = 2.0 * inverse

    for copy in small[4:] + large:
        copy.wait()
    table = legendre_ref[...]
    spectrum = spectrum_ref[...]
    factor = spectrum / (spectrum + 0.5)
    doubled_ref[...] = jnp.concatenate([table, table], axis=0)
    factor_ref[...] = factor
    filtered = (table.astype(jnp.float32) * factor).astype(jnp.bfloat16)
    gram = lax.dot_general(table, filtered, NT, preferred_element_type=jnp.float32)
    table_rows = table.shape[0]
    pixel_rows = outer.shape[0]
    blocks, real_groups = lax.axis_size("blk"), lax.axis_size("real")
    cycles = 2 * blocks
    same = (row_ids(gram.shape) >> log2(cycles)) == (lane_ids((1, table_rows)) >> log2(cycles))
    gram = jnp.where(same, gram, 0.0).reshape(table_rows // cycles, cycles, table_rows).sum(axis=0)
    gram = gram * syn_scale
    gram_ref[...] = jnp.concatenate([gram, gram], axis=1)
    even, odd = gram_ref[pl.ds(0, blocks, stride=2), :], gram_ref[pl.ds(1, blocks, stride=2), :]
    gram = jnp.where(lane_ids(even.shape) < LANES // 2, even, odd)
    gram_high = gram.astype(jnp.bfloat16).astype(jnp.float32)
    gram_low = gram - gram_high

    shape = (reals, pixel_rows, LANES)
    messenger = sky_ref[...].reshape(shape) * sky_gain + prev_ref[...].reshape(shape) * prev_gain
    rows = messenger.reshape(-1, LANES).astype(jnp.bfloat16)
    partial = jnp.dot(jnp.concatenate([rows, rows], axis=1), inner, preferred_element_type=jnp.float32)
    turned = partial.reshape(shape) * outer
    summed = turned.reshape(reals, pixel_rows // 8, 8, LANES).sum(axis=1)
    summed = summed.reshape(reals * 8, LANES)
    summed = summed + pltpu.roll(summed, LANES // 2, 1)
    own = (row_ids(summed.shape) & 1) == (lane_ids(summed.shape) >= LANES // 2)
    fourier = jnp.where(own, summed, 0.0).reshape(reals, 8, LANES).sum(axis=1) * cycle_len**-0.5
    rows = []
    for b in range(blocks):
        rows += [fourier, gram_high[b : b + 1], gram_low[b : b + 1]] * real_groups
    rows = jnp.concatenate(rows, axis=0).astype(jnp.bfloat16)
    for g in range(lax.axis_size("grp")):
        out_ref[pl.ds(g * rows.shape[0], rows.shape[0]), :] = rows


def backward_kernel(
    blocks, real_groups, reals, parts,
    gathered_ref, inner_ref, outer_ref, place_ref, pick_ref, table_ref, factor_ref,
    wiener_hbm, signal_hbm, wiener_ref, signal_ref, fourier_ref, out_sems,
):
    real_group = lax.axis_index("real")
    cycles = 2 * blocks
    per_block = table_ref.shape[0] // (2 * cycles)
    modes = per_block * blocks
    pixel_rows = outer_ref.shape[0]
    half = LANES // 2
    lane = lane_ids((1, LANES))
    holder = (lane & (modes - 1)) >> log2(per_block)
    lane_block = (lane & (cycles - 1)) >> 1
    total_reals = real_groups * reals
    fourier_rows = blocks * total_reals
    placed = jnp.dot(place_ref[...], gathered_ref[...], preferred_element_type=jnp.float32)
    fourier_ref[...] = placed[:fourier_rows]

    coeff_rows = jnp.dot(
        placed[:fourier_rows].astype(jnp.bfloat16), pick_ref[0], preferred_element_type=jnp.float32
    ).reshape(real_groups, blocks, reals, LANES)
    columns = jnp.zeros((total_reals, LANES), jnp.float32)
    for b in range(blocks):
        one = coeff_rows[:, b].reshape(total_reals, LANES)
        columns = columns + jnp.where(lane_block == b, one, 0.0)
    table = table_ref[...]
    factor = factor_ref[...]
    stores = []
    own = (lane >> log2(cycles)) == row_ids((2 * per_block, LANES))
    upper = row_ids((1, 2 * per_block, LANES)) < per_block
    for y in range(real_groups):
        span = slice(y * reals, (y + 1) * reals)
        pieces = jnp.where(own, columns[span, None, :], 0.0)
        filtered = factor * jnp.dot(
            pieces.reshape(-1, LANES).astype(jnp.bfloat16), table, preferred_element_type=jnp.float32
        )
        for pair in range(wiener_ref.shape[2]):
            one, two = (
                filtered[:, tile * LANES : (tile + 1) * LANES].reshape(reals, 2 * per_block, LANES)
                for tile in (2 * pair, 2 * pair + 1)
            )
            wiener_ref[span, 0, pair] = jnp.where(upper, one, pltpu.roll(two, per_block, 1))
            wiener_ref[span, 1, pair] = jnp.where(upper, pltpu.roll(one, per_block, 1), two)
        span = pl.ds(y * reals, reals)
        stores += start_copies([wiener_ref.at[span]], [wiener_hbm.at[span]], out_sems, len(stores))

    gram_all = jnp.where(
        (lane & (cycles - 1)) == row_ids((cycles, LANES)), placed[fourier_rows:, None, :], 0.0
    ).reshape(blocks * cycles, LANES)
    gram_high = gram_all.astype(jnp.bfloat16)
    gram_low = (gram_all - gram_high.astype(jnp.float32)).astype(jnp.bfloat16)
    gram_rows = jnp.dot(
        jnp.concatenate([gram_high, gram_low], axis=1),
        jnp.concatenate([pick_ref[1], pick_ref[1]], axis=0),
        preferred_element_type=jnp.float32,
    ).reshape(blocks, cycles, LANES)
    gram = jnp.zeros((cycles, LANES), jnp.float32)
    for b in range(blocks):
        gram = gram + jnp.where(holder == b, gram_rows[b], 0.0)

    first = lane < half
    cycle_modes = jnp.zeros((reals, LANES), jnp.float32)
    for b in range(blocks):
        first_row = pl.multiple_of((real_group * blocks + b) * reals, reals)
        pair = fourier_ref[pl.ds(first_row, reals), :]
        turned = pltpu.roll(pair, half, 1)
        cycle_modes = cycle_modes + jnp.where(first, pair, turned) * gram[2 * b : 2 * b + 1]
        cycle_modes = cycle_modes + jnp.where(first, turned, pair) * gram[2 * b + 1 : 2 * b + 2]
    cycle_modes = cycle_modes * modes**-0.5
    turned = pltpu.roll(cycle_modes, half, 1)
    even = jnp.where(first, cycle_modes, turned)
    odd = jnp.where(first, turned, cycle_modes)
    parity = (row_ids((1, 8, LANES)) & 1) == 0
    spread = jnp.where(parity, even[:, None, :], odd[:, None, :])
    inner = inner_ref[...]
    outer = outer_ref[...].reshape(1, pixel_rows // 8, 8, LANES)
    part_reals = reals // parts
    for i in range(parts):
        rotated = spread[i * part_reals : (i + 1) * part_reals, None] * outer
        rotated = rotated.reshape(part_reals * pixel_rows, LANES).astype(jnp.bfloat16)
        span = pl.ds(i * part_reals * pixel_rows, part_reals * pixel_rows)
        signal_ref[span, :] = lax.dot_general(
            jnp.concatenate([rotated, rotated], axis=1), inner, NT, preferred_element_type=jnp.float32
        )
        stores += start_copies([signal_ref.at[span]], [signal_hbm.at[span]], out_sems, len(stores))
    for store in stores:
        store.wait()


def split_tiles(array):
    lead, rows, columns = array.shape[:-2], array.shape[-2], array.shape[-1]
    split = array.reshape(*lead, rows, columns // LANES, LANES)
    return jnp.swapaxes(split, -2, -3).reshape(-1, LANES)


def gram_program(
    sky_data, signal_prev, noise_var, mask_flags, cycle_table, m_table, spectrum, legendre
):
    reals, cycle_dev, half_len = sky_data.shape
    groups, blocks, real_groups = (lax.axis_size(name) for name in AXES)
    cycle_len = half_len * groups
    per_block, multipoles, cycles = legendre.shape
    total_l = multipoles * groups * real_groups
    tiles = multipoles // LANES
    hbm = pl.BlockSpec(memory_space=pltpu.HBM)
    vmem = pl.BlockSpec(memory_space=pltpu.VMEM)
    orders = m_table[None, :]
    cycles_row = cycle_table[None, :]
    spectrum_row = spectrum[None, :]
    table = legendre.transpose(0, 2, 1).reshape(per_block * cycles, multipoles)
    inputs = (
        cycles_row, orders, split_tiles(noise_var), split_tiles(mask_flags), spectrum_row, table,
        split_tiles(sky_data), split_tiles(signal_prev),
    )
    sources = groups * blocks * real_groups
    total_reals = reals * real_groups
    local, *prepared = pl.pallas_call(
        functools.partial(forward_kernel, cycle_len, half_len, (cycles / total_l) ** 0.5, reals),
        out_shape=(
            jax.ShapeDtypeStruct((sources * (reals + 2), LANES), jnp.bfloat16),
            jax.ShapeDtypeStruct((LANES, 2 * LANES), jnp.bfloat16),
            jax.ShapeDtypeStruct((cycle_dev * half_len // LANES, LANES), jnp.float32),
            jax.ShapeDtypeStruct((blocks * (total_reals + 1), sources * (reals + 2)), jnp.bfloat16),
            jax.ShapeDtypeStruct((2, LANES, LANES), jnp.bfloat16),
            jax.ShapeDtypeStruct((2 * table.shape[0], multipoles), jnp.bfloat16),
            jax.ShapeDtypeStruct((1, multipoles), jnp.float32),
        ),
        in_specs=[hbm] * 8,
        out_specs=(vmem,) * 7,
        scratch_shapes=[pltpu.VMEM(x.shape, x.dtype) for x in inputs]
        + [pltpu.VMEM((cycles, LANES), jnp.float32), pltpu.SemaphoreType.DMA((8,))],
        compiler_params=pltpu.CompilerParams(vmem_limit_bytes=FORWARD_VMEM),
    )(*inputs)
    pairs = local.reshape(sources, reals // 2 + 1, 2, LANES)
    gathered = lax.all_to_all(pairs, AXES, 0, 0, tiled=True).reshape(local.shape)
    outputs = (
        jax.ShapeDtypeStruct((total_reals, 2, tiles // 2, 2 * per_block, LANES), jnp.float32),
        jax.ShapeDtypeStruct((reals * cycle_dev * half_len // LANES, LANES), jnp.float32),
    )
    wiener, signal = pl.pallas_call(
        functools.partial(backward_kernel, blocks, real_groups, reals, PARTS),
        out_shape=outputs,
        in_specs=[vmem] * 7,
        out_specs=(hbm, hbm),
        scratch_shapes=[pltpu.VMEM(x.shape, x.dtype) for x in outputs]
        + [pltpu.VMEM((blocks * total_reals, LANES), jnp.float32)]
        + [pltpu.SemaphoreType.DMA((real_groups + PARTS,))],
        compiler_params=pltpu.CompilerParams(vmem_limit_bytes=BACKWARD_VMEM),
    )(gathered, *prepared)
    wiener = wiener.reshape(total_reals, 2, tiles, per_block, LANES).transpose(0, 1, 3, 2, 4)
    signal = signal.reshape(reals, half_len // LANES, cycle_dev, LANES).transpose(0, 2, 1, 3)
    return (
        wiener.reshape(total_reals, 2, per_block, multipoles),
        signal.reshape(sky_data.shape),
    )


def gram_form_fits(mesh, sky_data, m_table, legendre):
    groups, blocks, real_groups = (mesh.shape[name] for name in AXES)
    reals, cycles, cycle_len = sky_data.shape
    modes = m_table.shape[0]
    per_block = modes // blocks
    multipoles = legendre.shape[1] // (groups * real_groups)
    half_len = cycle_len // groups
    reals_dev = reals // real_groups
    return (
        cycles < 2 * reals
        and 4 * modes == LANES
        and cycles == 2 * blocks
        and all(size & (size - 1) == 0 for size in (blocks, modes, cycles, real_groups))
        and 2 * reals * cycles < 2**12
        and 2 * per_block * cycles == LANES
        and cycle_len & (cycle_len - 1) == 0
        and half_len % (4 * LANES) == 0
        and multipoles % (2 * LANES) == 0
        and per_block == 4
        and reals_dev % 16 == 0
        and reals_dev % PARTS == 0
        and cycles % 16 == 0
    )


def phase_tables(col_ids, mode_ids, cycle_len):
    product_ids = col_ids[:, None] * mode_ids[None, :] % cycle_len
    angles = product_ids.astype(jnp.float32) * (2.0 * math.pi / cycle_len)
    return (jnp.cos(angles).astype(jnp.bfloat16), jnp.sin(angles).astype(jnp.bfloat16))


def cycle_offsets(cycle_ids, mode_ids, cycle_len):
    parity = (cycle_ids % 2).astype(jnp.float32)
    shifts = math.pi / cycle_len * parity[:, None] * mode_ids[None, :].astype(jnp.float32)
    return (jnp.cos(shifts), jnp.sin(shifts))


def forward_modes(re_part, im_part):
    summed = lax.psum((re_part, im_part), "grp")
    fourier_pair = (summed[0].astype(jnp.bfloat16), summed[1].astype(jnp.bfloat16))
    fourier_pair = (
        lax.all_gather(fourier_pair[0], "real", axis=0, tiled=True),
        lax.all_gather(fourier_pair[1], "real", axis=0, tiled=True),
    )
    fourier_pair = (
        lax.all_to_all(fourier_pair[0], "blk", split_axis=2, concat_axis=1, tiled=True),
        lax.all_to_all(fourier_pair[1], "blk", split_axis=2, concat_axis=1, tiled=True),
    )
    return fourier_pair


def backward_cycles(partial_value):
    summed = lax.psum_scatter(partial_value, "real", scatter_dimension=0, tiled=True)
    reduced = lax.psum(summed, "grp")
    cycle_pair = lax.all_to_all(
        reduced.astype(jnp.bfloat16), "blk", split_axis=2, concat_axis=3, tiled=True
    )
    return cycle_pair


def per_device(
    sky_data, signal_prev, noise_var, mask_flags, cycle_table, m_table, spectrum, legendre
):
    real_dev, cycle_dev, half_len = sky_data.shape
    cycle_len = half_len * lax.axis_size("grp")
    mode_count = m_table.shape[0]
    col_ids = lax.axis_index("grp") * half_len + jnp.arange(half_len, dtype=jnp.int32)
    cos_tab, sin_tab = phase_tables(col_ids, m_table, cycle_len)
    cos_shift, sin_shift = cycle_offsets(cycle_table, m_table, cycle_len)
    weight = mask_flags.astype(jnp.float32) / (noise_var - 0.5)
    messenger = (weight * sky_data + 2.0 * signal_prev) / (weight + 2.0)
    flat_rows = messenger.astype(jnp.bfloat16).reshape(real_dev * cycle_dev, half_len)
    base_cos = jnp.dot(flat_rows, cos_tab, preferred_element_type=jnp.float32).reshape(
        real_dev, cycle_dev, mode_count
    )
    base_sin = -jnp.dot(flat_rows, sin_tab, preferred_element_type=jnp.float32).reshape(
        real_dev, cycle_dev, mode_count
    )
    norm_scale = cycle_len ** (-0.5)
    re_part = (base_cos * cos_shift + base_sin * sin_shift) * norm_scale
    im_part = (base_sin * cos_shift - base_cos * sin_shift) * norm_scale
    fourier_re, fourier_im = forward_modes(re_part, im_part)
    fourier = jnp.stack([fourier_re, fourier_im], 1)
    coefficients = jnp.einsum(
        "mlr,kcrm->kcml", legendre, fourier, preferred_element_type=jnp.float32
    )
    factor = spectrum / (spectrum + 0.5)
    wiener_alm = coefficients * factor
    total_l = legendre.shape[1] * lax.axis_size("grp") * lax.axis_size("real")
    syn_scale = (legendre.shape[2] / total_l) ** 0.5
    partial_value = (
        jnp.einsum(
            "mlr,kcml->kcrm",
            legendre,
            wiener_alm.astype(jnp.bfloat16),
            preferred_element_type=jnp.float32,
        )
        * syn_scale
    )
    cycle_pair = backward_cycles(partial_value)
    cycle_modes = cycle_pair.astype(jnp.float32)
    modes_re = cycle_modes[:, 0]
    modes_im = cycle_modes[:, 1]
    rotated_re = (modes_re * cos_shift - modes_im * sin_shift).astype(jnp.bfloat16)
    rotated_im = (modes_im * cos_shift + modes_re * sin_shift).astype(jnp.bfloat16)
    contract = (((1,), (1,)), ((), ()))
    pixel_sum = lax.dot_general(
        rotated_re.reshape(-1, mode_count), cos_tab, contract, preferred_element_type=jnp.float32
    )
    pixel_sum = pixel_sum - lax.dot_general(
        rotated_im.reshape(-1, mode_count), sin_tab, contract, preferred_element_type=jnp.float32
    )
    signal_next = (pixel_sum * mode_count ** (-0.5)).reshape(real_dev, cycle_dev, half_len)
    return (wiener_alm, signal_next)


def solution(mesh):
    in_specs = (
        P("real", "blk", "grp"),
        P("real", "blk", "grp"),
        P("blk", "grp"),
        P("blk", "grp"),
        P("blk"),
        P(),
        P(("grp", "real")),
        P("blk", ("grp", "real"), None),
    )
    out_specs = (P(None, None, "blk", ("grp", "real")), P("real", "blk", "grp"))

    def step(sky_data, signal_prev, noise_var, mask_flags, cycle_table, m_table, spectrum, legendre):
        fits = gram_form_fits(mesh, sky_data, m_table, legendre)
        return jax.shard_map(
            gram_program if fits else per_device,
            mesh=mesh,
            in_specs=in_specs,
            out_specs=out_specs,
            check_vma=False,
        )(sky_data, signal_prev, noise_var, mask_flags, cycle_table, m_table, spectrum, legendre)

    return step
```

```python
import functools
import math

import jax
import jax.numpy as jnp
from jax import lax
from jax.experimental import pallas as pl
from jax.experimental.pallas import tpu as pltpu
from jax.sharding import PartitionSpec as P

LANES = 128
NT = (((1,), (1,)), ((), ()))
AXES = ("grp", "blk", "real")
PARTS = 2
FORWARD_VMEM = 32 << 20
BACKWARD_VMEM = 16 << 20


def unit_cosine(units, half_turn):
    wrapped = units & (2 * half_turn - 1)
    folded = jnp.minimum(wrapped, 2 * half_turn - wrapped)
    y = (half_turn // 2 - folded).astype(jnp.float32) * (math.pi / half_turn)
    y2 = y * y
    acc = jnp.full_like(y2, -1.0 / math.factorial(11))
    for order, sign in ((9, 1.0), (7, -1.0), (5, 1.0), (3, -1.0), (1, 1.0)):
        acc = acc * y2 + sign / math.factorial(order)
    return acc * y


def log2(size):
    return size.bit_length() - 1


def lane_ids(shape):
    return lax.broadcasted_iota(jnp.int32, shape, len(shape) - 1)


def row_ids(shape):
    return lax.broadcasted_iota(jnp.int32, shape, len(shape) - 2)


def phase_factors(cycles, orders, cycle_len, half_len, group):
    modes = orders.shape[1]
    orders = jnp.concatenate([orders] * (LANES // modes), axis=1)
    quarter = lane_ids((1, LANES)) >> log2(modes)
    quarter_turn = cycle_len // 2
    inner_units = 2 * orders * row_ids((LANES, LANES)) + ((quarter + 1) >> 1) * quarter_turn
    inner = unit_cosine(inner_units, cycle_len)
    rows = 2 * (half_len // LANES)
    row = row_ids((rows, LANES))
    parity = jnp.where((row & 1) == 0, cycles[:, :1], cycles[:, 1:]) & 1
    pixel = group * half_len + LANES * (row >> 1)
    outer_units = orders * (2 * pixel + parity) + (quarter >> 1) * (3 * quarter_turn)
    outer = unit_cosine(outer_units, cycle_len)
    high = inner.astype(jnp.bfloat16)
    low = (inner - high.astype(jnp.float32)).astype(jnp.bfloat16)
    return high, low, outer


def start_copies(sources, targets, sems, first=0):
    copies = [
        pltpu.make_async_copy(source, target, sems.at[first + i])
        for i, (source, target) in enumerate(zip(sources, targets))
    ]
    for copy in copies:
        copy.start()
    return copies


def selections(place_ref, pick_ref, per_block, reals):
    block = lax.axis_index("blk")
    blocks, real_groups = lax.axis_size("blk"), lax.axis_size("real")
    modes, cycles, half = per_block * blocks, 2 * blocks, LANES // 2

    lane = lane_ids((1, LANES))
    row = row_ids((LANES, LANES))
    lane_order = (lane & (half - 1)) >> log2(cycles)
    lane_row = (lane & 1) * half + (lane >> log2(half)) * modes + block * per_block + lane_order
    pick_ref[0] = (row == lane_row).astype(jnp.float32).astype(jnp.bfloat16)
    lane_row = (lane >> log2(half)) * per_block + (lane & (per_block - 1))
    pick_ref[1] = ((row >> log2(cycles)) == lane_row).astype(jnp.float32).astype(jnp.bfloat16)

    spacing = reals + 2
    column = lane_ids((1, place_ref.shape[1]))
    source = (column * (2**16 // spacing + 1)) >> 16
    inside = column - source * spacing
    source = source & (blocks * real_groups - 1)
    source_block = source >> log2(real_groups)
    target = ((source & (real_groups - 1)) * blocks + source_block) * reals + inside
    target = jnp.where(inside < reals, target, blocks * real_groups * reals + source_block)
    place = (row_ids(place_ref.shape) == target).astype(jnp.float32)
    place_ref[...] = place.astype(jnp.bfloat16)


def forward_kernel(
    cycle_len, half_len, syn_scale, reals,
    cycle_hbm, mode_hbm, noise_hbm, mask_hbm, spectrum_hbm, legendre_hbm, sky_hbm, prev_hbm,
    out_ref, inner_ref, outer_ref, place_ref, pick_ref, doubled_ref, factor_ref,
    cycle_ref, mode_ref, noise_ref, mask_ref, spectrum_ref, legendre_ref, sky_ref, prev_ref, gram_ref, sems,
):
    small = start_copies(
        (cycle_hbm, mode_hbm, noise_hbm, mask_hbm, spectrum_hbm, legendre_hbm),
        (cycle_ref, mode_ref, noise_ref, mask_ref, spectrum_ref, legendre_ref),
        sems,
    )
    large = start_copies((sky_hbm, prev_hbm), (sky_ref, prev_ref), sems, len(small))
    group = lax.axis_index("grp")
    per_block = legendre_ref.shape[0] // (2 * lax.axis_size("blk"))
    selections(place_ref, pick_ref, per_block, reals)
    small[0].wait()
    small[1].wait()
    high, low, outer = phase_factors(cycle_ref[...], mode_ref[...], cycle_len, half_len, group)
    inner = jnp.concatenate([high, low], axis=0)
    inner_ref[...] = jnp.concatenate([high, low], axis=1)
    outer_ref[...] = outer
    small[2].wait()
    small[3].wait()
    weight = mask_ref[...].astype(jnp.float32) / (noise_ref[...] - 0.5)
    inverse = 1.0 / (weight + 2.0)
    sky_gain = weight * inverse
    prev_gain = 2.0 * inverse

    for copy in small[4:] + large:
        copy.wait()
    table = legendre_ref[...]
    spectrum = spectrum_ref[...]
    factor = spectrum / (spectrum + 0.5)
    doubled_ref[...] = jnp.concatenate([table, table], axis=0)
    factor_ref[...] = factor
    filtered = (table.astype(jnp.float32) * factor).astype(jnp.bfloat16)
    gram = lax.dot_general(table, filtered, NT, preferred_element_type=jnp.float32)
    table_rows = table.shape[0]
    pixel_rows = outer.shape[0]
    blocks, real_groups = lax.axis_size("blk"), lax.axis_size("real")
    cycles = 2 * blocks
    same = (row_ids(gram.shape) >> log2(cycles)) == (lane_ids((1, table_rows)) >> log2(cycles))
    gram = jnp.where(same, gram, 0.0).reshape(table_rows // cycles, cycles, table_rows).sum(axis=0)
    gram = gram * syn_scale
    gram_ref[...] = jnp.concatenate([gram, gram], axis=1)
    even, odd = gram_ref[pl.ds(0, blocks, stride=2), :], gram_ref[pl.ds(1, blocks, stride=2), :]
    gram = jnp.where(lane_ids(even.shape) < LANES // 2, even, odd)
    gram_high = gram.astype(jnp.bfloat16).astype(jnp.float32)
    gram_low = gram - gram_high

    shape = (reals, pixel_rows, LANES)
    messenger = sky_ref[...].reshape(shape) * sky_gain + prev_ref[...].reshape(shape) * prev_gain
    rows = messenger.reshape(-1, LANES).astype(jnp.bfloat16)
    partial = jnp.dot(jnp.concatenate([rows, rows], axis=1), inner, preferred_element_type=jnp.float32)
    turned = partial.reshape(shape) * outer
    summed = turned.reshape(reals, pixel_rows // 8, 8, LANES).sum(axis=1)
    summed = summed.reshape(reals * 8, LANES)
    summed = summed + pltpu.roll(summed, LANES // 2, 1)
    own = (row_ids(summed.shape) & 1) == (lane_ids(summed.shape) >= LANES // 2)
    fourier = jnp.where(own, summed, 0.0).reshape(reals, 8, LANES).sum(axis=1) * cycle_len**-0.5
    rows = []
    for b in range(blocks):
        rows += [fourier, gram_high[b : b + 1], gram_low[b : b + 1]] * real_groups
    rows = jnp.concatenate(rows, axis=0).astype(jnp.bfloat16)
    for g in range(lax.axis_size("grp")):
        out_ref[pl.ds(g * rows.shape[0], rows.shape[0]), :] = rows


def backward_kernel(
    blocks, real_groups, reals, parts,
    gathered_ref, inner_ref, outer_ref, place_ref, pick_ref, table_ref, factor_ref,
    wiener_hbm, signal_hbm, wiener_ref, signal_ref, fourier_ref, out_sems,
):
    real_group = lax.axis_index("real")
    cycles = 2 * blocks
    per_block = table_ref.shape[0] // (2 * cycles)
    modes = per_block * blocks
    pixel_rows = outer_ref.shape[0]
    half = LANES // 2
    lane = lane_ids((1, LANES))
    holder = (lane & (modes - 1)) >> log2(per_block)
    lane_block = (lane & (cycles - 1)) >> 1
    total_reals = real_groups * reals
    fourier_rows = blocks * total_reals
    placed = jnp.dot(place_ref[...], gathered_ref[...], preferred_element_type=jnp.float32)
    fourier_ref[...] = placed[:fourier_rows]

    coeff_rows = jnp.dot(
        placed[:fourier_rows].astype(jnp.bfloat16), pick_ref[0], preferred_element_type=jnp.float32
    ).reshape(real_groups, blocks, reals, LANES)
    columns = jnp.zeros((total_reals, LANES), jnp.float32)
    for b in range(blocks):
        one = coeff_rows[:, b].reshape(total_reals, LANES)
        columns = columns + jnp.where(lane_block == b, one, 0.0)
    table = table_ref[...]
    factor = factor_ref[...]
    stores = []
    own = (lane >> log2(cycles)) == row_ids((2 * per_block, LANES))
    upper = row_ids((1, 2 * per_block, LANES)) < per_block
    for y in range(real_groups):
        span = slice(y * reals, (y + 1) * reals)
        pieces = jnp.where(own, columns[span, None, :], 0.0)
        filtered = factor * jnp.dot(
            pieces.reshape(-1, LANES).astype(jnp.bfloat16), table, preferred_element_type=jnp.float32
        )
        for pair in range(wiener_ref.shape[2]):
            one, two = (
                filtered[:, tile * LANES : (tile + 1) * LANES].reshape(reals, 2 * per_block, LANES)
                for tile in (2 * pair, 2 * pair + 1)
            )
            wiener_ref[span, 0, pair] = jnp.where(upper, one, pltpu.roll(two, per_block, 1))
            wiener_ref[span, 1, pair] = jnp.where(upper, pltpu.roll(one, per_block, 1), two)
        span = pl.ds(y * reals, reals)
        stores += start_copies([wiener_ref.at[span]], [wiener_hbm.at[span]], out_sems, len(stores))

    gram_all = jnp.where(
        (lane & (cycles - 1)) == row_ids((cycles, LANES)), placed[fourier_rows:, None, :], 0.0
    ).reshape(blocks * cycles, LANES)
    gram_high = gram_all.astype(jnp.bfloat16)
    gram_low = (gram_all - gram_high.astype(jnp.float32)).astype(jnp.bfloat16)
    gram_rows = jnp.dot(
        jnp.concatenate([gram_high, gram_low], axis=1),
        jnp.concatenate([pick_ref[1], pick_ref[1]], axis=0),
        preferred_element_type=jnp.float32,
    ).reshape(blocks, cycles, LANES)
    gram = jnp.zeros((cycles, LANES), jnp.float32)
    for b in range(blocks):
        gram = gram + jnp.where(holder == b, gram_rows[b], 0.0)

    first = lane < half
    cycle_modes = jnp.zeros((reals, LANES), jnp.float32)
    for b in range(blocks):
        first_row = pl.multiple_of((real_group * blocks + b) * reals, reals)
        pair = fourier_ref[pl.ds(first_row, reals), :]
        turned = pltpu.roll(pair, half, 1)
        cycle_modes = cycle_modes + jnp.where(first, pair, turned) * gram[2 * b : 2 * b + 1]
        cycle_modes = cycle_modes + jnp.where(first, turned, pair) * gram[2 * b + 1 : 2 * b + 2]
    cycle_modes = cycle_modes * modes**-0.5
    turned = pltpu.roll(cycle_modes, half, 1)
    even = jnp.where(first, cycle_modes, turned)
    odd = jnp.where(first, turned, cycle_modes)
    parity = (row_ids((1, 8, LANES)) & 1) == 0
    spread = jnp.where(parity, even[:, None, :], odd[:, None, :])
    inner = inner_ref[...]
    outer = outer_ref[...].reshape(1, pixel_rows // 8, 8, LANES)
    part_reals = reals // parts
    for i in range(parts):
        rotated = spread[i * part_reals : (i + 1) * part_reals, None] * outer
        rotated = rotated.reshape(part_reals * pixel_rows, LANES).astype(jnp.bfloat16)
        span = pl.ds(i * part_reals * pixel_rows, part_reals * pixel_rows)
        signal_ref[span, :] = lax.dot_general(
            jnp.concatenate([rotated, rotated], axis=1), inner, NT, preferred_element_type=jnp.float32
        )
        stores += start_copies([signal_ref.at[span]], [signal_hbm.at[span]], out_sems, len(stores))
    for store in stores:
        store.wait()


def split_tiles(array):
    lead, rows, columns = array.shape[:-2], array.shape[-2], array.shape[-1]
    split = array.reshape(*lead, rows, columns // LANES, LANES)
    return jnp.swapaxes(split, -2, -3).reshape(-1, LANES)


def gram_program(
    sky_data, signal_prev, noise_var, mask_flags, cycle_table, m_table, spectrum, legendre
):
    reals, cycle_dev, half_len = sky_data.shape
    groups, blocks, real_groups = (lax.axis_size(name) for name in AXES)
    cycle_len = half_len * groups
    per_block, multipoles, cycles = legendre.shape
    total_l = multipoles * groups * real_groups
    tiles = multipoles // LANES
    hbm = pl.BlockSpec(memory_space=pltpu.HBM)
    vmem = pl.BlockSpec(memory_space=pltpu.VMEM)
    orders = m_table[None, :]
    cycles_row = cycle_table[None, :]
    spectrum_row = spectrum[None, :]
    table = legendre.transpose(0, 2, 1).reshape(per_block * cycles, multipoles)
    inputs = (
        cycles_row, orders, split_tiles(noise_var), split_tiles(mask_flags), spectrum_row, table,
        split_tiles(sky_data), split_tiles(signal_prev),
    )
    sources = groups * blocks * real_groups
    total_reals = reals * real_groups
    local, *prepared = pl.pallas_call(
        functools.partial(forward_kernel, cycle_len, half_len, (cycles / total_l) ** 0.5, reals),
        out_shape=(
            jax.ShapeDtypeStruct((sources * (reals + 2), LANES), jnp.bfloat16),
            jax.ShapeDtypeStruct((LANES, 2 * LANES), jnp.bfloat16),
            jax.ShapeDtypeStruct((cycle_dev * half_len // LANES, LANES), jnp.float32),
            jax.ShapeDtypeStruct((blocks * (total_reals + 1), sources * (reals + 2)), jnp.bfloat16),
            jax.ShapeDtypeStruct((2, LANES, LANES), jnp.bfloat16),
            jax.ShapeDtypeStruct((2 * table.shape[0], multipoles), jnp.bfloat16),
            jax.ShapeDtypeStruct((1, multipoles), jnp.float32),
        ),
        in_specs=[hbm] * 8,
        out_specs=(vmem,) * 7,
        scratch_shapes=[pltpu.VMEM(x.shape, x.dtype) for x in inputs]
        + [pltpu.VMEM((cycles, LANES), jnp.float32), pltpu.SemaphoreType.DMA((8,))],
        compiler_params=pltpu.CompilerParams(vmem_limit_bytes=FORWARD_VMEM),
    )(*(pltpu.with_memory_space_constraint(x, pltpu.HBM) for x in inputs))
    pairs = local.reshape(sources, reals // 2 + 1, 2, LANES)
    gathered = lax.all_to_all(pairs, AXES, 0, 0, tiled=True).reshape(local.shape)
    outputs = (
        jax.ShapeDtypeStruct((total_reals, 2, tiles // 2, 2 * per_block, LANES), jnp.float32),
        jax.ShapeDtypeStruct((reals * cycle_dev * half_len // LANES, LANES), jnp.float32),
    )
    wiener, signal = pl.pallas_call(
        functools.partial(backward_kernel, blocks, real_groups, reals, PARTS),
        out_shape=outputs,
        in_specs=[vmem] * 7,
        out_specs=(hbm, hbm),
        scratch_shapes=[pltpu.VMEM(x.shape, x.dtype) for x in outputs]
        + [pltpu.VMEM((blocks * total_reals, LANES), jnp.float32)]
        + [pltpu.SemaphoreType.DMA((real_groups + PARTS,))],
        compiler_params=pltpu.CompilerParams(vmem_limit_bytes=BACKWARD_VMEM),
    )(gathered, *prepared)
    wiener = wiener.reshape(total_reals, 2, tiles, per_block, LANES).transpose(0, 1, 3, 2, 4)
    signal = signal.reshape(reals, half_len // LANES, cycle_dev, LANES).transpose(0, 2, 1, 3)
    return (
        wiener.reshape(total_reals, 2, per_block, multipoles),
        signal.reshape(sky_data.shape),
    )


def gram_form_fits(mesh, sky_data, m_table, legendre):
    groups, blocks, real_groups = (mesh.shape[name] for name in AXES)
    reals, cycles, cycle_len = sky_data.shape
    modes = m_table.shape[0]
    per_block = modes // blocks
    multipoles = legendre.shape[1] // (groups * real_groups)
    half_len = cycle_len // groups
    reals_dev = reals // real_groups
    return (
        cycles < 2 * reals
        and 4 * modes == LANES
        and cycles == 2 * blocks
        and all(size & (size - 1) == 0 for size in (blocks, modes, cycles, real_groups))
        and 2 * reals * cycles < 2**12
        and 2 * per_block * cycles == LANES
        and cycle_len & (cycle_len - 1) == 0
        and half_len % (4 * LANES) == 0
        and multipoles % (2 * LANES) == 0
        and per_block == 4
        and reals_dev % 16 == 0
        and reals_dev % PARTS == 0
        and cycles % 16 == 0
    )


def phase_tables(col_ids, mode_ids, cycle_len):
    product_ids = col_ids[:, None] * mode_ids[None, :] % cycle_len
    angles = product_ids.astype(jnp.float32) * (2.0 * math.pi / cycle_len)
    return (jnp.cos(angles).astype(jnp.bfloat16), jnp.sin(angles).astype(jnp.bfloat16))


def cycle_offsets(cycle_ids, mode_ids, cycle_len):
    parity = (cycle_ids % 2).astype(jnp.float32)
    shifts = math.pi / cycle_len * parity[:, None] * mode_ids[None, :].astype(jnp.float32)
    return (jnp.cos(shifts), jnp.sin(shifts))


def forward_modes(re_part, im_part):
    summed = lax.psum((re_part, im_part), "grp")
    fourier_pair = (summed[0].astype(jnp.bfloat16), summed[1].astype(jnp.bfloat16))
    fourier_pair = (
        lax.all_gather(fourier_pair[0], "real", axis=0, tiled=True),
        lax.all_gather(fourier_pair[1], "real", axis=0, tiled=True),
    )
    fourier_pair = (
        lax.all_to_all(fourier_pair[0], "blk", split_axis=2, concat_axis=1, tiled=True),
        lax.all_to_all(fourier_pair[1], "blk", split_axis=2, concat_axis=1, tiled=True),
    )
    return fourier_pair


def backward_cycles(partial_value):
    summed = lax.psum_scatter(partial_value, "real", scatter_dimension=0, tiled=True)
    reduced = lax.psum(summed, "grp")
    cycle_pair = lax.all_to_all(
        reduced.astype(jnp.bfloat16), "blk", split_axis=2, concat_axis=3, tiled=True
    )
    return cycle_pair


def per_device(
    sky_data, signal_prev, noise_var, mask_flags, cycle_table, m_table, spectrum, legendre
):
    real_dev, cycle_dev, half_len = sky_data.shape
    cycle_len = half_len * lax.axis_size("grp")
    mode_count = m_table.shape[0]
    col_ids = lax.axis_index("grp") * half_len + jnp.arange(half_len, dtype=jnp.int32)
    cos_tab, sin_tab = phase_tables(col_ids, m_table, cycle_len)
    cos_shift, sin_shift = cycle_offsets(cycle_table, m_table, cycle_len)
    weight = mask_flags.astype(jnp.float32) / (noise_var - 0.5)
    messenger = (weight * sky_data + 2.0 * signal_prev) / (weight + 2.0)
    flat_rows = messenger.astype(jnp.bfloat16).reshape(real_dev * cycle_dev, half_len)
    base_cos = jnp.dot(flat_rows, cos_tab, preferred_element_type=jnp.float32).reshape(
        real_dev, cycle_dev, mode_count
    )
    base_sin = -jnp.dot(flat_rows, sin_tab, preferred_element_type=jnp.float32).reshape(
        real_dev, cycle_dev, mode_count
    )
    norm_scale = cycle_len ** (-0.5)
    re_part = (base_cos * cos_shift + base_sin * sin_shift) * norm_scale
    im_part = (base_sin * cos_shift - base_cos * sin_shift) * norm_scale
    fourier_re, fourier_im = forward_modes(re_part, im_part)
    fourier = jnp.stack([fourier_re, fourier_im], 1)
    coefficients = jnp.einsum(
        "mlr,kcrm->kcml", legendre, fourier, preferred_element_type=jnp.float32
    )
    factor = spectrum / (spectrum + 0.5)
    wiener_alm = coefficients * factor
    total_l = legendre.shape[1] * lax.axis_size("grp") * lax.axis_size("real")
    syn_scale = (legendre.shape[2] / total_l) ** 0.5
    partial_value = (
        jnp.einsum(
            "mlr,kcml->kcrm",
            legendre,
            wiener_alm.astype(jnp.bfloat16),
            preferred_element_type=jnp.float32,
        )
        * syn_scale
    )
    cycle_pair = backward_cycles(partial_value)
    cycle_modes = cycle_pair.astype(jnp.float32)
    modes_re = cycle_modes[:, 0]
    modes_im = cycle_modes[:, 1]
    rotated_re = (modes_re * cos_shift - modes_im * sin_shift).astype(jnp.bfloat16)
    rotated_im = (modes_im * cos_shift + modes_re * sin_shift).astype(jnp.bfloat16)
    contract = (((1,), (1,)), ((), ()))
    pixel_sum = lax.dot_general(
        rotated_re.reshape(-1, mode_count), cos_tab, contract, preferred_element_type=jnp.float32
    )
    pixel_sum = pixel_sum - lax.dot_general(
        rotated_im.reshape(-1, mode_count), sin_tab, contract, preferred_element_type=jnp.float32
    )
    signal_next = (pixel_sum * mode_count ** (-0.5)).reshape(real_dev, cycle_dev, half_len)
    return (wiener_alm, signal_next)


def solution(mesh):
    in_specs = (
        P("real", "blk", "grp"),
        P("real", "blk", "grp"),
        P("blk", "grp"),
        P("blk", "grp"),
        P("blk"),
        P(),
        P(("grp", "real")),
        P("blk", ("grp", "real"), None),
    )
    out_specs = (P(None, None, "blk", ("grp", "real")), P("real", "blk", "grp"))

    def step(sky_data, signal_prev, noise_var, mask_flags, cycle_table, m_table, spectrum, legendre):
        fits = gram_form_fits(mesh, sky_data, m_table, legendre)
        return jax.shard_map(
            gram_program if fits else per_device,
            mesh=mesh,
            in_specs=in_specs,
            out_specs=out_specs,
            check_vma=False,
        )(sky_data, signal_prev, noise_var, mask_flags, cycle_table, m_table, spectrum, legendre)

    return step
```

```python
import functools
import math

import jax
import jax.numpy as jnp
from jax import lax
from jax.experimental import pallas as pl
from jax.experimental.pallas import tpu as pltpu
from jax.sharding import PartitionSpec as P

LANES = 128
NT = (((1,), (1,)), ((), ()))
AXES = ("grp", "blk", "real")
PARTS = 4
FORWARD_VMEM = 32 << 20
BACKWARD_VMEM = 16 << 20


def unit_cosine(units, half_turn):
    wrapped = units & (2 * half_turn - 1)
    folded = jnp.minimum(wrapped, 2 * half_turn - wrapped)
    y = (half_turn // 2 - folded).astype(jnp.float32) * (math.pi / half_turn)
    y2 = y * y
    acc = jnp.full_like(y2, -1.0 / math.factorial(11))
    for order, sign in ((9, 1.0), (7, -1.0), (5, 1.0), (3, -1.0), (1, 1.0)):
        acc = acc * y2 + sign / math.factorial(order)
    return acc * y


def log2(size):
    return size.bit_length() - 1


def lane_ids(shape):
    return lax.broadcasted_iota(jnp.int32, shape, len(shape) - 1)


def row_ids(shape):
    return lax.broadcasted_iota(jnp.int32, shape, len(shape) - 2)


def phase_factors(cycles, orders, cycle_len, half_len, group):
    modes = orders.shape[1]
    orders = jnp.concatenate([orders] * (LANES // modes), axis=1)
    quarter = lane_ids((1, LANES)) >> log2(modes)
    quarter_turn = cycle_len // 2
    inner_units = 2 * orders * row_ids((LANES, LANES)) + ((quarter + 1) >> 1) * quarter_turn
    inner = unit_cosine(inner_units, cycle_len)
    rows = 2 * (half_len // LANES)
    row = row_ids((rows, LANES))
    parity = jnp.where((row & 1) == 0, cycles[:, :1], cycles[:, 1:]) & 1
    pixel = group * half_len + LANES * (row >> 1)
    outer_units = orders * (2 * pixel + parity) + (quarter >> 1) * (3 * quarter_turn)
    outer = unit_cosine(outer_units, cycle_len)
    high = inner.astype(jnp.bfloat16)
    low = (inner - high.astype(jnp.float32)).astype(jnp.bfloat16)
    return high, low, outer


def start_copies(sources, targets, sems, first=0):
    copies = [
        pltpu.make_async_copy(source, target, sems.at[first + i])
        for i, (source, target) in enumerate(zip(sources, targets))
    ]
    for copy in copies:
        copy.start()
    return copies


def selections(place_ref, pick_ref, per_block, reals):
    block = lax.axis_index("blk")
    blocks, real_groups = lax.axis_size("blk"), lax.axis_size("real")
    modes, cycles, half = per_block * blocks, 2 * blocks, LANES // 2

    lane = lane_ids((1, LANES))
    row = row_ids((LANES, LANES))
    lane_order = (lane & (half - 1)) >> log2(cycles)
    lane_row = (lane & 1) * half + (lane >> log2(half)) * modes + block * per_block + lane_order
    pick_ref[0] = (row == lane_row).astype(jnp.float32).astype(jnp.bfloat16)
    lane_row = (lane >> log2(half)) * per_block + (lane & (per_block - 1))
    pick_ref[1] = ((row >> log2(cycles)) == lane_row).astype(jnp.float32).astype(jnp.bfloat16)

    spacing = reals + 2
    column = lane_ids((1, place_ref.shape[1]))
    source = (column * (2**16 // spacing + 1)) >> 16
    inside = column - source * spacing
    source = source & (blocks * real_groups - 1)
    source_block = source >> log2(real_groups)
    target = ((source & (real_groups - 1)) * blocks + source_block) * reals + inside
    target = jnp.where(inside < reals, target, blocks * real_groups * reals + source_block)
    place = (row_ids(place_ref.shape) == target).astype(jnp.float32)
    place_ref[...] = place.astype(jnp.bfloat16)


def forward_kernel(
    cycle_len, half_len, syn_scale, reals,
    cycle_hbm, mode_hbm, noise_hbm, mask_hbm, spectrum_hbm, legendre_hbm, sky_hbm, prev_hbm,
    out_ref, inner_ref, outer_ref, place_ref, pick_ref, doubled_ref, factor_ref,
    cycle_ref, mode_ref, noise_ref, mask_ref, spectrum_ref, legendre_ref, sky_ref, prev_ref, gram_ref, sems,
):
    small = start_copies(
        (cycle_hbm, mode_hbm, noise_hbm, mask_hbm, spectrum_hbm, legendre_hbm),
        (cycle_ref, mode_ref, noise_ref, mask_ref, spectrum_ref, legendre_ref),
        sems,
    )
    large = start_copies((sky_hbm, prev_hbm), (sky_ref, prev_ref), sems, len(small))
    group = lax.axis_index("grp")
    per_block = legendre_ref.shape[0] // (2 * lax.axis_size("blk"))
    selections(place_ref, pick_ref, per_block, reals)
    small[0].wait()
    small[1].wait()
    high, low, outer = phase_factors(cycle_ref[...], mode_ref[...], cycle_len, half_len, group)
    inner = jnp.concatenate([high, low], axis=0)
    inner_ref[...] = jnp.concatenate([high, low], axis=1)
    outer_ref[...] = outer
    small[2].wait()
    small[3].wait()
    weight = mask_ref[...].astype(jnp.float32) / (noise_ref[...] - 0.5)
    inverse = 1.0 / (weight + 2.0)
    sky_gain = weight * inverse
    prev_gain = 2.0 * inverse

    for copy in small[4:] + large:
        copy.wait()
    table = legendre_ref[...]
    spectrum = spectrum_ref[...]
    factor = spectrum / (spectrum + 0.5)
    doubled_ref[...] = jnp.concatenate([table, table], axis=0)
    factor_ref[...] = factor
    filtered = (table.astype(jnp.float32) * factor).astype(jnp.bfloat16)
    gram = lax.dot_general(table, filtered, NT, preferred_element_type=jnp.float32)
    table_rows = table.shape[0]
    pixel_rows = outer.shape[0]
    blocks, real_groups = lax.axis_size("blk"), lax.axis_size("real")
    cycles = 2 * blocks
    same = (row_ids(gram.shape) >> log2(cycles)) == (lane_ids((1, table_rows)) >> log2(cycles))
    gram = jnp.where(same, gram, 0.0).reshape(table_rows // cycles, cycles, table_rows).sum(axis=0)
    gram = gram * syn_scale
    gram_ref[...] = jnp.concatenate([gram, gram], axis=1)
    even, odd = gram_ref[pl.ds(0, blocks, stride=2), :], gram_ref[pl.ds(1, blocks, stride=2), :]
    gram = jnp.where(lane_ids(even.shape) < LANES // 2, even, odd)
    gram_high = gram.astype(jnp.bfloat16).astype(jnp.float32)
    gram_low = gram - gram_high

    shape = (reals, pixel_rows, LANES)
    messenger = sky_ref[...].reshape(shape) * sky_gain + prev_ref[...].reshape(shape) * prev_gain
    rows = messenger.reshape(-1, LANES).astype(jnp.bfloat16)
    partial = jnp.dot(jnp.concatenate([rows, rows], axis=1), inner, preferred_element_type=jnp.float32)
    turned = partial.reshape(shape) * outer
    summed = turned.reshape(reals, pixel_rows // 8, 8, LANES).sum(axis=1)
    summed = summed.reshape(reals * 8, LANES)
    summed = summed + pltpu.roll(summed, LANES // 2, 1)
    own = (row_ids(summed.shape) & 1) == (lane_ids(summed.shape) >= LANES // 2)
    fourier = jnp.where(own, summed, 0.0).reshape(reals, 8, LANES).sum(axis=1) * cycle_len**-0.5
    rows = []
    for b in range(blocks):
        rows += [fourier, gram_high[b : b + 1], gram_low[b : b + 1]] * real_groups
    rows = jnp.concatenate(rows, axis=0).astype(jnp.bfloat16)
    for g in range(lax.axis_size("grp")):
        out_ref[pl.ds(g * rows.shape[0], rows.shape[0]), :] = rows


def backward_kernel(
    blocks, real_groups, reals, parts,
    gathered_ref, inner_ref, outer_ref, place_ref, pick_ref, table_ref, factor_ref,
    wiener_hbm, signal_hbm, wiener_ref, signal_ref, fourier_ref, out_sems,
):
    real_group = lax.axis_index("real")
    cycles = 2 * blocks
    per_block = table_ref.shape[0] // (2 * cycles)
    modes = per_block * blocks
    pixel_rows = outer_ref.shape[0]
    half = LANES // 2
    lane = lane_ids((1, LANES))
    holder = (lane & (modes - 1)) >> log2(per_block)
    lane_block = (lane & (cycles - 1)) >> 1
    total_reals = real_groups * reals
    fourier_rows = blocks * total_reals
    placed = jnp.dot(place_ref[...], gathered_ref[...], preferred_element_type=jnp.float32)
    fourier_ref[...] = placed[:fourier_rows]

    coeff_rows = jnp.dot(
        placed[:fourier_rows].astype(jnp.bfloat16), pick_ref[0], preferred_element_type=jnp.float32
    ).reshape(real_groups, blocks, reals, LANES)
    columns = jnp.zeros((total_reals, LANES), jnp.float32)
    for b in range(blocks):
        one = coeff_rows[:, b].reshape(total_reals, LANES)
        columns = columns + jnp.where(lane_block == b, one, 0.0)
    table = table_ref[...]
    factor = factor_ref[...]
    stores = []
    own = (lane >> log2(cycles)) == row_ids((2 * per_block, LANES))
    upper = row_ids((1, 2 * per_block, LANES)) < per_block
    pieces = jnp.where(own, columns[:, None, :], 0.0).reshape(-1, LANES).astype(jnp.bfloat16)
    for pair in range(wiener_ref.shape[2]):
        span = slice(2 * pair * LANES, 2 * (pair + 1) * LANES)
        filtered = factor[:, span] * jnp.dot(pieces, table[:, span], preferred_element_type=jnp.float32)
        one, two = (
            filtered[:, tile * LANES : (tile + 1) * LANES].reshape(total_reals, 2 * per_block, LANES)
            for tile in range(2)
        )
        wiener_ref[:, 0, pair] = jnp.where(upper, one, pltpu.roll(two, per_block, 1))
        wiener_ref[:, 1, pair] = jnp.where(upper, pltpu.roll(one, per_block, 1), two)
        stores += start_copies([wiener_ref.at[:, :, pair]], [wiener_hbm.at[:, :, pair]], out_sems, pair)

    gram_all = jnp.where(
        (lane & (cycles - 1)) == row_ids((cycles, LANES)), placed[fourier_rows:, None, :], 0.0
    ).reshape(blocks * cycles, LANES)
    gram_high = gram_all.astype(jnp.bfloat16)
    gram_low = (gram_all - gram_high.astype(jnp.float32)).astype(jnp.bfloat16)
    gram_rows = jnp.dot(
        jnp.concatenate([gram_high, gram_low], axis=1),
        jnp.concatenate([pick_ref[1], pick_ref[1]], axis=0),
        preferred_element_type=jnp.float32,
    ).reshape(blocks, cycles, LANES)
    gram = jnp.zeros((cycles, LANES), jnp.float32)
    for b in range(blocks):
        gram = gram + jnp.where(holder == b, gram_rows[b], 0.0)

    first = lane < half
    cycle_modes = jnp.zeros((reals, LANES), jnp.float32)
    for b in range(blocks):
        first_row = pl.multiple_of((real_group * blocks + b) * reals, reals)
        pair = fourier_ref[pl.ds(first_row, reals), :]
        turned = pltpu.roll(pair, half, 1)
        cycle_modes = cycle_modes + jnp.where(first, pair, turned) * gram[2 * b : 2 * b + 1]
        cycle_modes = cycle_modes + jnp.where(first, turned, pair) * gram[2 * b + 1 : 2 * b + 2]
    cycle_modes = cycle_modes * modes**-0.5
    turned = pltpu.roll(cycle_modes, half, 1)
    even = jnp.where(first, cycle_modes, turned)
    odd = jnp.where(first, turned, cycle_modes)
    parity = (row_ids((1, 8, LANES)) & 1) == 0
    spread = jnp.where(parity, even[:, None, :], odd[:, None, :])
    inner = inner_ref[...]
    outer = outer_ref[...].reshape(1, pixel_rows // 8, 8, LANES)
    part_reals = reals // parts
    for i in range(parts):
        rotated = spread[i * part_reals : (i + 1) * part_reals, None] * outer
        rotated = rotated.reshape(part_reals * pixel_rows, LANES).astype(jnp.bfloat16)
        span = pl.ds(i * part_reals * pixel_rows, part_reals * pixel_rows)
        signal_ref[span, :] = lax.dot_general(
            jnp.concatenate([rotated, rotated], axis=1), inner, NT, preferred_element_type=jnp.float32
        )
        stores += start_copies([signal_ref.at[span]], [signal_hbm.at[span]], out_sems, len(stores))
    for store in stores:
        store.wait()


def split_tiles(array):
    lead, rows, columns = array.shape[:-2], array.shape[-2], array.shape[-1]
    split = array.reshape(*lead, rows, columns // LANES, LANES)
    return jnp.swapaxes(split, -2, -3).reshape(-1, LANES)


def gram_program(
    sky_data, signal_prev, noise_var, mask_flags, cycle_table, m_table, spectrum, legendre
):
    reals, cycle_dev, half_len = sky_data.shape
    groups, blocks, real_groups = (lax.axis_size(name) for name in AXES)
    cycle_len = half_len * groups
    per_block, multipoles, cycles = legendre.shape
    total_l = multipoles * groups * real_groups
    tiles = multipoles // LANES
    hbm = pl.BlockSpec(memory_space=pltpu.HBM)
    vmem = pl.BlockSpec(memory_space=pltpu.VMEM)
    orders = m_table[None, :]
    cycles_row = cycle_table[None, :]
    spectrum_row = spectrum[None, :]
    table = legendre.transpose(0, 2, 1).reshape(per_block * cycles, multipoles)
    inputs = (
        cycles_row, orders, split_tiles(noise_var), split_tiles(mask_flags), spectrum_row, table,
        split_tiles(sky_data), split_tiles(signal_prev),
    )
    sources = groups * blocks * real_groups
    total_reals = reals * real_groups
    local, *prepared = pl.pallas_call(
        functools.partial(forward_kernel, cycle_len, half_len, (cycles / total_l) ** 0.5, reals),
        out_shape=(
            jax.ShapeDtypeStruct((sources * (reals + 2), LANES), jnp.bfloat16),
            jax.ShapeDtypeStruct((LANES, 2 * LANES), jnp.bfloat16),
            jax.ShapeDtypeStruct((cycle_dev * half_len // LANES, LANES), jnp.float32),
            jax.ShapeDtypeStruct((blocks * (total_reals + 1), sources * (reals + 2)), jnp.bfloat16),
            jax.ShapeDtypeStruct((2, LANES, LANES), jnp.bfloat16),
            jax.ShapeDtypeStruct((2 * table.shape[0], multipoles), jnp.bfloat16),
            jax.ShapeDtypeStruct((1, multipoles), jnp.float32),
        ),
        in_specs=[hbm] * 8,
        out_specs=(vmem,) * 7,
        scratch_shapes=[pltpu.VMEM(x.shape, x.dtype) for x in inputs]
        + [pltpu.VMEM((cycles, LANES), jnp.float32), pltpu.SemaphoreType.DMA((8,))],
        compiler_params=pltpu.CompilerParams(vmem_limit_bytes=FORWARD_VMEM),
    )(*(pltpu.with_memory_space_constraint(x, pltpu.HBM) for x in inputs))
    pairs = local.reshape(sources, reals // 2 + 1, 2, LANES)
    gathered = lax.all_to_all(pairs, AXES, 0, 0, tiled=True).reshape(local.shape)
    outputs = (
        jax.ShapeDtypeStruct((total_reals, 2, tiles // 2, 2 * per_block, LANES), jnp.float32),
        jax.ShapeDtypeStruct((reals * cycle_dev * half_len // LANES, LANES), jnp.float32),
    )
    wiener, signal = pl.pallas_call(
        functools.partial(backward_kernel, blocks, real_groups, reals, PARTS),
        out_shape=outputs,
        in_specs=[vmem] * 7,
        out_specs=(hbm, hbm),
        scratch_shapes=[pltpu.VMEM(x.shape, x.dtype) for x in outputs]
        + [pltpu.VMEM((blocks * total_reals, LANES), jnp.float32)]
        + [pltpu.SemaphoreType.DMA((tiles // 2 + PARTS,))],
        compiler_params=pltpu.CompilerParams(vmem_limit_bytes=BACKWARD_VMEM),
    )(gathered, *prepared)
    wiener = wiener.reshape(total_reals, 2, tiles, per_block, LANES).transpose(0, 1, 3, 2, 4)
    signal = signal.reshape(reals, half_len // LANES, cycle_dev, LANES).transpose(0, 2, 1, 3)
    return (
        wiener.reshape(total_reals, 2, per_block, multipoles),
        signal.reshape(sky_data.shape),
    )


def gram_form_fits(mesh, sky_data, m_table, legendre):
    groups, blocks, real_groups = (mesh.shape[name] for name in AXES)
    reals, cycles, cycle_len = sky_data.shape
    modes = m_table.shape[0]
    per_block = modes // blocks
    multipoles = legendre.shape[1] // (groups * real_groups)
    half_len = cycle_len // groups
    reals_dev = reals // real_groups
    return (
        cycles < 2 * reals
        and 4 * modes == LANES
        and cycles == 2 * blocks
        and all(size & (size - 1) == 0 for size in (blocks, modes, cycles, real_groups))
        and 2 * reals * cycles < 2**12
        and 2 * per_block * cycles == LANES
        and cycle_len & (cycle_len - 1) == 0
        and half_len % (4 * LANES) == 0
        and multipoles % (2 * LANES) == 0
        and per_block == 4
        and reals_dev % 16 == 0
        and reals_dev % PARTS == 0
        and cycles % 16 == 0
    )


def phase_tables(col_ids, mode_ids, cycle_len):
    product_ids = col_ids[:, None] * mode_ids[None, :] % cycle_len
    angles = product_ids.astype(jnp.float32) * (2.0 * math.pi / cycle_len)
    return (jnp.cos(angles).astype(jnp.bfloat16), jnp.sin(angles).astype(jnp.bfloat16))


def cycle_offsets(cycle_ids, mode_ids, cycle_len):
    parity = (cycle_ids % 2).astype(jnp.float32)
    shifts = math.pi / cycle_len * parity[:, None] * mode_ids[None, :].astype(jnp.float32)
    return (jnp.cos(shifts), jnp.sin(shifts))


def forward_modes(re_part, im_part):
    summed = lax.psum((re_part, im_part), "grp")
    fourier_pair = (summed[0].astype(jnp.bfloat16), summed[1].astype(jnp.bfloat16))
    fourier_pair = (
        lax.all_gather(fourier_pair[0], "real", axis=0, tiled=True),
        lax.all_gather(fourier_pair[1], "real", axis=0, tiled=True),
    )
    fourier_pair = (
        lax.all_to_all(fourier_pair[0], "blk", split_axis=2, concat_axis=1, tiled=True),
        lax.all_to_all(fourier_pair[1], "blk", split_axis=2, concat_axis=1, tiled=True),
    )
    return fourier_pair


def backward_cycles(partial_value):
    summed = lax.psum_scatter(partial_value, "real", scatter_dimension=0, tiled=True)
    reduced = lax.psum(summed, "grp")
    cycle_pair = lax.all_to_all(
        reduced.astype(jnp.bfloat16), "blk", split_axis=2, concat_axis=3, tiled=True
    )
    return cycle_pair


def per_device(
    sky_data, signal_prev, noise_var, mask_flags, cycle_table, m_table, spectrum, legendre
):
    real_dev, cycle_dev, half_len = sky_data.shape
    cycle_len = half_len * lax.axis_size("grp")
    mode_count = m_table.shape[0]
    col_ids = lax.axis_index("grp") * half_len + jnp.arange(half_len, dtype=jnp.int32)
    cos_tab, sin_tab = phase_tables(col_ids, m_table, cycle_len)
    cos_shift, sin_shift = cycle_offsets(cycle_table, m_table, cycle_len)
    weight = mask_flags.astype(jnp.float32) / (noise_var - 0.5)
    messenger = (weight * sky_data + 2.0 * signal_prev) / (weight + 2.0)
    flat_rows = messenger.astype(jnp.bfloat16).reshape(real_dev * cycle_dev, half_len)
    base_cos = jnp.dot(flat_rows, cos_tab, preferred_element_type=jnp.float32).reshape(
        real_dev, cycle_dev, mode_count
    )
    base_sin = -jnp.dot(flat_rows, sin_tab, preferred_element_type=jnp.float32).reshape(
        real_dev, cycle_dev, mode_count
    )
    norm_scale = cycle_len ** (-0.5)
    re_part = (base_cos * cos_shift + base_sin * sin_shift) * norm_scale
    im_part = (base_sin * cos_shift - base_cos * sin_shift) * norm_scale
    fourier_re, fourier_im = forward_modes(re_part, im_part)
    fourier = jnp.stack([fourier_re, fourier_im], 1)
    coefficients = jnp.einsum(
        "mlr,kcrm->kcml", legendre, fourier, preferred_element_type=jnp.float32
    )
    factor = spectrum / (spectrum + 0.5)
    wiener_alm = coefficients * factor
    total_l = legendre.shape[1] * lax.axis_size("grp") * lax.axis_size("real")
    syn_scale = (legendre.shape[2] / total_l) ** 0.5
    partial_value = (
        jnp.einsum(
            "mlr,kcml->kcrm",
            legendre,
            wiener_alm.astype(jnp.bfloat16),
            preferred_element_type=jnp.float32,
        )
        * syn_scale
    )
    cycle_pair = backward_cycles(partial_value)
    cycle_modes = cycle_pair.astype(jnp.float32)
    modes_re = cycle_modes[:, 0]
    modes_im = cycle_modes[:, 1]
    rotated_re = (modes_re * cos_shift - modes_im * sin_shift).astype(jnp.bfloat16)
    rotated_im = (modes_im * cos_shift + modes_re * sin_shift).astype(jnp.bfloat16)
    contract = (((1,), (1,)), ((), ()))
    pixel_sum = lax.dot_general(
        rotated_re.reshape(-1, mode_count), cos_tab, contract, preferred_element_type=jnp.float32
    )
    pixel_sum = pixel_sum - lax.dot_general(
        rotated_im.reshape(-1, mode_count), sin_tab, contract, preferred_element_type=jnp.float32
    )
    signal_next = (pixel_sum * mode_count ** (-0.5)).reshape(real_dev, cycle_dev, half_len)
    return (wiener_alm, signal_next)


def solution(mesh):
    in_specs = (
        P("real", "blk", "grp"),
        P("real", "blk", "grp"),
        P("blk", "grp"),
        P("blk", "grp"),
        P("blk"),
        P(),
        P(("grp", "real")),
        P("blk", ("grp", "real"), None),
    )
    out_specs = (P(None, None, "blk", ("grp", "real")), P("real", "blk", "grp"))

    def step(sky_data, signal_prev, noise_var, mask_flags, cycle_table, m_table, spectrum, legendre):
        fits = gram_form_fits(mesh, sky_data, m_table, legendre)
        return jax.shard_map(
            gram_program if fits else per_device,
            mesh=mesh,
            in_specs=in_specs,
            out_specs=out_specs,
            check_vma=False,
        )(sky_data, signal_prev, noise_var, mask_flags, cycle_table, m_table, spectrum, legendre)

    return step
```

```python
import functools
import math

import jax
import jax.numpy as jnp
from jax import lax
from jax.experimental import pallas as pl
from jax.experimental.pallas import tpu as pltpu
from jax.sharding import PartitionSpec as P

LANES = 128
NT = (((1,), (1,)), ((), ()))
AXES = ("grp", "blk", "real")
PARTS = 2
FORWARD_VMEM = 32 << 20
BACKWARD_VMEM = 16 << 20


def unit_cosine(units, half_turn):
    wrapped = units & (2 * half_turn - 1)
    folded = jnp.minimum(wrapped, 2 * half_turn - wrapped)
    y = (half_turn // 2 - folded).astype(jnp.float32) * (math.pi / half_turn)
    y2 = y * y
    acc = jnp.full_like(y2, -1.0 / math.factorial(11))
    for order, sign in ((9, 1.0), (7, -1.0), (5, 1.0), (3, -1.0), (1, 1.0)):
        acc = acc * y2 + sign / math.factorial(order)
    return acc * y


def log2(size):
    return size.bit_length() - 1


def lane_ids(shape):
    return lax.broadcasted_iota(jnp.int32, shape, len(shape) - 1)


def row_ids(shape):
    return lax.broadcasted_iota(jnp.int32, shape, len(shape) - 2)


def phase_factors(cycles, orders, cycle_len, half_len, group):
    modes = orders.shape[1]
    orders = jnp.concatenate([orders] * (LANES // modes), axis=1)
    quarter = lane_ids((1, LANES)) >> log2(modes)
    quarter_turn = cycle_len // 2
    row = row_ids((2 * LANES, LANES))
    pixel = (row >> log2(LANES)) * (half_len // 2) + (row & (LANES - 1))
    inner_units = 2 * orders * pixel + ((quarter + 1) >> 1) * quarter_turn
    inner = unit_cosine(inner_units, cycle_len)
    rows = half_len // LANES
    row = row_ids((rows, LANES))
    parity = jnp.where((row & 1) == 0, cycles[:, :1], cycles[:, 1:]) & 1
    pixel = group * half_len + LANES * (row >> 1)
    outer_units = orders * (2 * pixel + parity) + (quarter >> 1) * (3 * quarter_turn)
    outer = unit_cosine(outer_units, cycle_len)
    high = inner.astype(jnp.bfloat16)
    low = (inner - high.astype(jnp.float32)).astype(jnp.bfloat16)
    return jnp.concatenate([high, low], axis=1), outer


def start_copies(sources, targets, sems, first=0):
    copies = [
        pltpu.make_async_copy(source, target, sems.at[first + i])
        for i, (source, target) in enumerate(zip(sources, targets))
    ]
    for copy in copies:
        copy.start()
    return copies


def selections(place_ref, pick_ref, per_block, reals):
    block = lax.axis_index("blk")
    blocks, real_groups = lax.axis_size("blk"), lax.axis_size("real")
    modes, cycles, half = per_block * blocks, 2 * blocks, LANES // 2

    lane = lane_ids((1, LANES))
    row = row_ids((LANES, LANES))
    lane_order = (lane & (half - 1)) >> log2(cycles)
    lane_row = (lane & 1) * half + (lane >> log2(half)) * modes + block * per_block + lane_order
    pick_ref[0] = (row == lane_row).astype(jnp.float32).astype(jnp.bfloat16)
    lane_row = (lane >> log2(half)) * per_block + (lane & (per_block - 1))
    pick_ref[1] = ((row >> log2(cycles)) == lane_row).astype(jnp.float32).astype(jnp.bfloat16)

    spacing = reals + 2
    column = lane_ids((1, place_ref.shape[1]))
    source = (column * (2**16 // spacing + 1)) >> 16
    inside = column - source * spacing
    source_block = source >> log2(real_groups)
    target = ((source & (real_groups - 1)) * blocks + source_block) * reals + inside
    target = jnp.where(inside < reals, target, blocks * real_groups * reals + source_block)
    place = (row_ids(place_ref.shape) == target).astype(jnp.float32)
    place_ref[...] = place.astype(jnp.bfloat16)


def forward_kernel(
    cycle_len, half_len, syn_scale, reals,
    cycle_hbm, mode_hbm, noise_hbm, mask_hbm, spectrum_hbm, legendre_hbm, sky_hbm, prev_hbm,
    out_ref, inner_ref, outer_ref, place_ref, pick_ref, doubled_ref, factor_ref,
    cycle_ref, mode_ref, noise_ref, mask_ref, spectrum_ref, legendre_ref, sky_ref, prev_ref, gram_ref, sems,
):
    small = start_copies(
        (cycle_hbm, mode_hbm, noise_hbm, mask_hbm, spectrum_hbm, legendre_hbm),
        (cycle_ref, mode_ref, noise_ref, mask_ref, spectrum_ref, legendre_ref),
        sems,
    )
    large = start_copies((sky_hbm, prev_hbm), (sky_ref, prev_ref), sems, len(small))
    group = lax.axis_index("grp")
    per_block = legendre_ref.shape[0] // (2 * lax.axis_size("blk"))
    selections(place_ref, pick_ref, per_block, reals)
    small[0].wait()
    small[1].wait()
    inner, outer = phase_factors(cycle_ref[...], mode_ref[...], cycle_len, half_len, group)
    inner_ref[...] = inner
    outer_ref[...] = outer
    small[2].wait()
    small[3].wait()
    weight = mask_ref[...].astype(jnp.float32) / (noise_ref[...] - 0.5)
    inverse = 1.0 / (weight + 2.0)
    sky_gain = weight * inverse
    prev_gain = 2.0 * inverse

    for copy in small[4:] + large:
        copy.wait()
    table = legendre_ref[...]
    spectrum = spectrum_ref[...]
    factor = spectrum / (spectrum + 0.5)
    doubled_ref[...] = jnp.concatenate([table, table], axis=0)
    factor_ref[...] = factor
    filtered = (table.astype(jnp.float32) * factor).astype(jnp.bfloat16)
    gram = lax.dot_general(table, filtered, NT, preferred_element_type=jnp.float32)
    table_rows = table.shape[0]
    pixel_rows = outer.shape[0]
    blocks, real_groups = lax.axis_size("blk"), lax.axis_size("real")
    cycles = 2 * blocks
    same = (row_ids(gram.shape) >> log2(cycles)) == (lane_ids((1, table_rows)) >> log2(cycles))
    gram = jnp.where(same, gram, 0.0).reshape(table_rows // cycles, cycles, table_rows).sum(axis=0)
    gram = gram * syn_scale
    gram_ref[...] = jnp.concatenate([gram, gram], axis=1)
    even, odd = gram_ref[pl.ds(0, blocks, stride=2), :], gram_ref[pl.ds(1, blocks, stride=2), :]
    gram = jnp.where(lane_ids(even.shape) < LANES // 2, even, odd)
    gram_high = gram.astype(jnp.bfloat16).astype(jnp.float32)
    gram_low = gram - gram_high

    shape = (reals, 2 * pixel_rows, LANES)
    messenger = sky_ref[...].reshape(shape) * sky_gain + prev_ref[...].reshape(shape) * prev_gain
    rows = jnp.concatenate([messenger[:, :pixel_rows], messenger[:, pixel_rows:]], axis=2)
    rows = rows.reshape(-1, 2 * LANES).astype(jnp.bfloat16)
    partial = jnp.dot(rows, inner, preferred_element_type=jnp.float32)
    partial = partial[:, :LANES] + partial[:, LANES:]
    turned = partial.reshape(reals, pixel_rows, LANES) * outer
    summed = turned.reshape(reals, pixel_rows // 8, 8, LANES).sum(axis=1)
    summed = summed.reshape(reals * 8, LANES)
    summed = summed + pltpu.roll(summed, LANES // 2, 1)
    own = (row_ids(summed.shape) & 1) == (lane_ids(summed.shape) >= LANES // 2)
    fourier = jnp.where(own, summed, 0.0).reshape(reals, 8, LANES).sum(axis=1) * cycle_len**-0.5
    rows = []
    for b in range(blocks):
        rows += [fourier, gram_high[b : b + 1], gram_low[b : b + 1]] * real_groups
    rows = jnp.concatenate(rows, axis=0).astype(jnp.bfloat16)
    for g in range(lax.axis_size("grp")):
        out_ref[pl.ds(g * rows.shape[0], rows.shape[0]), :] = rows


def backward_kernel(
    blocks, real_groups, reals, parts,
    gathered_ref, inner_ref, outer_ref, place_ref, pick_ref, table_ref, factor_ref,
    wiener_hbm, signal_hbm, wiener_ref, signal_ref, fourier_ref, out_sems,
):
    real_group = lax.axis_index("real")
    cycles = 2 * blocks
    per_block = table_ref.shape[0] // (2 * cycles)
    modes = per_block * blocks
    pixel_rows = outer_ref.shape[0]
    half = LANES // 2
    lane = lane_ids((1, LANES))
    holder = (lane & (modes - 1)) >> log2(per_block)
    lane_block = (lane & (cycles - 1)) >> 1
    total_reals = real_groups * reals
    fourier_rows = blocks * total_reals
    share = place_ref.shape[1]
    sides = jnp.concatenate([gathered_ref[:share, :], gathered_ref[share:, :]], axis=1)
    placed = jnp.dot(place_ref[...], sides, preferred_element_type=jnp.float32)
    placed = placed[:, :LANES] + placed[:, LANES:]
    fourier_ref[...] = placed[:fourier_rows]

    coeff_rows = jnp.dot(
        placed[:fourier_rows].astype(jnp.bfloat16), pick_ref[0], preferred_element_type=jnp.float32
    ).reshape(real_groups, blocks, reals, LANES)
    columns = jnp.zeros((total_reals, LANES), jnp.float32)
    for b in range(blocks):
        one = coeff_rows[:, b].reshape(total_reals, LANES)
        columns = columns + jnp.where(lane_block == b, one, 0.0)
    table = table_ref[...]
    factor = factor_ref[...]
    stores = []
    own = (lane >> log2(cycles)) == row_ids((2 * per_block, LANES))
    upper = row_ids((1, 2 * per_block, LANES)) < per_block
    for y in range(real_groups):
        span = slice(y * reals, (y + 1) * reals)
        pieces = jnp.where(own, columns[span, None, :], 0.0)
        filtered = factor * jnp.dot(
            pieces.reshape(-1, LANES).astype(jnp.bfloat16), table, preferred_element_type=jnp.float32
        )
        for pair in range(wiener_ref.shape[2]):
            one, two = (
                filtered[:, tile * LANES : (tile + 1) * LANES].reshape(reals, 2 * per_block, LANES)
                for tile in (2 * pair, 2 * pair + 1)
            )
            wiener_ref[span, 0, pair] = jnp.where(upper, one, pltpu.roll(two, per_block, 1))
            wiener_ref[span, 1, pair] = jnp.where(upper, pltpu.roll(one, per_block, 1), two)
        span = pl.ds(y * reals, reals)
        stores += start_copies([wiener_ref.at[span]], [wiener_hbm.at[span]], out_sems, len(stores))

    gram_all = jnp.where(
        (lane & (cycles - 1)) == row_ids((cycles, LANES)), placed[fourier_rows:, None, :], 0.0
    ).reshape(blocks * cycles, LANES)
    gram_high = gram_all.astype(jnp.bfloat16)
    gram_low = (gram_all - gram_high.astype(jnp.float32)).astype(jnp.bfloat16)
    gram_rows = jnp.dot(
        jnp.concatenate([gram_high, gram_low], axis=1),
        jnp.concatenate([pick_ref[1], pick_ref[1]], axis=0),
        preferred_element_type=jnp.float32,
    ).reshape(blocks, cycles, LANES)
    gram = jnp.zeros((cycles, LANES), jnp.float32)
    for b in range(blocks):
        gram = gram + jnp.where(holder == b, gram_rows[b], 0.0)

    first = lane < half
    cycle_modes = jnp.zeros((reals, LANES), jnp.float32)
    for b in range(blocks):
        first_row = pl.multiple_of((real_group * blocks + b) * reals, reals)
        pair = fourier_ref[pl.ds(first_row, reals), :]
        turned = pltpu.roll(pair, half, 1)
        cycle_modes = cycle_modes + jnp.where(first, pair, turned) * gram[2 * b : 2 * b + 1]
        cycle_modes = cycle_modes + jnp.where(first, turned, pair) * gram[2 * b + 1 : 2 * b + 2]
    cycle_modes = cycle_modes * modes**-0.5
    turned = pltpu.roll(cycle_modes, half, 1)
    even = jnp.where(first, cycle_modes, turned)
    odd = jnp.where(first, turned, cycle_modes)
    parity = (row_ids((1, 8, LANES)) & 1) == 0
    spread = jnp.where(parity, even[:, None, :], odd[:, None, :])
    inner = inner_ref[...]
    outer = outer_ref[...].reshape(1, pixel_rows // 8, 8, LANES)
    part_reals = reals // parts
    for i in range(parts):
        span = slice(i * part_reals, (i + 1) * part_reals)
        rotated = (spread[span, None] * outer).reshape(-1, LANES).astype(jnp.bfloat16)
        signal = lax.dot_general(
            jnp.concatenate([rotated, rotated], axis=1), inner, NT, preferred_element_type=jnp.float32
        ).reshape(part_reals, pixel_rows, 2 * LANES)
        signal_ref[span, 0] = signal[:, :, :LANES]
        signal_ref[span, 1] = signal[:, :, LANES:]
        span = pl.ds(i * part_reals, part_reals)
        stores += start_copies([signal_ref.at[span]], [signal_hbm.at[span]], out_sems, len(stores))
    for store in stores:
        store.wait()


def split_tiles(array):
    lead, rows, columns = array.shape[:-2], array.shape[-2], array.shape[-1]
    split = array.reshape(*lead, rows, columns // LANES, LANES)
    return jnp.swapaxes(split, -2, -3).reshape(-1, LANES)


def gram_program(
    sky_data, signal_prev, noise_var, mask_flags, cycle_table, m_table, spectrum, legendre
):
    reals, cycle_dev, half_len = sky_data.shape
    groups, blocks, real_groups = (lax.axis_size(name) for name in AXES)
    cycle_len = half_len * groups
    per_block, multipoles, cycles = legendre.shape
    total_l = multipoles * groups * real_groups
    tiles = multipoles // LANES
    hbm = pl.BlockSpec(memory_space=pltpu.HBM)
    vmem = pl.BlockSpec(memory_space=pltpu.VMEM)
    orders = m_table[None, :]
    cycles_row = cycle_table[None, :]
    spectrum_row = spectrum[None, :]
    table = legendre.transpose(0, 2, 1).reshape(per_block * cycles, multipoles)
    inputs = (
        cycles_row, orders, split_tiles(noise_var), split_tiles(mask_flags), spectrum_row, table,
        split_tiles(sky_data), split_tiles(signal_prev),
    )
    sources = groups * blocks * real_groups
    total_reals = reals * real_groups
    local, *prepared = pl.pallas_call(
        functools.partial(forward_kernel, cycle_len, half_len, (cycles / total_l) ** 0.5, reals),
        out_shape=(
            jax.ShapeDtypeStruct((sources * (reals + 2), LANES), jnp.bfloat16),
            jax.ShapeDtypeStruct((2 * LANES, 2 * LANES), jnp.bfloat16),
            jax.ShapeDtypeStruct((half_len // LANES, LANES), jnp.float32),
            jax.ShapeDtypeStruct(
                (blocks * (total_reals + 1), blocks * real_groups * (reals + 2)), jnp.bfloat16
            ),
            jax.ShapeDtypeStruct((2, LANES, LANES), jnp.bfloat16),
            jax.ShapeDtypeStruct((2 * table.shape[0], multipoles), jnp.bfloat16),
            jax.ShapeDtypeStruct((1, multipoles), jnp.float32),
        ),
        in_specs=[hbm] * 8,
        out_specs=(vmem,) * 7,
        scratch_shapes=[pltpu.VMEM(x.shape, x.dtype) for x in inputs]
        + [pltpu.VMEM((cycles, LANES), jnp.float32), pltpu.SemaphoreType.DMA((8,))],
        compiler_params=pltpu.CompilerParams(vmem_limit_bytes=FORWARD_VMEM),
    )(*(pltpu.with_memory_space_constraint(x, pltpu.HBM) for x in inputs))
    pairs = local.reshape(sources, reals // 2 + 1, 2, LANES)
    gathered = lax.all_to_all(pairs, AXES, 0, 0, tiled=True).reshape(local.shape)
    outputs = (
        jax.ShapeDtypeStruct((total_reals, 2, tiles // 2, 2 * per_block, LANES), jnp.float32),
        jax.ShapeDtypeStruct((reals, 2, half_len // LANES, LANES), jnp.float32),
    )
    wiener, signal = pl.pallas_call(
        functools.partial(backward_kernel, blocks, real_groups, reals, PARTS),
        out_shape=outputs,
        in_specs=[vmem] * 7,
        out_specs=(hbm, hbm),
        scratch_shapes=[pltpu.VMEM(x.shape, x.dtype) for x in outputs]
        + [pltpu.VMEM((blocks * total_reals, LANES), jnp.float32)]
        + [pltpu.SemaphoreType.DMA((real_groups + PARTS,))],
        compiler_params=pltpu.CompilerParams(vmem_limit_bytes=BACKWARD_VMEM),
    )(gathered, *prepared)
    wiener = wiener.reshape(total_reals, 2, tiles, per_block, LANES).transpose(0, 1, 3, 2, 4)
    signal = signal.reshape(reals, half_len // LANES, cycle_dev, LANES).transpose(0, 2, 1, 3)
    return (
        wiener.reshape(total_reals, 2, per_block, multipoles),
        signal.reshape(sky_data.shape),
    )


def gram_form_fits(mesh, sky_data, m_table, legendre):
    groups, blocks, real_groups = (mesh.shape[name] for name in AXES)
    reals, cycles, cycle_len = sky_data.shape
    modes = m_table.shape[0]
    per_block = modes // blocks
    multipoles = legendre.shape[1] // (groups * real_groups)
    half_len = cycle_len // groups
    reals_dev = reals // real_groups
    return (
        cycles < 2 * reals
        and 4 * modes == LANES
        and cycles == 2 * blocks
        and all(size & (size - 1) == 0 for size in (blocks, modes, cycles, real_groups))
        and 2 * reals * cycles < 2**12
        and 2 * per_block * cycles == LANES
        and cycle_len & (cycle_len - 1) == 0
        and half_len % (8 * LANES) == 0
        and multipoles % (2 * LANES) == 0
        and per_block == 4
        and reals_dev % 16 == 0
        and reals_dev % PARTS == 0
        and cycles % 16 == 0
    )


def phase_tables(col_ids, mode_ids, cycle_len):
    product_ids = col_ids[:, None] * mode_ids[None, :] % cycle_len
    angles = product_ids.astype(jnp.float32) * (2.0 * math.pi / cycle_len)
    return (jnp.cos(angles).astype(jnp.bfloat16), jnp.sin(angles).astype(jnp.bfloat16))


def cycle_offsets(cycle_ids, mode_ids, cycle_len):
    parity = (cycle_ids % 2).astype(jnp.float32)
    shifts = math.pi / cycle_len * parity[:, None] * mode_ids[None, :].astype(jnp.float32)
    return (jnp.cos(shifts), jnp.sin(shifts))


def forward_modes(re_part, im_part):
    summed = lax.psum((re_part, im_part), "grp")
    fourier_pair = (summed[0].astype(jnp.bfloat16), summed[1].astype(jnp.bfloat16))
    fourier_pair = (
        lax.all_gather(fourier_pair[0], "real", axis=0, tiled=True),
        lax.all_gather(fourier_pair[1], "real", axis=0, tiled=True),
    )
    fourier_pair = (
        lax.all_to_all(fourier_pair[0], "blk", split_axis=2, concat_axis=1, tiled=True),
        lax.all_to_all(fourier_pair[1], "blk", split_axis=2, concat_axis=1, tiled=True),
    )
    return fourier_pair


def backward_cycles(partial_value):
    summed = lax.psum_scatter(partial_value, "real", scatter_dimension=0, tiled=True)
    reduced = lax.psum(summed, "grp")
    cycle_pair = lax.all_to_all(
        reduced.astype(jnp.bfloat16), "blk", split_axis=2, concat_axis=3, tiled=True
    )
    return cycle_pair


def per_device(
    sky_data, signal_prev, noise_var, mask_flags, cycle_table, m_table, spectrum, legendre
):
    real_dev, cycle_dev, half_len = sky_data.shape
    cycle_len = half_len * lax.axis_size("grp")
    mode_count = m_table.shape[0]
    col_ids = lax.axis_index("grp") * half_len + jnp.arange(half_len, dtype=jnp.int32)
    cos_tab, sin_tab = phase_tables(col_ids, m_table, cycle_len)
    cos_shift, sin_shift = cycle_offsets(cycle_table, m_table, cycle_len)
    weight = mask_flags.astype(jnp.float32) / (noise_var - 0.5)
    messenger = (weight * sky_data + 2.0 * signal_prev) / (weight + 2.0)
    flat_rows = messenger.astype(jnp.bfloat16).reshape(real_dev * cycle_dev, half_len)
    base_cos = jnp.dot(flat_rows, cos_tab, preferred_element_type=jnp.float32).reshape(
        real_dev, cycle_dev, mode_count
    )
    base_sin = -jnp.dot(flat_rows, sin_tab, preferred_element_type=jnp.float32).reshape(
        real_dev, cycle_dev, mode_count
    )
    norm_scale = cycle_len ** (-0.5)
    re_part = (base_cos * cos_shift + base_sin * sin_shift) * norm_scale
    im_part = (base_sin * cos_shift - base_cos * sin_shift) * norm_scale
    fourier_re, fourier_im = forward_modes(re_part, im_part)
    fourier = jnp.stack([fourier_re, fourier_im], 1)
    coefficients = jnp.einsum(
        "mlr,kcrm->kcml", legendre, fourier, preferred_element_type=jnp.float32
    )
    factor = spectrum / (spectrum + 0.5)
    wiener_alm = coefficients * factor
    total_l = legendre.shape[1] * lax.axis_size("grp") * lax.axis_size("real")
    syn_scale = (legendre.shape[2] / total_l) ** 0.5
    partial_value = (
        jnp.einsum(
            "mlr,kcml->kcrm",
            legendre,
            wiener_alm.astype(jnp.bfloat16),
            preferred_element_type=jnp.float32,
        )
        * syn_scale
    )
    cycle_pair = backward_cycles(partial_value)
    cycle_modes = cycle_pair.astype(jnp.float32)
    modes_re = cycle_modes[:, 0]
    modes_im = cycle_modes[:, 1]
    rotated_re = (modes_re * cos_shift - modes_im * sin_shift).astype(jnp.bfloat16)
    rotated_im = (modes_im * cos_shift + modes_re * sin_shift).astype(jnp.bfloat16)
    contract = (((1,), (1,)), ((), ()))
    pixel_sum = lax.dot_general(
        rotated_re.reshape(-1, mode_count), cos_tab, contract, preferred_element_type=jnp.float32
    )
    pixel_sum = pixel_sum - lax.dot_general(
        rotated_im.reshape(-1, mode_count), sin_tab, contract, preferred_element_type=jnp.float32
    )
    signal_next = (pixel_sum * mode_count ** (-0.5)).reshape(real_dev, cycle_dev, half_len)
    return (wiener_alm, signal_next)


def solution(mesh):
    in_specs = (
        P("real", "blk", "grp"),
        P("real", "blk", "grp"),
        P("blk", "grp"),
        P("blk", "grp"),
        P("blk"),
        P(),
        P(("grp", "real")),
        P("blk", ("grp", "real"), None),
    )
    out_specs = (P(None, None, "blk", ("grp", "real")), P("real", "blk", "grp"))

    def step(sky_data, signal_prev, noise_var, mask_flags, cycle_table, m_table, spectrum, legendre):
        fits = gram_form_fits(mesh, sky_data, m_table, legendre)
        return jax.shard_map(
            gram_program if fits else per_device,
            mesh=mesh,
            in_specs=in_specs,
            out_specs=out_specs,
            check_vma=False,
        )(sky_data, signal_prev, noise_var, mask_flags, cycle_table, m_table, spectrum, legendre)

    return step
```

```python
import functools
import math

import jax
import jax.numpy as jnp
from jax import lax
from jax.experimental import pallas as pl
from jax.experimental.pallas import tpu as pltpu
from jax.sharding import PartitionSpec as P

LANES = 128
NT = (((1,), (1,)), ((), ()))
AXES = ("grp", "blk", "real")
PARTS = 2
STREAMS = 4
FORWARD_VMEM = 32 << 20
BACKWARD_VMEM = 16 << 20


def unit_cosine(units, half_turn):
    wrapped = units & (2 * half_turn - 1)
    folded = jnp.minimum(wrapped, 2 * half_turn - wrapped)
    y = (half_turn // 2 - folded).astype(jnp.float32) * (math.pi / half_turn)
    y2 = y * y
    acc = jnp.full_like(y2, -1.0 / math.factorial(11))
    for order, sign in ((9, 1.0), (7, -1.0), (5, 1.0), (3, -1.0), (1, 1.0)):
        acc = acc * y2 + sign / math.factorial(order)
    return acc * y


def log2(size):
    return size.bit_length() - 1


def lane_ids(shape):
    return lax.broadcasted_iota(jnp.int32, shape, len(shape) - 1)


def row_ids(shape):
    return lax.broadcasted_iota(jnp.int32, shape, len(shape) - 2)


def phase_factors(cycles, orders, cycle_len, half_len, group):
    modes = orders.shape[1]
    orders = jnp.concatenate([orders] * (LANES // modes), axis=1)
    quarter = lane_ids((1, LANES)) >> log2(modes)
    quarter_turn = cycle_len // 2
    row = row_ids((2 * LANES, LANES))
    pixel = (row >> log2(LANES)) * (half_len // 2) + (row & (LANES - 1))
    inner_units = 2 * orders * pixel + ((quarter + 1) >> 1) * quarter_turn
    inner = unit_cosine(inner_units, cycle_len)
    rows = half_len // LANES
    row = row_ids((rows, LANES))
    parity = jnp.where((row & 1) == 0, cycles[:, :1], cycles[:, 1:]) & 1
    pixel = group * half_len + LANES * (row >> 1)
    outer_units = orders * (2 * pixel + parity) + (quarter >> 1) * (3 * quarter_turn)
    outer = unit_cosine(outer_units, cycle_len)
    high = inner.astype(jnp.bfloat16)
    low = (inner - high.astype(jnp.float32)).astype(jnp.bfloat16)
    return jnp.concatenate([high, low], axis=1), outer


def start_copies(sources, targets, sems, first=0):
    copies = [
        pltpu.make_async_copy(source, target, sems.at[first + i])
        for i, (source, target) in enumerate(zip(sources, targets))
    ]
    for copy in copies:
        copy.start()
    return copies


def row_parts(ref, first, size, parts):
    return [ref.at[pl.ds(first + i * (size // parts), size // parts)] for i in range(parts)]


def selections(place_ref, pick_ref, per_block, reals):
    block = lax.axis_index("blk")
    blocks, real_groups = lax.axis_size("blk"), lax.axis_size("real")
    modes, cycles, half = per_block * blocks, 2 * blocks, LANES // 2

    lane = lane_ids((1, LANES))
    row = row_ids((LANES, LANES))
    lane_order = (lane & (half - 1)) >> log2(cycles)
    lane_row = (lane & 1) * half + (lane >> log2(half)) * modes + block * per_block + lane_order
    pick_ref[0] = (row == lane_row).astype(jnp.float32).astype(jnp.bfloat16)
    lane_row = (lane >> log2(half)) * per_block + (lane & (per_block - 1))
    pick_ref[1] = ((row >> log2(cycles)) == lane_row).astype(jnp.float32).astype(jnp.bfloat16)

    spacing = reals + 2
    column = lane_ids((1, place_ref.shape[1]))
    source = (column * (2**16 // spacing + 1)) >> 16
    inside = column - source * spacing
    source_block = source >> log2(real_groups)
    target = ((source & (real_groups - 1)) * blocks + source_block) * reals + inside
    target = jnp.where(inside < reals, target, blocks * real_groups * reals + source_block)
    place = (row_ids(place_ref.shape) == target).astype(jnp.float32)
    place_ref[...] = place.astype(jnp.bfloat16)


def forward_kernel(
    cycle_len, half_len, syn_scale, reals,
    cycle_hbm, mode_hbm, noise_hbm, mask_hbm, spectrum_hbm, legendre_hbm, sky_hbm, prev_hbm,
    out_ref, inner_ref, outer_ref, place_ref, pick_ref, doubled_ref, factor_ref,
    cycle_ref, mode_ref, noise_ref, mask_ref, spectrum_ref, legendre_ref, sky_ref, prev_ref, gram_ref, sems,
):
    small = start_copies(
        (cycle_hbm, mode_hbm, noise_hbm, mask_hbm, spectrum_hbm, legendre_hbm),
        (cycle_ref, mode_ref, noise_ref, mask_ref, spectrum_ref, legendre_ref),
        sems,
    )
    pixels = sky_ref.shape[0]
    large = start_copies(
        row_parts(sky_hbm, 0, pixels, STREAMS) + row_parts(prev_hbm, 0, pixels, STREAMS),
        row_parts(sky_ref, 0, pixels, STREAMS) + row_parts(prev_ref, 0, pixels, STREAMS),
        sems,
        len(small),
    )
    group = lax.axis_index("grp")
    per_block = legendre_ref.shape[0] // (2 * lax.axis_size("blk"))
    selections(place_ref, pick_ref, per_block, reals)
    small[0].wait()
    small[1].wait()
    inner, outer = phase_factors(cycle_ref[...], mode_ref[...], cycle_len, half_len, group)
    inner_ref[...] = inner
    outer_ref[...] = outer
    small[2].wait()
    small[3].wait()
    weight = mask_ref[...].astype(jnp.float32) / (noise_ref[...] - 0.5)
    inverse = 1.0 / (weight + 2.0)
    sky_gain = weight * inverse
    prev_gain = 2.0 * inverse

    for copy in small[4:] + large:
        copy.wait()
    table = legendre_ref[...]
    spectrum = spectrum_ref[...]
    factor = spectrum / (spectrum + 0.5)
    doubled_ref[...] = jnp.concatenate([table, table], axis=0)
    factor_ref[...] = factor
    filtered = (table.astype(jnp.float32) * factor).astype(jnp.bfloat16)
    gram = lax.dot_general(table, filtered, NT, preferred_element_type=jnp.float32)
    table_rows = table.shape[0]
    pixel_rows = outer.shape[0]
    blocks, real_groups = lax.axis_size("blk"), lax.axis_size("real")
    cycles = 2 * blocks
    same = (row_ids(gram.shape) >> log2(cycles)) == (lane_ids((1, table_rows)) >> log2(cycles))
    gram = jnp.where(same, gram, 0.0).reshape(table_rows // cycles, cycles, table_rows).sum(axis=0)
    gram = gram * syn_scale
    gram_ref[...] = jnp.concatenate([gram, gram], axis=1)
    even, odd = gram_ref[pl.ds(0, blocks, stride=2), :], gram_ref[pl.ds(1, blocks, stride=2), :]
    gram = jnp.where(lane_ids(even.shape) < LANES // 2, even, odd)
    gram_high = gram.astype(jnp.bfloat16).astype(jnp.float32)
    gram_low = gram - gram_high

    shape = (reals, 2 * pixel_rows, LANES)
    messenger = sky_ref[...].reshape(shape) * sky_gain + prev_ref[...].reshape(shape) * prev_gain
    rows = jnp.concatenate([messenger[:, :pixel_rows], messenger[:, pixel_rows:]], axis=2)
    rows = rows.reshape(-1, 2 * LANES).astype(jnp.bfloat16)
    partial = jnp.dot(rows, inner, preferred_element_type=jnp.float32)
    partial = partial[:, :LANES] + partial[:, LANES:]
    turned = partial.reshape(reals, pixel_rows, LANES) * outer
    summed = turned.reshape(reals, pixel_rows // 8, 8, LANES).sum(axis=1)
    summed = summed.reshape(reals * 8, LANES)
    summed = summed + pltpu.roll(summed, LANES // 2, 1)
    own = (row_ids(summed.shape) & 1) == (lane_ids(summed.shape) >= LANES // 2)
    fourier = jnp.where(own, summed, 0.0).reshape(reals, 8, LANES).sum(axis=1) * cycle_len**-0.5
    rows = []
    for b in range(blocks):
        rows += [fourier, gram_high[b : b + 1], gram_low[b : b + 1]] * real_groups
    rows = jnp.concatenate(rows, axis=0).astype(jnp.bfloat16)
    for g in range(lax.axis_size("grp")):
        out_ref[pl.ds(g * rows.shape[0], rows.shape[0]), :] = rows


def backward_kernel(
    blocks, real_groups, reals, parts,
    gathered_ref, inner_ref, outer_ref, place_ref, pick_ref, table_ref, factor_ref,
    wiener_hbm, signal_hbm, wiener_ref, signal_ref, fourier_ref, out_sems,
):
    real_group = lax.axis_index("real")
    cycles = 2 * blocks
    per_block = table_ref.shape[0] // (2 * cycles)
    modes = per_block * blocks
    pixel_rows = outer_ref.shape[0]
    half = LANES // 2
    lane = lane_ids((1, LANES))
    holder = (lane & (modes - 1)) >> log2(per_block)
    lane_block = (lane & (cycles - 1)) >> 1
    total_reals = real_groups * reals
    fourier_rows = blocks * total_reals
    share = place_ref.shape[1]
    sides = jnp.concatenate([gathered_ref[:share, :], gathered_ref[share:, :]], axis=1)
    placed = jnp.dot(place_ref[...], sides, preferred_element_type=jnp.float32)
    placed = placed[:, :LANES] + placed[:, LANES:]
    fourier_ref[...] = placed[:fourier_rows]

    coeff_rows = jnp.dot(
        placed[:fourier_rows].astype(jnp.bfloat16), pick_ref[0], preferred_element_type=jnp.float32
    ).reshape(real_groups, blocks, reals, LANES)
    columns = jnp.zeros((total_reals, LANES), jnp.float32)
    for b in range(blocks):
        one = coeff_rows[:, b].reshape(total_reals, LANES)
        columns = columns + jnp.where(lane_block == b, one, 0.0)
    table = table_ref[...]
    factor = factor_ref[...]
    stores = []
    own = (lane >> log2(cycles)) == row_ids((2 * per_block, LANES))
    upper = row_ids((1, 2 * per_block, LANES)) < per_block
    for y in range(real_groups):
        span = slice(y * reals, (y + 1) * reals)
        pieces = jnp.where(own, columns[span, None, :], 0.0)
        filtered = factor * jnp.dot(
            pieces.reshape(-1, LANES).astype(jnp.bfloat16), table, preferred_element_type=jnp.float32
        )
        for pair in range(wiener_ref.shape[2]):
            one, two = (
                filtered[:, tile * LANES : (tile + 1) * LANES].reshape(reals, 2 * per_block, LANES)
                for tile in (2 * pair, 2 * pair + 1)
            )
            wiener_ref[span, 0, pair] = jnp.where(upper, one, pltpu.roll(two, per_block, 1))
            wiener_ref[span, 1, pair] = jnp.where(upper, pltpu.roll(one, per_block, 1), two)
        stores += start_copies(
            row_parts(wiener_ref, y * reals, reals, STREAMS),
            row_parts(wiener_hbm, y * reals, reals, STREAMS),
            out_sems,
            len(stores),
        )

    gram_all = jnp.where(
        (lane & (cycles - 1)) == row_ids((cycles, LANES)), placed[fourier_rows:, None, :], 0.0
    ).reshape(blocks * cycles, LANES)
    gram_high = gram_all.astype(jnp.bfloat16)
    gram_low = (gram_all - gram_high.astype(jnp.float32)).astype(jnp.bfloat16)
    gram_rows = jnp.dot(
        jnp.concatenate([gram_high, gram_low], axis=1),
        jnp.concatenate([pick_ref[1], pick_ref[1]], axis=0),
        preferred_element_type=jnp.float32,
    ).reshape(blocks, cycles, LANES)
    gram = jnp.zeros((cycles, LANES), jnp.float32)
    for b in range(blocks):
        gram = gram + jnp.where(holder == b, gram_rows[b], 0.0)

    first = lane < half
    cycle_modes = jnp.zeros((reals, LANES), jnp.float32)
    for b in range(blocks):
        first_row = pl.multiple_of((real_group * blocks + b) * reals, reals)
        pair = fourier_ref[pl.ds(first_row, reals), :]
        turned = pltpu.roll(pair, half, 1)
        cycle_modes = cycle_modes + jnp.where(first, pair, turned) * gram[2 * b : 2 * b + 1]
        cycle_modes = cycle_modes + jnp.where(first, turned, pair) * gram[2 * b + 1 : 2 * b + 2]
    cycle_modes = cycle_modes * modes**-0.5
    turned = pltpu.roll(cycle_modes, half, 1)
    even = jnp.where(first, cycle_modes, turned)
    odd = jnp.where(first, turned, cycle_modes)
    parity = (row_ids((1, 8, LANES)) & 1) == 0
    spread = jnp.where(parity, even[:, None, :], odd[:, None, :])
    inner = inner_ref[...]
    outer = outer_ref[...].reshape(1, pixel_rows // 8, 8, LANES)
    part_reals = reals // parts
    for i in range(parts):
        span = slice(i * part_reals, (i + 1) * part_reals)
        rotated = (spread[span, None] * outer).reshape(-1, LANES).astype(jnp.bfloat16)
        signal = lax.dot_general(
            jnp.concatenate([rotated, rotated], axis=1), inner, NT, preferred_element_type=jnp.float32
        ).reshape(part_reals, pixel_rows, 2 * LANES)
        signal_ref[span, 0] = signal[:, :, :LANES]
        signal_ref[span, 1] = signal[:, :, LANES:]
        stores += start_copies(
            row_parts(signal_ref, i * part_reals, part_reals, STREAMS),
            row_parts(signal_hbm, i * part_reals, part_reals, STREAMS),
            out_sems,
            len(stores),
        )
    for store in stores:
        store.wait()


def split_tiles(array):
    lead, rows, columns = array.shape[:-2], array.shape[-2], array.shape[-1]
    split = array.reshape(*lead, rows, columns // LANES, LANES)
    return jnp.swapaxes(split, -2, -3).reshape(-1, LANES)


def gram_program(
    sky_data, signal_prev, noise_var, mask_flags, cycle_table, m_table, spectrum, legendre
):
    reals, cycle_dev, half_len = sky_data.shape
    groups, blocks, real_groups = (lax.axis_size(name) for name in AXES)
    cycle_len = half_len * groups
    per_block, multipoles, cycles = legendre.shape
    total_l = multipoles * groups * real_groups
    tiles = multipoles // LANES
    hbm = pl.BlockSpec(memory_space=pltpu.HBM)
    vmem = pl.BlockSpec(memory_space=pltpu.VMEM)
    orders = m_table[None, :]
    cycles_row = cycle_table[None, :]
    spectrum_row = spectrum[None, :]
    table = legendre.transpose(0, 2, 1).reshape(per_block * cycles, multipoles)
    inputs = (
        cycles_row, orders, split_tiles(noise_var), split_tiles(mask_flags), spectrum_row, table,
        split_tiles(sky_data), split_tiles(signal_prev),
    )
    sources = groups * blocks * real_groups
    total_reals = reals * real_groups
    local, *prepared = pl.pallas_call(
        functools.partial(forward_kernel, cycle_len, half_len, (cycles / total_l) ** 0.5, reals),
        out_shape=(
            jax.ShapeDtypeStruct((sources * (reals + 2), LANES), jnp.bfloat16),
            jax.ShapeDtypeStruct((2 * LANES, 2 * LANES), jnp.bfloat16),
            jax.ShapeDtypeStruct((half_len // LANES, LANES), jnp.float32),
            jax.ShapeDtypeStruct(
                (blocks * (total_reals + 1), blocks * real_groups * (reals + 2)), jnp.bfloat16
            ),
            jax.ShapeDtypeStruct((2, LANES, LANES), jnp.bfloat16),
            jax.ShapeDtypeStruct((2 * table.shape[0], multipoles), jnp.bfloat16),
            jax.ShapeDtypeStruct((1, multipoles), jnp.float32),
        ),
        in_specs=[hbm] * 8,
        out_specs=(vmem,) * 7,
        scratch_shapes=[pltpu.VMEM(x.shape, x.dtype) for x in inputs]
        + [pltpu.VMEM((cycles, LANES), jnp.float32), pltpu.SemaphoreType.DMA((6 + 2 * STREAMS,))],
        compiler_params=pltpu.CompilerParams(vmem_limit_bytes=FORWARD_VMEM),
    )(*(pltpu.with_memory_space_constraint(x, pltpu.HBM) for x in inputs))
    pairs = local.reshape(sources, reals // 2 + 1, 2, LANES)
    gathered = lax.all_to_all(pairs, AXES, 0, 0, tiled=True).reshape(local.shape)
    outputs = (
        jax.ShapeDtypeStruct((total_reals, 2, tiles // 2, 2 * per_block, LANES), jnp.float32),
        jax.ShapeDtypeStruct((reals, 2, half_len // LANES, LANES), jnp.float32),
    )
    wiener, signal = pl.pallas_call(
        functools.partial(backward_kernel, blocks, real_groups, reals, PARTS),
        out_shape=outputs,
        in_specs=[vmem] * 7,
        out_specs=(hbm, hbm),
        scratch_shapes=[pltpu.VMEM(x.shape, x.dtype) for x in outputs]
        + [pltpu.VMEM((blocks * total_reals, LANES), jnp.float32)]
        + [pltpu.SemaphoreType.DMA(((real_groups + PARTS) * STREAMS,))],
        compiler_params=pltpu.CompilerParams(vmem_limit_bytes=BACKWARD_VMEM),
    )(gathered, *prepared)
    wiener = wiener.reshape(total_reals, 2, tiles, per_block, LANES).transpose(0, 1, 3, 2, 4)
    signal = signal.reshape(reals, half_len // LANES, cycle_dev, LANES).transpose(0, 2, 1, 3)
    return (
        wiener.reshape(total_reals, 2, per_block, multipoles),
        signal.reshape(sky_data.shape),
    )


def gram_form_fits(mesh, sky_data, m_table, legendre):
    groups, blocks, real_groups = (mesh.shape[name] for name in AXES)
    reals, cycles, cycle_len = sky_data.shape
    modes = m_table.shape[0]
    per_block = modes // blocks
    multipoles = legendre.shape[1] // (groups * real_groups)
    half_len = cycle_len // groups
    reals_dev = reals // real_groups
    return (
        cycles < 2 * reals
        and 4 * modes == LANES
        and cycles == 2 * blocks
        and all(size & (size - 1) == 0 for size in (blocks, modes, cycles, real_groups))
        and 2 * reals * cycles < 2**12
        and 2 * per_block * cycles == LANES
        and cycle_len & (cycle_len - 1) == 0
        and half_len % (8 * LANES) == 0
        and multipoles % (2 * LANES) == 0
        and per_block == 4
        and reals_dev % 16 == 0
        and reals_dev % (PARTS * STREAMS) == 0
        and cycles % 16 == 0
    )


def phase_tables(col_ids, mode_ids, cycle_len):
    product_ids = col_ids[:, None] * mode_ids[None, :] % cycle_len
    angles = product_ids.astype(jnp.float32) * (2.0 * math.pi / cycle_len)
    return (jnp.cos(angles).astype(jnp.bfloat16), jnp.sin(angles).astype(jnp.bfloat16))


def cycle_offsets(cycle_ids, mode_ids, cycle_len):
    parity = (cycle_ids % 2).astype(jnp.float32)
    shifts = math.pi / cycle_len * parity[:, None] * mode_ids[None, :].astype(jnp.float32)
    return (jnp.cos(shifts), jnp.sin(shifts))


def forward_modes(re_part, im_part):
    summed = lax.psum((re_part, im_part), "grp")
    fourier_pair = (summed[0].astype(jnp.bfloat16), summed[1].astype(jnp.bfloat16))
    fourier_pair = (
        lax.all_gather(fourier_pair[0], "real", axis=0, tiled=True),
        lax.all_gather(fourier_pair[1], "real", axis=0, tiled=True),
    )
    fourier_pair = (
        lax.all_to_all(fourier_pair[0], "blk", split_axis=2, concat_axis=1, tiled=True),
        lax.all_to_all(fourier_pair[1], "blk", split_axis=2, concat_axis=1, tiled=True),
    )
    return fourier_pair


def backward_cycles(partial_value):
    summed = lax.psum_scatter(partial_value, "real", scatter_dimension=0, tiled=True)
    reduced = lax.psum(summed, "grp")
    cycle_pair = lax.all_to_all(
        reduced.astype(jnp.bfloat16), "blk", split_axis=2, concat_axis=3, tiled=True
    )
    return cycle_pair


def per_device(
    sky_data, signal_prev, noise_var, mask_flags, cycle_table, m_table, spectrum, legendre
):
    real_dev, cycle_dev, half_len = sky_data.shape
    cycle_len = half_len * lax.axis_size("grp")
    mode_count = m_table.shape[0]
    col_ids = lax.axis_index("grp") * half_len + jnp.arange(half_len, dtype=jnp.int32)
    cos_tab, sin_tab = phase_tables(col_ids, m_table, cycle_len)
    cos_shift, sin_shift = cycle_offsets(cycle_table, m_table, cycle_len)
    weight = mask_flags.astype(jnp.float32) / (noise_var - 0.5)
    messenger = (weight * sky_data + 2.0 * signal_prev) / (weight + 2.0)
    flat_rows = messenger.astype(jnp.bfloat16).reshape(real_dev * cycle_dev, half_len)
    base_cos = jnp.dot(flat_rows, cos_tab, preferred_element_type=jnp.float32).reshape(
        real_dev, cycle_dev, mode_count
    )
    base_sin = -jnp.dot(flat_rows, sin_tab, preferred_element_type=jnp.float32).reshape(
        real_dev, cycle_dev, mode_count
    )
    norm_scale = cycle_len ** (-0.5)
    re_part = (base_cos * cos_shift + base_sin * sin_shift) * norm_scale
    im_part = (base_sin * cos_shift - base_cos * sin_shift) * norm_scale
    fourier_re, fourier_im = forward_modes(re_part, im_part)
    fourier = jnp.stack([fourier_re, fourier_im], 1)
    coefficients = jnp.einsum(
        "mlr,kcrm->kcml", legendre, fourier, preferred_element_type=jnp.float32
    )
    factor = spectrum / (spectrum + 0.5)
    wiener_alm = coefficients * factor
    total_l = legendre.shape[1] * lax.axis_size("grp") * lax.axis_size("real")
    syn_scale = (legendre.shape[2] / total_l) ** 0.5
    partial_value = (
        jnp.einsum(
            "mlr,kcml->kcrm",
            legendre,
            wiener_alm.astype(jnp.bfloat16),
            preferred_element_type=jnp.float32,
        )
        * syn_scale
    )
    cycle_pair = backward_cycles(partial_value)
    cycle_modes = cycle_pair.astype(jnp.float32)
    modes_re = cycle_modes[:, 0]
    modes_im = cycle_modes[:, 1]
    rotated_re = (modes_re * cos_shift - modes_im * sin_shift).astype(jnp.bfloat16)
    rotated_im = (modes_im * cos_shift + modes_re * sin_shift).astype(jnp.bfloat16)
    contract = (((1,), (1,)), ((), ()))
    pixel_sum = lax.dot_general(
        rotated_re.reshape(-1, mode_count), cos_tab, contract, preferred_element_type=jnp.float32
    )
    pixel_sum = pixel_sum - lax.dot_general(
        rotated_im.reshape(-1, mode_count), sin_tab, contract, preferred_element_type=jnp.float32
    )
    signal_next = (pixel_sum * mode_count ** (-0.5)).reshape(real_dev, cycle_dev, half_len)
    return (wiener_alm, signal_next)


def solution(mesh):
    in_specs = (
        P("real", "blk", "grp"),
        P("real", "blk", "grp"),
        P("blk", "grp"),
        P("blk", "grp"),
        P("blk"),
        P(),
        P(("grp", "real")),
        P("blk", ("grp", "real"), None),
    )
    out_specs = (P(None, None, "blk", ("grp", "real")), P("real", "blk", "grp"))

    def step(sky_data, signal_prev, noise_var, mask_flags, cycle_table, m_table, spectrum, legendre):
        fits = gram_form_fits(mesh, sky_data, m_table, legendre)
        return jax.shard_map(
            gram_program if fits else per_device,
            mesh=mesh,
            in_specs=in_specs,
            out_specs=out_specs,
            check_vma=False,
        )(sky_data, signal_prev, noise_var, mask_flags, cycle_table, m_table, spectrum, legendre)

    return step
```

```python
import functools
import math

import jax
import jax.numpy as jnp
from jax import lax
from jax.experimental import pallas as pl
from jax.experimental.pallas import tpu as pltpu
from jax.sharding import PartitionSpec as P

LANES = 128
NT = (((1,), (1,)), ((), ()))
AXES = ("grp", "blk", "real")
PARTS = 2
FORWARD_VMEM = 32 << 20
BACKWARD_VMEM = 16 << 20


def unit_cosine(units, half_turn):
    wrapped = units & (2 * half_turn - 1)
    folded = jnp.minimum(wrapped, 2 * half_turn - wrapped)
    y = (half_turn // 2 - folded).astype(jnp.float32) * (math.pi / half_turn)
    y2 = y * y
    acc = jnp.full_like(y2, -1.0 / math.factorial(11))
    for order, sign in ((9, 1.0), (7, -1.0), (5, 1.0), (3, -1.0), (1, 1.0)):
        acc = acc * y2 + sign / math.factorial(order)
    return acc * y


def log2(size):
    return size.bit_length() - 1


def lane_ids(shape):
    return lax.broadcasted_iota(jnp.int32, shape, len(shape) - 1)


def row_ids(shape):
    return lax.broadcasted_iota(jnp.int32, shape, len(shape) - 2)


def phase_factors(cycles, orders, cycle_len, half_len, group):
    modes = orders.shape[1]
    orders = jnp.concatenate([orders] * (LANES // modes), axis=1)
    quarter = lane_ids((1, LANES)) >> log2(modes)
    quarter_turn = cycle_len // 2
    row = row_ids((2 * LANES, LANES))
    pixel = (row >> log2(LANES)) * (half_len // 2) + (row & (LANES - 1))
    inner_units = 2 * orders * pixel + ((quarter + 1) >> 1) * quarter_turn
    inner = unit_cosine(inner_units, cycle_len)
    rows = half_len // LANES
    row = row_ids((rows, LANES))
    parity = jnp.where((row & 1) == 0, cycles[:, :1], cycles[:, 1:]) & 1
    pixel = group * half_len + LANES * (row >> 1)
    outer_units = orders * (2 * pixel + parity) + (quarter >> 1) * (3 * quarter_turn)
    outer = unit_cosine(outer_units, cycle_len)
    high = inner.astype(jnp.bfloat16)
    low = (inner - high.astype(jnp.float32)).astype(jnp.bfloat16)
    return jnp.concatenate([high, low], axis=1), outer


def start_copies(sources, targets, sems, first=0):
    copies = [
        pltpu.make_async_copy(source, target, sems.at[first + i])
        for i, (source, target) in enumerate(zip(sources, targets))
    ]
    for copy in copies:
        copy.start()
    return copies


def selections(place_ref, pick_ref, per_block, reals):
    block = lax.axis_index("blk")
    blocks, real_groups = lax.axis_size("blk"), lax.axis_size("real")
    modes, cycles, half = per_block * blocks, 2 * blocks, LANES // 2

    lane = lane_ids((1, LANES))
    row = row_ids((LANES, LANES))
    lane_order = (lane & (half - 1)) >> log2(cycles)
    lane_row = (lane & 1) * half + (lane >> log2(half)) * modes + block * per_block + lane_order
    pick_ref[0] = (row == lane_row).astype(jnp.float32).astype(jnp.bfloat16)
    lane_row = (lane >> log2(half)) * per_block + (lane & (per_block - 1))
    pick_ref[1] = ((row >> log2(cycles)) == lane_row).astype(jnp.float32).astype(jnp.bfloat16)

    spacing = reals + 2
    column = lane_ids((1, place_ref.shape[1]))
    source = (column * (2**16 // spacing + 1)) >> 16
    inside = column - source * spacing
    source_block = source >> log2(real_groups)
    target = ((source & (real_groups - 1)) * blocks + source_block) * reals + inside
    target = jnp.where(inside < reals, target, blocks * real_groups * reals + source_block)
    place = (row_ids(place_ref.shape) == target).astype(jnp.float32)
    place_ref[...] = place.astype(jnp.bfloat16)


def forward_kernel(
    cycle_len, half_len, syn_scale, reals,
    cycle_hbm, mode_hbm, noise_hbm, mask_hbm, spectrum_hbm, legendre_hbm, sky_hbm, prev_hbm,
    out_ref, inner_ref, outer_ref, place_ref, pick_ref, doubled_ref, factor_ref,
    cycle_ref, mode_ref, noise_ref, mask_ref, spectrum_ref, legendre_ref, sky_ref, prev_ref, gram_ref, sems,
):
    small = start_copies(
        (cycle_hbm, mode_hbm, noise_hbm, mask_hbm, spectrum_hbm, legendre_hbm),
        (cycle_ref, mode_ref, noise_ref, mask_ref, spectrum_ref, legendre_ref),
        sems,
    )
    large = start_copies((sky_hbm, prev_hbm), (sky_ref, prev_ref), sems, len(small))
    group = lax.axis_index("grp")
    per_block = legendre_ref.shape[0] // (2 * lax.axis_size("blk"))
    selections(place_ref, pick_ref, per_block, reals)
    small[0].wait()
    small[1].wait()
    inner, outer = phase_factors(cycle_ref[...], mode_ref[...], cycle_len, half_len, group)
    inner_ref[...] = inner
    outer_ref[...] = outer
    small[2].wait()
    small[3].wait()
    weight = mask_ref[...].astype(jnp.float32) / (noise_ref[...] - 0.5)
    inverse = 1.0 / (weight + 2.0)
    sky_gain = weight * inverse
    prev_gain = 2.0 * inverse

    for copy in small[4:] + large:
        copy.wait()
    table = legendre_ref[...]
    spectrum = spectrum_ref[...]
    factor = spectrum / (spectrum + 0.5)
    doubled_ref[...] = jnp.concatenate([table, table], axis=0)
    factor_ref[...] = factor
    filtered = (table.astype(jnp.float32) * factor).astype(jnp.bfloat16)
    gram = lax.dot_general(table, filtered, NT, preferred_element_type=jnp.float32)
    table_rows = table.shape[0]
    pixel_rows = outer.shape[0]
    blocks, real_groups = lax.axis_size("blk"), lax.axis_size("real")
    cycles = 2 * blocks
    same = (row_ids(gram.shape) >> log2(cycles)) == (lane_ids((1, table_rows)) >> log2(cycles))
    gram = jnp.where(same, gram, 0.0).reshape(table_rows // cycles, cycles, table_rows).sum(axis=0)
    gram = gram * syn_scale
    gram_ref[...] = jnp.concatenate([gram, gram], axis=1)
    even, odd = gram_ref[pl.ds(0, blocks, stride=2), :], gram_ref[pl.ds(1, blocks, stride=2), :]
    gram = jnp.where(lane_ids(even.shape) < LANES // 2, even, odd)
    gram_high = gram.astype(jnp.bfloat16).astype(jnp.float32)
    gram_low = gram - gram_high

    shape = (reals, 2 * pixel_rows, LANES)
    messenger = sky_ref[...].reshape(shape) * sky_gain + prev_ref[...].reshape(shape) * prev_gain
    rows = jnp.concatenate([messenger[:, :pixel_rows], messenger[:, pixel_rows:]], axis=2)
    rows = rows.reshape(-1, 2 * LANES).astype(jnp.bfloat16)
    partial = jnp.dot(rows, inner, preferred_element_type=jnp.float32)
    partial = partial[:, :LANES] + partial[:, LANES:]
    turned = partial.reshape(reals, pixel_rows, LANES) * outer
    summed = turned.reshape(reals, pixel_rows // 8, 8, LANES).sum(axis=1)
    summed = summed.reshape(reals * 8, LANES)
    summed = summed + pltpu.roll(summed, LANES // 2, 1)
    own = (row_ids(summed.shape) & 1) == (lane_ids(summed.shape) >= LANES // 2)
    fourier = jnp.where(own, summed, 0.0).reshape(reals, 8, LANES).sum(axis=1) * cycle_len**-0.5
    rows = []
    for b in range(blocks):
        rows += [fourier, gram_high[b : b + 1], gram_low[b : b + 1]] * real_groups
    out_ref[...] = jnp.concatenate(rows, axis=0).astype(jnp.bfloat16)


def backward_kernel(
    blocks, real_groups, reals, parts,
    gathered_ref, swapped_ref, inner_ref, outer_ref, place_ref, pick_ref, table_ref, factor_ref,
    wiener_hbm, signal_hbm, wiener_ref, signal_ref, fourier_ref, out_sems,
):
    real_group = lax.axis_index("real")
    cycles = 2 * blocks
    per_block = table_ref.shape[0] // (2 * cycles)
    modes = per_block * blocks
    pixel_rows = outer_ref.shape[0]
    half = LANES // 2
    lane = lane_ids((1, LANES))
    holder = (lane & (modes - 1)) >> log2(per_block)
    lane_block = (lane & (cycles - 1)) >> 1
    total_reals = real_groups * reals
    fourier_rows = blocks * total_reals
    sides = jnp.concatenate([gathered_ref[...], swapped_ref[...]], axis=1)
    placed = jnp.dot(place_ref[...], sides, preferred_element_type=jnp.float32)
    placed = placed[:, :LANES] + placed[:, LANES:]
    fourier_ref[...] = placed[:fourier_rows]

    coeff_rows = jnp.dot(
        placed[:fourier_rows].astype(jnp.bfloat16), pick_ref[0], preferred_element_type=jnp.float32
    ).reshape(real_groups, blocks, reals, LANES)
    columns = jnp.zeros((total_reals, LANES), jnp.float32)
    for b in range(blocks):
        one = coeff_rows[:, b].reshape(total_reals, LANES)
        columns = columns + jnp.where(lane_block == b, one, 0.0)
    table = table_ref[...]
    factor = factor_ref[...]
    stores = []
    own = (lane >> log2(cycles)) == row_ids((2 * per_block, LANES))
    upper = row_ids((1, 2 * per_block, LANES)) < per_block
    for y in range(real_groups):
        span = slice(y * reals, (y + 1) * reals)
        pieces = jnp.where(own, columns[span, None, :], 0.0)
        filtered = factor * jnp.dot(
            pieces.reshape(-1, LANES).astype(jnp.bfloat16), table, preferred_element_type=jnp.float32
        )
        for pair in range(wiener_ref.shape[2]):
            one, two = (
                filtered[:, tile * LANES : (tile + 1) * LANES].reshape(reals, 2 * per_block, LANES)
                for tile in (2 * pair, 2 * pair + 1)
            )
            wiener_ref[span, 0, pair] = jnp.where(upper, one, pltpu.roll(two, per_block, 1))
            wiener_ref[span, 1, pair] = jnp.where(upper, pltpu.roll(one, per_block, 1), two)
        span = pl.ds(y * reals, reals)
        stores += start_copies([wiener_ref.at[span]], [wiener_hbm.at[span]], out_sems, len(stores))

    gram_all = jnp.where(
        (lane & (cycles - 1)) == row_ids((cycles, LANES)), placed[fourier_rows:, None, :], 0.0
    ).reshape(blocks * cycles, LANES)
    gram_high = gram_all.astype(jnp.bfloat16)
    gram_low = (gram_all - gram_high.astype(jnp.float32)).astype(jnp.bfloat16)
    gram_rows = jnp.dot(
        jnp.concatenate([gram_high, gram_low], axis=1),
        jnp.concatenate([pick_ref[1], pick_ref[1]], axis=0),
        preferred_element_type=jnp.float32,
    ).reshape(blocks, cycles, LANES)
    gram = jnp.zeros((cycles, LANES), jnp.float32)
    for b in range(blocks):
        gram = gram + jnp.where(holder == b, gram_rows[b], 0.0)

    first = lane < half
    cycle_modes = jnp.zeros((reals, LANES), jnp.float32)
    for b in range(blocks):
        first_row = pl.multiple_of((real_group * blocks + b) * reals, reals)
        pair = fourier_ref[pl.ds(first_row, reals), :]
        turned = pltpu.roll(pair, half, 1)
        cycle_modes = cycle_modes + jnp.where(first, pair, turned) * gram[2 * b : 2 * b + 1]
        cycle_modes = cycle_modes + jnp.where(first, turned, pair) * gram[2 * b + 1 : 2 * b + 2]
    cycle_modes = cycle_modes * modes**-0.5
    turned = pltpu.roll(cycle_modes, half, 1)
    even = jnp.where(first, cycle_modes, turned)
    odd = jnp.where(first, turned, cycle_modes)
    parity = (row_ids((1, 8, LANES)) & 1) == 0
    spread = jnp.where(parity, even[:, None, :], odd[:, None, :])
    inner = inner_ref[...]
    outer = outer_ref[...].reshape(1, pixel_rows // 8, 8, LANES)
    part_reals = reals // parts
    for i in range(parts):
        span = slice(i * part_reals, (i + 1) * part_reals)
        rotated = (spread[span, None] * outer).reshape(-1, LANES).astype(jnp.bfloat16)
        signal = lax.dot_general(
            jnp.concatenate([rotated, rotated], axis=1), inner, NT, preferred_element_type=jnp.float32
        ).reshape(part_reals, pixel_rows, 2 * LANES)
        signal_ref[span, 0] = signal[:, :, :LANES]
        signal_ref[span, 1] = signal[:, :, LANES:]
        span = pl.ds(i * part_reals, part_reals)
        stores += start_copies([signal_ref.at[span]], [signal_hbm.at[span]], out_sems, len(stores))
    for store in stores:
        store.wait()


def split_tiles(array):
    lead, rows, columns = array.shape[:-2], array.shape[-2], array.shape[-1]
    split = array.reshape(*lead, rows, columns // LANES, LANES)
    return jnp.swapaxes(split, -2, -3).reshape(-1, LANES)


def gram_program(
    sky_data, signal_prev, noise_var, mask_flags, cycle_table, m_table, spectrum, legendre
):
    reals, cycle_dev, half_len = sky_data.shape
    groups, blocks, real_groups = (lax.axis_size(name) for name in AXES)
    cycle_len = half_len * groups
    per_block, multipoles, cycles = legendre.shape
    total_l = multipoles * groups * real_groups
    tiles = multipoles // LANES
    hbm = pl.BlockSpec(memory_space=pltpu.HBM)
    vmem = pl.BlockSpec(memory_space=pltpu.VMEM)
    orders = m_table[None, :]
    cycles_row = cycle_table[None, :]
    spectrum_row = spectrum[None, :]
    table = legendre.transpose(0, 2, 1).reshape(per_block * cycles, multipoles)
    inputs = (
        cycles_row, orders, split_tiles(noise_var), split_tiles(mask_flags), spectrum_row, table,
        split_tiles(sky_data), split_tiles(signal_prev),
    )
    sources = blocks * real_groups
    total_reals = reals * real_groups
    local, *prepared = pl.pallas_call(
        functools.partial(forward_kernel, cycle_len, half_len, (cycles / total_l) ** 0.5, reals),
        out_shape=(
            jax.ShapeDtypeStruct((sources * (reals + 2), LANES), jnp.bfloat16),
            jax.ShapeDtypeStruct((2 * LANES, 2 * LANES), jnp.bfloat16),
            jax.ShapeDtypeStruct((half_len // LANES, LANES), jnp.float32),
            jax.ShapeDtypeStruct((blocks * (total_reals + 1), sources * (reals + 2)), jnp.bfloat16),
            jax.ShapeDtypeStruct((2, LANES, LANES), jnp.bfloat16),
            jax.ShapeDtypeStruct((2 * table.shape[0], multipoles), jnp.bfloat16),
            jax.ShapeDtypeStruct((1, multipoles), jnp.float32),
        ),
        in_specs=[hbm] * 8,
        out_specs=(vmem,) * 7,
        scratch_shapes=[pltpu.VMEM(x.shape, x.dtype) for x in inputs]
        + [pltpu.VMEM((cycles, LANES), jnp.float32), pltpu.SemaphoreType.DMA((8,))],
        compiler_params=pltpu.CompilerParams(vmem_limit_bytes=FORWARD_VMEM),
    )(*(pltpu.with_memory_space_constraint(x, pltpu.HBM) for x in inputs))
    pairs = local.reshape(sources, reals // 2 + 1, 2, LANES)
    gathered = lax.all_to_all(pairs, ("blk", "real"), 0, 0, tiled=True)
    swapped = lax.ppermute(gathered, "grp", [(i, i ^ 1) for i in range(groups)])
    outputs = (
        jax.ShapeDtypeStruct((total_reals, 2, tiles // 2, 2 * per_block, LANES), jnp.float32),
        jax.ShapeDtypeStruct((reals, 2, half_len // LANES, LANES), jnp.float32),
    )
    wiener, signal = pl.pallas_call(
        functools.partial(backward_kernel, blocks, real_groups, reals, PARTS),
        out_shape=outputs,
        in_specs=[vmem] * 8,
        out_specs=(hbm, hbm),
        scratch_shapes=[pltpu.VMEM(x.shape, x.dtype) for x in outputs]
        + [pltpu.VMEM((blocks * total_reals, LANES), jnp.float32)]
        + [pltpu.SemaphoreType.DMA((real_groups + PARTS,))],
        compiler_params=pltpu.CompilerParams(vmem_limit_bytes=BACKWARD_VMEM),
    )(gathered.reshape(local.shape), swapped.reshape(local.shape), *prepared)
    wiener = wiener.reshape(total_reals, 2, tiles, per_block, LANES).transpose(0, 1, 3, 2, 4)
    signal = signal.reshape(reals, half_len // LANES, cycle_dev, LANES).transpose(0, 2, 1, 3)
    return (
        wiener.reshape(total_reals, 2, per_block, multipoles),
        signal.reshape(sky_data.shape),
    )


def gram_form_fits(mesh, sky_data, m_table, legendre):
    groups, blocks, real_groups = (mesh.shape[name] for name in AXES)
    reals, cycles, cycle_len = sky_data.shape
    modes = m_table.shape[0]
    per_block = modes // blocks
    multipoles = legendre.shape[1] // (groups * real_groups)
    half_len = cycle_len // groups
    reals_dev = reals // real_groups
    return (
        cycles < 2 * reals
        and groups == 2
        and 4 * modes == LANES
        and cycles == 2 * blocks
        and all(size & (size - 1) == 0 for size in (blocks, modes, cycles, real_groups))
        and 2 * reals * cycles < 2**12
        and 2 * per_block * cycles == LANES
        and cycle_len & (cycle_len - 1) == 0
        and half_len % (8 * LANES) == 0
        and multipoles % (2 * LANES) == 0
        and per_block == 4
        and reals_dev % 16 == 0
        and reals_dev % PARTS == 0
        and cycles % 16 == 0
    )


def phase_tables(col_ids, mode_ids, cycle_len):
    product_ids = col_ids[:, None] * mode_ids[None, :] % cycle_len
    angles = product_ids.astype(jnp.float32) * (2.0 * math.pi / cycle_len)
    return (jnp.cos(angles).astype(jnp.bfloat16), jnp.sin(angles).astype(jnp.bfloat16))


def cycle_offsets(cycle_ids, mode_ids, cycle_len):
    parity = (cycle_ids % 2).astype(jnp.float32)
    shifts = math.pi / cycle_len * parity[:, None] * mode_ids[None, :].astype(jnp.float32)
    return (jnp.cos(shifts), jnp.sin(shifts))


def forward_modes(re_part, im_part):
    summed = lax.psum((re_part, im_part), "grp")
    fourier_pair = (summed[0].astype(jnp.bfloat16), summed[1].astype(jnp.bfloat16))
    fourier_pair = (
        lax.all_gather(fourier_pair[0], "real", axis=0, tiled=True),
        lax.all_gather(fourier_pair[1], "real", axis=0, tiled=True),
    )
    fourier_pair = (
        lax.all_to_all(fourier_pair[0], "blk", split_axis=2, concat_axis=1, tiled=True),
        lax.all_to_all(fourier_pair[1], "blk", split_axis=2, concat_axis=1, tiled=True),
    )
    return fourier_pair


def backward_cycles(partial_value):
    summed = lax.psum_scatter(partial_value, "real", scatter_dimension=0, tiled=True)
    reduced = lax.psum(summed, "grp")
    cycle_pair = lax.all_to_all(
        reduced.astype(jnp.bfloat16), "blk", split_axis=2, concat_axis=3, tiled=True
    )
    return cycle_pair


def per_device(
    sky_data, signal_prev, noise_var, mask_flags, cycle_table, m_table, spectrum, legendre
):
    real_dev, cycle_dev, half_len = sky_data.shape
    cycle_len = half_len * lax.axis_size("grp")
    mode_count = m_table.shape[0]
    col_ids = lax.axis_index("grp") * half_len + jnp.arange(half_len, dtype=jnp.int32)
    cos_tab, sin_tab = phase_tables(col_ids, m_table, cycle_len)
    cos_shift, sin_shift = cycle_offsets(cycle_table, m_table, cycle_len)
    weight = mask_flags.astype(jnp.float32) / (noise_var - 0.5)
    messenger = (weight * sky_data + 2.0 * signal_prev) / (weight + 2.0)
    flat_rows = messenger.astype(jnp.bfloat16).reshape(real_dev * cycle_dev, half_len)
    base_cos = jnp.dot(flat_rows, cos_tab, preferred_element_type=jnp.float32).reshape(
        real_dev, cycle_dev, mode_count
    )
    base_sin = -jnp.dot(flat_rows, sin_tab, preferred_element_type=jnp.float32).reshape(
        real_dev, cycle_dev, mode_count
    )
    norm_scale = cycle_len ** (-0.5)
    re_part = (base_cos * cos_shift + base_sin * sin_shift) * norm_scale
    im_part = (base_sin * cos_shift - base_cos * sin_shift) * norm_scale
    fourier_re, fourier_im = forward_modes(re_part, im_part)
    fourier = jnp.stack([fourier_re, fourier_im], 1)
    coefficients = jnp.einsum(
        "mlr,kcrm->kcml", legendre, fourier, preferred_element_type=jnp.float32
    )
    factor = spectrum / (spectrum + 0.5)
    wiener_alm = coefficients * factor
    total_l = legendre.shape[1] * lax.axis_size("grp") * lax.axis_size("real")
    syn_scale = (legendre.shape[2] / total_l) ** 0.5
    partial_value = (
        jnp.einsum(
            "mlr,kcml->kcrm",
            legendre,
            wiener_alm.astype(jnp.bfloat16),
            preferred_element_type=jnp.float32,
        )
        * syn_scale
    )
    cycle_pair = backward_cycles(partial_value)
    cycle_modes = cycle_pair.astype(jnp.float32)
    modes_re = cycle_modes[:, 0]
    modes_im = cycle_modes[:, 1]
    rotated_re = (modes_re * cos_shift - modes_im * sin_shift).astype(jnp.bfloat16)
    rotated_im = (modes_im * cos_shift + modes_re * sin_shift).astype(jnp.bfloat16)
    contract = (((1,), (1,)), ((), ()))
    pixel_sum = lax.dot_general(
        rotated_re.reshape(-1, mode_count), cos_tab, contract, preferred_element_type=jnp.float32
    )
    pixel_sum = pixel_sum - lax.dot_general(
        rotated_im.reshape(-1, mode_count), sin_tab, contract, preferred_element_type=jnp.float32
    )
    signal_next = (pixel_sum * mode_count ** (-0.5)).reshape(real_dev, cycle_dev, half_len)
    return (wiener_alm, signal_next)


def solution(mesh):
    in_specs = (
        P("real", "blk", "grp"),
        P("real", "blk", "grp"),
        P("blk", "grp"),
        P("blk", "grp"),
        P("blk"),
        P(),
        P(("grp", "real")),
        P("blk", ("grp", "real"), None),
    )
    out_specs = (P(None, None, "blk", ("grp", "real")), P("real", "blk", "grp"))

    def step(sky_data, signal_prev, noise_var, mask_flags, cycle_table, m_table, spectrum, legendre):
        fits = gram_form_fits(mesh, sky_data, m_table, legendre)
        return jax.shard_map(
            gram_program if fits else per_device,
            mesh=mesh,
            in_specs=in_specs,
            out_specs=out_specs,
            check_vma=False,
        )(sky_data, signal_prev, noise_var, mask_flags, cycle_table, m_table, spectrum, legendre)

    return step
```

```python
import functools
import math

import jax
import jax.numpy as jnp
from jax import lax
from jax.experimental import pallas as pl
from jax.experimental.pallas import tpu as pltpu
from jax.sharding import PartitionSpec as P

LANES = 128
NT = (((1,), (1,)), ((), ()))
AXES = ("grp", "blk", "real")
PARTS = 2
FORWARD_VMEM = 32 << 20
BACKWARD_VMEM = 16 << 20


def unit_cosine(units, half_turn):
    wrapped = units & (2 * half_turn - 1)
    folded = jnp.minimum(wrapped, 2 * half_turn - wrapped)
    y = (half_turn // 2 - folded).astype(jnp.float32) * (math.pi / half_turn)
    y2 = y * y
    acc = jnp.full_like(y2, -1.0 / math.factorial(11))
    for order, sign in ((9, 1.0), (7, -1.0), (5, 1.0), (3, -1.0), (1, 1.0)):
        acc = acc * y2 + sign / math.factorial(order)
    return acc * y


def log2(size):
    return size.bit_length() - 1


def lane_ids(shape):
    return lax.broadcasted_iota(jnp.int32, shape, len(shape) - 1)


def row_ids(shape):
    return lax.broadcasted_iota(jnp.int32, shape, len(shape) - 2)


def phase_factors(cycles, orders, cycle_len, half_len, group):
    modes = orders.shape[1]
    orders = jnp.concatenate([orders] * (LANES // modes), axis=1)
    quarter = lane_ids((1, LANES)) >> log2(modes)
    quarter_turn = cycle_len // 2
    row = row_ids((2 * LANES, LANES))
    pixel = (row >> log2(LANES)) * (half_len // 2) + (row & (LANES - 1))
    inner_units = 2 * orders * pixel + ((quarter + 1) >> 1) * quarter_turn
    inner = unit_cosine(inner_units, cycle_len)
    rows = half_len // LANES
    row = row_ids((rows, LANES))
    parity = jnp.where((row & 1) == 0, cycles[:, :1], cycles[:, 1:]) & 1
    pixel = group * half_len + LANES * (row >> 1)
    outer_units = orders * (2 * pixel + parity) + (quarter >> 1) * (3 * quarter_turn)
    outer = unit_cosine(outer_units, cycle_len)
    high = inner.astype(jnp.bfloat16)
    low = (inner - high.astype(jnp.float32)).astype(jnp.bfloat16)
    return jnp.concatenate([high, low], axis=1), outer


def start_copies(sources, targets, sems, first=0):
    copies = [
        pltpu.make_async_copy(source, target, sems.at[first + i])
        for i, (source, target) in enumerate(zip(sources, targets))
    ]
    for copy in copies:
        copy.start()
    return copies


def selections(place_ref, pick_ref, per_block, reals):
    block = lax.axis_index("blk")
    blocks, real_groups = lax.axis_size("blk"), lax.axis_size("real")
    modes, cycles, half = per_block * blocks, 2 * blocks, LANES // 2

    lane = lane_ids((1, LANES))
    row = row_ids((LANES, LANES))
    lane_order = (lane & (half - 1)) >> log2(cycles)
    lane_row = (lane & 1) * half + (lane >> log2(half)) * modes + block * per_block + lane_order
    pick_ref[0] = (row == lane_row).astype(jnp.float32).astype(jnp.bfloat16)
    lane_row = (lane >> log2(half)) * per_block + (lane & (per_block - 1))
    pick_ref[1] = ((row >> log2(cycles)) == lane_row).astype(jnp.float32).astype(jnp.bfloat16)

    spacing = reals + 2
    column = lane_ids((1, place_ref.shape[1]))
    source = (column * (2**16 // spacing + 1)) >> 16
    inside = column - source * spacing
    source_block = source >> log2(real_groups)
    target = ((source & (real_groups - 1)) * blocks + source_block) * reals + inside
    target = jnp.where(inside < reals, target, blocks * real_groups * reals + source_block)
    place = (row_ids(place_ref.shape) == target).astype(jnp.float32)
    place_ref[...] = place.astype(jnp.bfloat16)


def forward_kernel(
    cycle_len, half_len, syn_scale, reals,
    cycle_hbm, mode_hbm, noise_hbm, mask_hbm, spectrum_hbm, legendre_hbm, sky_hbm, prev_hbm,
    out_ref, inner_ref, outer_ref, place_ref, pick_ref, doubled_ref, factor_ref,
    cycle_ref, mode_ref, noise_ref, mask_ref, spectrum_ref, legendre_ref, sky_ref, prev_ref, gram_ref, sems,
):
    small = start_copies(
        (cycle_hbm, mode_hbm, noise_hbm, mask_hbm, spectrum_hbm, legendre_hbm),
        (cycle_ref, mode_ref, noise_ref, mask_ref, spectrum_ref, legendre_ref),
        sems,
    )
    large = start_copies((sky_hbm, prev_hbm), (sky_ref, prev_ref), sems, len(small))
    group = lax.axis_index("grp")
    per_block = legendre_ref.shape[0] // (2 * lax.axis_size("blk"))
    selections(place_ref, pick_ref, per_block, reals)
    small[0].wait()
    small[1].wait()
    inner, outer = phase_factors(cycle_ref[...], mode_ref[...], cycle_len, half_len, group)
    inner_ref[...] = inner
    outer_ref[...] = outer
    small[2].wait()
    small[3].wait()
    weight = mask_ref[...].astype(jnp.float32) / (noise_ref[...] - 0.5)
    inverse = 1.0 / (weight + 2.0)
    sky_gain = weight * inverse
    prev_gain = 2.0 * inverse

    for copy in small[4:] + large:
        copy.wait()
    table = legendre_ref[...]
    spectrum = spectrum_ref[...]
    factor = spectrum / (spectrum + 0.5)
    doubled_ref[...] = jnp.concatenate([table, table], axis=0)
    factor_ref[...] = factor
    filtered = (table.astype(jnp.float32) * factor).astype(jnp.bfloat16)
    gram = lax.dot_general(table, filtered, NT, preferred_element_type=jnp.float32)
    table_rows = table.shape[0]
    pixel_rows = outer.shape[0]
    blocks, real_groups = lax.axis_size("blk"), lax.axis_size("real")
    cycles = 2 * blocks
    same = (row_ids(gram.shape) >> log2(cycles)) == (lane_ids((1, table_rows)) >> log2(cycles))
    gram = jnp.where(same, gram, 0.0).reshape(table_rows // cycles, cycles, table_rows).sum(axis=0)
    gram = gram * syn_scale
    gram_ref[...] = jnp.concatenate([gram, gram], axis=1)
    even, odd = gram_ref[pl.ds(0, blocks, stride=2), :], gram_ref[pl.ds(1, blocks, stride=2), :]
    gram = jnp.where(lane_ids(even.shape) < LANES // 2, even, odd)
    gram_high = gram.astype(jnp.bfloat16).astype(jnp.float32)
    gram_low = gram - gram_high

    shape = (reals, 2 * pixel_rows, LANES)
    messenger = sky_ref[...].reshape(shape) * sky_gain + prev_ref[...].reshape(shape) * prev_gain
    rows = jnp.concatenate([messenger[:, :pixel_rows], messenger[:, pixel_rows:]], axis=2)
    rows = rows.reshape(-1, 2 * LANES).astype(jnp.bfloat16)
    partial = jnp.dot(rows, inner, preferred_element_type=jnp.float32)
    partial = partial[:, :LANES] + partial[:, LANES:]
    turned = partial.reshape(reals, pixel_rows, LANES) * outer
    summed = turned.reshape(reals, pixel_rows // 8, 8, LANES).sum(axis=1)
    summed = summed.reshape(reals * 8, LANES)
    summed = summed + pltpu.roll(summed, LANES // 2, 1)
    own = (row_ids(summed.shape) & 1) == (lane_ids(summed.shape) >= LANES // 2)
    fourier = jnp.where(own, summed, 0.0).reshape(reals, 8, LANES).sum(axis=1) * cycle_len**-0.5
    rows = []
    for b in range(blocks):
        rows += [fourier, gram_high[b : b + 1], gram_low[b : b + 1]] * real_groups
    rows = jnp.concatenate(rows, axis=0).astype(jnp.bfloat16)
    for g in range(lax.axis_size("grp")):
        out_ref[pl.ds(g * rows.shape[0], rows.shape[0]), :] = rows


def backward_kernel(
    blocks, real_groups, reals, parts,
    gathered_ref, inner_ref, outer_ref, place_ref, pick_ref, table_ref, factor_ref,
    wiener_hbm, signal_hbm, wiener_ref, signal_ref, fourier_ref, out_sems,
):
    real_group = lax.axis_index("real")
    cycles = 2 * blocks
    per_block = table_ref.shape[0] // (2 * cycles)
    modes = per_block * blocks
    pixel_rows = outer_ref.shape[0]
    half = LANES // 2
    lane = lane_ids((1, LANES))
    holder = (lane & (modes - 1)) >> log2(per_block)
    lane_block = (lane & (cycles - 1)) >> 1
    total_reals = real_groups * reals
    fourier_rows = blocks * total_reals
    share = place_ref.shape[1]
    sides = jnp.concatenate([gathered_ref[:share, :], gathered_ref[share:, :]], axis=1)
    placed = jnp.dot(place_ref[...], sides, preferred_element_type=jnp.float32)
    placed = placed[:, :LANES] + placed[:, LANES:]
    fourier_ref[...] = placed[:fourier_rows]

    coeff_rows = jnp.dot(
        placed[:fourier_rows].astype(jnp.bfloat16), pick_ref[0], preferred_element_type=jnp.float32
    ).reshape(real_groups, blocks, reals, LANES)
    columns = jnp.zeros((total_reals, LANES), jnp.float32)
    for b in range(blocks):
        one = coeff_rows[:, b].reshape(total_reals, LANES)
        columns = columns + jnp.where(lane_block == b, one, 0.0)
    table = table_ref[...]
    factor = factor_ref[...]
    stores = []
    own = (lane >> log2(cycles)) == row_ids((2 * per_block, LANES))
    upper = row_ids((1, 2 * per_block, LANES)) < per_block
    pieces = jnp.where(own, columns[:, None, :], 0.0).reshape(-1, LANES).astype(jnp.bfloat16)
    filtered = factor * jnp.dot(pieces, table, preferred_element_type=jnp.float32)
    filtered = filtered.reshape(total_reals, 2 * per_block, -1)
    for y in range(real_groups):
        span = slice(y * reals, (y + 1) * reals)
        for pair in range(wiener_ref.shape[2]):
            one, two = (
                filtered[span, :, tile * LANES : (tile + 1) * LANES] for tile in (2 * pair, 2 * pair + 1)
            )
            wiener_ref[span, 0, pair] = jnp.where(upper, one, pltpu.roll(two, per_block, 1))
            wiener_ref[span, 1, pair] = jnp.where(upper, pltpu.roll(one, per_block, 1), two)
        span = pl.ds(y * reals, reals)
        stores += start_copies([wiener_ref.at[span]], [wiener_hbm.at[span]], out_sems, len(stores))

    gram_all = jnp.where(
        (lane & (cycles - 1)) == row_ids((cycles, LANES)), placed[fourier_rows:, None, :], 0.0
    ).reshape(blocks * cycles, LANES)
    gram_high = gram_all.astype(jnp.bfloat16)
    gram_low = (gram_all - gram_high.astype(jnp.float32)).astype(jnp.bfloat16)
    gram_rows = jnp.dot(
        jnp.concatenate([gram_high, gram_low], axis=1),
        jnp.concatenate([pick_ref[1], pick_ref[1]], axis=0),
        preferred_element_type=jnp.float32,
    ).reshape(blocks, cycles, LANES)
    gram = jnp.zeros((cycles, LANES), jnp.float32)
    for b in range(blocks):
        gram = gram + jnp.where(holder == b, gram_rows[b], 0.0)

    first = lane < half
    cycle_modes = jnp.zeros((reals, LANES), jnp.float32)
    for b in range(blocks):
        first_row = pl.multiple_of((real_group * blocks + b) * reals, reals)
        pair = fourier_ref[pl.ds(first_row, reals), :]
        turned = pltpu.roll(pair, half, 1)
        cycle_modes = cycle_modes + jnp.where(first, pair, turned) * gram[2 * b : 2 * b + 1]
        cycle_modes = cycle_modes + jnp.where(first, turned, pair) * gram[2 * b + 1 : 2 * b + 2]
    cycle_modes = cycle_modes * modes**-0.5
    turned = pltpu.roll(cycle_modes, half, 1)
    even = jnp.where(first, cycle_modes, turned)
    odd = jnp.where(first, turned, cycle_modes)
    parity = (row_ids((1, 8, LANES)) & 1) == 0
    spread = jnp.where(parity, even[:, None, :], odd[:, None, :])
    inner = inner_ref[...]
    outer = outer_ref[...].reshape(1, pixel_rows // 8, 8, LANES)
    rotated = (spread[:, None] * outer).reshape(-1, LANES).astype(jnp.bfloat16)
    signal = lax.dot_general(
        jnp.concatenate([rotated, rotated], axis=1), inner, NT, preferred_element_type=jnp.float32
    ).reshape(reals, pixel_rows, 2 * LANES)
    part_reals = reals // parts
    for i in range(parts):
        span = slice(i * part_reals, (i + 1) * part_reals)
        signal_ref[span, 0] = signal[span, :, :LANES]
        signal_ref[span, 1] = signal[span, :, LANES:]
        span = pl.ds(i * part_reals, part_reals)
        stores += start_copies([signal_ref.at[span]], [signal_hbm.at[span]], out_sems, len(stores))
    for store in stores:
        store.wait()


def split_tiles(array):
    lead, rows, columns = array.shape[:-2], array.shape[-2], array.shape[-1]
    split = array.reshape(*lead, rows, columns // LANES, LANES)
    return jnp.swapaxes(split, -2, -3).reshape(-1, LANES)


def gram_program(
    sky_data, signal_prev, noise_var, mask_flags, cycle_table, m_table, spectrum, legendre
):
    reals, cycle_dev, half_len = sky_data.shape
    groups, blocks, real_groups = (lax.axis_size(name) for name in AXES)
    cycle_len = half_len * groups
    per_block, multipoles, cycles = legendre.shape
    total_l = multipoles * groups * real_groups
    tiles = multipoles // LANES
    hbm = pl.BlockSpec(memory_space=pltpu.HBM)
    vmem = pl.BlockSpec(memory_space=pltpu.VMEM)
    orders = m_table[None, :]
    cycles_row = cycle_table[None, :]
    spectrum_row = spectrum[None, :]
    table = legendre.transpose(0, 2, 1).reshape(per_block * cycles, multipoles)
    inputs = (
        cycles_row, orders, split_tiles(noise_var), split_tiles(mask_flags), spectrum_row, table,
        split_tiles(sky_data), split_tiles(signal_prev),
    )
    sources = groups * blocks * real_groups
    total_reals = reals * real_groups
    local, *prepared = pl.pallas_call(
        functools.partial(forward_kernel, cycle_len, half_len, (cycles / total_l) ** 0.5, reals),
        out_shape=(
            jax.ShapeDtypeStruct((sources * (reals + 2), LANES), jnp.bfloat16),
            jax.ShapeDtypeStruct((2 * LANES, 2 * LANES), jnp.bfloat16),
            jax.ShapeDtypeStruct((half_len // LANES, LANES), jnp.float32),
            jax.ShapeDtypeStruct(
                (blocks * (total_reals + 1), blocks * real_groups * (reals + 2)), jnp.bfloat16
            ),
            jax.ShapeDtypeStruct((2, LANES, LANES), jnp.bfloat16),
            jax.ShapeDtypeStruct((2 * table.shape[0], multipoles), jnp.bfloat16),
            jax.ShapeDtypeStruct((1, multipoles), jnp.float32),
        ),
        in_specs=[hbm] * 8,
        out_specs=(vmem,) * 7,
        scratch_shapes=[pltpu.VMEM(x.shape, x.dtype) for x in inputs]
        + [pltpu.VMEM((cycles, LANES), jnp.float32), pltpu.SemaphoreType.DMA((8,))],
        compiler_params=pltpu.CompilerParams(vmem_limit_bytes=FORWARD_VMEM),
    )(*(pltpu.with_memory_space_constraint(x, pltpu.HBM) for x in inputs))
    pairs = local.reshape(sources, reals // 2 + 1, 2, LANES)
    gathered = lax.all_to_all(pairs, AXES, 0, 0, tiled=True).reshape(local.shape)
    outputs = (
        jax.ShapeDtypeStruct((total_reals, 2, tiles // 2, 2 * per_block, LANES), jnp.float32),
        jax.ShapeDtypeStruct((reals, 2, half_len // LANES, LANES), jnp.float32),
    )
    wiener, signal = pl.pallas_call(
        functools.partial(backward_kernel, blocks, real_groups, reals, PARTS),
        out_shape=outputs,
        in_specs=[vmem] * 7,
        out_specs=(hbm, hbm),
        scratch_shapes=[pltpu.VMEM(x.shape, x.dtype) for x in outputs]
        + [pltpu.VMEM((blocks * total_reals, LANES), jnp.float32)]
        + [pltpu.SemaphoreType.DMA((real_groups + PARTS,))],
        compiler_params=pltpu.CompilerParams(vmem_limit_bytes=BACKWARD_VMEM),
    )(gathered, *prepared)
    wiener = wiener.reshape(total_reals, 2, tiles, per_block, LANES).transpose(0, 1, 3, 2, 4)
    signal = signal.reshape(reals, half_len // LANES, cycle_dev, LANES).transpose(0, 2, 1, 3)
    return (
        wiener.reshape(total_reals, 2, per_block, multipoles),
        signal.reshape(sky_data.shape),
    )


def gram_form_fits(mesh, sky_data, m_table, legendre):
    groups, blocks, real_groups = (mesh.shape[name] for name in AXES)
    reals, cycles, cycle_len = sky_data.shape
    modes = m_table.shape[0]
    per_block = modes // blocks
    multipoles = legendre.shape[1] // (groups * real_groups)
    half_len = cycle_len // groups
    reals_dev = reals // real_groups
    return (
        cycles < 2 * reals
        and 4 * modes == LANES
        and cycles == 2 * blocks
        and all(size & (size - 1) == 0 for size in (blocks, modes, cycles, real_groups))
        and 2 * reals * cycles < 2**12
        and 2 * per_block * cycles == LANES
        and cycle_len & (cycle_len - 1) == 0
        and half_len % (8 * LANES) == 0
        and multipoles % (2 * LANES) == 0
        and per_block == 4
        and reals_dev % 16 == 0
        and reals_dev % PARTS == 0
        and cycles % 16 == 0
    )


def phase_tables(col_ids, mode_ids, cycle_len):
    product_ids = col_ids[:, None] * mode_ids[None, :] % cycle_len
    angles = product_ids.astype(jnp.float32) * (2.0 * math.pi / cycle_len)
    return (jnp.cos(angles).astype(jnp.bfloat16), jnp.sin(angles).astype(jnp.bfloat16))


def cycle_offsets(cycle_ids, mode_ids, cycle_len):
    parity = (cycle_ids % 2).astype(jnp.float32)
    shifts = math.pi / cycle_len * parity[:, None] * mode_ids[None, :].astype(jnp.float32)
    return (jnp.cos(shifts), jnp.sin(shifts))


def forward_modes(re_part, im_part):
    summed = lax.psum((re_part, im_part), "grp")
    fourier_pair = (summed[0].astype(jnp.bfloat16), summed[1].astype(jnp.bfloat16))
    fourier_pair = (
        lax.all_gather(fourier_pair[0], "real", axis=0, tiled=True),
        lax.all_gather(fourier_pair[1], "real", axis=0, tiled=True),
    )
    fourier_pair = (
        lax.all_to_all(fourier_pair[0], "blk", split_axis=2, concat_axis=1, tiled=True),
        lax.all_to_all(fourier_pair[1], "blk", split_axis=2, concat_axis=1, tiled=True),
    )
    return fourier_pair


def backward_cycles(partial_value):
    summed = lax.psum_scatter(partial_value, "real", scatter_dimension=0, tiled=True)
    reduced = lax.psum(summed, "grp")
    cycle_pair = lax.all_to_all(
        reduced.astype(jnp.bfloat16), "blk", split_axis=2, concat_axis=3, tiled=True
    )
    return cycle_pair


def per_device(
    sky_data, signal_prev, noise_var, mask_flags, cycle_table, m_table, spectrum, legendre
):
    real_dev, cycle_dev, half_len = sky_data.shape
    cycle_len = half_len * lax.axis_size("grp")
    mode_count = m_table.shape[0]
    col_ids = lax.axis_index("grp") * half_len + jnp.arange(half_len, dtype=jnp.int32)
    cos_tab, sin_tab = phase_tables(col_ids, m_table, cycle_len)
    cos_shift, sin_shift = cycle_offsets(cycle_table, m_table, cycle_len)
    weight = mask_flags.astype(jnp.float32) / (noise_var - 0.5)
    messenger = (weight * sky_data + 2.0 * signal_prev) / (weight + 2.0)
    flat_rows = messenger.astype(jnp.bfloat16).reshape(real_dev * cycle_dev, half_len)
    base_cos = jnp.dot(flat_rows, cos_tab, preferred_element_type=jnp.float32).reshape(
        real_dev, cycle_dev, mode_count
    )
    base_sin = -jnp.dot(flat_rows, sin_tab, preferred_element_type=jnp.float32).reshape(
        real_dev, cycle_dev, mode_count
    )
    norm_scale = cycle_len ** (-0.5)
    re_part = (base_cos * cos_shift + base_sin * sin_shift) * norm_scale
    im_part = (base_sin * cos_shift - base_cos * sin_shift) * norm_scale
    fourier_re, fourier_im = forward_modes(re_part, im_part)
    fourier = jnp.stack([fourier_re, fourier_im], 1)
    coefficients = jnp.einsum(
        "mlr,kcrm->kcml", legendre, fourier, preferred_element_type=jnp.float32
    )
    factor = spectrum / (spectrum + 0.5)
    wiener_alm = coefficients * factor
    total_l = legendre.shape[1] * lax.axis_size("grp") * lax.axis_size("real")
    syn_scale = (legendre.shape[2] / total_l) ** 0.5
    partial_value = (
        jnp.einsum(
            "mlr,kcml->kcrm",
            legendre,
            wiener_alm.astype(jnp.bfloat16),
            preferred_element_type=jnp.float32,
        )
        * syn_scale
    )
    cycle_pair = backward_cycles(partial_value)
    cycle_modes = cycle_pair.astype(jnp.float32)
    modes_re = cycle_modes[:, 0]
    modes_im = cycle_modes[:, 1]
    rotated_re = (modes_re * cos_shift - modes_im * sin_shift).astype(jnp.bfloat16)
    rotated_im = (modes_im * cos_shift + modes_re * sin_shift).astype(jnp.bfloat16)
    contract = (((1,), (1,)), ((), ()))
    pixel_sum = lax.dot_general(
        rotated_re.reshape(-1, mode_count), cos_tab, contract, preferred_element_type=jnp.float32
    )
    pixel_sum = pixel_sum - lax.dot_general(
        rotated_im.reshape(-1, mode_count), sin_tab, contract, preferred_element_type=jnp.float32
    )
    signal_next = (pixel_sum * mode_count ** (-0.5)).reshape(real_dev, cycle_dev, half_len)
    return (wiener_alm, signal_next)


def solution(mesh):
    in_specs = (
        P("real", "blk", "grp"),
        P("real", "blk", "grp"),
        P("blk", "grp"),
        P("blk", "grp"),
        P("blk"),
        P(),
        P(("grp", "real")),
        P("blk", ("grp", "real"), None),
    )
    out_specs = (P(None, None, "blk", ("grp", "real")), P("real", "blk", "grp"))

    def step(sky_data, signal_prev, noise_var, mask_flags, cycle_table, m_table, spectrum, legendre):
        fits = gram_form_fits(mesh, sky_data, m_table, legendre)
        return jax.shard_map(
            gram_program if fits else per_device,
            mesh=mesh,
            in_specs=in_specs,
            out_specs=out_specs,
            check_vma=False,
        )(sky_data, signal_prev, noise_var, mask_flags, cycle_table, m_table, spectrum, legendre)

    return step
```

```python
import functools
import math

import jax
import jax.numpy as jnp
from jax import lax
from jax.experimental import pallas as pl
from jax.experimental.pallas import tpu as pltpu
from jax.sharding import PartitionSpec as P

LANES = 128
NT = (((1,), (1,)), ((), ()))
AXES = ("grp", "blk", "real")
PARTS = 2
FORWARD_VMEM = 32 << 20
BACKWARD_VMEM = 16 << 20


def unit_cosine(units, half_turn):
    wrapped = units & (2 * half_turn - 1)
    folded = jnp.minimum(wrapped, 2 * half_turn - wrapped)
    y = (half_turn // 2 - folded).astype(jnp.float32) * (math.pi / half_turn)
    y2 = y * y
    acc = jnp.full_like(y2, -1.0 / math.factorial(11))
    for order, sign in ((9, 1.0), (7, -1.0), (5, 1.0), (3, -1.0), (1, 1.0)):
        acc = acc * y2 + sign / math.factorial(order)
    return acc * y


def log2(size):
    return size.bit_length() - 1


def lane_ids(shape):
    return lax.broadcasted_iota(jnp.int32, shape, len(shape) - 1)


def row_ids(shape):
    return lax.broadcasted_iota(jnp.int32, shape, len(shape) - 2)


def phase_factors(cycles, orders, cycle_len, half_len, group):
    modes = orders.shape[1]
    orders = jnp.concatenate([orders] * (LANES // modes), axis=1)
    quarter = lane_ids((1, LANES)) >> log2(modes)
    quarter_turn = cycle_len // 2
    row = row_ids((2 * LANES, LANES))
    pixel = (row >> log2(LANES)) * (half_len // 2) + (row & (LANES - 1))
    inner_units = 2 * orders * pixel + ((quarter + 1) >> 1) * quarter_turn
    inner = unit_cosine(inner_units, cycle_len)
    rows = half_len // LANES
    row = row_ids((rows, LANES))
    parity = jnp.where((row & 1) == 0, cycles[:, :1], cycles[:, 1:]) & 1
    pixel = group * half_len + LANES * (row >> 1)
    outer_units = orders * (2 * pixel + parity) + (quarter >> 1) * (3 * quarter_turn)
    outer = unit_cosine(outer_units, cycle_len)
    high = inner.astype(jnp.bfloat16)
    low = (inner - high.astype(jnp.float32)).astype(jnp.bfloat16)
    return jnp.concatenate([high, low], axis=1), outer


def start_copies(sources, targets, sems, first=0):
    copies = [
        pltpu.make_async_copy(source, target, sems.at[first + i])
        for i, (source, target) in enumerate(zip(sources, targets))
    ]
    for copy in copies:
        copy.start()
    return copies


def selections(place_ref, pick_ref, per_block, reals):
    block = lax.axis_index("blk")
    blocks, real_groups = lax.axis_size("blk"), lax.axis_size("real")
    modes, cycles, half = per_block * blocks, 2 * blocks, LANES // 2

    lane = lane_ids((1, LANES))
    row = row_ids((LANES, LANES))
    lane_order = (lane & (half - 1)) >> log2(cycles)
    lane_row = (lane & 1) * half + (lane >> log2(half)) * modes + block * per_block + lane_order
    pick_ref[0] = (row == lane_row).astype(jnp.float32).astype(jnp.bfloat16)
    lane_row = (lane >> log2(half)) * per_block + (lane & (per_block - 1))
    pick_ref[1] = ((row >> log2(cycles)) == lane_row).astype(jnp.float32).astype(jnp.bfloat16)

    spacing = reals + 2
    column = lane_ids((1, place_ref.shape[1]))
    source = (column * (2**16 // spacing + 1)) >> 16
    inside = column - source * spacing
    source_block = source >> log2(real_groups)
    target = ((source & (real_groups - 1)) * blocks + source_block) * reals + inside
    target = jnp.where(inside < reals, target, blocks * real_groups * reals + source_block)
    place = (row_ids(place_ref.shape) == target).astype(jnp.float32)
    place_ref[...] = place.astype(jnp.bfloat16)


def forward_kernel(
    cycle_len, half_len, syn_scale, reals, parts,
    cycle_hbm, mode_hbm, noise_hbm, mask_hbm, spectrum_hbm, legendre_hbm, sky_hbm, prev_hbm,
    out_ref, inner_ref, outer_ref, place_ref, pick_ref, doubled_ref, factor_ref,
    cycle_ref, mode_ref, noise_ref, mask_ref, spectrum_ref, legendre_ref, sky_ref, prev_ref, gram_ref, sems,
):
    small = start_copies(
        (cycle_hbm, mode_hbm, noise_hbm, mask_hbm, spectrum_hbm, legendre_hbm),
        (cycle_ref, mode_ref, noise_ref, mask_ref, spectrum_ref, legendre_ref),
        sems,
    )
    spans = [pl.ds(i * (sky_ref.shape[0] // parts), sky_ref.shape[0] // parts) for i in range(parts)]
    large = start_copies(
        [ref.at[span] for span in spans for ref in (sky_hbm, prev_hbm)],
        [ref.at[span] for span in spans for ref in (sky_ref, prev_ref)],
        sems,
        len(small),
    )
    group = lax.axis_index("grp")
    per_block = legendre_ref.shape[0] // (2 * lax.axis_size("blk"))
    selections(place_ref, pick_ref, per_block, reals)
    small[0].wait()
    small[1].wait()
    inner, outer = phase_factors(cycle_ref[...], mode_ref[...], cycle_len, half_len, group)
    inner_ref[...] = inner
    outer_ref[...] = outer
    small[2].wait()
    small[3].wait()
    weight = mask_ref[...].astype(jnp.float32) / (noise_ref[...] - 0.5)
    inverse = 1.0 / (weight + 2.0)
    sky_gain = weight * inverse
    prev_gain = 2.0 * inverse

    small[4].wait()
    small[5].wait()
    table = legendre_ref[...]
    spectrum = spectrum_ref[...]
    factor = spectrum / (spectrum + 0.5)
    doubled_ref[...] = jnp.concatenate([table, table], axis=0)
    factor_ref[...] = factor
    filtered = (table.astype(jnp.float32) * factor).astype(jnp.bfloat16)
    gram = lax.dot_general(table, filtered, NT, preferred_element_type=jnp.float32)
    table_rows = table.shape[0]
    pixel_rows = outer.shape[0]
    blocks, real_groups = lax.axis_size("blk"), lax.axis_size("real")
    cycles = 2 * blocks
    same = (row_ids(gram.shape) >> log2(cycles)) == (lane_ids((1, table_rows)) >> log2(cycles))
    gram = jnp.where(same, gram, 0.0).reshape(table_rows // cycles, cycles, table_rows).sum(axis=0)
    gram = gram * syn_scale
    gram_ref[...] = jnp.concatenate([gram, gram], axis=1)
    even, odd = gram_ref[pl.ds(0, blocks, stride=2), :], gram_ref[pl.ds(1, blocks, stride=2), :]
    gram = jnp.where(lane_ids(even.shape) < LANES // 2, even, odd)
    gram_high = gram.astype(jnp.bfloat16).astype(jnp.float32)
    gram_low = gram - gram_high

    part_reals = reals // parts
    shape = (part_reals, 2 * pixel_rows, LANES)
    fourier = []
    for i, span in enumerate(spans):
        large[2 * i].wait()
        large[2 * i + 1].wait()
        messenger = sky_ref[span, :].reshape(shape) * sky_gain + prev_ref[span, :].reshape(shape) * prev_gain
        rows = jnp.concatenate([messenger[:, :pixel_rows], messenger[:, pixel_rows:]], axis=2)
        rows = rows.reshape(-1, 2 * LANES).astype(jnp.bfloat16)
        partial = jnp.dot(rows, inner, preferred_element_type=jnp.float32)
        partial = partial[:, :LANES] + partial[:, LANES:]
        turned = partial.reshape(part_reals, pixel_rows, LANES) * outer
        summed = turned.reshape(part_reals, pixel_rows // 8, 8, LANES).sum(axis=1)
        summed = summed.reshape(part_reals * 8, LANES)
        summed = summed + pltpu.roll(summed, LANES // 2, 1)
        own = (row_ids(summed.shape) & 1) == (lane_ids(summed.shape) >= LANES // 2)
        fourier.append(jnp.where(own, summed, 0.0).reshape(part_reals, 8, LANES).sum(axis=1))
    fourier = jnp.concatenate(fourier, axis=0) * cycle_len**-0.5
    rows = []
    for b in range(blocks):
        rows += [fourier, gram_high[b : b + 1], gram_low[b : b + 1]] * real_groups
    rows = jnp.concatenate(rows, axis=0).astype(jnp.bfloat16)
    for g in range(lax.axis_size("grp")):
        out_ref[pl.ds(g * rows.shape[0], rows.shape[0]), :] = rows


def backward_kernel(
    blocks, real_groups, reals, parts,
    gathered_ref, inner_ref, outer_ref, place_ref, pick_ref, table_ref, factor_ref,
    wiener_hbm, signal_hbm, wiener_ref, signal_ref, fourier_ref, out_sems,
):
    real_group = lax.axis_index("real")
    cycles = 2 * blocks
    per_block = table_ref.shape[0] // (2 * cycles)
    modes = per_block * blocks
    pixel_rows = outer_ref.shape[0]
    half = LANES // 2
    lane = lane_ids((1, LANES))
    holder = (lane & (modes - 1)) >> log2(per_block)
    lane_block = (lane & (cycles - 1)) >> 1
    total_reals = real_groups * reals
    fourier_rows = blocks * total_reals
    share = place_ref.shape[1]
    sides = jnp.concatenate([gathered_ref[:share, :], gathered_ref[share:, :]], axis=1)
    placed = jnp.dot(place_ref[...], sides, preferred_element_type=jnp.float32)
    placed = placed[:, :LANES] + placed[:, LANES:]
    fourier_ref[...] = placed[:fourier_rows]

    stores = []
    gram_all = jnp.where(
        (lane & (cycles - 1)) == row_ids((cycles, LANES)), placed[fourier_rows:, None, :], 0.0
    ).reshape(blocks * cycles, LANES)
    gram_high = gram_all.astype(jnp.bfloat16)
    gram_low = (gram_all - gram_high.astype(jnp.float32)).astype(jnp.bfloat16)
    gram_rows = jnp.dot(
        jnp.concatenate([gram_high, gram_low], axis=1),
        jnp.concatenate([pick_ref[1], pick_ref[1]], axis=0),
        preferred_element_type=jnp.float32,
    ).reshape(blocks, cycles, LANES)
    gram = jnp.zeros((cycles, LANES), jnp.float32)
    for b in range(blocks):
        gram = gram + jnp.where(holder == b, gram_rows[b], 0.0)

    first = lane < half
    cycle_modes = jnp.zeros((reals, LANES), jnp.float32)
    for b in range(blocks):
        first_row = pl.multiple_of((real_group * blocks + b) * reals, reals)
        pair = fourier_ref[pl.ds(first_row, reals), :]
        turned = pltpu.roll(pair, half, 1)
        cycle_modes = cycle_modes + jnp.where(first, pair, turned) * gram[2 * b : 2 * b + 1]
        cycle_modes = cycle_modes + jnp.where(first, turned, pair) * gram[2 * b + 1 : 2 * b + 2]
    cycle_modes = cycle_modes * modes**-0.5
    turned = pltpu.roll(cycle_modes, half, 1)
    even = jnp.where(first, cycle_modes, turned)
    odd = jnp.where(first, turned, cycle_modes)
    parity = (row_ids((1, 8, LANES)) & 1) == 0
    spread = jnp.where(parity, even[:, None, :], odd[:, None, :])
    inner = inner_ref[...]
    outer = outer_ref[...].reshape(1, pixel_rows // 8, 8, LANES)
    rotated = (spread[:, None] * outer).reshape(-1, LANES).astype(jnp.bfloat16)
    signal = lax.dot_general(
        jnp.concatenate([rotated, rotated], axis=1), inner, NT, preferred_element_type=jnp.float32
    ).reshape(reals, pixel_rows, 2 * LANES)
    part_reals = reals // parts
    for i in range(parts):
        span = slice(i * part_reals, (i + 1) * part_reals)
        signal_ref[span, 0] = signal[span, :, :LANES]
        signal_ref[span, 1] = signal[span, :, LANES:]
        span = pl.ds(i * part_reals, part_reals)
        stores += start_copies([signal_ref.at[span]], [signal_hbm.at[span]], out_sems, len(stores))
    coeff_rows = jnp.dot(
        placed[:fourier_rows].astype(jnp.bfloat16), pick_ref[0], preferred_element_type=jnp.float32
    ).reshape(real_groups, blocks, reals, LANES)
    columns = jnp.zeros((total_reals, LANES), jnp.float32)
    for b in range(blocks):
        one = coeff_rows[:, b].reshape(total_reals, LANES)
        columns = columns + jnp.where(lane_block == b, one, 0.0)
    table = table_ref[...]
    factor = factor_ref[...]
    own = (lane >> log2(cycles)) == row_ids((2 * per_block, LANES))
    upper = row_ids((1, 2 * per_block, LANES)) < per_block
    pieces = jnp.where(own, columns[:, None, :], 0.0).reshape(-1, LANES).astype(jnp.bfloat16)
    filtered = factor * jnp.dot(pieces, table, preferred_element_type=jnp.float32)
    filtered = filtered.reshape(total_reals, 2 * per_block, -1)
    for y in range(real_groups):
        span = slice(y * reals, (y + 1) * reals)
        for pair in range(wiener_ref.shape[2]):
            one, two = (
                filtered[span, :, tile * LANES : (tile + 1) * LANES] for tile in (2 * pair, 2 * pair + 1)
            )
            wiener_ref[span, 0, pair] = jnp.where(upper, one, pltpu.roll(two, per_block, 1))
            wiener_ref[span, 1, pair] = jnp.where(upper, pltpu.roll(one, per_block, 1), two)
        span = pl.ds(y * reals, reals)
        stores += start_copies([wiener_ref.at[span]], [wiener_hbm.at[span]], out_sems, len(stores))

    for store in stores:
        store.wait()


def split_tiles(array):
    lead, rows, columns = array.shape[:-2], array.shape[-2], array.shape[-1]
    split = array.reshape(*lead, rows, columns // LANES, LANES)
    return jnp.swapaxes(split, -2, -3).reshape(-1, LANES)


def gram_program(
    sky_data, signal_prev, noise_var, mask_flags, cycle_table, m_table, spectrum, legendre
):
    reals, cycle_dev, half_len = sky_data.shape
    groups, blocks, real_groups = (lax.axis_size(name) for name in AXES)
    cycle_len = half_len * groups
    per_block, multipoles, cycles = legendre.shape
    total_l = multipoles * groups * real_groups
    tiles = multipoles // LANES
    hbm = pl.BlockSpec(memory_space=pltpu.HBM)
    vmem = pl.BlockSpec(memory_space=pltpu.VMEM)
    orders = m_table[None, :]
    cycles_row = cycle_table[None, :]
    spectrum_row = spectrum[None, :]
    table = legendre.transpose(0, 2, 1).reshape(per_block * cycles, multipoles)
    inputs = (
        cycles_row, orders, split_tiles(noise_var), split_tiles(mask_flags), spectrum_row, table,
        split_tiles(sky_data), split_tiles(signal_prev),
    )
    sources = groups * blocks * real_groups
    total_reals = reals * real_groups
    local, *prepared = pl.pallas_call(
        functools.partial(forward_kernel, cycle_len, half_len, (cycles / total_l) ** 0.5, reals, PARTS),
        out_shape=(
            jax.ShapeDtypeStruct((sources * (reals + 2), LANES), jnp.bfloat16),
            jax.ShapeDtypeStruct((2 * LANES, 2 * LANES), jnp.bfloat16),
            jax.ShapeDtypeStruct((half_len // LANES, LANES), jnp.float32),
            jax.ShapeDtypeStruct(
                (blocks * (total_reals + 1), blocks * real_groups * (reals + 2)), jnp.bfloat16
            ),
            jax.ShapeDtypeStruct((2, LANES, LANES), jnp.bfloat16),
            jax.ShapeDtypeStruct((2 * table.shape[0], multipoles), jnp.bfloat16),
            jax.ShapeDtypeStruct((1, multipoles), jnp.float32),
        ),
        in_specs=[hbm] * 8,
        out_specs=(vmem,) * 7,
        scratch_shapes=[pltpu.VMEM(x.shape, x.dtype) for x in inputs]
        + [pltpu.VMEM((cycles, LANES), jnp.float32), pltpu.SemaphoreType.DMA((6 + 2 * PARTS,))],
        compiler_params=pltpu.CompilerParams(vmem_limit_bytes=FORWARD_VMEM),
    )(*(pltpu.with_memory_space_constraint(x, pltpu.HBM) for x in inputs))
    pairs = local.reshape(sources, reals // 2 + 1, 2, LANES)
    gathered = lax.all_to_all(pairs, AXES, 0, 0, tiled=True).reshape(local.shape)
    outputs = (
        jax.ShapeDtypeStruct((total_reals, 2, tiles // 2, 2 * per_block, LANES), jnp.float32),
        jax.ShapeDtypeStruct((reals, 2, half_len // LANES, LANES), jnp.float32),
    )
    wiener, signal = pl.pallas_call(
        functools.partial(backward_kernel, blocks, real_groups, reals, PARTS),
        out_shape=outputs,
        in_specs=[vmem] * 7,
        out_specs=(hbm, hbm),
        scratch_shapes=[pltpu.VMEM(x.shape, x.dtype) for x in outputs]
        + [pltpu.VMEM((blocks * total_reals, LANES), jnp.float32)]
        + [pltpu.SemaphoreType.DMA((real_groups + PARTS,))],
        compiler_params=pltpu.CompilerParams(vmem_limit_bytes=BACKWARD_VMEM),
    )(gathered, *prepared)
    wiener = wiener.reshape(total_reals, 2, tiles, per_block, LANES).transpose(0, 1, 3, 2, 4)
    signal = signal.reshape(reals, half_len // LANES, cycle_dev, LANES).transpose(0, 2, 1, 3)
    return (
        wiener.reshape(total_reals, 2, per_block, multipoles),
        signal.reshape(sky_data.shape),
    )


def gram_form_fits(mesh, sky_data, m_table, legendre):
    groups, blocks, real_groups = (mesh.shape[name] for name in AXES)
    reals, cycles, cycle_len = sky_data.shape
    modes = m_table.shape[0]
    per_block = modes // blocks
    multipoles = legendre.shape[1] // (groups * real_groups)
    half_len = cycle_len // groups
    reals_dev = reals // real_groups
    return (
        cycles < 2 * reals
        and 4 * modes == LANES
        and cycles == 2 * blocks
        and all(size & (size - 1) == 0 for size in (blocks, modes, cycles, real_groups))
        and 2 * reals * cycles < 2**12
        and 2 * per_block * cycles == LANES
        and cycle_len & (cycle_len - 1) == 0
        and half_len % (8 * LANES) == 0
        and multipoles % (2 * LANES) == 0
        and per_block == 4
        and reals_dev % 16 == 0
        and reals_dev % PARTS == 0
        and cycles % 16 == 0
    )


def phase_tables(col_ids, mode_ids, cycle_len):
    product_ids = col_ids[:, None] * mode_ids[None, :] % cycle_len
    angles = product_ids.astype(jnp.float32) * (2.0 * math.pi / cycle_len)
    return (jnp.cos(angles).astype(jnp.bfloat16), jnp.sin(angles).astype(jnp.bfloat16))


def cycle_offsets(cycle_ids, mode_ids, cycle_len):
    parity = (cycle_ids % 2).astype(jnp.float32)
    shifts = math.pi / cycle_len * parity[:, None] * mode_ids[None, :].astype(jnp.float32)
    return (jnp.cos(shifts), jnp.sin(shifts))


def forward_modes(re_part, im_part):
    summed = lax.psum((re_part, im_part), "grp")
    fourier_pair = (summed[0].astype(jnp.bfloat16), summed[1].astype(jnp.bfloat16))
    fourier_pair = (
        lax.all_gather(fourier_pair[0], "real", axis=0, tiled=True),
        lax.all_gather(fourier_pair[1], "real", axis=0, tiled=True),
    )
    fourier_pair = (
        lax.all_to_all(fourier_pair[0], "blk", split_axis=2, concat_axis=1, tiled=True),
        lax.all_to_all(fourier_pair[1], "blk", split_axis=2, concat_axis=1, tiled=True),
    )
    return fourier_pair


def backward_cycles(partial_value):
    summed = lax.psum_scatter(partial_value, "real", scatter_dimension=0, tiled=True)
    reduced = lax.psum(summed, "grp")
    cycle_pair = lax.all_to_all(
        reduced.astype(jnp.bfloat16), "blk", split_axis=2, concat_axis=3, tiled=True
    )
    return cycle_pair


def per_device(
    sky_data, signal_prev, noise_var, mask_flags, cycle_table, m_table, spectrum, legendre
):
    real_dev, cycle_dev, half_len = sky_data.shape
    cycle_len = half_len * lax.axis_size("grp")
    mode_count = m_table.shape[0]
    col_ids = lax.axis_index("grp") * half_len + jnp.arange(half_len, dtype=jnp.int32)
    cos_tab, sin_tab = phase_tables(col_ids, m_table, cycle_len)
    cos_shift, sin_shift = cycle_offsets(cycle_table, m_table, cycle_len)
    weight = mask_flags.astype(jnp.float32) / (noise_var - 0.5)
    messenger = (weight * sky_data + 2.0 * signal_prev) / (weight + 2.0)
    flat_rows = messenger.astype(jnp.bfloat16).reshape(real_dev * cycle_dev, half_len)
    base_cos = jnp.dot(flat_rows, cos_tab, preferred_element_type=jnp.float32).reshape(
        real_dev, cycle_dev, mode_count
    )
    base_sin = -jnp.dot(flat_rows, sin_tab, preferred_element_type=jnp.float32).reshape(
        real_dev, cycle_dev, mode_count
    )
    norm_scale = cycle_len ** (-0.5)
    re_part = (base_cos * cos_shift + base_sin * sin_shift) * norm_scale
    im_part = (base_sin * cos_shift - base_cos * sin_shift) * norm_scale
    fourier_re, fourier_im = forward_modes(re_part, im_part)
    fourier = jnp.stack([fourier_re, fourier_im], 1)
    coefficients = jnp.einsum(
        "mlr,kcrm->kcml", legendre, fourier, preferred_element_type=jnp.float32
    )
    factor = spectrum / (spectrum + 0.5)
    wiener_alm = coefficients * factor
    total_l = legendre.shape[1] * lax.axis_size("grp") * lax.axis_size("real")
    syn_scale = (legendre.shape[2] / total_l) ** 0.5
    partial_value = (
        jnp.einsum(
            "mlr,kcml->kcrm",
            legendre,
            wiener_alm.astype(jnp.bfloat16),
            preferred_element_type=jnp.float32,
        )
        * syn_scale
    )
    cycle_pair = backward_cycles(partial_value)
    cycle_modes = cycle_pair.astype(jnp.float32)
    modes_re = cycle_modes[:, 0]
    modes_im = cycle_modes[:, 1]
    rotated_re = (modes_re * cos_shift - modes_im * sin_shift).astype(jnp.bfloat16)
    rotated_im = (modes_im * cos_shift + modes_re * sin_shift).astype(jnp.bfloat16)
    contract = (((1,), (1,)), ((), ()))
    pixel_sum = lax.dot_general(
        rotated_re.reshape(-1, mode_count), cos_tab, contract, preferred_element_type=jnp.float32
    )
    pixel_sum = pixel_sum - lax.dot_general(
        rotated_im.reshape(-1, mode_count), sin_tab, contract, preferred_element_type=jnp.float32
    )
    signal_next = (pixel_sum * mode_count ** (-0.5)).reshape(real_dev, cycle_dev, half_len)
    return (wiener_alm, signal_next)


def solution(mesh):
    in_specs = (
        P("real", "blk", "grp"),
        P("real", "blk", "grp"),
        P("blk", "grp"),
        P("blk", "grp"),
        P("blk"),
        P(),
        P(("grp", "real")),
        P("blk", ("grp", "real"), None),
    )
    out_specs = (P(None, None, "blk", ("grp", "real")), P("real", "blk", "grp"))

    def step(sky_data, signal_prev, noise_var, mask_flags, cycle_table, m_table, spectrum, legendre):
        fits = gram_form_fits(mesh, sky_data, m_table, legendre)
        return jax.shard_map(
            gram_program if fits else per_device,
            mesh=mesh,
            in_specs=in_specs,
            out_specs=out_specs,
            check_vma=False,
        )(sky_data, signal_prev, noise_var, mask_flags, cycle_table, m_table, spectrum, legendre)

    return step
```

```python
import functools
import math

import jax
import jax.numpy as jnp
from jax import lax
from jax.experimental import pallas as pl
from jax.experimental.pallas import tpu as pltpu
from jax.sharding import PartitionSpec as P

LANES = 128
NT = (((1,), (1,)), ((), ()))
AXES = ("grp", "blk", "real")
PARTS = 2
FORWARD_VMEM = 32 << 20
BACKWARD_VMEM = 16 << 20


def unit_cosine(units, half_turn):
    wrapped = units & (2 * half_turn - 1)
    folded = jnp.minimum(wrapped, 2 * half_turn - wrapped)
    y = (half_turn // 2 - folded).astype(jnp.float32) * (math.pi / half_turn)
    y2 = y * y
    acc = jnp.full_like(y2, -1.0 / math.factorial(11))
    for order, sign in ((9, 1.0), (7, -1.0), (5, 1.0), (3, -1.0), (1, 1.0)):
        acc = acc * y2 + sign / math.factorial(order)
    return acc * y


def log2(size):
    return size.bit_length() - 1


def lane_ids(shape):
    return lax.broadcasted_iota(jnp.int32, shape, len(shape) - 1)


def row_ids(shape):
    return lax.broadcasted_iota(jnp.int32, shape, len(shape) - 2)


def phase_factors(cycles, orders, cycle_len, half_len, group):
    modes = orders.shape[1]
    orders = jnp.concatenate([orders] * (LANES // modes), axis=1)
    quarter = lane_ids((1, LANES)) >> log2(modes)
    quarter_turn = cycle_len // 2
    row = row_ids((2 * LANES, LANES))
    pixel = (row >> log2(LANES)) * (half_len // 2) + (row & (LANES - 1))
    inner_units = 2 * orders * pixel + ((quarter + 1) >> 1) * quarter_turn
    inner = unit_cosine(inner_units, cycle_len)
    rows = half_len // LANES
    row = row_ids((rows, LANES))
    parity = jnp.where((row & 1) == 0, cycles[:, :1], cycles[:, 1:]) & 1
    pixel = group * half_len + LANES * (row >> 1)
    outer_units = orders * (2 * pixel + parity) + (quarter >> 1) * (3 * quarter_turn)
    outer = unit_cosine(outer_units, cycle_len)
    high = inner.astype(jnp.bfloat16)
    low = (inner - high.astype(jnp.float32)).astype(jnp.bfloat16)
    return jnp.concatenate([high, low], axis=1), outer


def start_copies(sources, targets, sems, first=0):
    copies = [
        pltpu.make_async_copy(source, target, sems.at[first + i])
        for i, (source, target) in enumerate(zip(sources, targets))
    ]
    for copy in copies:
        copy.start()
    return copies


def selections(place_ref, pick_ref, per_block, reals):
    block = lax.axis_index("blk")
    blocks, real_groups = lax.axis_size("blk"), lax.axis_size("real")
    modes, cycles, half = per_block * blocks, 2 * blocks, LANES // 2

    lane = lane_ids((1, LANES))
    row = row_ids((LANES, LANES))
    lane_order = (lane & (half - 1)) >> log2(cycles)
    lane_row = (lane & 1) * half + (lane >> log2(half)) * modes + block * per_block + lane_order
    pick_ref[0] = (row == lane_row).astype(jnp.float32).astype(jnp.bfloat16)
    lane_row = (lane >> log2(half)) * per_block + (lane & (per_block - 1))
    pick_ref[1] = ((row >> log2(cycles)) == lane_row).astype(jnp.float32).astype(jnp.bfloat16)

    spacing = reals + 2
    column = lane_ids((1, place_ref.shape[1]))
    source = (column * (2**16 // spacing + 1)) >> 16
    inside = column - source * spacing
    source_block = source >> log2(real_groups)
    target = ((source & (real_groups - 1)) * blocks + source_block) * reals + inside
    target = jnp.where(inside < reals, target, blocks * real_groups * reals + source_block)
    place = (row_ids(place_ref.shape) == target).astype(jnp.float32)
    place_ref[...] = place.astype(jnp.bfloat16)


def forward_kernel(
    cycle_len, half_len, syn_scale, reals,
    cycle_hbm, mode_hbm, noise_hbm, mask_hbm, spectrum_hbm, legendre_hbm, sky_hbm, prev_hbm,
    out_ref, inner_ref, outer_ref, place_ref, pick_ref, doubled_ref, factor_ref,
    cycle_ref, mode_ref, noise_ref, mask_ref, spectrum_ref, legendre_ref, sky_ref, prev_ref, gram_ref, sems,
):
    copies = start_copies(
        (cycle_hbm, mode_hbm, sky_hbm, prev_hbm, noise_hbm, mask_hbm, spectrum_hbm, legendre_hbm),
        (cycle_ref, mode_ref, sky_ref, prev_ref, noise_ref, mask_ref, spectrum_ref, legendre_ref),
        sems,
    )
    group = lax.axis_index("grp")
    per_block = legendre_ref.shape[0] // (2 * lax.axis_size("blk"))
    selections(place_ref, pick_ref, per_block, reals)
    copies[0].wait()
    copies[1].wait()
    inner, outer = phase_factors(cycle_ref[...], mode_ref[...], cycle_len, half_len, group)
    inner_ref[...] = inner
    outer_ref[...] = outer
    for copy in copies[2:]:
        copy.wait()
    weight = mask_ref[...].astype(jnp.float32) / (noise_ref[...] - 0.5)
    inverse = 1.0 / (weight + 2.0)
    sky_gain = weight * inverse
    prev_gain = 2.0 * inverse

    table = legendre_ref[...]
    spectrum = spectrum_ref[...]
    factor = spectrum / (spectrum + 0.5)
    doubled_ref[...] = jnp.concatenate([table, table], axis=0)
    factor_ref[...] = factor
    filtered = (table.astype(jnp.float32) * factor).astype(jnp.bfloat16)
    gram = lax.dot_general(table, filtered, NT, preferred_element_type=jnp.float32)
    table_rows = table.shape[0]
    pixel_rows = outer.shape[0]
    blocks, real_groups = lax.axis_size("blk"), lax.axis_size("real")
    cycles = 2 * blocks
    same = (row_ids(gram.shape) >> log2(cycles)) == (lane_ids((1, table_rows)) >> log2(cycles))
    gram = jnp.where(same, gram, 0.0).reshape(table_rows // cycles, cycles, table_rows).sum(axis=0)
    gram = gram * syn_scale
    gram_ref[...] = jnp.concatenate([gram, gram], axis=1)
    even, odd = gram_ref[pl.ds(0, blocks, stride=2), :], gram_ref[pl.ds(1, blocks, stride=2), :]
    gram = jnp.where(lane_ids(even.shape) < LANES // 2, even, odd)
    gram_high = gram.astype(jnp.bfloat16).astype(jnp.float32)
    gram_low = gram - gram_high

    shape = (reals, 2 * pixel_rows, LANES)
    messenger = sky_ref[...].reshape(shape) * sky_gain + prev_ref[...].reshape(shape) * prev_gain
    rows = jnp.concatenate([messenger[:, :pixel_rows], messenger[:, pixel_rows:]], axis=2)
    rows = rows.reshape(-1, 2 * LANES).astype(jnp.bfloat16)
    partial = jnp.dot(rows, inner, preferred_element_type=jnp.float32)
    partial = partial[:, :LANES] + partial[:, LANES:]
    turned = partial.reshape(reals, pixel_rows, LANES) * outer
    summed = turned.reshape(reals, pixel_rows // 8, 8, LANES).sum(axis=1)
    summed = summed.reshape(reals * 8, LANES)
    summed = summed + pltpu.roll(summed, LANES // 2, 1)
    own = (row_ids(summed.shape) & 1) == (lane_ids(summed.shape) >= LANES // 2)
    fourier = jnp.where(own, summed, 0.0).reshape(reals, 8, LANES).sum(axis=1) * cycle_len**-0.5
    rows = []
    for b in range(blocks):
        rows += [fourier, gram_high[b : b + 1], gram_low[b : b + 1]] * real_groups
    rows = jnp.concatenate(rows, axis=0).astype(jnp.bfloat16)
    for g in range(lax.axis_size("grp")):
        out_ref[pl.ds(g * rows.shape[0], rows.shape[0]), :] = rows


def backward_kernel(
    blocks, real_groups, reals, parts,
    gathered_ref, inner_ref, outer_ref, place_ref, pick_ref, table_ref, factor_ref,
    wiener_hbm, signal_hbm, wiener_ref, signal_ref, fourier_ref, out_sems,
):
    real_group = lax.axis_index("real")
    cycles = 2 * blocks
    per_block = table_ref.shape[0] // (2 * cycles)
    modes = per_block * blocks
    pixel_rows = outer_ref.shape[0]
    half = LANES // 2
    lane = lane_ids((1, LANES))
    holder = (lane & (modes - 1)) >> log2(per_block)
    lane_block = (lane & (cycles - 1)) >> 1
    total_reals = real_groups * reals
    fourier_rows = blocks * total_reals
    share = place_ref.shape[1]
    sides = jnp.concatenate([gathered_ref[:share, :], gathered_ref[share:, :]], axis=1)
    placed = jnp.dot(place_ref[...], sides, preferred_element_type=jnp.float32)
    placed = placed[:, :LANES] + placed[:, LANES:]
    fourier_ref[...] = placed[:fourier_rows]

    coeff_rows = jnp.dot(
        placed[:fourier_rows].astype(jnp.bfloat16), pick_ref[0], preferred_element_type=jnp.float32
    ).reshape(real_groups, blocks, reals, LANES)
    columns = jnp.zeros((total_reals, LANES), jnp.float32)
    for b in range(blocks):
        one = coeff_rows[:, b].reshape(total_reals, LANES)
        columns = columns + jnp.where(lane_block == b, one, 0.0)
    table = table_ref[...]
    factor = factor_ref[...]
    stores = []
    own = (lane >> log2(cycles)) == row_ids((2 * per_block, LANES))
    upper = row_ids((1, 2 * per_block, LANES)) < per_block
    pieces = jnp.where(own, columns[:, None, :], 0.0).reshape(-1, LANES).astype(jnp.bfloat16)
    filtered = factor * jnp.dot(pieces, table, preferred_element_type=jnp.float32)
    filtered = filtered.reshape(total_reals, 2 * per_block, -1)
    for y in range(real_groups):
        span = slice(y * reals, (y + 1) * reals)
        for pair in range(wiener_ref.shape[2]):
            one, two = (
                filtered[span, :, tile * LANES : (tile + 1) * LANES] for tile in (2 * pair, 2 * pair + 1)
            )
            wiener_ref[span, 0, pair] = jnp.where(upper, one, pltpu.roll(two, per_block, 1))
            wiener_ref[span, 1, pair] = jnp.where(upper, pltpu.roll(one, per_block, 1), two)
        span = pl.ds(y * reals, reals)
        stores += start_copies([wiener_ref.at[span]], [wiener_hbm.at[span]], out_sems, len(stores))

    gram_all = jnp.where(
        (lane & (cycles - 1)) == row_ids((cycles, LANES)), placed[fourier_rows:, None, :], 0.0
    ).reshape(blocks * cycles, LANES)
    gram_high = gram_all.astype(jnp.bfloat16)
    gram_low = (gram_all - gram_high.astype(jnp.float32)).astype(jnp.bfloat16)
    gram_rows = jnp.dot(
        jnp.concatenate([gram_high, gram_low], axis=1),
        jnp.concatenate([pick_ref[1], pick_ref[1]], axis=0),
        preferred_element_type=jnp.float32,
    ).reshape(blocks, cycles, LANES)
    gram = jnp.zeros((cycles, LANES), jnp.float32)
    for b in range(blocks):
        gram = gram + jnp.where(holder == b, gram_rows[b], 0.0)

    first = lane < half
    cycle_modes = jnp.zeros((reals, LANES), jnp.float32)
    for b in range(blocks):
        first_row = pl.multiple_of((real_group * blocks + b) * reals, reals)
        pair = fourier_ref[pl.ds(first_row, reals), :]
        turned = pltpu.roll(pair, half, 1)
        cycle_modes = cycle_modes + jnp.where(first, pair, turned) * gram[2 * b : 2 * b + 1]
        cycle_modes = cycle_modes + jnp.where(first, turned, pair) * gram[2 * b + 1 : 2 * b + 2]
    cycle_modes = cycle_modes * modes**-0.5
    turned = pltpu.roll(cycle_modes, half, 1)
    even = jnp.where(first, cycle_modes, turned)
    odd = jnp.where(first, turned, cycle_modes)
    parity = (row_ids((1, 8, LANES)) & 1) == 0
    spread = jnp.where(parity, even[:, None, :], odd[:, None, :])
    inner = inner_ref[...]
    outer = outer_ref[...].reshape(1, pixel_rows // 8, 8, LANES)
    rotated = (spread[:, None] * outer).reshape(-1, LANES).astype(jnp.bfloat16)
    signal = lax.dot_general(
        jnp.concatenate([rotated, rotated], axis=1), inner, NT, preferred_element_type=jnp.float32
    ).reshape(reals, pixel_rows, 2 * LANES)
    part_reals = reals // parts
    for i in range(parts):
        span = slice(i * part_reals, (i + 1) * part_reals)
        signal_ref[span, 0] = signal[span, :, :LANES]
        signal_ref[span, 1] = signal[span, :, LANES:]
        span = pl.ds(i * part_reals, part_reals)
        stores += start_copies([signal_ref.at[span]], [signal_hbm.at[span]], out_sems, len(stores))
    for store in stores:
        store.wait()


def split_tiles(array):
    lead, rows, columns = array.shape[:-2], array.shape[-2], array.shape[-1]
    split = array.reshape(*lead, rows, columns // LANES, LANES)
    return jnp.swapaxes(split, -2, -3).reshape(-1, LANES)


def gram_program(
    sky_data, signal_prev, noise_var, mask_flags, cycle_table, m_table, spectrum, legendre
):
    reals, cycle_dev, half_len = sky_data.shape
    groups, blocks, real_groups = (lax.axis_size(name) for name in AXES)
    cycle_len = half_len * groups
    per_block, multipoles, cycles = legendre.shape
    total_l = multipoles * groups * real_groups
    tiles = multipoles // LANES
    hbm = pl.BlockSpec(memory_space=pltpu.HBM)
    vmem = pl.BlockSpec(memory_space=pltpu.VMEM)
    orders = m_table[None, :]
    cycles_row = cycle_table[None, :]
    spectrum_row = spectrum[None, :]
    table = legendre.transpose(0, 2, 1).reshape(per_block * cycles, multipoles)
    inputs = (
        cycles_row, orders, split_tiles(noise_var), split_tiles(mask_flags), spectrum_row, table,
        split_tiles(sky_data), split_tiles(signal_prev),
    )
    sources = groups * blocks * real_groups
    total_reals = reals * real_groups
    local, *prepared = pl.pallas_call(
        functools.partial(forward_kernel, cycle_len, half_len, (cycles / total_l) ** 0.5, reals),
        out_shape=(
            jax.ShapeDtypeStruct((sources * (reals + 2), LANES), jnp.bfloat16),
            jax.ShapeDtypeStruct((2 * LANES, 2 * LANES), jnp.bfloat16),
            jax.ShapeDtypeStruct((half_len // LANES, LANES), jnp.float32),
            jax.ShapeDtypeStruct(
                (blocks * (total_reals + 1), blocks * real_groups * (reals + 2)), jnp.bfloat16
            ),
            jax.ShapeDtypeStruct((2, LANES, LANES), jnp.bfloat16),
            jax.ShapeDtypeStruct((2 * table.shape[0], multipoles), jnp.bfloat16),
            jax.ShapeDtypeStruct((1, multipoles), jnp.float32),
        ),
        in_specs=[hbm] * 8,
        out_specs=(vmem,) * 7,
        scratch_shapes=[pltpu.VMEM(x.shape, x.dtype) for x in inputs]
        + [pltpu.VMEM((cycles, LANES), jnp.float32), pltpu.SemaphoreType.DMA((8,))],
        compiler_params=pltpu.CompilerParams(vmem_limit_bytes=FORWARD_VMEM),
    )(*(pltpu.with_memory_space_constraint(x, pltpu.HBM) for x in inputs))
    pairs = local.reshape(sources, reals // 2 + 1, 2, LANES)
    gathered = lax.all_to_all(pairs, AXES, 0, 0, tiled=True).reshape(local.shape)
    outputs = (
        jax.ShapeDtypeStruct((total_reals, 2, tiles // 2, 2 * per_block, LANES), jnp.float32),
        jax.ShapeDtypeStruct((reals, 2, half_len // LANES, LANES), jnp.float32),
    )
    wiener, signal = pl.pallas_call(
        functools.partial(backward_kernel, blocks, real_groups, reals, PARTS),
        out_shape=outputs,
        in_specs=[vmem] * 7,
        out_specs=(hbm, hbm),
        scratch_shapes=[pltpu.VMEM(x.shape, x.dtype) for x in outputs]
        + [pltpu.VMEM((blocks * total_reals, LANES), jnp.float32)]
        + [pltpu.SemaphoreType.DMA((real_groups + PARTS,))],
        compiler_params=pltpu.CompilerParams(vmem_limit_bytes=BACKWARD_VMEM),
    )(gathered, *prepared)
    wiener = wiener.reshape(total_reals, 2, tiles, per_block, LANES).transpose(0, 1, 3, 2, 4)
    signal = signal.reshape(reals, half_len // LANES, cycle_dev, LANES).transpose(0, 2, 1, 3)
    return (
        wiener.reshape(total_reals, 2, per_block, multipoles),
        signal.reshape(sky_data.shape),
    )


def gram_form_fits(mesh, sky_data, m_table, legendre):
    groups, blocks, real_groups = (mesh.shape[name] for name in AXES)
    reals, cycles, cycle_len = sky_data.shape
    modes = m_table.shape[0]
    per_block = modes // blocks
    multipoles = legendre.shape[1] // (groups * real_groups)
    half_len = cycle_len // groups
    reals_dev = reals // real_groups
    return (
        cycles < 2 * reals
        and 4 * modes == LANES
        and cycles == 2 * blocks
        and all(size & (size - 1) == 0 for size in (blocks, modes, cycles, real_groups))
        and 2 * reals * cycles < 2**12
        and 2 * per_block * cycles == LANES
        and cycle_len & (cycle_len - 1) == 0
        and half_len % (8 * LANES) == 0
        and multipoles % (2 * LANES) == 0
        and per_block == 4
        and reals_dev % 16 == 0
        and reals_dev % PARTS == 0
        and cycles % 16 == 0
    )


def phase_tables(col_ids, mode_ids, cycle_len):
    product_ids = col_ids[:, None] * mode_ids[None, :] % cycle_len
    angles = product_ids.astype(jnp.float32) * (2.0 * math.pi / cycle_len)
    return (jnp.cos(angles).astype(jnp.bfloat16), jnp.sin(angles).astype(jnp.bfloat16))


def cycle_offsets(cycle_ids, mode_ids, cycle_len):
    parity = (cycle_ids % 2).astype(jnp.float32)
    shifts = math.pi / cycle_len * parity[:, None] * mode_ids[None, :].astype(jnp.float32)
    return (jnp.cos(shifts), jnp.sin(shifts))


def forward_modes(re_part, im_part):
    summed = lax.psum((re_part, im_part), "grp")
    fourier_pair = (summed[0].astype(jnp.bfloat16), summed[1].astype(jnp.bfloat16))
    fourier_pair = (
        lax.all_gather(fourier_pair[0], "real", axis=0, tiled=True),
        lax.all_gather(fourier_pair[1], "real", axis=0, tiled=True),
    )
    fourier_pair = (
        lax.all_to_all(fourier_pair[0], "blk", split_axis=2, concat_axis=1, tiled=True),
        lax.all_to_all(fourier_pair[1], "blk", split_axis=2, concat_axis=1, tiled=True),
    )
    return fourier_pair


def backward_cycles(partial_value):
    summed = lax.psum_scatter(partial_value, "real", scatter_dimension=0, tiled=True)
    reduced = lax.psum(summed, "grp")
    cycle_pair = lax.all_to_all(
        reduced.astype(jnp.bfloat16), "blk", split_axis=2, concat_axis=3, tiled=True
    )
    return cycle_pair


def per_device(
    sky_data, signal_prev, noise_var, mask_flags, cycle_table, m_table, spectrum, legendre
):
    real_dev, cycle_dev, half_len = sky_data.shape
    cycle_len = half_len * lax.axis_size("grp")
    mode_count = m_table.shape[0]
    col_ids = lax.axis_index("grp") * half_len + jnp.arange(half_len, dtype=jnp.int32)
    cos_tab, sin_tab = phase_tables(col_ids, m_table, cycle_len)
    cos_shift, sin_shift = cycle_offsets(cycle_table, m_table, cycle_len)
    weight = mask_flags.astype(jnp.float32) / (noise_var - 0.5)
    messenger = (weight * sky_data + 2.0 * signal_prev) / (weight + 2.0)
    flat_rows = messenger.astype(jnp.bfloat16).reshape(real_dev * cycle_dev, half_len)
    base_cos = jnp.dot(flat_rows, cos_tab, preferred_element_type=jnp.float32).reshape(
        real_dev, cycle_dev, mode_count
    )
    base_sin = -jnp.dot(flat_rows, sin_tab, preferred_element_type=jnp.float32).reshape(
        real_dev, cycle_dev, mode_count
    )
    norm_scale = cycle_len ** (-0.5)
    re_part = (base_cos * cos_shift + base_sin * sin_shift) * norm_scale
    im_part = (base_sin * cos_shift - base_cos * sin_shift) * norm_scale
    fourier_re, fourier_im = forward_modes(re_part, im_part)
    fourier = jnp.stack([fourier_re, fourier_im], 1)
    coefficients = jnp.einsum(
        "mlr,kcrm->kcml", legendre, fourier, preferred_element_type=jnp.float32
    )
    factor = spectrum / (spectrum + 0.5)
    wiener_alm = coefficients * factor
    total_l = legendre.shape[1] * lax.axis_size("grp") * lax.axis_size("real")
    syn_scale = (legendre.shape[2] / total_l) ** 0.5
    partial_value = (
        jnp.einsum(
            "mlr,kcml->kcrm",
            legendre,
            wiener_alm.astype(jnp.bfloat16),
            preferred_element_type=jnp.float32,
        )
        * syn_scale
    )
    cycle_pair = backward_cycles(partial_value)
    cycle_modes = cycle_pair.astype(jnp.float32)
    modes_re = cycle_modes[:, 0]
    modes_im = cycle_modes[:, 1]
    rotated_re = (modes_re * cos_shift - modes_im * sin_shift).astype(jnp.bfloat16)
    rotated_im = (modes_im * cos_shift + modes_re * sin_shift).astype(jnp.bfloat16)
    contract = (((1,), (1,)), ((), ()))
    pixel_sum = lax.dot_general(
        rotated_re.reshape(-1, mode_count), cos_tab, contract, preferred_element_type=jnp.float32
    )
    pixel_sum = pixel_sum - lax.dot_general(
        rotated_im.reshape(-1, mode_count), sin_tab, contract, preferred_element_type=jnp.float32
    )
    signal_next = (pixel_sum * mode_count ** (-0.5)).reshape(real_dev, cycle_dev, half_len)
    return (wiener_alm, signal_next)


def solution(mesh):
    in_specs = (
        P("real", "blk", "grp"),
        P("real", "blk", "grp"),
        P("blk", "grp"),
        P("blk", "grp"),
        P("blk"),
        P(),
        P(("grp", "real")),
        P("blk", ("grp", "real"), None),
    )
    out_specs = (P(None, None, "blk", ("grp", "real")), P("real", "blk", "grp"))

    def step(sky_data, signal_prev, noise_var, mask_flags, cycle_table, m_table, spectrum, legendre):
        fits = gram_form_fits(mesh, sky_data, m_table, legendre)
        return jax.shard_map(
            gram_program if fits else per_device,
            mesh=mesh,
            in_specs=in_specs,
            out_specs=out_specs,
            check_vma=False,
        )(sky_data, signal_prev, noise_var, mask_flags, cycle_table, m_table, spectrum, legendre)

    return step
```

```python
import functools
import math

import jax
import jax.numpy as jnp
from jax import lax
from jax.experimental import pallas as pl
from jax.experimental.pallas import tpu as pltpu
from jax.sharding import PartitionSpec as P

LANES = 128
NT = (((1,), (1,)), ((), ()))
AXES = ("grp", "blk", "real")
PARTS = 2
FORWARD_VMEM = 32 << 20
BACKWARD_VMEM = 16 << 20


def unit_cosine(units, half_turn):
    wrapped = units & (2 * half_turn - 1)
    folded = jnp.minimum(wrapped, 2 * half_turn - wrapped)
    y = (half_turn // 2 - folded).astype(jnp.float32) * (math.pi / half_turn)
    y2 = y * y
    acc = jnp.full_like(y2, -1.0 / math.factorial(11))
    for order, sign in ((9, 1.0), (7, -1.0), (5, 1.0), (3, -1.0), (1, 1.0)):
        acc = acc * y2 + sign / math.factorial(order)
    return acc * y


def log2(size):
    return size.bit_length() - 1


def lane_ids(shape):
    return lax.broadcasted_iota(jnp.int32, shape, len(shape) - 1)


def row_ids(shape):
    return lax.broadcasted_iota(jnp.int32, shape, len(shape) - 2)


def phase_factors(cycles, orders, cycle_len, half_len, group):
    modes = orders.shape[1]
    orders = jnp.concatenate([orders] * (LANES // modes), axis=1)
    quarter = lane_ids((1, LANES)) >> log2(modes)
    quarter_turn = cycle_len // 2
    row = row_ids((2 * LANES, LANES))
    pixel = (row >> log2(LANES)) * (half_len // 2) + (row & (LANES - 1))
    inner_units = 2 * orders * pixel + ((quarter + 1) >> 1) * quarter_turn
    inner = unit_cosine(inner_units, cycle_len)
    rows = half_len // LANES
    row = row_ids((rows, LANES))
    parity = jnp.where((row & 1) == 0, cycles[:, :1], cycles[:, 1:]) & 1
    pixel = group * half_len + LANES * (row >> 1)
    outer_units = orders * (2 * pixel + parity) + (quarter >> 1) * (3 * quarter_turn)
    outer = unit_cosine(outer_units, cycle_len)
    high = inner.astype(jnp.bfloat16)
    low = (inner - high.astype(jnp.float32)).astype(jnp.bfloat16)
    return jnp.concatenate([high, low], axis=1), outer


def start_copies(sources, targets, sems, first=0):
    copies = [
        pltpu.make_async_copy(source, target, sems.at[first + i])
        for i, (source, target) in enumerate(zip(sources, targets))
    ]
    for copy in copies:
        copy.start()
    return copies


def selections(place_ref, pick_ref, per_block, reals):
    block = lax.axis_index("blk")
    blocks, real_groups = lax.axis_size("blk"), lax.axis_size("real")
    modes, cycles, half = per_block * blocks, 2 * blocks, LANES // 2

    lane = lane_ids((1, LANES))
    row = row_ids((LANES, LANES))
    lane_order = (lane & (half - 1)) >> log2(cycles)
    lane_row = (lane & 1) * half + (lane >> log2(half)) * modes + block * per_block + lane_order
    pick_ref[0] = (row == lane_row).astype(jnp.float32).astype(jnp.bfloat16)
    lane_row = (lane >> log2(half)) * per_block + (lane & (per_block - 1))
    pick_ref[1] = ((row >> log2(cycles)) == lane_row).astype(jnp.float32).astype(jnp.bfloat16)

    share = reals // lax.axis_size("grp")
    spacing = share + 2
    column = lane_ids((1, place_ref.shape[1]))
    source = (column * (2**16 // spacing + 1)) >> 16
    inside = column - source * spacing
    source_block = (source >> log2(real_groups)) & (blocks - 1)
    target = ((source & (real_groups - 1)) * blocks + source_block) * reals + inside
    target = target + (source >> log2(blocks * real_groups)) * share
    target = jnp.where(inside < share, target, blocks * real_groups * reals + source_block)
    place = (row_ids(place_ref.shape) == target).astype(jnp.float32)
    place_ref[...] = place.astype(jnp.bfloat16)


def forward_kernel(
    cycle_len, half_len, syn_scale, reals,
    cycle_hbm, mode_hbm, noise_hbm, mask_hbm, spectrum_hbm, legendre_hbm, sky_hbm, prev_hbm,
    fourier_ref, pairs_ref, inner_ref, outer_ref, place_ref, pick_ref, doubled_ref, factor_ref,
    cycle_ref, mode_ref, noise_ref, mask_ref, spectrum_ref, legendre_ref, sky_ref, prev_ref, gram_ref, sems,
):
    copies = start_copies(
        (cycle_hbm, mode_hbm, sky_hbm, prev_hbm, noise_hbm, mask_hbm, spectrum_hbm, legendre_hbm),
        (cycle_ref, mode_ref, sky_ref, prev_ref, noise_ref, mask_ref, spectrum_ref, legendre_ref),
        sems,
    )
    group = lax.axis_index("grp")
    per_block = legendre_ref.shape[0] // (2 * lax.axis_size("blk"))
    selections(place_ref, pick_ref, per_block, reals)
    copies[0].wait()
    copies[1].wait()
    inner, outer = phase_factors(cycle_ref[...], mode_ref[...], cycle_len, half_len, group)
    inner_ref[...] = inner
    outer_ref[...] = outer
    for copy in copies[2:]:
        copy.wait()
    weight = mask_ref[...].astype(jnp.float32) / (noise_ref[...] - 0.5)
    inverse = 1.0 / (weight + 2.0)
    sky_gain = weight * inverse
    prev_gain = 2.0 * inverse

    table = legendre_ref[...]
    spectrum = spectrum_ref[...]
    factor = spectrum / (spectrum + 0.5)
    doubled_ref[...] = jnp.concatenate([table, table], axis=0)
    factor_ref[...] = factor
    filtered = (table.astype(jnp.float32) * factor).astype(jnp.bfloat16)
    gram = lax.dot_general(table, filtered, NT, preferred_element_type=jnp.float32)
    table_rows = table.shape[0]
    pixel_rows = outer.shape[0]
    blocks, real_groups = lax.axis_size("blk"), lax.axis_size("real")
    cycles = 2 * blocks
    same = (row_ids(gram.shape) >> log2(cycles)) == (lane_ids((1, table_rows)) >> log2(cycles))
    gram = jnp.where(same, gram, 0.0).reshape(table_rows // cycles, cycles, table_rows).sum(axis=0)
    gram = gram * syn_scale
    gram_ref[...] = jnp.concatenate([gram, gram], axis=1)
    even, odd = gram_ref[pl.ds(0, blocks, stride=2), :], gram_ref[pl.ds(1, blocks, stride=2), :]
    gram = jnp.where(lane_ids(even.shape) < LANES // 2, even, odd)
    gram_high = gram.astype(jnp.bfloat16).astype(jnp.float32)
    pairs_ref[...] = jnp.concatenate([gram_high, gram - gram_high], axis=0).astype(jnp.bfloat16)

    shape = (reals, 2 * pixel_rows, LANES)
    messenger = sky_ref[...].reshape(shape) * sky_gain + prev_ref[...].reshape(shape) * prev_gain
    rows = jnp.concatenate([messenger[:, :pixel_rows], messenger[:, pixel_rows:]], axis=2)
    rows = rows.reshape(-1, 2 * LANES).astype(jnp.bfloat16)
    partial = jnp.dot(rows, inner, preferred_element_type=jnp.float32)
    partial = partial[:, :LANES] + partial[:, LANES:]
    turned = partial.reshape(reals, pixel_rows, LANES) * outer
    summed = turned.reshape(reals, pixel_rows // 8, 8, LANES).sum(axis=1)
    summed = summed.reshape(reals * 8, LANES)
    summed = summed + pltpu.roll(summed, LANES // 2, 1)
    own = (row_ids(summed.shape) & 1) == (lane_ids(summed.shape) >= LANES // 2)
    fourier = jnp.where(own, summed, 0.0).reshape(reals, 8, LANES).sum(axis=1) * cycle_len**-0.5
    fourier_ref[...] = fourier.astype(jnp.bfloat16)


def pack_kernel(fourier_ref, swapped_ref, pairs_ref, out_ref):
    fourier = fourier_ref[...].astype(jnp.float32) + swapped_ref[...].astype(jnp.float32)
    share = fourier.shape[0] // lax.axis_size("grp")
    fourier = jnp.where(lax.axis_index("grp") == 0, fourier[:share], fourier[share:])
    pairs = pairs_ref[...].astype(jnp.float32)
    blocks = lax.axis_size("blk")
    rows = []
    for b in range(blocks):
        rows += [fourier, pairs[b : b + 1], pairs[blocks + b : blocks + b + 1]] * lax.axis_size("real")
    rows = jnp.concatenate(rows, axis=0).astype(jnp.bfloat16)
    for g in range(lax.axis_size("grp")):
        out_ref[pl.ds(g * rows.shape[0], rows.shape[0]), :] = rows


def backward_kernel(
    blocks, real_groups, reals, parts,
    gathered_ref, inner_ref, outer_ref, place_ref, pick_ref, table_ref, factor_ref,
    wiener_hbm, signal_hbm, wiener_ref, signal_ref, fourier_ref, out_sems,
):
    real_group = lax.axis_index("real")
    cycles = 2 * blocks
    per_block = table_ref.shape[0] // (2 * cycles)
    modes = per_block * blocks
    pixel_rows = outer_ref.shape[0]
    half = LANES // 2
    lane = lane_ids((1, LANES))
    holder = (lane & (modes - 1)) >> log2(per_block)
    lane_block = (lane & (cycles - 1)) >> 1
    total_reals = real_groups * reals
    fourier_rows = blocks * total_reals
    placed = jnp.dot(place_ref[...], gathered_ref[...], preferred_element_type=jnp.float32)
    fourier_ref[...] = placed[:fourier_rows]

    coeff_rows = jnp.dot(
        placed[:fourier_rows].astype(jnp.bfloat16), pick_ref[0], preferred_element_type=jnp.float32
    ).reshape(real_groups, blocks, reals, LANES)
    columns = jnp.zeros((total_reals, LANES), jnp.float32)
    for b in range(blocks):
        one = coeff_rows[:, b].reshape(total_reals, LANES)
        columns = columns + jnp.where(lane_block == b, one, 0.0)
    table = table_ref[...]
    factor = factor_ref[...]
    stores = []
    own = (lane >> log2(cycles)) == row_ids((2 * per_block, LANES))
    upper = row_ids((1, 2 * per_block, LANES)) < per_block
    pieces = jnp.where(own, columns[:, None, :], 0.0).reshape(-1, LANES).astype(jnp.bfloat16)
    filtered = factor * jnp.dot(pieces, table, preferred_element_type=jnp.float32)
    filtered = filtered.reshape(total_reals, 2 * per_block, -1)
    for y in range(real_groups):
        span = slice(y * reals, (y + 1) * reals)
        for pair in range(wiener_ref.shape[2]):
            one, two = (
                filtered[span, :, tile * LANES : (tile + 1) * LANES] for tile in (2 * pair, 2 * pair + 1)
            )
            wiener_ref[span, 0, pair] = jnp.where(upper, one, pltpu.roll(two, per_block, 1))
            wiener_ref[span, 1, pair] = jnp.where(upper, pltpu.roll(one, per_block, 1), two)
        span = pl.ds(y * reals, reals)
        stores += start_copies([wiener_ref.at[span]], [wiener_hbm.at[span]], out_sems, len(stores))

    gram_all = jnp.where(
        (lane & (cycles - 1)) == row_ids((cycles, LANES)), placed[fourier_rows:, None, :], 0.0
    ).reshape(blocks * cycles, LANES)
    gram_high = gram_all.astype(jnp.bfloat16)
    gram_low = (gram_all - gram_high.astype(jnp.float32)).astype(jnp.bfloat16)
    gram_rows = jnp.dot(
        jnp.concatenate([gram_high, gram_low], axis=1),
        jnp.concatenate([pick_ref[1], pick_ref[1]], axis=0),
        preferred_element_type=jnp.float32,
    ).reshape(blocks, cycles, LANES)
    gram = jnp.zeros((cycles, LANES), jnp.float32)
    for b in range(blocks):
        gram = gram + jnp.where(holder == b, gram_rows[b], 0.0)

    first = lane < half
    cycle_modes = jnp.zeros((reals, LANES), jnp.float32)
    for b in range(blocks):
        first_row = pl.multiple_of((real_group * blocks + b) * reals, reals)
        pair = fourier_ref[pl.ds(first_row, reals), :]
        turned = pltpu.roll(pair, half, 1)
        cycle_modes = cycle_modes + jnp.where(first, pair, turned) * gram[2 * b : 2 * b + 1]
        cycle_modes = cycle_modes + jnp.where(first, turned, pair) * gram[2 * b + 1 : 2 * b + 2]
    cycle_modes = cycle_modes * modes**-0.5
    turned = pltpu.roll(cycle_modes, half, 1)
    even = jnp.where(first, cycle_modes, turned)
    odd = jnp.where(first, turned, cycle_modes)
    parity = (row_ids((1, 8, LANES)) & 1) == 0
    spread = jnp.where(parity, even[:, None, :], odd[:, None, :])
    inner = inner_ref[...]
    outer = outer_ref[...].reshape(1, pixel_rows // 8, 8, LANES)
    rotated = (spread[:, None] * outer).reshape(-1, LANES).astype(jnp.bfloat16)
    signal = lax.dot_general(
        jnp.concatenate([rotated, rotated], axis=1), inner, NT, preferred_element_type=jnp.float32
    ).reshape(reals, pixel_rows, 2 * LANES)
    part_reals = reals // parts
    for i in range(parts):
        span = slice(i * part_reals, (i + 1) * part_reals)
        signal_ref[span, 0] = signal[span, :, :LANES]
        signal_ref[span, 1] = signal[span, :, LANES:]
        span = pl.ds(i * part_reals, part_reals)
        stores += start_copies([signal_ref.at[span]], [signal_hbm.at[span]], out_sems, len(stores))
    for store in stores:
        store.wait()


def split_tiles(array):
    lead, rows, columns = array.shape[:-2], array.shape[-2], array.shape[-1]
    split = array.reshape(*lead, rows, columns // LANES, LANES)
    return jnp.swapaxes(split, -2, -3).reshape(-1, LANES)


def gram_program(
    sky_data, signal_prev, noise_var, mask_flags, cycle_table, m_table, spectrum, legendre
):
    reals, cycle_dev, half_len = sky_data.shape
    groups, blocks, real_groups = (lax.axis_size(name) for name in AXES)
    cycle_len = half_len * groups
    per_block, multipoles, cycles = legendre.shape
    total_l = multipoles * groups * real_groups
    tiles = multipoles // LANES
    hbm = pl.BlockSpec(memory_space=pltpu.HBM)
    vmem = pl.BlockSpec(memory_space=pltpu.VMEM)
    orders = m_table[None, :]
    cycles_row = cycle_table[None, :]
    spectrum_row = spectrum[None, :]
    table = legendre.transpose(0, 2, 1).reshape(per_block * cycles, multipoles)
    inputs = (
        cycles_row, orders, split_tiles(noise_var), split_tiles(mask_flags), spectrum_row, table,
        split_tiles(sky_data), split_tiles(signal_prev),
    )
    sources = groups * blocks * real_groups
    total_reals = reals * real_groups
    rows = sources * (reals // groups + 2)
    fourier, pairs, *prepared = pl.pallas_call(
        functools.partial(forward_kernel, cycle_len, half_len, (cycles / total_l) ** 0.5, reals),
        out_shape=(
            jax.ShapeDtypeStruct((reals, LANES), jnp.bfloat16),
            jax.ShapeDtypeStruct((cycles, LANES), jnp.bfloat16),
            jax.ShapeDtypeStruct((2 * LANES, 2 * LANES), jnp.bfloat16),
            jax.ShapeDtypeStruct((half_len // LANES, LANES), jnp.float32),
            jax.ShapeDtypeStruct((blocks * (total_reals + 1), rows), jnp.bfloat16),
            jax.ShapeDtypeStruct((2, LANES, LANES), jnp.bfloat16),
            jax.ShapeDtypeStruct((2 * table.shape[0], multipoles), jnp.bfloat16),
            jax.ShapeDtypeStruct((1, multipoles), jnp.float32),
        ),
        in_specs=[hbm] * 8,
        out_specs=(vmem,) * 8,
        scratch_shapes=[pltpu.VMEM(x.shape, x.dtype) for x in inputs]
        + [pltpu.VMEM((cycles, LANES), jnp.float32), pltpu.SemaphoreType.DMA((8,))],
        compiler_params=pltpu.CompilerParams(vmem_limit_bytes=FORWARD_VMEM),
    )(*(pltpu.with_memory_space_constraint(x, pltpu.HBM) for x in inputs))
    swapped = lax.ppermute(fourier, "grp", [(i, i ^ 1) for i in range(groups)])
    local = pl.pallas_call(
        pack_kernel,
        out_shape=jax.ShapeDtypeStruct((rows, LANES), jnp.bfloat16),
        in_specs=[vmem] * 3,
        out_specs=vmem,
        compiler_params=pltpu.CompilerParams(vmem_limit_bytes=BACKWARD_VMEM),
    )(fourier, swapped, pairs)
    local = local.reshape(sources, rows // (2 * sources), 2, LANES)
    gathered = lax.all_to_all(local, AXES, 0, 0, tiled=True).reshape(rows, LANES)
    outputs = (
        jax.ShapeDtypeStruct((total_reals, 2, tiles // 2, 2 * per_block, LANES), jnp.float32),
        jax.ShapeDtypeStruct((reals, 2, half_len // LANES, LANES), jnp.float32),
    )
    wiener, signal = pl.pallas_call(
        functools.partial(backward_kernel, blocks, real_groups, reals, PARTS),
        out_shape=outputs,
        in_specs=[vmem] * 7,
        out_specs=(hbm, hbm),
        scratch_shapes=[pltpu.VMEM(x.shape, x.dtype) for x in outputs]
        + [pltpu.VMEM((blocks * total_reals, LANES), jnp.float32)]
        + [pltpu.SemaphoreType.DMA((real_groups + PARTS,))],
        compiler_params=pltpu.CompilerParams(vmem_limit_bytes=BACKWARD_VMEM),
    )(gathered, *prepared)
    wiener = wiener.reshape(total_reals, 2, tiles, per_block, LANES).transpose(0, 1, 3, 2, 4)
    signal = signal.reshape(reals, half_len // LANES, cycle_dev, LANES).transpose(0, 2, 1, 3)
    return (
        wiener.reshape(total_reals, 2, per_block, multipoles),
        signal.reshape(sky_data.shape),
    )


def gram_form_fits(mesh, sky_data, m_table, legendre):
    groups, blocks, real_groups = (mesh.shape[name] for name in AXES)
    reals, cycles, cycle_len = sky_data.shape
    modes = m_table.shape[0]
    per_block = modes // blocks
    multipoles = legendre.shape[1] // (groups * real_groups)
    half_len = cycle_len // groups
    reals_dev = reals // real_groups
    return (
        cycles < 2 * reals
        and groups == 2
        and 4 * modes == LANES
        and cycles == 2 * blocks
        and all(size & (size - 1) == 0 for size in (blocks, modes, cycles, real_groups))
        and 2 * reals * cycles < 2**12
        and 2 * per_block * cycles == LANES
        and cycle_len & (cycle_len - 1) == 0
        and half_len % (8 * LANES) == 0
        and multipoles % (2 * LANES) == 0
        and per_block == 4
        and reals_dev % 16 == 0
        and reals_dev // groups % 8 == 0
        and reals_dev % PARTS == 0
        and cycles % 16 == 0
    )


def phase_tables(col_ids, mode_ids, cycle_len):
    product_ids = col_ids[:, None] * mode_ids[None, :] % cycle_len
    angles = product_ids.astype(jnp.float32) * (2.0 * math.pi / cycle_len)
    return (jnp.cos(angles).astype(jnp.bfloat16), jnp.sin(angles).astype(jnp.bfloat16))


def cycle_offsets(cycle_ids, mode_ids, cycle_len):
    parity = (cycle_ids % 2).astype(jnp.float32)
    shifts = math.pi / cycle_len * parity[:, None] * mode_ids[None, :].astype(jnp.float32)
    return (jnp.cos(shifts), jnp.sin(shifts))


def forward_modes(re_part, im_part):
    summed = lax.psum((re_part, im_part), "grp")
    fourier_pair = (summed[0].astype(jnp.bfloat16), summed[1].astype(jnp.bfloat16))
    fourier_pair = (
        lax.all_gather(fourier_pair[0], "real", axis=0, tiled=True),
        lax.all_gather(fourier_pair[1], "real", axis=0, tiled=True),
    )
    fourier_pair = (
        lax.all_to_all(fourier_pair[0], "blk", split_axis=2, concat_axis=1, tiled=True),
        lax.all_to_all(fourier_pair[1], "blk", split_axis=2, concat_axis=1, tiled=True),
    )
    return fourier_pair


def backward_cycles(partial_value):
    summed = lax.psum_scatter(partial_value, "real", scatter_dimension=0, tiled=True)
    reduced = lax.psum(summed, "grp")
    cycle_pair = lax.all_to_all(
        reduced.astype(jnp.bfloat16), "blk", split_axis=2, concat_axis=3, tiled=True
    )
    return cycle_pair


def per_device(
    sky_data, signal_prev, noise_var, mask_flags, cycle_table, m_table, spectrum, legendre
):
    real_dev, cycle_dev, half_len = sky_data.shape
    cycle_len = half_len * lax.axis_size("grp")
    mode_count = m_table.shape[0]
    col_ids = lax.axis_index("grp") * half_len + jnp.arange(half_len, dtype=jnp.int32)
    cos_tab, sin_tab = phase_tables(col_ids, m_table, cycle_len)
    cos_shift, sin_shift = cycle_offsets(cycle_table, m_table, cycle_len)
    weight = mask_flags.astype(jnp.float32) / (noise_var - 0.5)
    messenger = (weight * sky_data + 2.0 * signal_prev) / (weight + 2.0)
    flat_rows = messenger.astype(jnp.bfloat16).reshape(real_dev * cycle_dev, half_len)
    base_cos = jnp.dot(flat_rows, cos_tab, preferred_element_type=jnp.float32).reshape(
        real_dev, cycle_dev, mode_count
    )
    base_sin = -jnp.dot(flat_rows, sin_tab, preferred_element_type=jnp.float32).reshape(
        real_dev, cycle_dev, mode_count
    )
    norm_scale = cycle_len ** (-0.5)
    re_part = (base_cos * cos_shift + base_sin * sin_shift) * norm_scale
    im_part = (base_sin * cos_shift - base_cos * sin_shift) * norm_scale
    fourier_re, fourier_im = forward_modes(re_part, im_part)
    fourier = jnp.stack([fourier_re, fourier_im], 1)
    coefficients = jnp.einsum(
        "mlr,kcrm->kcml", legendre, fourier, preferred_element_type=jnp.float32
    )
    factor = spectrum / (spectrum + 0.5)
    wiener_alm = coefficients * factor
    total_l = legendre.shape[1] * lax.axis_size("grp") * lax.axis_size("real")
    syn_scale = (legendre.shape[2] / total_l) ** 0.5
    partial_value = (
        jnp.einsum(
            "mlr,kcml->kcrm",
            legendre,
            wiener_alm.astype(jnp.bfloat16),
            preferred_element_type=jnp.float32,
        )
        * syn_scale
    )
    cycle_pair = backward_cycles(partial_value)
    cycle_modes = cycle_pair.astype(jnp.float32)
    modes_re = cycle_modes[:, 0]
    modes_im = cycle_modes[:, 1]
    rotated_re = (modes_re * cos_shift - modes_im * sin_shift).astype(jnp.bfloat16)
    rotated_im = (modes_im * cos_shift + modes_re * sin_shift).astype(jnp.bfloat16)
    contract = (((1,), (1,)), ((), ()))
    pixel_sum = lax.dot_general(
        rotated_re.reshape(-1, mode_count), cos_tab, contract, preferred_element_type=jnp.float32
    )
    pixel_sum = pixel_sum - lax.dot_general(
        rotated_im.reshape(-1, mode_count), sin_tab, contract, preferred_element_type=jnp.float32
    )
    signal_next = (pixel_sum * mode_count ** (-0.5)).reshape(real_dev, cycle_dev, half_len)
    return (wiener_alm, signal_next)


def solution(mesh):
    in_specs = (
        P("real", "blk", "grp"),
        P("real", "blk", "grp"),
        P("blk", "grp"),
        P("blk", "grp"),
        P("blk"),
        P(),
        P(("grp", "real")),
        P("blk", ("grp", "real"), None),
    )
    out_specs = (P(None, None, "blk", ("grp", "real")), P("real", "blk", "grp"))

    def step(sky_data, signal_prev, noise_var, mask_flags, cycle_table, m_table, spectrum, legendre):
        fits = gram_form_fits(mesh, sky_data, m_table, legendre)
        return jax.shard_map(
            gram_program if fits else per_device,
            mesh=mesh,
            in_specs=in_specs,
            out_specs=out_specs,
            check_vma=False,
        )(sky_data, signal_prev, noise_var, mask_flags, cycle_table, m_table, spectrum, legendre)

    return step
```

```python
import functools
import math

import jax
import jax.numpy as jnp
from jax import lax
from jax.experimental import pallas as pl
from jax.experimental.pallas import tpu as pltpu
from jax.sharding import PartitionSpec as P

LANES = 128
NT = (((1,), (1,)), ((), ()))
AXES = ("grp", "blk", "real")
PARTS = 2
FORWARD_VMEM = 32 << 20
BACKWARD_VMEM = 16 << 20


def unit_cosine(units, half_turn):
    wrapped = units & (2 * half_turn - 1)
    folded = jnp.minimum(wrapped, 2 * half_turn - wrapped)
    y = (half_turn // 2 - folded).astype(jnp.float32) * (math.pi / half_turn)
    y2 = y * y
    acc = jnp.full_like(y2, -1.0 / math.factorial(11))
    for order, sign in ((9, 1.0), (7, -1.0), (5, 1.0), (3, -1.0), (1, 1.0)):
        acc = acc * y2 + sign / math.factorial(order)
    return acc * y


def log2(size):
    return size.bit_length() - 1


def lane_ids(shape):
    return lax.broadcasted_iota(jnp.int32, shape, len(shape) - 1)


def row_ids(shape):
    return lax.broadcasted_iota(jnp.int32, shape, len(shape) - 2)


def phase_factors(cycles, orders, cycle_len, half_len, group):
    modes = orders.shape[1]
    orders = jnp.concatenate([orders] * (LANES // modes), axis=1)
    quarter = lane_ids((1, LANES)) >> log2(modes)
    quarter_turn = cycle_len // 2
    row = row_ids((2 * LANES, LANES))
    pixel = (row >> log2(LANES)) * (half_len // 2) + (row & (LANES - 1))
    inner_units = 2 * orders * pixel + ((quarter + 1) >> 1) * quarter_turn
    inner = unit_cosine(inner_units, cycle_len)
    rows = half_len // LANES
    row = row_ids((rows, LANES))
    parity = jnp.where((row & 1) == 0, cycles[:, :1], cycles[:, 1:]) & 1
    pixel = group * half_len + LANES * (row >> 1)
    outer_units = orders * (2 * pixel + parity) + (quarter >> 1) * (3 * quarter_turn)
    outer = unit_cosine(outer_units, cycle_len)
    high = inner.astype(jnp.bfloat16)
    low = (inner - high.astype(jnp.float32)).astype(jnp.bfloat16)
    return jnp.concatenate([high, low], axis=1), outer


def start_copies(sources, targets, sems, first=0):
    copies = [
        pltpu.make_async_copy(source, target, sems.at[first + i])
        for i, (source, target) in enumerate(zip(sources, targets))
    ]
    for copy in copies:
        copy.start()
    return copies


def selections(place_ref, pick_ref, per_block, reals):
    block = lax.axis_index("blk")
    blocks, real_groups = lax.axis_size("blk"), lax.axis_size("real")
    modes, cycles, half = per_block * blocks, 2 * blocks, LANES // 2

    lane = lane_ids((1, LANES))
    row = row_ids((LANES, LANES))
    lane_order = (lane & (half - 1)) >> log2(cycles)
    lane_row = (lane & 1) * half + (lane >> log2(half)) * modes + block * per_block + lane_order
    pick_ref[0] = (row == lane_row).astype(jnp.float32).astype(jnp.bfloat16)
    lane_row = (lane >> log2(half)) * per_block + (lane & (per_block - 1))
    pick_ref[1] = ((row >> log2(cycles)) == lane_row).astype(jnp.float32).astype(jnp.bfloat16)

    spacing = reals + 2
    column = lane_ids((1, place_ref.shape[1]))
    source = (column * (2**16 // spacing + 1)) >> 16
    inside = column - source * spacing
    source_block = source & (blocks - 1)
    target = source * reals + inside
    target = jnp.where(inside < reals, target, blocks * real_groups * reals + source_block)
    place = (row_ids(place_ref.shape) == target).astype(jnp.float32)
    place_ref[...] = place.astype(jnp.bfloat16)


def forward_kernel(
    cycle_len, half_len, syn_scale, reals,
    cycle_hbm, mode_hbm, noise_hbm, mask_hbm, spectrum_hbm, legendre_hbm, sky_hbm, prev_hbm,
    out_ref, inner_ref, outer_ref, place_ref, pick_ref, doubled_ref, factor_ref,
    cycle_ref, mode_ref, noise_ref, mask_ref, spectrum_ref, legendre_ref, sky_ref, prev_ref, gram_ref, sems,
):
    copies = start_copies(
        (cycle_hbm, mode_hbm, sky_hbm, prev_hbm, noise_hbm, mask_hbm, spectrum_hbm, legendre_hbm),
        (cycle_ref, mode_ref, sky_ref, prev_ref, noise_ref, mask_ref, spectrum_ref, legendre_ref),
        sems,
    )
    group = lax.axis_index("grp")
    per_block = legendre_ref.shape[0] // (2 * lax.axis_size("blk"))
    selections(place_ref, pick_ref, per_block, reals)
    copies[0].wait()
    copies[1].wait()
    inner, outer = phase_factors(cycle_ref[...], mode_ref[...], cycle_len, half_len, group)
    inner_ref[...] = inner
    outer_ref[...] = outer
    for copy in copies[2:]:
        copy.wait()
    weight = mask_ref[...].astype(jnp.float32) / (noise_ref[...] - 0.5)
    inverse = 1.0 / (weight + 2.0)
    sky_gain = weight * inverse
    prev_gain = 2.0 * inverse

    table = legendre_ref[...]
    spectrum = spectrum_ref[...]
    factor = spectrum / (spectrum + 0.5)
    doubled_ref[...] = jnp.concatenate([table, table], axis=0)
    factor_ref[...] = factor
    filtered = (table.astype(jnp.float32) * factor).astype(jnp.bfloat16)
    gram = lax.dot_general(table, filtered, NT, preferred_element_type=jnp.float32)
    table_rows = table.shape[0]
    pixel_rows = outer.shape[0]
    blocks, real_groups = lax.axis_size("blk"), lax.axis_size("real")
    cycles = 2 * blocks
    same = (row_ids(gram.shape) >> log2(cycles)) == (lane_ids((1, table_rows)) >> log2(cycles))
    gram = jnp.where(same, gram, 0.0).reshape(table_rows // cycles, cycles, table_rows).sum(axis=0)
    gram = gram * syn_scale
    gram_ref[...] = jnp.concatenate([gram, gram], axis=1)
    even, odd = gram_ref[pl.ds(0, blocks, stride=2), :], gram_ref[pl.ds(1, blocks, stride=2), :]
    gram = jnp.where(lane_ids(even.shape) < LANES // 2, even, odd)
    gram_high = gram.astype(jnp.bfloat16).astype(jnp.float32)
    gram_low = gram - gram_high

    shape = (reals, 2 * pixel_rows, LANES)
    messenger = sky_ref[...].reshape(shape) * sky_gain + prev_ref[...].reshape(shape) * prev_gain
    rows = jnp.concatenate([messenger[:, :pixel_rows], messenger[:, pixel_rows:]], axis=2)
    rows = rows.reshape(-1, 2 * LANES).astype(jnp.bfloat16)
    partial = jnp.dot(rows, inner, preferred_element_type=jnp.float32)
    partial = partial[:, :LANES] + partial[:, LANES:]
    turned = partial.reshape(reals, pixel_rows, LANES) * outer
    summed = turned.reshape(reals, pixel_rows // 8, 8, LANES).sum(axis=1)
    summed = summed.reshape(reals * 8, LANES)
    summed = summed + pltpu.roll(summed, LANES // 2, 1)
    own = (row_ids(summed.shape) & 1) == (lane_ids(summed.shape) >= LANES // 2)
    fourier = jnp.where(own, summed, 0.0).reshape(reals, 8, LANES).sum(axis=1) * cycle_len**-0.5
    rows = []
    for b in range(blocks):
        rows += [fourier, gram_high[b : b + 1], gram_low[b : b + 1]]
    rows = jnp.concatenate(rows * real_groups, axis=0).astype(jnp.bfloat16)
    for g in range(lax.axis_size("grp")):
        out_ref[pl.ds(g * rows.shape[0], rows.shape[0]), :] = rows


def backward_kernel(
    blocks, real_groups, reals, parts,
    gathered_ref, inner_ref, outer_ref, place_ref, pick_ref, table_ref, factor_ref,
    wiener_hbm, signal_hbm, wiener_ref, signal_ref, fourier_ref, out_sems,
):
    real_group = lax.axis_index("real")
    cycles = 2 * blocks
    per_block = table_ref.shape[0] // (2 * cycles)
    modes = per_block * blocks
    pixel_rows = outer_ref.shape[0]
    half = LANES // 2
    lane = lane_ids((1, LANES))
    holder = (lane & (modes - 1)) >> log2(per_block)
    lane_block = (lane & (cycles - 1)) >> 1
    total_reals = real_groups * reals
    fourier_rows = blocks * total_reals
    share = place_ref.shape[1]
    sides = jnp.concatenate([gathered_ref[:share, :], gathered_ref[share:, :]], axis=1)
    placed = jnp.dot(place_ref[...], sides, preferred_element_type=jnp.float32)
    placed = placed[:, :LANES] + placed[:, LANES:]
    fourier_ref[...] = placed[:fourier_rows]

    coeff_rows = jnp.dot(
        placed[:fourier_rows].astype(jnp.bfloat16), pick_ref[0], preferred_element_type=jnp.float32
    ).reshape(real_groups, blocks, reals, LANES)
    columns = jnp.zeros((total_reals, LANES), jnp.float32)
    for b in range(blocks):
        one = coeff_rows[:, b].reshape(total_reals, LANES)
        columns = columns + jnp.where(lane_block == b, one, 0.0)
    table = table_ref[...]
    factor = factor_ref[...]
    stores = []
    own = (lane >> log2(cycles)) == row_ids((2 * per_block, LANES))
    upper = row_ids((1, 2 * per_block, LANES)) < per_block
    pieces = jnp.where(own, columns[:, None, :], 0.0).reshape(-1, LANES).astype(jnp.bfloat16)
    filtered = factor * jnp.dot(pieces, table, preferred_element_type=jnp.float32)
    filtered = filtered.reshape(total_reals, 2 * per_block, -1)
    for y in range(real_groups):
        span = slice(y * reals, (y + 1) * reals)
        for pair in range(wiener_ref.shape[2]):
            one, two = (
                filtered[span, :, tile * LANES : (tile + 1) * LANES] for tile in (2 * pair, 2 * pair + 1)
            )
            wiener_ref[span, 0, pair] = jnp.where(upper, one, pltpu.roll(two, per_block, 1))
            wiener_ref[span, 1, pair] = jnp.where(upper, pltpu.roll(one, per_block, 1), two)
        span = pl.ds(y * reals, reals)
        stores += start_copies([wiener_ref.at[span]], [wiener_hbm.at[span]], out_sems, len(stores))

    gram_all = jnp.where(
        (lane & (cycles - 1)) == row_ids((cycles, LANES)), placed[fourier_rows:, None, :], 0.0
    ).reshape(blocks * cycles, LANES)
    gram_high = gram_all.astype(jnp.bfloat16)
    gram_low = (gram_all - gram_high.astype(jnp.float32)).astype(jnp.bfloat16)
    gram_rows = jnp.dot(
        jnp.concatenate([gram_high, gram_low], axis=1),
        jnp.concatenate([pick_ref[1], pick_ref[1]], axis=0),
        preferred_element_type=jnp.float32,
    ).reshape(blocks, cycles, LANES)
    gram = jnp.zeros((cycles, LANES), jnp.float32)
    for b in range(blocks):
        gram = gram + jnp.where(holder == b, gram_rows[b], 0.0)

    first = lane < half
    cycle_modes = jnp.zeros((reals, LANES), jnp.float32)
    for b in range(blocks):
        first_row = pl.multiple_of((real_group * blocks + b) * reals, reals)
        pair = fourier_ref[pl.ds(first_row, reals), :]
        turned = pltpu.roll(pair, half, 1)
        cycle_modes = cycle_modes + jnp.where(first, pair, turned) * gram[2 * b : 2 * b + 1]
        cycle_modes = cycle_modes + jnp.where(first, turned, pair) * gram[2 * b + 1 : 2 * b + 2]
    cycle_modes = cycle_modes * modes**-0.5
    turned = pltpu.roll(cycle_modes, half, 1)
    even = jnp.where(first, cycle_modes, turned)
    odd = jnp.where(first, turned, cycle_modes)
    parity = (row_ids((1, 8, LANES)) & 1) == 0
    spread = jnp.where(parity, even[:, None, :], odd[:, None, :])
    inner = inner_ref[...]
    outer = outer_ref[...].reshape(1, pixel_rows // 8, 8, LANES)
    rotated = (spread[:, None] * outer).reshape(-1, LANES).astype(jnp.bfloat16)
    signal = lax.dot_general(
        jnp.concatenate([rotated, rotated], axis=1), inner, NT, preferred_element_type=jnp.float32
    ).reshape(reals, pixel_rows, 2 * LANES)
    part_reals = reals // parts
    for i in range(parts):
        span = slice(i * part_reals, (i + 1) * part_reals)
        signal_ref[span, 0] = signal[span, :, :LANES]
        signal_ref[span, 1] = signal[span, :, LANES:]
        span = pl.ds(i * part_reals, part_reals)
        stores += start_copies([signal_ref.at[span]], [signal_hbm.at[span]], out_sems, len(stores))
    for store in stores:
        store.wait()


def split_tiles(array):
    lead, rows, columns = array.shape[:-2], array.shape[-2], array.shape[-1]
    split = array.reshape(*lead, rows, columns // LANES, LANES)
    return jnp.swapaxes(split, -2, -3).reshape(-1, LANES)


def gram_program(
    sky_data, signal_prev, noise_var, mask_flags, cycle_table, m_table, spectrum, legendre
):
    reals, cycle_dev, half_len = sky_data.shape
    groups, blocks, real_groups = (lax.axis_size(name) for name in AXES)
    cycle_len = half_len * groups
    per_block, multipoles, cycles = legendre.shape
    total_l = multipoles * groups * real_groups
    tiles = multipoles // LANES
    hbm = pl.BlockSpec(memory_space=pltpu.HBM)
    vmem = pl.BlockSpec(memory_space=pltpu.VMEM)
    orders = m_table[None, :]
    cycles_row = cycle_table[None, :]
    spectrum_row = spectrum[None, :]
    table = legendre.transpose(0, 2, 1).reshape(per_block * cycles, multipoles)
    inputs = (
        cycles_row, orders, split_tiles(noise_var), split_tiles(mask_flags), spectrum_row, table,
        split_tiles(sky_data), split_tiles(signal_prev),
    )
    sources = groups * blocks * real_groups
    total_reals = reals * real_groups
    local, *prepared = pl.pallas_call(
        functools.partial(forward_kernel, cycle_len, half_len, (cycles / total_l) ** 0.5, reals),
        out_shape=(
            jax.ShapeDtypeStruct((sources * (reals + 2), LANES), jnp.bfloat16),
            jax.ShapeDtypeStruct((2 * LANES, 2 * LANES), jnp.bfloat16),
            jax.ShapeDtypeStruct((half_len // LANES, LANES), jnp.float32),
            jax.ShapeDtypeStruct(
                (blocks * (total_reals + 1), blocks * real_groups * (reals + 2)), jnp.bfloat16
            ),
            jax.ShapeDtypeStruct((2, LANES, LANES), jnp.bfloat16),
            jax.ShapeDtypeStruct((2 * table.shape[0], multipoles), jnp.bfloat16),
            jax.ShapeDtypeStruct((1, multipoles), jnp.float32),
        ),
        in_specs=[hbm] * 8,
        out_specs=(vmem,) * 7,
        scratch_shapes=[pltpu.VMEM(x.shape, x.dtype) for x in inputs]
        + [pltpu.VMEM((cycles, LANES), jnp.float32), pltpu.SemaphoreType.DMA((8,))],
        compiler_params=pltpu.CompilerParams(vmem_limit_bytes=FORWARD_VMEM),
    )(*(pltpu.with_memory_space_constraint(x, pltpu.HBM) for x in inputs))
    pairs = local.reshape(sources, reals // 2 + 1, 2, LANES)
    gathered = lax.all_to_all(pairs, ("grp", "real", "blk"), 0, 0, tiled=True).reshape(local.shape)
    outputs = (
        jax.ShapeDtypeStruct((total_reals, 2, tiles // 2, 2 * per_block, LANES), jnp.float32),
        jax.ShapeDtypeStruct((reals, 2, half_len // LANES, LANES), jnp.float32),
    )
    wiener, signal = pl.pallas_call(
        functools.partial(backward_kernel, blocks, real_groups, reals, PARTS),
        out_shape=outputs,
        in_specs=[vmem] * 7,
        out_specs=(hbm, hbm),
        scratch_shapes=[pltpu.VMEM(x.shape, x.dtype) for x in outputs]
        + [pltpu.VMEM((blocks * total_reals, LANES), jnp.float32)]
        + [pltpu.SemaphoreType.DMA((real_groups + PARTS,))],
        compiler_params=pltpu.CompilerParams(vmem_limit_bytes=BACKWARD_VMEM),
    )(gathered, *prepared)
    wiener = wiener.reshape(total_reals, 2, tiles, per_block, LANES).transpose(0, 1, 3, 2, 4)
    signal = signal.reshape(reals, half_len // LANES, cycle_dev, LANES).transpose(0, 2, 1, 3)
    return (
        wiener.reshape(total_reals, 2, per_block, multipoles),
        signal.reshape(sky_data.shape),
    )


def gram_form_fits(mesh, sky_data, m_table, legendre):
    groups, blocks, real_groups = (mesh.shape[name] for name in AXES)
    reals, cycles, cycle_len = sky_data.shape
    modes = m_table.shape[0]
    per_block = modes // blocks
    multipoles = legendre.shape[1] // (groups * real_groups)
    half_len = cycle_len // groups
    reals_dev = reals // real_groups
    return (
        cycles < 2 * reals
        and 4 * modes == LANES
        and cycles == 2 * blocks
        and all(size & (size - 1) == 0 for size in (blocks, modes, cycles, real_groups))
        and 2 * reals * cycles < 2**12
        and 2 * per_block * cycles == LANES
        and cycle_len & (cycle_len - 1) == 0
        and half_len % (8 * LANES) == 0
        and multipoles % (2 * LANES) == 0
        and per_block == 4
        and reals_dev % 16 == 0
        and reals_dev % PARTS == 0
        and cycles % 16 == 0
    )


def phase_tables(col_ids, mode_ids, cycle_len):
    product_ids = col_ids[:, None] * mode_ids[None, :] % cycle_len
    angles = product_ids.astype(jnp.float32) * (2.0 * math.pi / cycle_len)
    return (jnp.cos(angles).astype(jnp.bfloat16), jnp.sin(angles).astype(jnp.bfloat16))


def cycle_offsets(cycle_ids, mode_ids, cycle_len):
    parity = (cycle_ids % 2).astype(jnp.float32)
    shifts = math.pi / cycle_len * parity[:, None] * mode_ids[None, :].astype(jnp.float32)
    return (jnp.cos(shifts), jnp.sin(shifts))


def forward_modes(re_part, im_part):
    summed = lax.psum((re_part, im_part), "grp")
    fourier_pair = (summed[0].astype(jnp.bfloat16), summed[1].astype(jnp.bfloat16))
    fourier_pair = (
        lax.all_gather(fourier_pair[0], "real", axis=0, tiled=True),
        lax.all_gather(fourier_pair[1], "real", axis=0, tiled=True),
    )
    fourier_pair = (
        lax.all_to_all(fourier_pair[0], "blk", split_axis=2, concat_axis=1, tiled=True),
        lax.all_to_all(fourier_pair[1], "blk", split_axis=2, concat_axis=1, tiled=True),
    )
    return fourier_pair


def backward_cycles(partial_value):
    summed = lax.psum_scatter(partial_value, "real", scatter_dimension=0, tiled=True)
    reduced = lax.psum(summed, "grp")
    cycle_pair = lax.all_to_all(
        reduced.astype(jnp.bfloat16), "blk", split_axis=2, concat_axis=3, tiled=True
    )
    return cycle_pair


def per_device(
    sky_data, signal_prev, noise_var, mask_flags, cycle_table, m_table, spectrum, legendre
):
    real_dev, cycle_dev, half_len = sky_data.shape
    cycle_len = half_len * lax.axis_size("grp")
    mode_count = m_table.shape[0]
    col_ids = lax.axis_index("grp") * half_len + jnp.arange(half_len, dtype=jnp.int32)
    cos_tab, sin_tab = phase_tables(col_ids, m_table, cycle_len)
    cos_shift, sin_shift = cycle_offsets(cycle_table, m_table, cycle_len)
    weight = mask_flags.astype(jnp.float32) / (noise_var - 0.5)
    messenger = (weight * sky_data + 2.0 * signal_prev) / (weight + 2.0)
    flat_rows = messenger.astype(jnp.bfloat16).reshape(real_dev * cycle_dev, half_len)
    base_cos = jnp.dot(flat_rows, cos_tab, preferred_element_type=jnp.float32).reshape(
        real_dev, cycle_dev, mode_count
    )
    base_sin = -jnp.dot(flat_rows, sin_tab, preferred_element_type=jnp.float32).reshape(
        real_dev, cycle_dev, mode_count
    )
    norm_scale = cycle_len ** (-0.5)
    re_part = (base_cos * cos_shift + base_sin * sin_shift) * norm_scale
    im_part = (base_sin * cos_shift - base_cos * sin_shift) * norm_scale
    fourier_re, fourier_im = forward_modes(re_part, im_part)
    fourier = jnp.stack([fourier_re, fourier_im], 1)
    coefficients = jnp.einsum(
        "mlr,kcrm->kcml", legendre, fourier, preferred_element_type=jnp.float32
    )
    factor = spectrum / (spectrum + 0.5)
    wiener_alm = coefficients * factor
    total_l = legendre.shape[1] * lax.axis_size("grp") * lax.axis_size("real")
    syn_scale = (legendre.shape[2] / total_l) ** 0.5
    partial_value = (
        jnp.einsum(
            "mlr,kcml->kcrm",
            legendre,
            wiener_alm.astype(jnp.bfloat16),
            preferred_element_type=jnp.float32,
        )
        * syn_scale
    )
    cycle_pair = backward_cycles(partial_value)
    cycle_modes = cycle_pair.astype(jnp.float32)
    modes_re = cycle_modes[:, 0]
    modes_im = cycle_modes[:, 1]
    rotated_re = (modes_re * cos_shift - modes_im * sin_shift).astype(jnp.bfloat16)
    rotated_im = (modes_im * cos_shift + modes_re * sin_shift).astype(jnp.bfloat16)
    contract = (((1,), (1,)), ((), ()))
    pixel_sum = lax.dot_general(
        rotated_re.reshape(-1, mode_count), cos_tab, contract, preferred_element_type=jnp.float32
    )
    pixel_sum = pixel_sum - lax.dot_general(
        rotated_im.reshape(-1, mode_count), sin_tab, contract, preferred_element_type=jnp.float32
    )
    signal_next = (pixel_sum * mode_count ** (-0.5)).reshape(real_dev, cycle_dev, half_len)
    return (wiener_alm, signal_next)


def solution(mesh):
    in_specs = (
        P("real", "blk", "grp"),
        P("real", "blk", "grp"),
        P("blk", "grp"),
        P("blk", "grp"),
        P("blk"),
        P(),
        P(("grp", "real")),
        P("blk", ("grp", "real"), None),
    )
    out_specs = (P(None, None, "blk", ("grp", "real")), P("real", "blk", "grp"))

    def step(sky_data, signal_prev, noise_var, mask_flags, cycle_table, m_table, spectrum, legendre):
        fits = gram_form_fits(mesh, sky_data, m_table, legendre)
        return jax.shard_map(
            gram_program if fits else per_device,
            mesh=mesh,
            in_specs=in_specs,
            out_specs=out_specs,
            check_vma=False,
        )(sky_data, signal_prev, noise_var, mask_flags, cycle_table, m_table, spectrum, legendre)

    return step
```

```python
import functools
import math

import jax
import jax.numpy as jnp
from jax import lax
from jax.experimental import pallas as pl
from jax.experimental.pallas import tpu as pltpu
from jax.sharding import PartitionSpec as P

LANES = 128
NT = (((1,), (1,)), ((), ()))
AXES = ("grp", "blk", "real")
PARTS = 2
FORWARD_VMEM = 32 << 20
BACKWARD_VMEM = 16 << 20


def unit_cosine(units, half_turn):
    wrapped = units & (2 * half_turn - 1)
    folded = jnp.minimum(wrapped, 2 * half_turn - wrapped)
    y = (half_turn // 2 - folded).astype(jnp.float32) * (math.pi / half_turn)
    y2 = y * y
    acc = jnp.full_like(y2, -1.0 / math.factorial(11))
    for order, sign in ((9, 1.0), (7, -1.0), (5, 1.0), (3, -1.0), (1, 1.0)):
        acc = acc * y2 + sign / math.factorial(order)
    return acc * y


def log2(size):
    return size.bit_length() - 1


def lane_ids(shape):
    return lax.broadcasted_iota(jnp.int32, shape, len(shape) - 1)


def row_ids(shape):
    return lax.broadcasted_iota(jnp.int32, shape, len(shape) - 2)


def phase_factors(cycles, orders, cycle_len, half_len, group):
    modes = orders.shape[1]
    orders = jnp.concatenate([orders] * (LANES // modes), axis=1)
    quarter = lane_ids((1, LANES)) >> log2(modes)
    quarter_turn = cycle_len // 2
    row = row_ids((2 * LANES, LANES))
    pixel = (row >> log2(LANES)) * (half_len // 2) + (row & (LANES - 1))
    inner_units = 2 * orders * pixel + ((quarter + 1) >> 1) * quarter_turn
    inner = unit_cosine(inner_units, cycle_len)
    rows = half_len // LANES
    row = row_ids((rows, LANES))
    parity = jnp.where((row & 1) == 0, cycles[:, :1], cycles[:, 1:]) & 1
    pixel = group * half_len + LANES * (row >> 1)
    outer_units = orders * (2 * pixel + parity) + (quarter >> 1) * (3 * quarter_turn)
    outer = unit_cosine(outer_units, cycle_len)
    high = inner.astype(jnp.bfloat16)
    low = (inner - high.astype(jnp.float32)).astype(jnp.bfloat16)
    return jnp.concatenate([high, low], axis=1), outer


def start_copies(sources, targets, sems, first=0):
    copies = [
        pltpu.make_async_copy(source, target, sems.at[first + i])
        for i, (source, target) in enumerate(zip(sources, targets))
    ]
    for copy in copies:
        copy.start()
    return copies


def selections(place_ref, pick_ref, per_block, reals):
    block = lax.axis_index("blk")
    blocks, real_groups = lax.axis_size("blk"), lax.axis_size("real")
    modes, cycles, half = per_block * blocks, 2 * blocks, LANES // 2

    lane = lane_ids((1, LANES))
    row = row_ids((LANES, LANES))
    lane_order = (lane & (half - 1)) >> log2(cycles)
    lane_row = (lane & 1) * half + (lane >> log2(half)) * modes + block * per_block + lane_order
    pick_ref[0] = (row == lane_row).astype(jnp.float32).astype(jnp.bfloat16)
    lane_row = (lane >> log2(half)) * per_block + (lane & (per_block - 1))
    pick_ref[1] = ((row >> log2(cycles)) == lane_row).astype(jnp.float32).astype(jnp.bfloat16)

    spacing = reals + 2
    column = lane_ids((1, place_ref.shape[1]))
    source = (column * (2**16 // spacing + 1)) >> 16
    inside = column - source * spacing
    source = source >> log2(lax.axis_size("grp"))
    source_block = source >> log2(real_groups)
    target = ((source & (real_groups - 1)) * blocks + source_block) * reals + inside
    target = jnp.where(inside < reals, target, blocks * real_groups * reals + source_block)
    place = (row_ids(place_ref.shape) == target).astype(jnp.float32)
    place_ref[...] = place.astype(jnp.bfloat16)


def forward_kernel(
    cycle_len, half_len, syn_scale, reals,
    cycle_hbm, mode_hbm, noise_hbm, mask_hbm, spectrum_hbm, legendre_hbm, sky_hbm, prev_hbm,
    out_ref, inner_ref, outer_ref, place_ref, pick_ref, doubled_ref, factor_ref,
    cycle_ref, mode_ref, noise_ref, mask_ref, spectrum_ref, legendre_ref, sky_ref, prev_ref, gram_ref, sems,
):
    copies = start_copies(
        (cycle_hbm, mode_hbm, sky_hbm, prev_hbm, noise_hbm, mask_hbm, spectrum_hbm, legendre_hbm),
        (cycle_ref, mode_ref, sky_ref, prev_ref, noise_ref, mask_ref, spectrum_ref, legendre_ref),
        sems,
    )
    group = lax.axis_index("grp")
    per_block = legendre_ref.shape[0] // (2 * lax.axis_size("blk"))
    selections(place_ref, pick_ref, per_block, reals)
    copies[0].wait()
    copies[1].wait()
    inner, outer = phase_factors(cycle_ref[...], mode_ref[...], cycle_len, half_len, group)
    inner_ref[...] = inner
    outer_ref[...] = outer
    for copy in copies[2:]:
        copy.wait()
    weight = mask_ref[...].astype(jnp.float32) / (noise_ref[...] - 0.5)
    inverse = 1.0 / (weight + 2.0)
    sky_gain = weight * inverse
    prev_gain = 2.0 * inverse

    table = legendre_ref[...]
    spectrum = spectrum_ref[...]
    factor = spectrum / (spectrum + 0.5)
    doubled_ref[...] = jnp.concatenate([table, table], axis=0)
    factor_ref[...] = factor
    filtered = (table.astype(jnp.float32) * factor).astype(jnp.bfloat16)
    gram = lax.dot_general(table, filtered, NT, preferred_element_type=jnp.float32)
    table_rows = table.shape[0]
    pixel_rows = outer.shape[0]
    blocks, real_groups = lax.axis_size("blk"), lax.axis_size("real")
    cycles = 2 * blocks
    same = (row_ids(gram.shape) >> log2(cycles)) == (lane_ids((1, table_rows)) >> log2(cycles))
    gram = jnp.where(same, gram, 0.0).reshape(table_rows // cycles, cycles, table_rows).sum(axis=0)
    gram = gram * syn_scale
    gram_ref[...] = jnp.concatenate([gram, gram], axis=1)
    even, odd = gram_ref[pl.ds(0, blocks, stride=2), :], gram_ref[pl.ds(1, blocks, stride=2), :]
    gram = jnp.where(lane_ids(even.shape) < LANES // 2, even, odd)
    gram_high = gram.astype(jnp.bfloat16).astype(jnp.float32)
    gram_low = gram - gram_high

    shape = (reals, 2 * pixel_rows, LANES)
    messenger = sky_ref[...].reshape(shape) * sky_gain + prev_ref[...].reshape(shape) * prev_gain
    rows = jnp.concatenate([messenger[:, :pixel_rows], messenger[:, pixel_rows:]], axis=2)
    rows = rows.reshape(-1, 2 * LANES).astype(jnp.bfloat16)
    partial = jnp.dot(rows, inner, preferred_element_type=jnp.float32)
    partial = partial[:, :LANES] + partial[:, LANES:]
    turned = partial.reshape(reals, pixel_rows, LANES) * outer
    summed = turned.reshape(reals, pixel_rows // 8, 8, LANES).sum(axis=1)
    summed = summed.reshape(reals * 8, LANES)
    summed = summed + pltpu.roll(summed, LANES // 2, 1)
    own = (row_ids(summed.shape) & 1) == (lane_ids(summed.shape) >= LANES // 2)
    fourier = jnp.where(own, summed, 0.0).reshape(reals, 8, LANES).sum(axis=1) * cycle_len**-0.5
    rows = []
    for b in range(blocks):
        rows += [fourier, gram_high[b : b + 1], gram_low[b : b + 1]] * (real_groups * lax.axis_size("grp"))
    out_ref[...] = jnp.concatenate(rows, axis=0).astype(jnp.bfloat16)


def backward_kernel(
    blocks, real_groups, reals, parts,
    gathered_ref, inner_ref, outer_ref, place_ref, pick_ref, table_ref, factor_ref,
    wiener_hbm, signal_hbm, wiener_ref, signal_ref, fourier_ref, out_sems,
):
    real_group = lax.axis_index("real")
    cycles = 2 * blocks
    per_block = table_ref.shape[0] // (2 * cycles)
    modes = per_block * blocks
    pixel_rows = outer_ref.shape[0]
    half = LANES // 2
    lane = lane_ids((1, LANES))
    holder = (lane & (modes - 1)) >> log2(per_block)
    lane_block = (lane & (cycles - 1)) >> 1
    total_reals = real_groups * reals
    fourier_rows = blocks * total_reals
    placed = jnp.dot(place_ref[...], gathered_ref[...], preferred_element_type=jnp.float32)
    fourier_ref[...] = placed[:fourier_rows]

    coeff_rows = jnp.dot(
        placed[:fourier_rows].astype(jnp.bfloat16), pick_ref[0], preferred_element_type=jnp.float32
    ).reshape(real_groups, blocks, reals, LANES)
    columns = jnp.zeros((total_reals, LANES), jnp.float32)
    for b in range(blocks):
        one = coeff_rows[:, b].reshape(total_reals, LANES)
        columns = columns + jnp.where(lane_block == b, one, 0.0)
    table = table_ref[...]
    factor = factor_ref[...]
    stores = []
    own = (lane >> log2(cycles)) == row_ids((2 * per_block, LANES))
    upper = row_ids((1, 2 * per_block, LANES)) < per_block
    pieces = jnp.where(own, columns[:, None, :], 0.0).reshape(-1, LANES).astype(jnp.bfloat16)
    filtered = factor * jnp.dot(pieces, table, preferred_element_type=jnp.float32)
    filtered = filtered.reshape(total_reals, 2 * per_block, -1)
    for y in range(real_groups):
        span = slice(y * reals, (y + 1) * reals)
        for pair in range(wiener_ref.shape[2]):
            one, two = (
                filtered[span, :, tile * LANES : (tile + 1) * LANES] for tile in (2 * pair, 2 * pair + 1)
            )
            wiener_ref[span, 0, pair] = jnp.where(upper, one, pltpu.roll(two, per_block, 1))
            wiener_ref[span, 1, pair] = jnp.where(upper, pltpu.roll(one, per_block, 1), two)
        span = pl.ds(y * reals, reals)
        stores += start_copies([wiener_ref.at[span]], [wiener_hbm.at[span]], out_sems, len(stores))

    gram_all = jnp.where(
        (lane & (cycles - 1)) == row_ids((cycles, LANES)), placed[fourier_rows:, None, :], 0.0
    ).reshape(blocks * cycles, LANES)
    gram_high = gram_all.astype(jnp.bfloat16)
    gram_low = (gram_all - gram_high.astype(jnp.float32)).astype(jnp.bfloat16)
    gram_rows = jnp.dot(
        jnp.concatenate([gram_high, gram_low], axis=1),
        jnp.concatenate([pick_ref[1], pick_ref[1]], axis=0),
        preferred_element_type=jnp.float32,
    ).reshape(blocks, cycles, LANES)
    gram = jnp.zeros((cycles, LANES), jnp.float32)
    for b in range(blocks):
        gram = gram + jnp.where(holder == b, gram_rows[b], 0.0)

    first = lane < half
    cycle_modes = jnp.zeros((reals, LANES), jnp.float32)
    for b in range(blocks):
        first_row = pl.multiple_of((real_group * blocks + b) * reals, reals)
        pair = fourier_ref[pl.ds(first_row, reals), :]
        turned = pltpu.roll(pair, half, 1)
        cycle_modes = cycle_modes + jnp.where(first, pair, turned) * gram[2 * b : 2 * b + 1]
        cycle_modes = cycle_modes + jnp.where(first, turned, pair) * gram[2 * b + 1 : 2 * b + 2]
    cycle_modes = cycle_modes * modes**-0.5
    turned = pltpu.roll(cycle_modes, half, 1)
    even = jnp.where(first, cycle_modes, turned)
    odd = jnp.where(first, turned, cycle_modes)
    parity = (row_ids((1, 8, LANES)) & 1) == 0
    spread = jnp.where(parity, even[:, None, :], odd[:, None, :])
    inner = inner_ref[...]
    outer = outer_ref[...].reshape(1, pixel_rows // 8, 8, LANES)
    rotated = (spread[:, None] * outer).reshape(-1, LANES).astype(jnp.bfloat16)
    signal = lax.dot_general(
        jnp.concatenate([rotated, rotated], axis=1), inner, NT, preferred_element_type=jnp.float32
    ).reshape(reals, pixel_rows, 2 * LANES)
    part_reals = reals // parts
    for i in range(parts):
        span = slice(i * part_reals, (i + 1) * part_reals)
        signal_ref[span, 0] = signal[span, :, :LANES]
        signal_ref[span, 1] = signal[span, :, LANES:]
        span = pl.ds(i * part_reals, part_reals)
        stores += start_copies([signal_ref.at[span]], [signal_hbm.at[span]], out_sems, len(stores))
    for store in stores:
        store.wait()


def split_tiles(array):
    lead, rows, columns = array.shape[:-2], array.shape[-2], array.shape[-1]
    split = array.reshape(*lead, rows, columns // LANES, LANES)
    return jnp.swapaxes(split, -2, -3).reshape(-1, LANES)


def gram_program(
    sky_data, signal_prev, noise_var, mask_flags, cycle_table, m_table, spectrum, legendre
):
    reals, cycle_dev, half_len = sky_data.shape
    groups, blocks, real_groups = (lax.axis_size(name) for name in AXES)
    cycle_len = half_len * groups
    per_block, multipoles, cycles = legendre.shape
    total_l = multipoles * groups * real_groups
    tiles = multipoles // LANES
    hbm = pl.BlockSpec(memory_space=pltpu.HBM)
    vmem = pl.BlockSpec(memory_space=pltpu.VMEM)
    orders = m_table[None, :]
    cycles_row = cycle_table[None, :]
    spectrum_row = spectrum[None, :]
    table = legendre.transpose(0, 2, 1).reshape(per_block * cycles, multipoles)
    inputs = (
        cycles_row, orders, split_tiles(noise_var), split_tiles(mask_flags), spectrum_row, table,
        split_tiles(sky_data), split_tiles(signal_prev),
    )
    sources = groups * blocks * real_groups
    total_reals = reals * real_groups
    local, *prepared = pl.pallas_call(
        functools.partial(forward_kernel, cycle_len, half_len, (cycles / total_l) ** 0.5, reals),
        out_shape=(
            jax.ShapeDtypeStruct((sources * (reals + 2), LANES), jnp.bfloat16),
            jax.ShapeDtypeStruct((2 * LANES, 2 * LANES), jnp.bfloat16),
            jax.ShapeDtypeStruct((half_len // LANES, LANES), jnp.float32),
            jax.ShapeDtypeStruct((blocks * (total_reals + 1), sources * (reals + 2)), jnp.bfloat16),
            jax.ShapeDtypeStruct((2, LANES, LANES), jnp.bfloat16),
            jax.ShapeDtypeStruct((2 * table.shape[0], multipoles), jnp.bfloat16),
            jax.ShapeDtypeStruct((1, multipoles), jnp.float32),
        ),
        in_specs=[hbm] * 8,
        out_specs=(vmem,) * 7,
        scratch_shapes=[pltpu.VMEM(x.shape, x.dtype) for x in inputs]
        + [pltpu.VMEM((cycles, LANES), jnp.float32), pltpu.SemaphoreType.DMA((8,))],
        compiler_params=pltpu.CompilerParams(vmem_limit_bytes=FORWARD_VMEM),
    )(*(pltpu.with_memory_space_constraint(x, pltpu.HBM) for x in inputs))
    pairs = local.reshape(sources, reals // 2 + 1, 2, LANES)
    gathered = lax.all_to_all(pairs, ("blk", "real", "grp"), 0, 0, tiled=True).reshape(local.shape)
    outputs = (
        jax.ShapeDtypeStruct((total_reals, 2, tiles // 2, 2 * per_block, LANES), jnp.float32),
        jax.ShapeDtypeStruct((reals, 2, half_len // LANES, LANES), jnp.float32),
    )
    wiener, signal = pl.pallas_call(
        functools.partial(backward_kernel, blocks, real_groups, reals, PARTS),
        out_shape=outputs,
        in_specs=[vmem] * 7,
        out_specs=(hbm, hbm),
        scratch_shapes=[pltpu.VMEM(x.shape, x.dtype) for x in outputs]
        + [pltpu.VMEM((blocks * total_reals, LANES), jnp.float32)]
        + [pltpu.SemaphoreType.DMA((real_groups + PARTS,))],
        compiler_params=pltpu.CompilerParams(vmem_limit_bytes=BACKWARD_VMEM),
    )(gathered, *prepared)
    wiener = wiener.reshape(total_reals, 2, tiles, per_block, LANES).transpose(0, 1, 3, 2, 4)
    signal = signal.reshape(reals, half_len // LANES, cycle_dev, LANES).transpose(0, 2, 1, 3)
    return (
        wiener.reshape(total_reals, 2, per_block, multipoles),
        signal.reshape(sky_data.shape),
    )


def gram_form_fits(mesh, sky_data, m_table, legendre):
    groups, blocks, real_groups = (mesh.shape[name] for name in AXES)
    reals, cycles, cycle_len = sky_data.shape
    modes = m_table.shape[0]
    per_block = modes // blocks
    multipoles = legendre.shape[1] // (groups * real_groups)
    half_len = cycle_len // groups
    reals_dev = reals // real_groups
    return (
        cycles < 2 * reals
        and 4 * modes == LANES
        and cycles == 2 * blocks
        and all(size & (size - 1) == 0 for size in (blocks, modes, cycles, real_groups))
        and 2 * reals * cycles < 2**12
        and 2 * per_block * cycles == LANES
        and cycle_len & (cycle_len - 1) == 0
        and half_len % (8 * LANES) == 0
        and multipoles % (2 * LANES) == 0
        and per_block == 4
        and reals_dev % 16 == 0
        and reals_dev % PARTS == 0
        and cycles % 16 == 0
    )


def phase_tables(col_ids, mode_ids, cycle_len):
    product_ids = col_ids[:, None] * mode_ids[None, :] % cycle_len
    angles = product_ids.astype(jnp.float32) * (2.0 * math.pi / cycle_len)
    return (jnp.cos(angles).astype(jnp.bfloat16), jnp.sin(angles).astype(jnp.bfloat16))


def cycle_offsets(cycle_ids, mode_ids, cycle_len):
    parity = (cycle_ids % 2).astype(jnp.float32)
    shifts = math.pi / cycle_len * parity[:, None] * mode_ids[None, :].astype(jnp.float32)
    return (jnp.cos(shifts), jnp.sin(shifts))


def forward_modes(re_part, im_part):
    summed = lax.psum((re_part, im_part), "grp")
    fourier_pair = (summed[0].astype(jnp.bfloat16), summed[1].astype(jnp.bfloat16))
    fourier_pair = (
        lax.all_gather(fourier_pair[0], "real", axis=0, tiled=True),
        lax.all_gather(fourier_pair[1], "real", axis=0, tiled=True),
    )
    fourier_pair = (
        lax.all_to_all(fourier_pair[0], "blk", split_axis=2, concat_axis=1, tiled=True),
        lax.all_to_all(fourier_pair[1], "blk", split_axis=2, concat_axis=1, tiled=True),
    )
    return fourier_pair


def backward_cycles(partial_value):
    summed = lax.psum_scatter(partial_value, "real", scatter_dimension=0, tiled=True)
    reduced = lax.psum(summed, "grp")
    cycle_pair = lax.all_to_all(
        reduced.astype(jnp.bfloat16), "blk", split_axis=2, concat_axis=3, tiled=True
    )
    return cycle_pair


def per_device(
    sky_data, signal_prev, noise_var, mask_flags, cycle_table, m_table, spectrum, legendre
):
    real_dev, cycle_dev, half_len = sky_data.shape
    cycle_len = half_len * lax.axis_size("grp")
    mode_count = m_table.shape[0]
    col_ids = lax.axis_index("grp") * half_len + jnp.arange(half_len, dtype=jnp.int32)
    cos_tab, sin_tab = phase_tables(col_ids, m_table, cycle_len)
    cos_shift, sin_shift = cycle_offsets(cycle_table, m_table, cycle_len)
    weight = mask_flags.astype(jnp.float32) / (noise_var - 0.5)
    messenger = (weight * sky_data + 2.0 * signal_prev) / (weight + 2.0)
    flat_rows = messenger.astype(jnp.bfloat16).reshape(real_dev * cycle_dev, half_len)
    base_cos = jnp.dot(flat_rows, cos_tab, preferred_element_type=jnp.float32).reshape(
        real_dev, cycle_dev, mode_count
    )
    base_sin = -jnp.dot(flat_rows, sin_tab, preferred_element_type=jnp.float32).reshape(
        real_dev, cycle_dev, mode_count
    )
    norm_scale = cycle_len ** (-0.5)
    re_part = (base_cos * cos_shift + base_sin * sin_shift) * norm_scale
    im_part = (base_sin * cos_shift - base_cos * sin_shift) * norm_scale
    fourier_re, fourier_im = forward_modes(re_part, im_part)
    fourier = jnp.stack([fourier_re, fourier_im], 1)
    coefficients = jnp.einsum(
        "mlr,kcrm->kcml", legendre, fourier, preferred_element_type=jnp.float32
    )
    factor = spectrum / (spectrum + 0.5)
    wiener_alm = coefficients * factor
    total_l = legendre.shape[1] * lax.axis_size("grp") * lax.axis_size("real")
    syn_scale = (legendre.shape[2] / total_l) ** 0.5
    partial_value = (
        jnp.einsum(
            "mlr,kcml->kcrm",
            legendre,
            wiener_alm.astype(jnp.bfloat16),
            preferred_element_type=jnp.float32,
        )
        * syn_scale
    )
    cycle_pair = backward_cycles(partial_value)
    cycle_modes = cycle_pair.astype(jnp.float32)
    modes_re = cycle_modes[:, 0]
    modes_im = cycle_modes[:, 1]
    rotated_re = (modes_re * cos_shift - modes_im * sin_shift).astype(jnp.bfloat16)
    rotated_im = (modes_im * cos_shift + modes_re * sin_shift).astype(jnp.bfloat16)
    contract = (((1,), (1,)), ((), ()))
    pixel_sum = lax.dot_general(
        rotated_re.reshape(-1, mode_count), cos_tab, contract, preferred_element_type=jnp.float32
    )
    pixel_sum = pixel_sum - lax.dot_general(
        rotated_im.reshape(-1, mode_count), sin_tab, contract, preferred_element_type=jnp.float32
    )
    signal_next = (pixel_sum * mode_count ** (-0.5)).reshape(real_dev, cycle_dev, half_len)
    return (wiener_alm, signal_next)


def solution(mesh):
    in_specs = (
        P("real", "blk", "grp"),
        P("real", "blk", "grp"),
        P("blk", "grp"),
        P("blk", "grp"),
        P("blk"),
        P(),
        P(("grp", "real")),
        P("blk", ("grp", "real"), None),
    )
    out_specs = (P(None, None, "blk", ("grp", "real")), P("real", "blk", "grp"))

    def step(sky_data, signal_prev, noise_var, mask_flags, cycle_table, m_table, spectrum, legendre):
        fits = gram_form_fits(mesh, sky_data, m_table, legendre)
        return jax.shard_map(
            gram_program if fits else per_device,
            mesh=mesh,
            in_specs=in_specs,
            out_specs=out_specs,
            check_vma=False,
        )(sky_data, signal_prev, noise_var, mask_flags, cycle_table, m_table, spectrum, legendre)

    return step
```

```python
import functools
import math

import jax
import jax.numpy as jnp
from jax import lax
from jax.experimental import pallas as pl
from jax.experimental.pallas import tpu as pltpu
from jax.sharding import PartitionSpec as P

LANES = 128
NT = (((1,), (1,)), ((), ()))
AXES = ("grp", "blk", "real")
PARTS = 2
FORWARD_VMEM = 32 << 20
BACKWARD_VMEM = 16 << 20


def unit_cosine(units, half_turn):
    wrapped = units & (2 * half_turn - 1)
    folded = jnp.minimum(wrapped, 2 * half_turn - wrapped)
    y = (half_turn // 2 - folded).astype(jnp.float32) * (math.pi / half_turn)
    y2 = y * y
    acc = jnp.full_like(y2, -1.0 / math.factorial(11))
    for order, sign in ((9, 1.0), (7, -1.0), (5, 1.0), (3, -1.0), (1, 1.0)):
        acc = acc * y2 + sign / math.factorial(order)
    return acc * y


def log2(size):
    return size.bit_length() - 1


def lane_ids(shape):
    return lax.broadcasted_iota(jnp.int32, shape, len(shape) - 1)


def row_ids(shape):
    return lax.broadcasted_iota(jnp.int32, shape, len(shape) - 2)


def phase_factors(cycles, orders, cycle_len, half_len, group):
    modes = orders.shape[1]
    orders = jnp.concatenate([orders] * (LANES // modes), axis=1)
    quarter = lane_ids((1, LANES)) >> log2(modes)
    quarter_turn = cycle_len // 2
    row = row_ids((2 * LANES, LANES))
    pixel = (row >> log2(LANES)) * (half_len // 2) + (row & (LANES - 1))
    inner_units = 2 * orders * pixel + ((quarter + 1) >> 1) * quarter_turn
    inner = unit_cosine(inner_units, cycle_len)
    rows = half_len // LANES
    row = row_ids((rows, LANES))
    parity = jnp.where((row & 1) == 0, cycles[:, :1], cycles[:, 1:]) & 1
    pixel = group * half_len + LANES * (row >> 1)
    outer_units = orders * (2 * pixel + parity) + (quarter >> 1) * (3 * quarter_turn)
    outer = unit_cosine(outer_units, cycle_len)
    high = inner.astype(jnp.bfloat16)
    low = (inner - high.astype(jnp.float32)).astype(jnp.bfloat16)
    return jnp.concatenate([high, low], axis=1), outer


def start_copies(sources, targets, sems, first=0):
    copies = [
        pltpu.make_async_copy(source, target, sems.at[first + i])
        for i, (source, target) in enumerate(zip(sources, targets))
    ]
    for copy in copies:
        copy.start()
    return copies


def selections(place_ref, pick_ref, per_block, reals):
    block = lax.axis_index("blk")
    blocks, real_groups = lax.axis_size("blk"), lax.axis_size("real")
    modes, cycles, half = per_block * blocks, 2 * blocks, LANES // 2

    lane = lane_ids((1, LANES))
    row = row_ids((LANES, LANES))
    lane_order = (lane & (half - 1)) >> log2(cycles)
    lane_row = (lane & 1) * half + (lane >> log2(half)) * modes + block * per_block + lane_order
    pick_ref[0] = (row == lane_row).astype(jnp.float32).astype(jnp.bfloat16)
    lane_row = (lane >> log2(half)) * per_block + (lane & (per_block - 1))
    pick_ref[1] = ((row >> log2(cycles)) == lane_row).astype(jnp.float32).astype(jnp.bfloat16)

    spacing = reals + 2
    column = lane_ids((1, place_ref.shape[1]))
    source = (column * (2**16 // spacing + 1)) >> 16
    inside = column - source * spacing
    source = (-source & (blocks * real_groups * lax.axis_size("grp") - 1)) >> log2(lax.axis_size("grp"))
    source_block = source >> log2(real_groups)
    target = ((source & (real_groups - 1)) * blocks + source_block) * reals + inside
    target = jnp.where(inside < reals, target, blocks * real_groups * reals + source_block)
    place = (row_ids(place_ref.shape) == target).astype(jnp.float32)
    place_ref[...] = place.astype(jnp.bfloat16)


def forward_kernel(
    cycle_len, half_len, syn_scale, reals,
    cycle_hbm, mode_hbm, noise_hbm, mask_hbm, spectrum_hbm, legendre_hbm, sky_hbm, prev_hbm,
    out_ref, inner_ref, outer_ref, place_ref, pick_ref, doubled_ref, factor_ref,
    cycle_ref, mode_ref, noise_ref, mask_ref, spectrum_ref, legendre_ref, sky_ref, prev_ref, gram_ref, sems,
):
    copies = start_copies(
        (cycle_hbm, mode_hbm, sky_hbm, prev_hbm, noise_hbm, mask_hbm, spectrum_hbm, legendre_hbm),
        (cycle_ref, mode_ref, sky_ref, prev_ref, noise_ref, mask_ref, spectrum_ref, legendre_ref),
        sems,
    )
    group = lax.axis_index("grp")
    per_block = legendre_ref.shape[0] // (2 * lax.axis_size("blk"))
    selections(place_ref, pick_ref, per_block, reals)
    copies[0].wait()
    copies[1].wait()
    inner, outer = phase_factors(cycle_ref[...], mode_ref[...], cycle_len, half_len, group)
    inner_ref[...] = inner
    outer_ref[...] = outer
    for copy in copies[2:]:
        copy.wait()
    weight = mask_ref[...].astype(jnp.float32) / (noise_ref[...] - 0.5)
    inverse = 1.0 / (weight + 2.0)
    sky_gain = weight * inverse
    prev_gain = 2.0 * inverse

    table = legendre_ref[...]
    spectrum = spectrum_ref[...]
    factor = spectrum / (spectrum + 0.5)
    doubled_ref[...] = jnp.concatenate([table, table], axis=0)
    factor_ref[...] = factor
    filtered = (table.astype(jnp.float32) * factor).astype(jnp.bfloat16)
    gram = lax.dot_general(table, filtered, NT, preferred_element_type=jnp.float32)
    table_rows = table.shape[0]
    pixel_rows = outer.shape[0]
    blocks, real_groups = lax.axis_size("blk"), lax.axis_size("real")
    cycles = 2 * blocks
    same = (row_ids(gram.shape) >> log2(cycles)) == (lane_ids((1, table_rows)) >> log2(cycles))
    gram = jnp.where(same, gram, 0.0).reshape(table_rows // cycles, cycles, table_rows).sum(axis=0)
    gram = gram * syn_scale
    gram_ref[...] = jnp.concatenate([gram, gram], axis=1)
    even, odd = gram_ref[pl.ds(0, blocks, stride=2), :], gram_ref[pl.ds(1, blocks, stride=2), :]
    gram = jnp.where(lane_ids(even.shape) < LANES // 2, even, odd)
    gram_high = gram.astype(jnp.bfloat16).astype(jnp.float32)
    gram_low = gram - gram_high

    shape = (reals, 2 * pixel_rows, LANES)
    messenger = sky_ref[...].reshape(shape) * sky_gain + prev_ref[...].reshape(shape) * prev_gain
    rows = jnp.concatenate([messenger[:, :pixel_rows], messenger[:, pixel_rows:]], axis=2)
    rows = rows.reshape(-1, 2 * LANES).astype(jnp.bfloat16)
    partial = jnp.dot(rows, inner, preferred_element_type=jnp.float32)
    partial = partial[:, :LANES] + partial[:, LANES:]
    turned = partial.reshape(reals, pixel_rows, LANES) * outer
    summed = turned.reshape(reals, pixel_rows // 8, 8, LANES).sum(axis=1)
    summed = summed.reshape(reals * 8, LANES)
    summed = summed + pltpu.roll(summed, LANES // 2, 1)
    own = (row_ids(summed.shape) & 1) == (lane_ids(summed.shape) >= LANES // 2)
    fourier = jnp.where(own, summed, 0.0).reshape(reals, 8, LANES).sum(axis=1) * cycle_len**-0.5
    rows = []
    per_blk = real_groups * lax.axis_size("grp")
    for place in range(blocks * per_blk):
        b = -place % (blocks * per_blk) // per_blk
        rows += [fourier, gram_high[b : b + 1], gram_low[b : b + 1]]
    out_ref[...] = jnp.concatenate(rows, axis=0).astype(jnp.bfloat16)


def backward_kernel(
    blocks, real_groups, reals, parts,
    gathered_ref, inner_ref, outer_ref, place_ref, pick_ref, table_ref, factor_ref,
    wiener_hbm, signal_hbm, wiener_ref, signal_ref, fourier_ref, out_sems,
):
    real_group = lax.axis_index("real")
    cycles = 2 * blocks
    per_block = table_ref.shape[0] // (2 * cycles)
    modes = per_block * blocks
    pixel_rows = outer_ref.shape[0]
    half = LANES // 2
    lane = lane_ids((1, LANES))
    holder = (lane & (modes - 1)) >> log2(per_block)
    lane_block = (lane & (cycles - 1)) >> 1
    total_reals = real_groups * reals
    fourier_rows = blocks * total_reals
    placed = jnp.dot(place_ref[...], gathered_ref[...], preferred_element_type=jnp.float32)
    fourier_ref[...] = placed[:fourier_rows]

    coeff_rows = jnp.dot(
        placed[:fourier_rows].astype(jnp.bfloat16), pick_ref[0], preferred_element_type=jnp.float32
    ).reshape(real_groups, blocks, reals, LANES)
    columns = jnp.zeros((total_reals, LANES), jnp.float32)
    for b in range(blocks):
        one = coeff_rows[:, b].reshape(total_reals, LANES)
        columns = columns + jnp.where(lane_block == b, one, 0.0)
    table = table_ref[...]
    factor = factor_ref[...]
    stores = []
    own = (lane >> log2(cycles)) == row_ids((2 * per_block, LANES))
    upper = row_ids((1, 2 * per_block, LANES)) < per_block
    pieces = jnp.where(own, columns[:, None, :], 0.0).reshape(-1, LANES).astype(jnp.bfloat16)
    filtered = factor * jnp.dot(pieces, table, preferred_element_type=jnp.float32)
    filtered = filtered.reshape(total_reals, 2 * per_block, -1)
    for y in range(real_groups):
        span = slice(y * reals, (y + 1) * reals)
        for pair in range(wiener_ref.shape[2]):
            one, two = (
                filtered[span, :, tile * LANES : (tile + 1) * LANES] for tile in (2 * pair, 2 * pair + 1)
            )
            wiener_ref[span, 0, pair] = jnp.where(upper, one, pltpu.roll(two, per_block, 1))
            wiener_ref[span, 1, pair] = jnp.where(upper, pltpu.roll(one, per_block, 1), two)
        span = pl.ds(y * reals, reals)
        stores += start_copies([wiener_ref.at[span]], [wiener_hbm.at[span]], out_sems, len(stores))

    gram_all = jnp.where(
        (lane & (cycles - 1)) == row_ids((cycles, LANES)), placed[fourier_rows:, None, :], 0.0
    ).reshape(blocks * cycles, LANES)
    gram_high = gram_all.astype(jnp.bfloat16)
    gram_low = (gram_all - gram_high.astype(jnp.float32)).astype(jnp.bfloat16)
    gram_rows = jnp.dot(
        jnp.concatenate([gram_high, gram_low], axis=1),
        jnp.concatenate([pick_ref[1], pick_ref[1]], axis=0),
        preferred_element_type=jnp.float32,
    ).reshape(blocks, cycles, LANES)
    gram = jnp.zeros((cycles, LANES), jnp.float32)
    for b in range(blocks):
        gram = gram + jnp.where(holder == b, gram_rows[b], 0.0)

    first = lane < half
    cycle_modes = jnp.zeros((reals, LANES), jnp.float32)
    for b in range(blocks):
        first_row = pl.multiple_of((real_group * blocks + b) * reals, reals)
        pair = fourier_ref[pl.ds(first_row, reals), :]
        turned = pltpu.roll(pair, half, 1)
        cycle_modes = cycle_modes + jnp.where(first, pair, turned) * gram[2 * b : 2 * b + 1]
        cycle_modes = cycle_modes + jnp.where(first, turned, pair) * gram[2 * b + 1 : 2 * b + 2]
    cycle_modes = cycle_modes * modes**-0.5
    turned = pltpu.roll(cycle_modes, half, 1)
    even = jnp.where(first, cycle_modes, turned)
    odd = jnp.where(first, turned, cycle_modes)
    parity = (row_ids((1, 8, LANES)) & 1) == 0
    spread = jnp.where(parity, even[:, None, :], odd[:, None, :])
    inner = inner_ref[...]
    outer = outer_ref[...].reshape(1, pixel_rows // 8, 8, LANES)
    rotated = (spread[:, None] * outer).reshape(-1, LANES).astype(jnp.bfloat16)
    signal = lax.dot_general(
        jnp.concatenate([rotated, rotated], axis=1), inner, NT, preferred_element_type=jnp.float32
    ).reshape(reals, pixel_rows, 2 * LANES)
    part_reals = reals // parts
    for i in range(parts):
        span = slice(i * part_reals, (i + 1) * part_reals)
        signal_ref[span, 0] = signal[span, :, :LANES]
        signal_ref[span, 1] = signal[span, :, LANES:]
        span = pl.ds(i * part_reals, part_reals)
        stores += start_copies([signal_ref.at[span]], [signal_hbm.at[span]], out_sems, len(stores))
    for store in stores:
        store.wait()


def split_tiles(array):
    lead, rows, columns = array.shape[:-2], array.shape[-2], array.shape[-1]
    split = array.reshape(*lead, rows, columns // LANES, LANES)
    return jnp.swapaxes(split, -2, -3).reshape(-1, LANES)


def gram_program(
    sky_data, signal_prev, noise_var, mask_flags, cycle_table, m_table, spectrum, legendre
):
    reals, cycle_dev, half_len = sky_data.shape
    groups, blocks, real_groups = (lax.axis_size(name) for name in AXES)
    cycle_len = half_len * groups
    per_block, multipoles, cycles = legendre.shape
    total_l = multipoles * groups * real_groups
    tiles = multipoles // LANES
    hbm = pl.BlockSpec(memory_space=pltpu.HBM)
    vmem = pl.BlockSpec(memory_space=pltpu.VMEM)
    orders = m_table[None, :]
    cycles_row = cycle_table[None, :]
    spectrum_row = spectrum[None, :]
    table = legendre.transpose(0, 2, 1).reshape(per_block * cycles, multipoles)
    inputs = (
        cycles_row, orders, split_tiles(noise_var), split_tiles(mask_flags), spectrum_row, table,
        split_tiles(sky_data), split_tiles(signal_prev),
    )
    sources = groups * blocks * real_groups
    total_reals = reals * real_groups
    local, *prepared = pl.pallas_call(
        functools.partial(forward_kernel, cycle_len, half_len, (cycles / total_l) ** 0.5, reals),
        out_shape=(
            jax.ShapeDtypeStruct((sources * (reals + 2), LANES), jnp.bfloat16),
            jax.ShapeDtypeStruct((2 * LANES, 2 * LANES), jnp.bfloat16),
            jax.ShapeDtypeStruct((half_len // LANES, LANES), jnp.float32),
            jax.ShapeDtypeStruct((blocks * (total_reals + 1), sources * (reals + 2)), jnp.bfloat16),
            jax.ShapeDtypeStruct((2, LANES, LANES), jnp.bfloat16),
            jax.ShapeDtypeStruct((2 * table.shape[0], multipoles), jnp.bfloat16),
            jax.ShapeDtypeStruct((1, multipoles), jnp.float32),
        ),
        in_specs=[hbm] * 8,
        out_specs=(vmem,) * 7,
        scratch_shapes=[pltpu.VMEM(x.shape, x.dtype) for x in inputs]
        + [pltpu.VMEM((cycles, LANES), jnp.float32), pltpu.SemaphoreType.DMA((8,))],
        compiler_params=pltpu.CompilerParams(vmem_limit_bytes=FORWARD_VMEM),
    )(*(pltpu.with_memory_space_constraint(x, pltpu.HBM) for x in inputs))
    pairs = local.reshape(sources, reals // 2 + 1, 2, LANES)
    order = [[-place % sources for place in range(sources)]]
    gathered = lax.all_to_all(pairs, ("blk", "real", "grp"), 0, 0, axis_index_groups=order, tiled=True)
    gathered = gathered.reshape(local.shape)
    outputs = (
        jax.ShapeDtypeStruct((total_reals, 2, tiles // 2, 2 * per_block, LANES), jnp.float32),
        jax.ShapeDtypeStruct((reals, 2, half_len // LANES, LANES), jnp.float32),
    )
    wiener, signal = pl.pallas_call(
        functools.partial(backward_kernel, blocks, real_groups, reals, PARTS),
        out_shape=outputs,
        in_specs=[vmem] * 7,
        out_specs=(hbm, hbm),
        scratch_shapes=[pltpu.VMEM(x.shape, x.dtype) for x in outputs]
        + [pltpu.VMEM((blocks * total_reals, LANES), jnp.float32)]
        + [pltpu.SemaphoreType.DMA((real_groups + PARTS,))],
        compiler_params=pltpu.CompilerParams(vmem_limit_bytes=BACKWARD_VMEM),
    )(gathered, *prepared)
    wiener = wiener.reshape(total_reals, 2, tiles, per_block, LANES).transpose(0, 1, 3, 2, 4)
    signal = signal.reshape(reals, half_len // LANES, cycle_dev, LANES).transpose(0, 2, 1, 3)
    return (
        wiener.reshape(total_reals, 2, per_block, multipoles),
        signal.reshape(sky_data.shape),
    )


def gram_form_fits(mesh, sky_data, m_table, legendre):
    groups, blocks, real_groups = (mesh.shape[name] for name in AXES)
    reals, cycles, cycle_len = sky_data.shape
    modes = m_table.shape[0]
    per_block = modes // blocks
    multipoles = legendre.shape[1] // (groups * real_groups)
    half_len = cycle_len // groups
    reals_dev = reals // real_groups
    return (
        cycles < 2 * reals
        and 4 * modes == LANES
        and cycles == 2 * blocks
        and all(size & (size - 1) == 0 for size in (blocks, modes, cycles, real_groups))
        and 2 * reals * cycles < 2**12
        and 2 * per_block * cycles == LANES
        and cycle_len & (cycle_len - 1) == 0
        and half_len % (8 * LANES) == 0
        and multipoles % (2 * LANES) == 0
        and per_block == 4
        and reals_dev % 16 == 0
        and reals_dev % PARTS == 0
        and cycles % 16 == 0
    )


def phase_tables(col_ids, mode_ids, cycle_len):
    product_ids = col_ids[:, None] * mode_ids[None, :] % cycle_len
    angles = product_ids.astype(jnp.float32) * (2.0 * math.pi / cycle_len)
    return (jnp.cos(angles).astype(jnp.bfloat16), jnp.sin(angles).astype(jnp.bfloat16))


def cycle_offsets(cycle_ids, mode_ids, cycle_len):
    parity = (cycle_ids % 2).astype(jnp.float32)
    shifts = math.pi / cycle_len * parity[:, None] * mode_ids[None, :].astype(jnp.float32)
    return (jnp.cos(shifts), jnp.sin(shifts))


def forward_modes(re_part, im_part):
    summed = lax.psum((re_part, im_part), "grp")
    fourier_pair = (summed[0].astype(jnp.bfloat16), summed[1].astype(jnp.bfloat16))
    fourier_pair = (
        lax.all_gather(fourier_pair[0], "real", axis=0, tiled=True),
        lax.all_gather(fourier_pair[1], "real", axis=0, tiled=True),
    )
    fourier_pair = (
        lax.all_to_all(fourier_pair[0], "blk", split_axis=2, concat_axis=1, tiled=True),
        lax.all_to_all(fourier_pair[1], "blk", split_axis=2, concat_axis=1, tiled=True),
    )
    return fourier_pair


def backward_cycles(partial_value):
    summed = lax.psum_scatter(partial_value, "real", scatter_dimension=0, tiled=True)
    reduced = lax.psum(summed, "grp")
    cycle_pair = lax.all_to_all(
        reduced.astype(jnp.bfloat16), "blk", split_axis=2, concat_axis=3, tiled=True
    )
    return cycle_pair


def per_device(
    sky_data, signal_prev, noise_var, mask_flags, cycle_table, m_table, spectrum, legendre
):
    real_dev, cycle_dev, half_len = sky_data.shape
    cycle_len = half_len * lax.axis_size("grp")
    mode_count = m_table.shape[0]
    col_ids = lax.axis_index("grp") * half_len + jnp.arange(half_len, dtype=jnp.int32)
    cos_tab, sin_tab = phase_tables(col_ids, m_table, cycle_len)
    cos_shift, sin_shift = cycle_offsets(cycle_table, m_table, cycle_len)
    weight = mask_flags.astype(jnp.float32) / (noise_var - 0.5)
    messenger = (weight * sky_data + 2.0 * signal_prev) / (weight + 2.0)
    flat_rows = messenger.astype(jnp.bfloat16).reshape(real_dev * cycle_dev, half_len)
    base_cos = jnp.dot(flat_rows, cos_tab, preferred_element_type=jnp.float32).reshape(
        real_dev, cycle_dev, mode_count
    )
    base_sin = -jnp.dot(flat_rows, sin_tab, preferred_element_type=jnp.float32).reshape(
        real_dev, cycle_dev, mode_count
    )
    norm_scale = cycle_len ** (-0.5)
    re_part = (base_cos * cos_shift + base_sin * sin_shift) * norm_scale
    im_part = (base_sin * cos_shift - base_cos * sin_shift) * norm_scale
    fourier_re, fourier_im = forward_modes(re_part, im_part)
    fourier = jnp.stack([fourier_re, fourier_im], 1)
    coefficients = jnp.einsum(
        "mlr,kcrm->kcml", legendre, fourier, preferred_element_type=jnp.float32
    )
    factor = spectrum / (spectrum + 0.5)
    wiener_alm = coefficients * factor
    total_l = legendre.shape[1] * lax.axis_size("grp") * lax.axis_size("real")
    syn_scale = (legendre.shape[2] / total_l) ** 0.5
    partial_value = (
        jnp.einsum(
            "mlr,kcml->kcrm",
            legendre,
            wiener_alm.astype(jnp.bfloat16),
            preferred_element_type=jnp.float32,
        )
        * syn_scale
    )
    cycle_pair = backward_cycles(partial_value)
    cycle_modes = cycle_pair.astype(jnp.float32)
    modes_re = cycle_modes[:, 0]
    modes_im = cycle_modes[:, 1]
    rotated_re = (modes_re * cos_shift - modes_im * sin_shift).astype(jnp.bfloat16)
    rotated_im = (modes_im * cos_shift + modes_re * sin_shift).astype(jnp.bfloat16)
    contract = (((1,), (1,)), ((), ()))
    pixel_sum = lax.dot_general(
        rotated_re.reshape(-1, mode_count), cos_tab, contract, preferred_element_type=jnp.float32
    )
    pixel_sum = pixel_sum - lax.dot_general(
        rotated_im.reshape(-1, mode_count), sin_tab, contract, preferred_element_type=jnp.float32
    )
    signal_next = (pixel_sum * mode_count ** (-0.5)).reshape(real_dev, cycle_dev, half_len)
    return (wiener_alm, signal_next)


def solution(mesh):
    in_specs = (
        P("real", "blk", "grp"),
        P("real", "blk", "grp"),
        P("blk", "grp"),
        P("blk", "grp"),
        P("blk"),
        P(),
        P(("grp", "real")),
        P("blk", ("grp", "real"), None),
    )
    out_specs = (P(None, None, "blk", ("grp", "real")), P("real", "blk", "grp"))

    def step(sky_data, signal_prev, noise_var, mask_flags, cycle_table, m_table, spectrum, legendre):
        fits = gram_form_fits(mesh, sky_data, m_table, legendre)
        return jax.shard_map(
            gram_program if fits else per_device,
            mesh=mesh,
            in_specs=in_specs,
            out_specs=out_specs,
            check_vma=False,
        )(sky_data, signal_prev, noise_var, mask_flags, cycle_table, m_table, spectrum, legendre)

    return step
```

```python
import functools
import math

import jax
import jax.numpy as jnp
from jax import lax
from jax.experimental import pallas as pl
from jax.experimental.pallas import tpu as pltpu
from jax.sharding import PartitionSpec as P

LANES = 128
NT = (((1,), (1,)), ((), ()))
AXES = ("grp", "blk", "real")
PARTS = 2
FORWARD_VMEM = 32 << 20
BACKWARD_VMEM = 16 << 20


def unit_cosine(units, half_turn):
    wrapped = units & (2 * half_turn - 1)
    folded = jnp.minimum(wrapped, 2 * half_turn - wrapped)
    y = (half_turn // 2 - folded).astype(jnp.float32) * (math.pi / half_turn)
    y2 = y * y
    acc = jnp.full_like(y2, -1.0 / math.factorial(11))
    for order, sign in ((9, 1.0), (7, -1.0), (5, 1.0), (3, -1.0), (1, 1.0)):
        acc = acc * y2 + sign / math.factorial(order)
    return acc * y


def log2(size):
    return size.bit_length() - 1


def lane_ids(shape):
    return lax.broadcasted_iota(jnp.int32, shape, len(shape) - 1)


def row_ids(shape):
    return lax.broadcasted_iota(jnp.int32, shape, len(shape) - 2)


def phase_factors(cycles, orders, cycle_len, half_len, group):
    modes = orders.shape[1]
    orders = jnp.concatenate([orders] * (LANES // modes), axis=1)
    quarter = lane_ids((1, LANES)) >> log2(modes)
    quarter_turn = cycle_len // 2
    row = row_ids((2 * LANES, LANES))
    pixel = (row >> log2(LANES)) * (half_len // 2) + (row & (LANES - 1))
    inner_units = 2 * orders * pixel + ((quarter + 1) >> 1) * quarter_turn
    inner = unit_cosine(inner_units, cycle_len)
    rows = half_len // LANES
    row = row_ids((rows, LANES))
    parity = jnp.where((row & 1) == 0, cycles[:, :1], cycles[:, 1:]) & 1
    pixel = group * half_len + LANES * (row >> 1)
    outer_units = orders * (2 * pixel + parity) + (quarter >> 1) * (3 * quarter_turn)
    outer = unit_cosine(outer_units, cycle_len)
    high = inner.astype(jnp.bfloat16)
    low = (inner - high.astype(jnp.float32)).astype(jnp.bfloat16)
    return jnp.concatenate([high, low], axis=1), outer


def start_copies(sources, targets, sems, first=0):
    copies = [
        pltpu.make_async_copy(source, target, sems.at[first + i])
        for i, (source, target) in enumerate(zip(sources, targets))
    ]
    for copy in copies:
        copy.start()
    return copies


def selections(place_ref, pick_ref, per_block, reals):
    block = lax.axis_index("blk")
    blocks, real_groups = lax.axis_size("blk"), lax.axis_size("real")
    modes, cycles, half = per_block * blocks, 2 * blocks, LANES // 2

    lane = lane_ids((1, LANES))
    row = row_ids((LANES, LANES))
    lane_order = (lane & (half - 1)) >> log2(cycles)
    lane_row = (lane & 1) * half + (lane >> log2(half)) * modes + block * per_block + lane_order
    pick_ref[0] = (row == lane_row).astype(jnp.float32).astype(jnp.bfloat16)
    lane_row = (lane >> log2(half)) * per_block + (lane & (per_block - 1))
    pick_ref[1] = ((row >> log2(cycles)) == lane_row).astype(jnp.float32).astype(jnp.bfloat16)

    spacing = reals + 2
    column = lane_ids((1, place_ref.shape[1]))
    source = (column * (2**16 // spacing + 1)) >> 16
    inside = column - source * spacing
    source = -source & (blocks * real_groups - 1)
    source_block = source >> log2(real_groups)
    target = ((source & (real_groups - 1)) * blocks + source_block) * reals + inside
    target = jnp.where(inside < reals, target, blocks * real_groups * reals + source_block)
    place = (row_ids(place_ref.shape) == target).astype(jnp.float32)
    place_ref[...] = place.astype(jnp.bfloat16)


def forward_kernel(
    cycle_len, half_len, syn_scale, reals,
    cycle_hbm, mode_hbm, noise_hbm, mask_hbm, spectrum_hbm, legendre_hbm, sky_hbm, prev_hbm,
    out_ref, inner_ref, outer_ref, place_ref, pick_ref, doubled_ref, factor_ref,
    cycle_ref, mode_ref, noise_ref, mask_ref, spectrum_ref, legendre_ref, sky_ref, prev_ref, gram_ref, sems,
):
    copies = start_copies(
        (cycle_hbm, mode_hbm, sky_hbm, prev_hbm, noise_hbm, mask_hbm, spectrum_hbm, legendre_hbm),
        (cycle_ref, mode_ref, sky_ref, prev_ref, noise_ref, mask_ref, spectrum_ref, legendre_ref),
        sems,
    )
    group = lax.axis_index("grp")
    per_block = legendre_ref.shape[0] // (2 * lax.axis_size("blk"))
    selections(place_ref, pick_ref, per_block, reals)
    copies[0].wait()
    copies[1].wait()
    inner, outer = phase_factors(cycle_ref[...], mode_ref[...], cycle_len, half_len, group)
    inner_ref[...] = inner
    outer_ref[...] = outer
    for copy in copies[2:]:
        copy.wait()
    weight = mask_ref[...].astype(jnp.float32) / (noise_ref[...] - 0.5)
    inverse = 1.0 / (weight + 2.0)
    sky_gain = weight * inverse
    prev_gain = 2.0 * inverse

    table = legendre_ref[...]
    spectrum = spectrum_ref[...]
    factor = spectrum / (spectrum + 0.5)
    doubled_ref[...] = jnp.concatenate([table, table], axis=0)
    factor_ref[...] = factor
    filtered = (table.astype(jnp.float32) * factor).astype(jnp.bfloat16)
    gram = lax.dot_general(table, filtered, NT, preferred_element_type=jnp.float32)
    table_rows = table.shape[0]
    pixel_rows = outer.shape[0]
    blocks, real_groups = lax.axis_size("blk"), lax.axis_size("real")
    cycles = 2 * blocks
    same = (row_ids(gram.shape) >> log2(cycles)) == (lane_ids((1, table_rows)) >> log2(cycles))
    gram = jnp.where(same, gram, 0.0).reshape(table_rows // cycles, cycles, table_rows).sum(axis=0)
    gram = gram * syn_scale
    gram_ref[...] = jnp.concatenate([gram, gram], axis=1)
    even, odd = gram_ref[pl.ds(0, blocks, stride=2), :], gram_ref[pl.ds(1, blocks, stride=2), :]
    gram = jnp.where(lane_ids(even.shape) < LANES // 2, even, odd)
    gram_high = gram.astype(jnp.bfloat16).astype(jnp.float32)
    gram_low = gram - gram_high

    shape = (reals, 2 * pixel_rows, LANES)
    messenger = sky_ref[...].reshape(shape) * sky_gain + prev_ref[...].reshape(shape) * prev_gain
    rows = jnp.concatenate([messenger[:, :pixel_rows], messenger[:, pixel_rows:]], axis=2)
    rows = rows.reshape(-1, 2 * LANES).astype(jnp.bfloat16)
    partial = jnp.dot(rows, inner, preferred_element_type=jnp.float32)
    partial = partial[:, :LANES] + partial[:, LANES:]
    turned = partial.reshape(reals, pixel_rows, LANES) * outer
    summed = turned.reshape(reals, pixel_rows // 8, 8, LANES).sum(axis=1)
    summed = summed.reshape(reals * 8, LANES)
    summed = summed + pltpu.roll(summed, LANES // 2, 1)
    own = (row_ids(summed.shape) & 1) == (lane_ids(summed.shape) >= LANES // 2)
    fourier = jnp.where(own, summed, 0.0).reshape(reals, 8, LANES).sum(axis=1) * cycle_len**-0.5
    rows = []
    for place in range(blocks * real_groups):
        b = -place % (blocks * real_groups) // real_groups
        rows += [fourier, gram_high[b : b + 1], gram_low[b : b + 1]]
    rows = jnp.concatenate(rows, axis=0).astype(jnp.bfloat16)
    for g in range(lax.axis_size("grp")):
        out_ref[pl.ds(g * rows.shape[0], rows.shape[0]), :] = rows


def backward_kernel(
    blocks, real_groups, reals, parts,
    gathered_ref, inner_ref, outer_ref, place_ref, pick_ref, table_ref, factor_ref,
    wiener_hbm, signal_hbm, wiener_ref, signal_ref, fourier_ref, out_sems,
):
    real_group = lax.axis_index("real")
    cycles = 2 * blocks
    per_block = table_ref.shape[0] // (2 * cycles)
    modes = per_block * blocks
    pixel_rows = outer_ref.shape[0]
    half = LANES // 2
    lane = lane_ids((1, LANES))
    holder = (lane & (modes - 1)) >> log2(per_block)
    lane_block = (lane & (cycles - 1)) >> 1
    total_reals = real_groups * reals
    fourier_rows = blocks * total_reals
    share = place_ref.shape[1]
    sides = jnp.concatenate([gathered_ref[:share, :], gathered_ref[share:, :]], axis=1)
    placed = jnp.dot(place_ref[...], sides, preferred_element_type=jnp.float32)
    placed = placed[:, :LANES] + placed[:, LANES:]
    fourier_ref[...] = placed[:fourier_rows]

    coeff_rows = jnp.dot(
        placed[:fourier_rows].astype(jnp.bfloat16), pick_ref[0], preferred_element_type=jnp.float32
    ).reshape(real_groups, blocks, reals, LANES)
    columns = jnp.zeros((total_reals, LANES), jnp.float32)
    for b in range(blocks):
        one = coeff_rows[:, b].reshape(total_reals, LANES)
        columns = columns + jnp.where(lane_block == b, one, 0.0)
    table = table_ref[...]
    factor = factor_ref[...]
    stores = []
    own = (lane >> log2(cycles)) == row_ids((2 * per_block, LANES))
    upper = row_ids((1, 2 * per_block, LANES)) < per_block
    pieces = jnp.where(own, columns[:, None, :], 0.0).reshape(-1, LANES).astype(jnp.bfloat16)
    filtered = factor * jnp.dot(pieces, table, preferred_element_type=jnp.float32)
    filtered = filtered.reshape(total_reals, 2 * per_block, -1)
    for y in range(real_groups):
        span = slice(y * reals, (y + 1) * reals)
        for pair in range(wiener_ref.shape[2]):
            one, two = (
                filtered[span, :, tile * LANES : (tile + 1) * LANES] for tile in (2 * pair, 2 * pair + 1)
            )
            wiener_ref[span, 0, pair] = jnp.where(upper, one, pltpu.roll(two, per_block, 1))
            wiener_ref[span, 1, pair] = jnp.where(upper, pltpu.roll(one, per_block, 1), two)
        span = pl.ds(y * reals, reals)
        stores += start_copies([wiener_ref.at[span]], [wiener_hbm.at[span]], out_sems, len(stores))

    gram_all = jnp.where(
        (lane & (cycles - 1)) == row_ids((cycles, LANES)), placed[fourier_rows:, None, :], 0.0
    ).reshape(blocks * cycles, LANES)
    gram_high = gram_all.astype(jnp.bfloat16)
    gram_low = (gram_all - gram_high.astype(jnp.float32)).astype(jnp.bfloat16)
    gram_rows = jnp.dot(
        jnp.concatenate([gram_high, gram_low], axis=1),
        jnp.concatenate([pick_ref[1], pick_ref[1]], axis=0),
        preferred_element_type=jnp.float32,
    ).reshape(blocks, cycles, LANES)
    gram = jnp.zeros((cycles, LANES), jnp.float32)
    for b in range(blocks):
        gram = gram + jnp.where(holder == b, gram_rows[b], 0.0)

    first = lane < half
    cycle_modes = jnp.zeros((reals, LANES), jnp.float32)
    for b in range(blocks):
        first_row = pl.multiple_of((real_group * blocks + b) * reals, reals)
        pair = fourier_ref[pl.ds(first_row, reals), :]
        turned = pltpu.roll(pair, half, 1)
        cycle_modes = cycle_modes + jnp.where(first, pair, turned) * gram[2 * b : 2 * b + 1]
        cycle_modes = cycle_modes + jnp.where(first, turned, pair) * gram[2 * b + 1 : 2 * b + 2]
    cycle_modes = cycle_modes * modes**-0.5
    turned = pltpu.roll(cycle_modes, half, 1)
    even = jnp.where(first, cycle_modes, turned)
    odd = jnp.where(first, turned, cycle_modes)
    parity = (row_ids((1, 8, LANES)) & 1) == 0
    spread = jnp.where(parity, even[:, None, :], odd[:, None, :])
    inner = inner_ref[...]
    outer = outer_ref[...].reshape(1, pixel_rows // 8, 8, LANES)
    rotated = (spread[:, None] * outer).reshape(-1, LANES).astype(jnp.bfloat16)
    signal = lax.dot_general(
        jnp.concatenate([rotated, rotated], axis=1), inner, NT, preferred_element_type=jnp.float32
    ).reshape(reals, pixel_rows, 2 * LANES)
    part_reals = reals // parts
    for i in range(parts):
        span = slice(i * part_reals, (i + 1) * part_reals)
        signal_ref[span, 0] = signal[span, :, :LANES]
        signal_ref[span, 1] = signal[span, :, LANES:]
        span = pl.ds(i * part_reals, part_reals)
        stores += start_copies([signal_ref.at[span]], [signal_hbm.at[span]], out_sems, len(stores))
    for store in stores:
        store.wait()


def split_tiles(array):
    lead, rows, columns = array.shape[:-2], array.shape[-2], array.shape[-1]
    split = array.reshape(*lead, rows, columns // LANES, LANES)
    return jnp.swapaxes(split, -2, -3).reshape(-1, LANES)


def gram_program(
    sky_data, signal_prev, noise_var, mask_flags, cycle_table, m_table, spectrum, legendre
):
    reals, cycle_dev, half_len = sky_data.shape
    groups, blocks, real_groups = (lax.axis_size(name) for name in AXES)
    cycle_len = half_len * groups
    per_block, multipoles, cycles = legendre.shape
    total_l = multipoles * groups * real_groups
    tiles = multipoles // LANES
    hbm = pl.BlockSpec(memory_space=pltpu.HBM)
    vmem = pl.BlockSpec(memory_space=pltpu.VMEM)
    orders = m_table[None, :]
    cycles_row = cycle_table[None, :]
    spectrum_row = spectrum[None, :]
    table = legendre.transpose(0, 2, 1).reshape(per_block * cycles, multipoles)
    inputs = (
        cycles_row, orders, split_tiles(noise_var), split_tiles(mask_flags), spectrum_row, table,
        split_tiles(sky_data), split_tiles(signal_prev),
    )
    sources = groups * blocks * real_groups
    total_reals = reals * real_groups
    local, *prepared = pl.pallas_call(
        functools.partial(forward_kernel, cycle_len, half_len, (cycles / total_l) ** 0.5, reals),
        out_shape=(
            jax.ShapeDtypeStruct((sources * (reals + 2), LANES), jnp.bfloat16),
            jax.ShapeDtypeStruct((2 * LANES, 2 * LANES), jnp.bfloat16),
            jax.ShapeDtypeStruct((half_len // LANES, LANES), jnp.float32),
            jax.ShapeDtypeStruct(
                (blocks * (total_reals + 1), blocks * real_groups * (reals + 2)), jnp.bfloat16
            ),
            jax.ShapeDtypeStruct((2, LANES, LANES), jnp.bfloat16),
            jax.ShapeDtypeStruct((2 * table.shape[0], multipoles), jnp.bfloat16),
            jax.ShapeDtypeStruct((1, multipoles), jnp.float32),
        ),
        in_specs=[hbm] * 8,
        out_specs=(vmem,) * 7,
        scratch_shapes=[pltpu.VMEM(x.shape, x.dtype) for x in inputs]
        + [pltpu.VMEM((cycles, LANES), jnp.float32), pltpu.SemaphoreType.DMA((8,))],
        compiler_params=pltpu.CompilerParams(vmem_limit_bytes=FORWARD_VMEM),
    )(*(pltpu.with_memory_space_constraint(x, pltpu.HBM) for x in inputs))
    pairs = local.reshape(sources, reals // 2 + 1, 2, LANES)
    plane = blocks * real_groups
    order = [[g * plane + -place % plane for g in range(groups) for place in range(plane)]]
    gathered = lax.all_to_all(pairs, AXES, 0, 0, axis_index_groups=order, tiled=True)
    gathered = gathered.reshape(local.shape)
    outputs = (
        jax.ShapeDtypeStruct((total_reals, 2, tiles // 2, 2 * per_block, LANES), jnp.float32),
        jax.ShapeDtypeStruct((reals, 2, half_len // LANES, LANES), jnp.float32),
    )
    wiener, signal = pl.pallas_call(
        functools.partial(backward_kernel, blocks, real_groups, reals, PARTS),
        out_shape=outputs,
        in_specs=[vmem] * 7,
        out_specs=(hbm, hbm),
        scratch_shapes=[pltpu.VMEM(x.shape, x.dtype) for x in outputs]
        + [pltpu.VMEM((blocks * total_reals, LANES), jnp.float32)]
        + [pltpu.SemaphoreType.DMA((real_groups + PARTS,))],
        compiler_params=pltpu.CompilerParams(vmem_limit_bytes=BACKWARD_VMEM),
    )(gathered, *prepared)
    wiener = wiener.reshape(total_reals, 2, tiles, per_block, LANES).transpose(0, 1, 3, 2, 4)
    signal = signal.reshape(reals, half_len // LANES, cycle_dev, LANES).transpose(0, 2, 1, 3)
    return (
        wiener.reshape(total_reals, 2, per_block, multipoles),
        signal.reshape(sky_data.shape),
    )


def gram_form_fits(mesh, sky_data, m_table, legendre):
    groups, blocks, real_groups = (mesh.shape[name] for name in AXES)
    reals, cycles, cycle_len = sky_data.shape
    modes = m_table.shape[0]
    per_block = modes // blocks
    multipoles = legendre.shape[1] // (groups * real_groups)
    half_len = cycle_len // groups
    reals_dev = reals // real_groups
    return (
        cycles < 2 * reals
        and 4 * modes == LANES
        and cycles == 2 * blocks
        and all(size & (size - 1) == 0 for size in (blocks, modes, cycles, real_groups))
        and 2 * reals * cycles < 2**12
        and 2 * per_block * cycles == LANES
        and cycle_len & (cycle_len - 1) == 0
        and half_len % (8 * LANES) == 0
        and multipoles % (2 * LANES) == 0
        and per_block == 4
        and reals_dev % 16 == 0
        and reals_dev % PARTS == 0
        and cycles % 16 == 0
    )


def phase_tables(col_ids, mode_ids, cycle_len):
    product_ids = col_ids[:, None] * mode_ids[None, :] % cycle_len
    angles = product_ids.astype(jnp.float32) * (2.0 * math.pi / cycle_len)
    return (jnp.cos(angles).astype(jnp.bfloat16), jnp.sin(angles).astype(jnp.bfloat16))


def cycle_offsets(cycle_ids, mode_ids, cycle_len):
    parity = (cycle_ids % 2).astype(jnp.float32)
    shifts = math.pi / cycle_len * parity[:, None] * mode_ids[None, :].astype(jnp.float32)
    return (jnp.cos(shifts), jnp.sin(shifts))


def forward_modes(re_part, im_part):
    summed = lax.psum((re_part, im_part), "grp")
    fourier_pair = (summed[0].astype(jnp.bfloat16), summed[1].astype(jnp.bfloat16))
    fourier_pair = (
        lax.all_gather(fourier_pair[0], "real", axis=0, tiled=True),
        lax.all_gather(fourier_pair[1], "real", axis=0, tiled=True),
    )
    fourier_pair = (
        lax.all_to_all(fourier_pair[0], "blk", split_axis=2, concat_axis=1, tiled=True),
        lax.all_to_all(fourier_pair[1], "blk", split_axis=2, concat_axis=1, tiled=True),
    )
    return fourier_pair


def backward_cycles(partial_value):
    summed = lax.psum_scatter(partial_value, "real", scatter_dimension=0, tiled=True)
    reduced = lax.psum(summed, "grp")
    cycle_pair = lax.all_to_all(
        reduced.astype(jnp.bfloat16), "blk", split_axis=2, concat_axis=3, tiled=True
    )
    return cycle_pair


def per_device(
    sky_data, signal_prev, noise_var, mask_flags, cycle_table, m_table, spectrum, legendre
):
    real_dev, cycle_dev, half_len = sky_data.shape
    cycle_len = half_len * lax.axis_size("grp")
    mode_count = m_table.shape[0]
    col_ids = lax.axis_index("grp") * half_len + jnp.arange(half_len, dtype=jnp.int32)
    cos_tab, sin_tab = phase_tables(col_ids, m_table, cycle_len)
    cos_shift, sin_shift = cycle_offsets(cycle_table, m_table, cycle_len)
    weight = mask_flags.astype(jnp.float32) / (noise_var - 0.5)
    messenger = (weight * sky_data + 2.0 * signal_prev) / (weight + 2.0)
    flat_rows = messenger.astype(jnp.bfloat16).reshape(real_dev * cycle_dev, half_len)
    base_cos = jnp.dot(flat_rows, cos_tab, preferred_element_type=jnp.float32).reshape(
        real_dev, cycle_dev, mode_count
    )
    base_sin = -jnp.dot(flat_rows, sin_tab, preferred_element_type=jnp.float32).reshape(
        real_dev, cycle_dev, mode_count
    )
    norm_scale = cycle_len ** (-0.5)
    re_part = (base_cos * cos_shift + base_sin * sin_shift) * norm_scale
    im_part = (base_sin * cos_shift - base_cos * sin_shift) * norm_scale
    fourier_re, fourier_im = forward_modes(re_part, im_part)
    fourier = jnp.stack([fourier_re, fourier_im], 1)
    coefficients = jnp.einsum(
        "mlr,kcrm->kcml", legendre, fourier, preferred_element_type=jnp.float32
    )
    factor = spectrum / (spectrum + 0.5)
    wiener_alm = coefficients * factor
    total_l = legendre.shape[1] * lax.axis_size("grp") * lax.axis_size("real")
    syn_scale = (legendre.shape[2] / total_l) ** 0.5
    partial_value = (
        jnp.einsum(
            "mlr,kcml->kcrm",
            legendre,
            wiener_alm.astype(jnp.bfloat16),
            preferred_element_type=jnp.float32,
        )
        * syn_scale
    )
    cycle_pair = backward_cycles(partial_value)
    cycle_modes = cycle_pair.astype(jnp.float32)
    modes_re = cycle_modes[:, 0]
    modes_im = cycle_modes[:, 1]
    rotated_re = (modes_re * cos_shift - modes_im * sin_shift).astype(jnp.bfloat16)
    rotated_im = (modes_im * cos_shift + modes_re * sin_shift).astype(jnp.bfloat16)
    contract = (((1,), (1,)), ((), ()))
    pixel_sum = lax.dot_general(
        rotated_re.reshape(-1, mode_count), cos_tab, contract, preferred_element_type=jnp.float32
    )
    pixel_sum = pixel_sum - lax.dot_general(
        rotated_im.reshape(-1, mode_count), sin_tab, contract, preferred_element_type=jnp.float32
    )
    signal_next = (pixel_sum * mode_count ** (-0.5)).reshape(real_dev, cycle_dev, half_len)
    return (wiener_alm, signal_next)


def solution(mesh):
    in_specs = (
        P("real", "blk", "grp"),
        P("real", "blk", "grp"),
        P("blk", "grp"),
        P("blk", "grp"),
        P("blk"),
        P(),
        P(("grp", "real")),
        P("blk", ("grp", "real"), None),
    )
    out_specs = (P(None, None, "blk", ("grp", "real")), P("real", "blk", "grp"))

    def step(sky_data, signal_prev, noise_var, mask_flags, cycle_table, m_table, spectrum, legendre):
        fits = gram_form_fits(mesh, sky_data, m_table, legendre)
        return jax.shard_map(
            gram_program if fits else per_device,
            mesh=mesh,
            in_specs=in_specs,
            out_specs=out_specs,
            check_vma=False,
        )(sky_data, signal_prev, noise_var, mask_flags, cycle_table, m_table, spectrum, legendre)

    return step
```

```python
import functools
import math

import jax
import jax.numpy as jnp
from jax import lax
from jax.experimental import pallas as pl
from jax.experimental.pallas import tpu as pltpu
from jax.sharding import PartitionSpec as P

LANES = 128
NT = (((1,), (1,)), ((), ()))
AXES = ("grp", "blk", "real")
PARTS = 1
FORWARD_VMEM = 32 << 20
BACKWARD_VMEM = 16 << 20


def unit_cosine(units, half_turn):
    wrapped = units & (2 * half_turn - 1)
    folded = jnp.minimum(wrapped, 2 * half_turn - wrapped)
    y = (half_turn // 2 - folded).astype(jnp.float32) * (math.pi / half_turn)
    y2 = y * y
    acc = jnp.full_like(y2, -1.0 / math.factorial(11))
    for order, sign in ((9, 1.0), (7, -1.0), (5, 1.0), (3, -1.0), (1, 1.0)):
        acc = acc * y2 + sign / math.factorial(order)
    return acc * y


def log2(size):
    return size.bit_length() - 1


def lane_ids(shape):
    return lax.broadcasted_iota(jnp.int32, shape, len(shape) - 1)


def row_ids(shape):
    return lax.broadcasted_iota(jnp.int32, shape, len(shape) - 2)


def phase_factors(cycles, orders, cycle_len, half_len, group):
    modes = orders.shape[1]
    orders = jnp.concatenate([orders] * (LANES // modes), axis=1)
    quarter = lane_ids((1, LANES)) >> log2(modes)
    quarter_turn = cycle_len // 2
    row = row_ids((2 * LANES, LANES))
    pixel = (row >> log2(LANES)) * (half_len // 2) + (row & (LANES - 1))
    inner_units = 2 * orders * pixel + ((quarter + 1) >> 1) * quarter_turn
    inner = unit_cosine(inner_units, cycle_len)
    rows = half_len // LANES
    row = row_ids((rows, LANES))
    parity = jnp.where((row & 1) == 0, cycles[:, :1], cycles[:, 1:]) & 1
    pixel = group * half_len + LANES * (row >> 1)
    outer_units = orders * (2 * pixel + parity) + (quarter >> 1) * (3 * quarter_turn)
    outer = unit_cosine(outer_units, cycle_len)
    high = inner.astype(jnp.bfloat16)
    low = (inner - high.astype(jnp.float32)).astype(jnp.bfloat16)
    return jnp.concatenate([high, low], axis=1), outer


def start_copies(sources, targets, sems, first=0):
    copies = [
        pltpu.make_async_copy(source, target, sems.at[first + i])
        for i, (source, target) in enumerate(zip(sources, targets))
    ]
    for copy in copies:
        copy.start()
    return copies


def selections(place_ref, pick_ref, per_block, reals):
    block = lax.axis_index("blk")
    blocks, real_groups = lax.axis_size("blk"), lax.axis_size("real")
    modes, cycles, half = per_block * blocks, 2 * blocks, LANES // 2

    lane = lane_ids((1, LANES))
    row = row_ids((LANES, LANES))
    lane_order = (lane & (half - 1)) >> log2(cycles)
    lane_row = (lane & 1) * half + (lane >> log2(half)) * modes + block * per_block + lane_order
    pick_ref[0] = (row == lane_row).astype(jnp.float32).astype(jnp.bfloat16)
    lane_row = (lane >> log2(half)) * per_block + (lane & (per_block - 1))
    pick_ref[1] = ((row >> log2(cycles)) == lane_row).astype(jnp.float32).astype(jnp.bfloat16)

    spacing = reals + 2
    column = lane_ids((1, place_ref.shape[1]))
    source = (column * (2**16 // spacing + 1)) >> 16
    inside = column - source * spacing
    source_block = source & (blocks - 1)
    target = source * reals + inside
    target = jnp.where(inside < reals, target, blocks * real_groups * reals + source_block)
    place = (row_ids(place_ref.shape) == target).astype(jnp.float32)
    place_ref[...] = place.astype(jnp.bfloat16)


def forward_kernel(
    cycle_len, half_len, syn_scale, reals,
    cycle_hbm, mode_hbm, noise_hbm, mask_hbm, spectrum_hbm, legendre_hbm, sky_hbm, prev_hbm,
    out_ref, inner_ref, outer_ref, place_ref, pick_ref, doubled_ref, factor_ref,
    cycle_ref, mode_ref, noise_ref, mask_ref, spectrum_ref, legendre_ref, sky_ref, prev_ref, gram_ref, sems,
):
    copies = start_copies(
        (cycle_hbm, mode_hbm, sky_hbm, prev_hbm, noise_hbm, mask_hbm, spectrum_hbm, legendre_hbm),
        (cycle_ref, mode_ref, sky_ref, prev_ref, noise_ref, mask_ref, spectrum_ref, legendre_ref),
        sems,
    )
    group = lax.axis_index("grp")
    per_block = legendre_ref.shape[0] // (2 * lax.axis_size("blk"))
    selections(place_ref, pick_ref, per_block, reals)
    copies[0].wait()
    copies[1].wait()
    inner, outer = phase_factors(cycle_ref[...], mode_ref[...], cycle_len, half_len, group)
    inner_ref[...] = inner
    outer_ref[...] = outer
    for copy in copies[2:]:
        copy.wait()
    weight = mask_ref[...].astype(jnp.float32) / (noise_ref[...] - 0.5)
    inverse = 1.0 / (weight + 2.0)
    sky_gain = weight * inverse
    prev_gain = 2.0 * inverse

    table = legendre_ref[...]
    spectrum = spectrum_ref[...]
    factor = spectrum / (spectrum + 0.5)
    doubled_ref[...] = jnp.concatenate([table, table], axis=0)
    factor_ref[...] = factor
    filtered = (table.astype(jnp.float32) * factor).astype(jnp.bfloat16)
    gram = lax.dot_general(table, filtered, NT, preferred_element_type=jnp.float32)
    table_rows = table.shape[0]
    pixel_rows = outer.shape[0]
    blocks, real_groups = lax.axis_size("blk"), lax.axis_size("real")
    cycles = 2 * blocks
    same = (row_ids(gram.shape) >> log2(cycles)) == (lane_ids((1, table_rows)) >> log2(cycles))
    gram = jnp.where(same, gram, 0.0).reshape(table_rows // cycles, cycles, table_rows).sum(axis=0)
    gram = gram * syn_scale
    gram_ref[...] = jnp.concatenate([gram, gram], axis=1)
    even, odd = gram_ref[pl.ds(0, blocks, stride=2), :], gram_ref[pl.ds(1, blocks, stride=2), :]
    gram = jnp.where(lane_ids(even.shape) < LANES // 2, even, odd)
    gram_high = gram.astype(jnp.bfloat16).astype(jnp.float32)
    gram_low = gram - gram_high

    shape = (reals, 2 * pixel_rows, LANES)
    messenger = sky_ref[...].reshape(shape) * sky_gain + prev_ref[...].reshape(shape) * prev_gain
    rows = jnp.concatenate([messenger[:, :pixel_rows], messenger[:, pixel_rows:]], axis=2)
    rows = rows.reshape(-1, 2 * LANES).astype(jnp.bfloat16)
    partial = jnp.dot(rows, inner, preferred_element_type=jnp.float32)
    partial = partial[:, :LANES] + partial[:, LANES:]
    turned = partial.reshape(reals, pixel_rows, LANES) * outer
    summed = turned.reshape(reals, pixel_rows // 8, 8, LANES).sum(axis=1)
    summed = summed.reshape(reals * 8, LANES)
    summed = summed + pltpu.roll(summed, LANES // 2, 1)
    own = (row_ids(summed.shape) & 1) == (lane_ids(summed.shape) >= LANES // 2)
    fourier = jnp.where(own, summed, 0.0).reshape(reals, 8, LANES).sum(axis=1) * cycle_len**-0.5
    rows = []
    for b in range(blocks):
        rows += [fourier, gram_high[b : b + 1], gram_low[b : b + 1]]
    rows = jnp.concatenate(rows * real_groups, axis=0).astype(jnp.bfloat16)
    for g in range(lax.axis_size("grp")):
        out_ref[pl.ds(g * rows.shape[0], rows.shape[0]), :] = rows


def backward_kernel(
    blocks, real_groups, reals, parts,
    gathered_ref, inner_ref, outer_ref, place_ref, pick_ref, table_ref, factor_ref,
    wiener_hbm, signal_hbm, wiener_ref, signal_ref, fourier_ref, out_sems,
):
    real_group = lax.axis_index("real")
    cycles = 2 * blocks
    per_block = table_ref.shape[0] // (2 * cycles)
    modes = per_block * blocks
    pixel_rows = outer_ref.shape[0]
    half = LANES // 2
    lane = lane_ids((1, LANES))
    holder = (lane & (modes - 1)) >> log2(per_block)
    lane_block = (lane & (cycles - 1)) >> 1
    total_reals = real_groups * reals
    fourier_rows = blocks * total_reals
    share = place_ref.shape[1]
    sides = jnp.concatenate([gathered_ref[:share, :], gathered_ref[share:, :]], axis=1)
    placed = jnp.dot(place_ref[...], sides, preferred_element_type=jnp.float32)
    placed = placed[:, :LANES] + placed[:, LANES:]
    fourier_ref[...] = placed[:fourier_rows]

    coeff_rows = jnp.dot(
        placed[:fourier_rows].astype(jnp.bfloat16), pick_ref[0], preferred_element_type=jnp.float32
    ).reshape(real_groups, blocks, reals, LANES)
    columns = jnp.zeros((total_reals, LANES), jnp.float32)
    for b in range(blocks):
        one = coeff_rows[:, b].reshape(total_reals, LANES)
        columns = columns + jnp.where(lane_block == b, one, 0.0)
    table = table_ref[...]
    factor = factor_ref[...]
    stores = []
    own = (lane >> log2(cycles)) == row_ids((2 * per_block, LANES))
    upper = row_ids((1, 2 * per_block, LANES)) < per_block
    pieces = jnp.where(own, columns[:, None, :], 0.0).reshape(-1, LANES).astype(jnp.bfloat16)
    filtered = factor * jnp.dot(pieces, table, preferred_element_type=jnp.float32)
    filtered = filtered.reshape(total_reals, 2 * per_block, -1)
    for y in range(real_groups):
        span = slice(y * reals, (y + 1) * reals)
        for pair in range(wiener_ref.shape[2]):
            one, two = (
                filtered[span, :, tile * LANES : (tile + 1) * LANES] for tile in (2 * pair, 2 * pair + 1)
            )
            wiener_ref[span, 0, pair] = jnp.where(upper, one, pltpu.roll(two, per_block, 1))
            wiener_ref[span, 1, pair] = jnp.where(upper, pltpu.roll(one, per_block, 1), two)
        span = pl.ds(y * reals, reals)
        stores += start_copies([wiener_ref.at[span]], [wiener_hbm.at[span]], out_sems, len(stores))

    gram_all = jnp.where(
        (lane & (cycles - 1)) == row_ids((cycles, LANES)), placed[fourier_rows:, None, :], 0.0
    ).reshape(blocks * cycles, LANES)
    gram_high = gram_all.astype(jnp.bfloat16)
    gram_low = (gram_all - gram_high.astype(jnp.float32)).astype(jnp.bfloat16)
    gram_rows = jnp.dot(
        jnp.concatenate([gram_high, gram_low], axis=1),
        jnp.concatenate([pick_ref[1], pick_ref[1]], axis=0),
        preferred_element_type=jnp.float32,
    ).reshape(blocks, cycles, LANES)
    gram = jnp.zeros((cycles, LANES), jnp.float32)
    for b in range(blocks):
        gram = gram + jnp.where(holder == b, gram_rows[b], 0.0)

    first = lane < half
    cycle_modes = jnp.zeros((reals, LANES), jnp.float32)
    for b in range(blocks):
        first_row = pl.multiple_of((real_group * blocks + b) * reals, reals)
        pair = fourier_ref[pl.ds(first_row, reals), :]
        turned = pltpu.roll(pair, half, 1)
        cycle_modes = cycle_modes + jnp.where(first, pair, turned) * gram[2 * b : 2 * b + 1]
        cycle_modes = cycle_modes + jnp.where(first, turned, pair) * gram[2 * b + 1 : 2 * b + 2]
    cycle_modes = cycle_modes * modes**-0.5
    turned = pltpu.roll(cycle_modes, half, 1)
    even = jnp.where(first, cycle_modes, turned)
    odd = jnp.where(first, turned, cycle_modes)
    parity = (row_ids((1, 8, LANES)) & 1) == 0
    spread = jnp.where(parity, even[:, None, :], odd[:, None, :])
    inner = inner_ref[...]
    outer = outer_ref[...].reshape(1, pixel_rows // 8, 8, LANES)
    rotated = (spread[:, None] * outer).reshape(-1, LANES).astype(jnp.bfloat16)
    signal = lax.dot_general(
        jnp.concatenate([rotated, rotated], axis=1), inner, NT, preferred_element_type=jnp.float32
    ).reshape(reals, pixel_rows, 2 * LANES)
    part_reals = reals // parts
    for i in range(parts):
        span = slice(i * part_reals, (i + 1) * part_reals)
        signal_ref[span, 0] = signal[span, :, :LANES]
        signal_ref[span, 1] = signal[span, :, LANES:]
        span = pl.ds(i * part_reals, part_reals)
        stores += start_copies([signal_ref.at[span]], [signal_hbm.at[span]], out_sems, len(stores))
    for store in stores:
        store.wait()


def split_tiles(array):
    lead, rows, columns = array.shape[:-2], array.shape[-2], array.shape[-1]
    split = array.reshape(*lead, rows, columns // LANES, LANES)
    return jnp.swapaxes(split, -2, -3).reshape(-1, LANES)


def gram_program(
    sky_data, signal_prev, noise_var, mask_flags, cycle_table, m_table, spectrum, legendre
):
    reals, cycle_dev, half_len = sky_data.shape
    groups, blocks, real_groups = (lax.axis_size(name) for name in AXES)
    cycle_len = half_len * groups
    per_block, multipoles, cycles = legendre.shape
    total_l = multipoles * groups * real_groups
    tiles = multipoles // LANES
    hbm = pl.BlockSpec(memory_space=pltpu.HBM)
    vmem = pl.BlockSpec(memory_space=pltpu.VMEM)
    orders = m_table[None, :]
    cycles_row = cycle_table[None, :]
    spectrum_row = spectrum[None, :]
    table = legendre.transpose(0, 2, 1).reshape(per_block * cycles, multipoles)
    inputs = (
        cycles_row, orders, split_tiles(noise_var), split_tiles(mask_flags), spectrum_row, table,
        split_tiles(sky_data), split_tiles(signal_prev),
    )
    sources = groups * blocks * real_groups
    total_reals = reals * real_groups
    local, *prepared = pl.pallas_call(
        functools.partial(forward_kernel, cycle_len, half_len, (cycles / total_l) ** 0.5, reals),
        out_shape=(
            jax.ShapeDtypeStruct((sources * (reals + 2), LANES), jnp.bfloat16),
            jax.ShapeDtypeStruct((2 * LANES, 2 * LANES), jnp.bfloat16),
            jax.ShapeDtypeStruct((half_len // LANES, LANES), jnp.float32),
            jax.ShapeDtypeStruct(
                (blocks * (total_reals + 1), blocks * real_groups * (reals + 2)), jnp.bfloat16
            ),
            jax.ShapeDtypeStruct((2, LANES, LANES), jnp.bfloat16),
            jax.ShapeDtypeStruct((2 * table.shape[0], multipoles), jnp.bfloat16),
            jax.ShapeDtypeStruct((1, multipoles), jnp.float32),
        ),
        in_specs=[hbm] * 8,
        out_specs=(vmem,) * 7,
        scratch_shapes=[pltpu.VMEM(x.shape, x.dtype) for x in inputs]
        + [pltpu.VMEM((cycles, LANES), jnp.float32), pltpu.SemaphoreType.DMA((8,))],
        compiler_params=pltpu.CompilerParams(vmem_limit_bytes=FORWARD_VMEM),
    )(*(pltpu.with_memory_space_constraint(x, pltpu.HBM) for x in inputs))
    pairs = local.reshape(sources, reals // 2 + 1, 2, LANES)
    gathered = lax.all_to_all(pairs, ("grp", "real", "blk"), 0, 0, tiled=True).reshape(local.shape)
    outputs = (
        jax.ShapeDtypeStruct((total_reals, 2, tiles // 2, 2 * per_block, LANES), jnp.float32),
        jax.ShapeDtypeStruct((reals, 2, half_len // LANES, LANES), jnp.float32),
    )
    wiener, signal = pl.pallas_call(
        functools.partial(backward_kernel, blocks, real_groups, reals, PARTS),
        out_shape=outputs,
        in_specs=[vmem] * 7,
        out_specs=(hbm, hbm),
        scratch_shapes=[pltpu.VMEM(x.shape, x.dtype) for x in outputs]
        + [pltpu.VMEM((blocks * total_reals, LANES), jnp.float32)]
        + [pltpu.SemaphoreType.DMA((real_groups + PARTS,))],
        compiler_params=pltpu.CompilerParams(vmem_limit_bytes=BACKWARD_VMEM),
    )(gathered, *prepared)
    wiener = wiener.reshape(total_reals, 2, tiles, per_block, LANES).transpose(0, 1, 3, 2, 4)
    signal = signal.reshape(reals, half_len // LANES, cycle_dev, LANES).transpose(0, 2, 1, 3)
    return (
        wiener.reshape(total_reals, 2, per_block, multipoles),
        signal.reshape(sky_data.shape),
    )


def gram_form_fits(mesh, sky_data, m_table, legendre):
    groups, blocks, real_groups = (mesh.shape[name] for name in AXES)
    reals, cycles, cycle_len = sky_data.shape
    modes = m_table.shape[0]
    per_block = modes // blocks
    multipoles = legendre.shape[1] // (groups * real_groups)
    half_len = cycle_len // groups
    reals_dev = reals // real_groups
    return (
        cycles < 2 * reals
        and 4 * modes == LANES
        and cycles == 2 * blocks
        and all(size & (size - 1) == 0 for size in (blocks, modes, cycles, real_groups))
        and 2 * reals * cycles < 2**12
        and 2 * per_block * cycles == LANES
        and cycle_len & (cycle_len - 1) == 0
        and half_len % (8 * LANES) == 0
        and multipoles % (2 * LANES) == 0
        and per_block == 4
        and reals_dev % 16 == 0
        and reals_dev % PARTS == 0
        and cycles % 16 == 0
    )


def phase_tables(col_ids, mode_ids, cycle_len):
    product_ids = col_ids[:, None] * mode_ids[None, :] % cycle_len
    angles = product_ids.astype(jnp.float32) * (2.0 * math.pi / cycle_len)
    return (jnp.cos(angles).astype(jnp.bfloat16), jnp.sin(angles).astype(jnp.bfloat16))


def cycle_offsets(cycle_ids, mode_ids, cycle_len):
    parity = (cycle_ids % 2).astype(jnp.float32)
    shifts = math.pi / cycle_len * parity[:, None] * mode_ids[None, :].astype(jnp.float32)
    return (jnp.cos(shifts), jnp.sin(shifts))


def forward_modes(re_part, im_part):
    summed = lax.psum((re_part, im_part), "grp")
    fourier_pair = (summed[0].astype(jnp.bfloat16), summed[1].astype(jnp.bfloat16))
    fourier_pair = (
        lax.all_gather(fourier_pair[0], "real", axis=0, tiled=True),
        lax.all_gather(fourier_pair[1], "real", axis=0, tiled=True),
    )
    fourier_pair = (
        lax.all_to_all(fourier_pair[0], "blk", split_axis=2, concat_axis=1, tiled=True),
        lax.all_to_all(fourier_pair[1], "blk", split_axis=2, concat_axis=1, tiled=True),
    )
    return fourier_pair


def backward_cycles(partial_value):
    summed = lax.psum_scatter(partial_value, "real", scatter_dimension=0, tiled=True)
    reduced = lax.psum(summed, "grp")
    cycle_pair = lax.all_to_all(
        reduced.astype(jnp.bfloat16), "blk", split_axis=2, concat_axis=3, tiled=True
    )
    return cycle_pair


def per_device(
    sky_data, signal_prev, noise_var, mask_flags, cycle_table, m_table, spectrum, legendre
):
    real_dev, cycle_dev, half_len = sky_data.shape
    cycle_len = half_len * lax.axis_size("grp")
    mode_count = m_table.shape[0]
    col_ids = lax.axis_index("grp") * half_len + jnp.arange(half_len, dtype=jnp.int32)
    cos_tab, sin_tab = phase_tables(col_ids, m_table, cycle_len)
    cos_shift, sin_shift = cycle_offsets(cycle_table, m_table, cycle_len)
    weight = mask_flags.astype(jnp.float32) / (noise_var - 0.5)
    messenger = (weight * sky_data + 2.0 * signal_prev) / (weight + 2.0)
    flat_rows = messenger.astype(jnp.bfloat16).reshape(real_dev * cycle_dev, half_len)
    base_cos = jnp.dot(flat_rows, cos_tab, preferred_element_type=jnp.float32).reshape(
        real_dev, cycle_dev, mode_count
    )
    base_sin = -jnp.dot(flat_rows, sin_tab, preferred_element_type=jnp.float32).reshape(
        real_dev, cycle_dev, mode_count
    )
    norm_scale = cycle_len ** (-0.5)
    re_part = (base_cos * cos_shift + base_sin * sin_shift) * norm_scale
    im_part = (base_sin * cos_shift - base_cos * sin_shift) * norm_scale
    fourier_re, fourier_im = forward_modes(re_part, im_part)
    fourier = jnp.stack([fourier_re, fourier_im], 1)
    coefficients = jnp.einsum(
        "mlr,kcrm->kcml", legendre, fourier, preferred_element_type=jnp.float32
    )
    factor = spectrum / (spectrum + 0.5)
    wiener_alm = coefficients * factor
    total_l = legendre.shape[1] * lax.axis_size("grp") * lax.axis_size("real")
    syn_scale = (legendre.shape[2] / total_l) ** 0.5
    partial_value = (
        jnp.einsum(
            "mlr,kcml->kcrm",
            legendre,
            wiener_alm.astype(jnp.bfloat16),
            preferred_element_type=jnp.float32,
        )
        * syn_scale
    )
    cycle_pair = backward_cycles(partial_value)
    cycle_modes = cycle_pair.astype(jnp.float32)
    modes_re = cycle_modes[:, 0]
    modes_im = cycle_modes[:, 1]
    rotated_re = (modes_re * cos_shift - modes_im * sin_shift).astype(jnp.bfloat16)
    rotated_im = (modes_im * cos_shift + modes_re * sin_shift).astype(jnp.bfloat16)
    contract = (((1,), (1,)), ((), ()))
    pixel_sum = lax.dot_general(
        rotated_re.reshape(-1, mode_count), cos_tab, contract, preferred_element_type=jnp.float32
    )
    pixel_sum = pixel_sum - lax.dot_general(
        rotated_im.reshape(-1, mode_count), sin_tab, contract, preferred_element_type=jnp.float32
    )
    signal_next = (pixel_sum * mode_count ** (-0.5)).reshape(real_dev, cycle_dev, half_len)
    return (wiener_alm, signal_next)


def solution(mesh):
    in_specs = (
        P("real", "blk", "grp"),
        P("real", "blk", "grp"),
        P("blk", "grp"),
        P("blk", "grp"),
        P("blk"),
        P(),
        P(("grp", "real")),
        P("blk", ("grp", "real"), None),
    )
    out_specs = (P(None, None, "blk", ("grp", "real")), P("real", "blk", "grp"))

    def step(sky_data, signal_prev, noise_var, mask_flags, cycle_table, m_table, spectrum, legendre):
        fits = gram_form_fits(mesh, sky_data, m_table, legendre)
        return jax.shard_map(
            gram_program if fits else per_device,
            mesh=mesh,
            in_specs=in_specs,
            out_specs=out_specs,
            check_vma=False,
        )(sky_data, signal_prev, noise_var, mask_flags, cycle_table, m_table, spectrum, legendre)

    return step
```
